32 devices in a mesh: segment: 4 (over z), expert: 8 (over y, x, core).
Axes of the slice: x: 2, y: 2, z: 4, core: 2. Of those that a mesh axis runs over, the one named last changes fastest.
Arguments:
- states: bfloat16 [1024, 2048], P('expert'), may hold values from -40 to 40
- cand_len: int32 [16], P('expert'), may hold values from 48 to 64
- routes: int32 [4, 1024, 2], P('segment', 'expert'), may hold values from 0 to 3, as said below
- enc_kv: bfloat16 [4, 32, 2048], P(None, ('segment', 'expert')), may hold values from -900 to 900
- attn_gain: float32 [4, 2048], P('segment'), may hold values from 0.25 to 1.75
- ffn_gain: float32 [4, 2048], P('segment'), may hold values from 0.25 to 1.75
- w_query: bfloat16 [4, 2048, 1024], P('segment'), may hold values from -0.125 to 0.125
- w_out: bfloat16 [4, 1024, 2048], P('segment'), may hold values from -0.1875 to 0.1875
- w_router: bfloat16 [4, 2048, 4], P('segment'), may hold values from -0.125 to 0.125
- w_in: bfloat16 [4, 8, 2048, 2048], P('segment', 'expert'), may hold values from -0.125 to 0.125
- w_down: bfloat16 [4, 8, 2048, 2048], P('segment', 'expert'), may hold values from -0.09375 to 0.09375
Outputs:
- layer_states: bfloat16 [4, 1024, 2048], P('segment', 'expert')
The draws below stay inside these ranges and needn't reach their ends.
Inputs may be any that keep to these rules, and one draw needn't show every extreme that they name: `routes`: the two experts of a row differ. Within one layer and one candidate, at most 40 rows at positions below that candidate's length name any one expert; in every layer some expert is named by exactly 40 such rows of the first of the 2 candidates of every index of expert.
All inputs are finite; a program needn't handle non-finite values.
Results may differ from the reference program's by a relative error of at most 0.023.
Values may be sent and summed in bfloat16 or wider, within the bound.
No kernel may reach another device: no remote copies, remote signals or barrier semaphores. Data moves between devices by JAX's collectives and lax.ppermute only.
A program may use at most 128 MiB of HBM per device.

```python
import math
import jax
import jax.numpy as jnp
from jax import lax

D = 2048
FF = 4096
HEADS = 8
HEAD_DIM = 128
HD = 1024
EXPERTS = 4
CAND_LEN = 64
CAND_DEV = 2
CANDS = 16
TOKENS = 1024
CAP = 40
SRC_LEN = 32
N_SEGMENT = 4
N_EXPERT = 8


def draw_states(key, part):
    key = jax.random.fold_in(key, 3)
    key_entries = jax.random.fold_in(key, 0)
    entries = jax.random.normal(key_entries, (TOKENS, D), jnp.float32)
    return jnp.clip(entries, -40.0, 40.0).astype(jnp.bfloat16)


def draw_enc_kv(key, part):
    key = jax.random.fold_in(key, 5)
    key_entries = jax.random.fold_in(key, 0)
    entries = jax.random.normal(key_entries, (N_SEGMENT, SRC_LEN, 2 * HD), jnp.float32)
    return jnp.clip(entries, -900.0, 900.0).astype(jnp.bfloat16)


def draw_routes(key, part):
    key = jax.random.fold_in(key, 7)
    key_common, key_own, key_order, key_shift = jax.random.split(key, 4)
    blocks = TOKENS // CAND_LEN
    experts = EXPERTS
    capacity = CAP
    others = experts - 1
    shared = jax.random.randint(key_common, (N_SEGMENT, 1, 1), 0, experts)
    own_hot = jax.random.randint(key_own, (N_SEGMENT, blocks, 1), 0, experts)
    leading = (jnp.arange(blocks, dtype=jnp.int32) % CAND_DEV == 0).reshape(1, blocks, 1)
    hot_expert = jnp.where(leading, shared, own_hot)
    row_index = jnp.arange(CAND_LEN, dtype=jnp.int32).reshape(1, 1, CAND_LEN)
    noise = jax.random.randint(key_order, (N_SEGMENT, blocks, CAND_LEN), 0, 1 << 20)
    tail_rows = jnp.where(row_index >= 3 * CAND_LEN // 4, 1 << 20, 0)
    ordering = (noise + tail_rows) * (2 * CAND_LEN) + row_index
    ranking = jnp.argsort(jnp.argsort(ordering, axis=2), axis=2).astype(jnp.int32)
    shifts = jax.random.randint(key_shift, (N_SEGMENT, blocks, 2), 0, others)
    shift_main = shifts[:, :, 0:1]
    shift_hot = shifts[:, :, 1:2]
    later = ranking - capacity
    pick_main = (later + shift_main) % others
    pick_second = (later + shift_main + 1 + later // others % (experts - 2)) % others
    pick_hot = (ranking + shift_hot) % others
    hot_row = ranking < capacity
    route_main = jnp.where(hot_row, hot_expert, (hot_expert + 1 + pick_main) % experts)
    route_second = jnp.where(hot_row, (hot_expert + 1 + pick_hot) % experts, (hot_expert + 1 + pick_second) % experts)
    return jnp.stack([route_main, route_second], axis=3).reshape(N_SEGMENT, TOKENS, 2).astype(jnp.int32)


def touch_ends(values, own_key, least, top_value):
    dims = values.shape
    spot = [jax.random.randint(jax.random.fold_in(own_key, axis), (), 0, dims[axis]) for axis in range(len(dims))]
    values = values.at[tuple(spot)].set(least)
    longest = dims.index(max(dims))
    spot[longest] = (spot[longest] + 1) % dims[longest]
    return values.at[tuple(spot)].set(top_value)


def shard_levels(key, dims, pieces, least, high):
    gain = 1.0
    for dim, shards_of in pieces:
        heights = jax.random.uniform(jax.random.fold_in(jax.random.fold_in(key, 6), dim), (shards_of,), jnp.float32, least / len(pieces), high / len(pieces))
        gain = gain * jnp.repeat(jnp.exp(heights), dims[dim] // shards_of).reshape((-1,) + (1,) * (len(dims) - 1 - dim))
    return gain


def normal_values(stream_key, shape, width, bound, cuts=(), held_as=jnp.bfloat16):
    factor_of = shard_levels(stream_key, shape, cuts, -0.22, 0.18) if cuts else 1.0
    values = jax.random.normal(stream_key, shape, jnp.float32) * width * factor_of
    return jnp.minimum(jnp.maximum(values, -bound), bound).astype(held_as)


def setup_inputs(seed: int = 0) -> dict:
    arg_keys = jax.random.split(jax.random.key(seed), 12)
    states = draw_states(jax.random.fold_in(arg_keys[11], 71), 0)
    cand_len = touch_ends(jax.random.randint(arg_keys[1], (CANDS,), 3 * CAND_LEN // 4, CAND_LEN + 1), jax.random.fold_in(arg_keys[1], 1), 3 * CAND_LEN // 4, CAND_LEN).astype(jnp.int32)
    routes = draw_routes(jax.random.fold_in(arg_keys[11], 71), 0)
    enc_kv = draw_enc_kv(jax.random.fold_in(arg_keys[11], 71), 0)
    attn_gain = jnp.clip(1.0 + 0.15 * jax.random.normal(arg_keys[4], (N_SEGMENT, D), jnp.float32), 0.25, 1.75)
    ffn_gain = jnp.clip(1.0 + 0.15 * jax.random.normal(arg_keys[5], (N_SEGMENT, D), jnp.float32), 0.25, 1.75)
    w_query = normal_values(arg_keys[6], (N_SEGMENT, D, HD), D ** -0.5, 0.125, ((0, 4),))
    w_out = normal_values(arg_keys[7], (N_SEGMENT, HD, D), HD ** -0.5, 0.1875, ((0, 4),))
    w_router = normal_values(arg_keys[8], (N_SEGMENT, D, EXPERTS), D ** -0.5, 0.125, ((0, 4),))
    w_in = normal_values(arg_keys[9], (N_SEGMENT, N_EXPERT, D, FF // 2), D ** -0.5, 0.125, ((0, 4), (1, 8)))
    w_down = normal_values(arg_keys[10], (N_SEGMENT, N_EXPERT, FF // 2, D), FF ** -0.5, 0.09375, ((0, 4), (1, 8)))
    return dict(states=states, cand_len=cand_len, routes=routes, enc_kv=enc_kv, attn_gain=attn_gain, ffn_gain=ffn_gain, w_query=w_query, w_out=w_out, w_router=w_router, w_in=w_in, w_down=w_down)


EPSILON = 1e-05

def normalize(carried, gain_row):
    average = lax.optimization_barrier(jnp.mean(carried, axis=-1, keepdims=True))
    centered = carried - average
    variance = lax.optimization_barrier(jnp.mean(centered * centered, axis=-1, keepdims=True))
    return gain_row * centered * lax.rsqrt(variance + EPSILON)

def route_gates(ffn_input, router, route_block):
    logits = jnp.dot(ffn_input, router, preferred_element_type=jnp.float32)
    labels = jnp.arange(router.shape[1], dtype=jnp.int32)[None, :]
    logit_first = lax.optimization_barrier(jnp.sum(jnp.where(route_block[:, 0:1] == labels, logits, 0.0), axis=1))
    logit_second = lax.optimization_barrier(jnp.sum(jnp.where(route_block[:, 1:2] == labels, logits, 0.0), axis=1))
    gate_first = jax.nn.sigmoid(logit_first - logit_second)
    return jnp.stack([gate_first, 1.0 - gate_first], axis=1)

def slot_table(route_block, live_rows, experts, capacity):
    flat_routes = route_block.reshape(-1)
    usable = jnp.repeat(live_rows, 2)
    labels = jnp.arange(experts, dtype=jnp.int32)[None, :]
    onehot = ((flat_routes[:, None] == labels) & usable[:, None]).astype(jnp.int32)
    before = jnp.cumsum(onehot, axis=0) - onehot
    slot_index = lax.optimization_barrier(jnp.sum(before * onehot, axis=1))
    target = (flat_routes * capacity + slot_index).astype(jnp.int32)
    return (target.reshape(-1, 2), usable.reshape(-1, 2))

def dispatch(ffn_input, target, usable, slot_count):
    labels = jnp.arange(slot_count, dtype=jnp.int32)[:, None]
    select = (labels == target[None, :, 0]) & usable[None, :, 0] | (labels == target[None, :, 1]) & usable[None, :, 1]
    return jnp.dot(select.astype(jnp.bfloat16), ffn_input, preferred_element_type=jnp.float32).astype(jnp.bfloat16)

def combine(expert_out, target, usable, gate_pair):
    picked = jnp.take(expert_out, jnp.where(usable, target, 0), axis=0).astype(jnp.float32)
    weight = jnp.where(usable, gate_pair, 0.0)
    return lax.optimization_barrier(jnp.sum(picked * weight[:, :, None], axis=1))

def expert_rows(operands):
    rows_in, first_mats, second_mats = operands
    first_full = jnp.concatenate([first_mats[0], first_mats[1]], axis=1)
    hidden = jnp.maximum(jnp.dot(rows_in, first_full, preferred_element_type=jnp.float32), 0.0).astype(jnp.bfloat16)
    half_units = first_mats.shape[2]
    partial_first = jnp.dot(hidden[:, :half_units], second_mats[0], preferred_element_type=jnp.float32).astype(jnp.bfloat16)
    partial_second = jnp.dot(hidden[:, half_units:], second_mats[1], preferred_element_type=jnp.float32).astype(jnp.bfloat16)
    return (partial_first.astype(jnp.float32) + partial_second.astype(jnp.float32)).astype(jnp.bfloat16)

def reference(states, cand_len, routes, enc_kv, attn_gain, ffn_gain, w_query, w_out, w_router, w_in, w_down):
    head_total = HEADS * HEAD_DIM
    score_scale = 1.0 / math.sqrt(HEAD_DIM)
    position = jnp.arange(CAND_LEN, dtype=jnp.int32)
    live_rows = position[None, :] < cand_len[:, None]
    slot_count = EXPERTS * CAP
    hidden_state = states
    results = []
    for layer_index in range(N_SEGMENT):
        key_cache = enc_kv[layer_index, :, :head_total].astype(jnp.float32).reshape(SRC_LEN, HEADS, HEAD_DIM)
        value_cache = enc_kv[layer_index, :, head_total:].astype(jnp.float32).reshape(SRC_LEN, HEADS, HEAD_DIM)
        carried = hidden_state.astype(jnp.float32)
        normed = normalize(carried, attn_gain[layer_index]).astype(jnp.bfloat16)
        queries = jnp.dot(normed, w_query[layer_index], preferred_element_type=jnp.float32).astype(jnp.bfloat16)
        query_heads = queries.astype(jnp.float32).reshape(TOKENS, HEADS, HEAD_DIM)
        scores = jnp.einsum('tnk,snk->nts', query_heads, key_cache, precision=lax.Precision.HIGHEST) * score_scale
        largest = lax.optimization_barrier(jnp.max(scores, axis=2, keepdims=True))
        exponent = jnp.exp(scores - largest)
        attn_weights = (exponent / lax.optimization_barrier(jnp.sum(exponent, axis=2, keepdims=True))).astype(jnp.bfloat16)
        context = jnp.einsum('nts,snk->tnk', attn_weights.astype(jnp.float32), value_cache, precision=lax.Precision.HIGHEST)
        context = context.astype(jnp.bfloat16).reshape(TOKENS, head_total)
        after_attn = carried + jnp.dot(context, w_out[layer_index], preferred_element_type=jnp.float32)
        ffn_input = normalize(after_attn, ffn_gain[layer_index]).astype(jnp.bfloat16)
        route_block = routes[layer_index]
        gate_pair = route_gates(ffn_input, w_router[layer_index], route_block)
        target, usable = jax.vmap(slot_table, in_axes=(0, 0, None, None))(route_block.reshape(CANDS, CAND_LEN, 2), live_rows, EXPERTS, CAP)
        buffers = jax.vmap(dispatch, in_axes=(0, 0, 0, None))(ffn_input.reshape(CANDS, CAND_LEN, D), target, usable, slot_count)
        grouped = buffers.reshape(CANDS, EXPERTS, CAP, D).transpose(1, 0, 2, 3).reshape(EXPERTS, CANDS * CAP, D)
        first_mats = w_in[layer_index].reshape(EXPERTS, 2, D, FF // 2)
        second_mats = w_down[layer_index].reshape(EXPERTS, 2, FF // 2, D)
        served = lax.map(expert_rows, (grouped, first_mats, second_mats))
        expert_out = served.reshape(EXPERTS, CANDS, CAP, D).transpose(1, 0, 2, 3).reshape(CANDS, slot_count, D)
        mixture = jax.vmap(combine)(expert_out, target, usable, gate_pair.reshape(CANDS, CAND_LEN, 2))
        hidden_state = (after_attn + mixture.reshape(TOKENS, D)).astype(jnp.bfloat16)
        results.append(hidden_state)
    return jnp.stack(results)
```

```python
import math

import jax
import jax.numpy as jnp
from jax import lax
from jax.sharding import PartitionSpec as P

HEAD_DIM = 128
CAND_LEN = 64
CAND_DEV = 2


EPSILON = 1e-05


def shifted(shard, axis, by):
    length = lax.axis_size(axis)
    pairs = [(i, i + by) for i in range(length) if 0 <= i + by < length]
    return lax.ppermute(shard, axis, pairs)


def normalize(carried, gain_row):
    average = jnp.mean(carried, axis=-1, keepdims=True)
    centered = carried - average
    variance = jnp.mean(centered * centered, axis=-1, keepdims=True)
    return gain_row * centered * lax.rsqrt(variance + EPSILON)


def route_gates(ffn_input, router, route_block):
    logits = jnp.dot(ffn_input, router, preferred_element_type=jnp.float32)
    labels = jnp.arange(router.shape[1], dtype=jnp.int32)[None, :]
    logit_first = jnp.sum(jnp.where(route_block[:, 0:1] == labels, logits, 0.0), axis=1)
    logit_second = jnp.sum(jnp.where(route_block[:, 1:2] == labels, logits, 0.0), axis=1)
    gate_first = jax.nn.sigmoid(logit_first - logit_second)
    return jnp.stack([gate_first, 1.0 - gate_first], axis=1)


def slot_table(route_block, live_rows, experts, capacity):
    flat_routes = route_block.reshape(-1)
    usable = jnp.repeat(live_rows, 2)
    labels = jnp.arange(experts, dtype=jnp.int32)[None, :]
    onehot = ((flat_routes[:, None] == labels) & usable[:, None]).astype(jnp.int32)
    before = jnp.cumsum(onehot, axis=0) - onehot
    slot_index = jnp.sum(before * onehot, axis=1)
    target = flat_routes * capacity + slot_index
    return (target.reshape(-1, 2), usable.reshape(-1, 2))


def dispatch(ffn_input, target, usable, slot_count):
    labels = jnp.arange(slot_count, dtype=jnp.int32)[:, None]
    select = (labels == target[None, :, 0]) & usable[None, :, 0] | (
        labels == target[None, :, 1]
    ) & usable[None, :, 1]
    return jnp.dot(
        select.astype(jnp.bfloat16), ffn_input, preferred_element_type=jnp.float32
    ).astype(jnp.bfloat16)


def combine(expert_out, target, usable, gate_pair):
    picked = jnp.take(expert_out, jnp.where(usable, target, 0), axis=0).astype(jnp.float32)
    weight = jnp.where(usable, gate_pair, 0.0)
    return jnp.sum(picked * weight[:, :, None], axis=1)


def local(
    states, cand_len, routes, enc_kv, attn_gain, ffn_gain, w_query, w_out, w_router, w_in, w_down
):
    segment_index = lax.axis_index("segment")
    n_segment = lax.axis_size("segment")
    n_expert = lax.axis_size("expert")
    model_width = states.shape[1]
    head_total = w_query.shape[2]
    head_count = head_total // HEAD_DIM
    experts = w_router.shape[2]
    capacity = 2 * ((5 * CAND_LEN + 4 * experts - 1) // (4 * experts))
    score_scale = 1.0 / math.sqrt(HEAD_DIM)
    core_pairs = [(i, i ^ 1) for i in range(n_expert)]
    same_core = [list(range(core, n_expert, 2)) for core in range(2)]

    spread = jnp.repeat(enc_kv[:, 0, :], n_expert, axis=0)
    cached = lax.all_to_all(
        spread, ("segment", "expert"), split_axis=0, concat_axis=0, tiled=True
    )
    own_in, own_down = w_in[0, 0], w_down[0, 0]
    other_in = lax.ppermute(own_in, "expert", core_pairs)
    other_down = lax.ppermute(own_down, "expert", core_pairs)

    key_cache = cached[:, :head_total].reshape(-1, head_count, HEAD_DIM)
    value_cache = cached[:, head_total:].reshape(-1, head_count, HEAD_DIM)
    inputs = states.reshape(CAND_DEV, CAND_LEN, model_width)
    route_all = routes[0].reshape(CAND_DEV, CAND_LEN, 2)
    position = jnp.arange(CAND_LEN, dtype=jnp.int32)
    outputs = jnp.zeros((CAND_DEV, CAND_LEN, model_width), jnp.bfloat16)
    incoming = jnp.zeros((CAND_LEN, model_width), jnp.bfloat16)
    step_count = CAND_DEV + n_segment - 1
    for step_index in range(step_count):
        micro_step = step_index - segment_index
        active = (micro_step >= 0) & (micro_step < CAND_DEV)
        micro_index = jnp.clip(micro_step, 0, CAND_DEV - 1)
        fresh_rows = inputs[min(step_index, CAND_DEV - 1)]
        current = jnp.where(segment_index == 0, fresh_rows, incoming)
        route_block = lax.dynamic_index_in_dim(route_all, micro_index, 0, keepdims=False)
        length = lax.dynamic_index_in_dim(cand_len, micro_index, 0, keepdims=False)
        row_count = current.shape[0]
        carried = current.astype(jnp.float32)
        normed = normalize(carried, attn_gain[0]).astype(jnp.bfloat16)
        queries = jnp.dot(normed, w_query[0], preferred_element_type=jnp.float32).astype(
            jnp.bfloat16
        )
        query_heads = queries.reshape(row_count, head_count, HEAD_DIM)
        scores = (
            jnp.einsum("tnk,snk->nts", query_heads, key_cache, preferred_element_type=jnp.float32)
            * score_scale
        )
        largest = jnp.max(scores, axis=2, keepdims=True)
        exponent = jnp.exp(scores - largest)
        attn_weights = (exponent / jnp.sum(exponent, axis=2, keepdims=True)).astype(jnp.bfloat16)
        context = jnp.einsum(
            "nts,snk->tnk", attn_weights, value_cache, preferred_element_type=jnp.float32
        )
        context = context.astype(jnp.bfloat16).reshape(row_count, head_total)
        after_attn = carried + jnp.dot(context, w_out[0], preferred_element_type=jnp.float32)
        ffn_input = normalize(after_attn, ffn_gain[0]).astype(jnp.bfloat16)
        gate_pair = route_gates(ffn_input, w_router[0], route_block)
        target, usable = slot_table(route_block, position < length, experts, capacity)
        outgoing = dispatch(ffn_input, target, usable, experts * capacity)
        received = lax.all_to_all(
            outgoing.reshape(experts, capacity, model_width),
            "expert",
            split_axis=0,
            concat_axis=0,
            axis_index_groups=same_core,
            tiled=True,
        )
        flat_rows = received.reshape(-1, model_width)
        expert_rows = jnp.zeros(flat_rows.shape, jnp.float32)
        for first, second in ((own_in, own_down), (other_in, other_down)):
            hidden = jnp.maximum(
                jnp.dot(flat_rows, first, preferred_element_type=jnp.float32), 0.0
            ).astype(jnp.bfloat16)
            expert_rows += jnp.dot(hidden, second, preferred_element_type=jnp.float32)
        returned = lax.all_to_all(
            expert_rows.astype(jnp.bfloat16).reshape(received.shape),
            "expert",
            split_axis=0,
            concat_axis=0,
            axis_index_groups=same_core,
            tiled=True,
        )
        expert_out = returned.reshape(-1, model_width)
        result = (after_attn + combine(expert_out, target, usable, gate_pair)).astype(jnp.bfloat16)
        previous = lax.dynamic_index_in_dim(outputs, micro_index, 0, keepdims=False)
        outputs = lax.dynamic_update_index_in_dim(
            outputs, jnp.where(active, result, previous), micro_index, 0
        )
        if step_index + 1 < step_count:
            incoming = shifted(result, "segment", 1)
    return outputs.reshape(1, CAND_DEV * CAND_LEN, model_width)


def solution(mesh):
    return jax.shard_map(
        local,
        mesh=mesh,
        in_specs=(
            P("expert", None),
            P("expert"),
            P("segment", "expert", None),
            P(None, ("segment", "expert"), None),
            P("segment", None),
            P("segment", None),
            P("segment", None, None),
            P("segment", None, None),
            P("segment", None, None),
            P("segment", "expert", None, None),
            P("segment", "expert", None, None),
        ),
        out_specs=P("segment", "expert", None),
        check_vma=False,
    )
```

```python
import functools
import math

import jax
import jax.numpy as jnp
from jax import lax
from jax.experimental import pallas as pl
from jax.experimental.pallas import tpu as pltpu
from jax.sharding import PartitionSpec as P

HEAD_DIM = 128
CAND_LEN = 64
CAND_DEV = 2
HIDDEN_CHUNK = 512
MIB = 1 << 20

EPSILON = 1e-05

VMEM = pl.BlockSpec(memory_space=pltpu.VMEM)
SMEM = pl.BlockSpec(memory_space=pltpu.SMEM)
ANY = pl.BlockSpec(memory_space=pl.ANY)
F32 = jnp.float32
BF16 = jnp.bfloat16


def normalize(carried, gain_row):
    average = jnp.mean(carried, axis=-1, keepdims=True)
    centered = carried - average
    variance = jnp.mean(centered * centered, axis=-1, keepdims=True)
    return gain_row * centered * lax.rsqrt(variance + EPSILON)


def dot(left, right, contract=((1,), (0,))):
    return lax.dot_general(left, right, (contract, ((), ())), preferred_element_type=F32)


def attend_kernel(
    step, capacity, segment, cand_len, *refs
):
    if step == 0:
        fresh, refs = refs[0], refs[1:]
    elif step == 1:
        fresh, incoming, refs = refs[0], refs[1], refs[2:]
    else:
        incoming, refs = refs[0], refs[1:]
    (routes, cached, attn_gain, ffn_gain, w_query, w_out, router_t,
     after_ref, outgoing, weights, query_buf, out_buf, context, sems) = refs
    query_copy = pltpu.make_async_copy(w_query, query_buf, sems.at[0])
    out_copy = pltpu.make_async_copy(w_out, out_buf, sems.at[1])
    query_copy.start()
    out_copy.start()

    if step == 0:
        current = fresh[...]
    elif step == 1:
        current = jnp.where(segment[0] == 0, fresh[...], incoming[...])
    else:
        current = incoming[...]
    carried = current.astype(F32)
    normed = normalize(carried, attn_gain[...]).astype(BF16)
    query_copy.wait()
    queries = dot(normed, query_buf[...]).astype(BF16)
    head_total = queries.shape[1]
    scale = 1.0 / math.sqrt(HEAD_DIM)
    for start in range(0, head_total, HEAD_DIM):
        lanes = slice(start, start + HEAD_DIM)
        scores = dot(queries[:, lanes], cached[:, lanes], ((1,), (1,))) * scale
        exponent = jnp.exp(scores - jnp.max(scores, axis=1, keepdims=True))
        share = (exponent / jnp.sum(exponent, axis=1, keepdims=True)).astype(BF16)
        values = cached[:, head_total + start : head_total + start + HEAD_DIM]
        context[:, lanes] = dot(share, values).astype(BF16)
    out_copy.wait()
    after_attn = carried + dot(context[...], out_buf[...])
    after_ref[...] = after_attn
    ffn_input = normalize(after_attn, ffn_gain[...]).astype(BF16)

    rows, experts = after_attn.shape[0], router_t.shape[0]
    logits = dot(ffn_input, router_t[...], ((1,), (1,)))
    micro = jnp.clip(step - segment[0], 0, CAND_DEV - 1)
    live = lax.broadcasted_iota(jnp.int32, (rows, 1), 0) < cand_len[micro]
    route = routes[micro]
    labels = lax.broadcasted_iota(jnp.int32, (rows, experts), 1)
    first, second = route[:, 0:1] == labels, route[:, 1:2] == labels
    logit_first = jnp.sum(jnp.where(first, logits, 0.0), axis=1, keepdims=True)
    logit_second = jnp.sum(jnp.where(second, logits, 0.0), axis=1, keepdims=True)
    gate_first = jax.nn.sigmoid(logit_first - logit_second)
    gate_second = 1.0 - gate_first
    named = jnp.where((first | second) & live, 1.0, 0.0).astype(BF16)
    earlier = lax.broadcasted_iota(jnp.int32, (rows, rows), 1) < lax.broadcasted_iota(
        jnp.int32, (rows, rows), 0
    )
    before = dot(jnp.where(earlier, 1.0, 0.0).astype(BF16), named)
    slots = lax.broadcasted_iota(jnp.int32, (rows, experts * capacity), 1)
    chosen = []
    for mask, column in ((first, 0), (second, 1)):
        slot = jnp.sum(jnp.where(mask, before, 0.0), axis=1, keepdims=True).astype(jnp.int32)
        target = route[:, column : column + 1] * capacity + slot
        chosen.append((slots == target) & live)
    select = jnp.where(chosen[0] | chosen[1], 1.0, 0.0).astype(BF16)
    outgoing[...] = dot(select, ffn_input, ((0,), (0,))).astype(BF16)
    weights[...] = jnp.where(chosen[0], gate_first, 0.0) + jnp.where(chosen[1], gate_second, 0.0)


def attend(step, capacity, segment, cand_len, sources, routes, cached, gains, mats):
    w_query, w_out, router_t = mats
    width, head_total = w_query.shape
    slot_count = router_t.shape[0] * capacity
    specs = [SMEM, SMEM]
    for source in sources:
        if source.shape[0] == CAND_LEN:
            specs.append(VMEM)
        else:
            specs.append(pl.BlockSpec((CAND_LEN, width), lambda i: (min(step, CAND_DEV - 1), 0)))
    return pl.pallas_call(
        functools.partial(attend_kernel, step, capacity),
        grid=(1,),
        in_specs=specs + [VMEM, VMEM, VMEM, VMEM, ANY, ANY, VMEM],
        out_specs=[VMEM, VMEM, VMEM],
        out_shape=[
            jax.ShapeDtypeStruct((CAND_LEN, width), F32),
            jax.ShapeDtypeStruct((slot_count, width), BF16),
            jax.ShapeDtypeStruct((CAND_LEN, slot_count), F32),
        ],
        scratch_shapes=[
            pltpu.VMEM(w_query.shape, BF16),
            pltpu.VMEM(w_out.shape, BF16),
            pltpu.VMEM((CAND_LEN, head_total), BF16),
            pltpu.SemaphoreType.DMA((2,)),
        ],
        compiler_params=pltpu.CompilerParams(vmem_limit_bytes=24 * MIB),
        cost_estimate=pl.CostEstimate(
            flops=6 * CAND_LEN * width * head_total,
            bytes_accessed=4 * width * head_total + 8 * CAND_LEN * width,
            transcendentals=0,
        ),
        name="attend",
    )(segment, cand_len, *sources, routes, cached, *gains, w_query, w_out, router_t)


def expert_kernel(rows, own_in, own_down, other_in, other_down, served, in_buf, down_buf, total, in_sems, down_sems):
    chunks = in_buf.shape[0] // 2
    size = in_buf.shape[2]

    def copies(first_mat, second_mat, base, chunk):
        units = pl.ds(pl.multiple_of(chunk * size, size), size)
        slot = base + chunk
        return (
            pltpu.make_async_copy(first_mat.at[:, units], in_buf.at[slot], in_sems.at[slot]),
            pltpu.make_async_copy(second_mat.at[units, :], down_buf.at[slot], down_sems.at[slot]),
        )

    halves = ((own_in, own_down, 0), (other_in, other_down, chunks))
    for first_mat, second_mat, base in halves:
        for chunk in range(chunks):
            for copy in copies(first_mat, second_mat, base, chunk):
                copy.start()
    total[...] = jnp.zeros_like(total)
    for first_mat, second_mat, base in halves:

        @pl.loop(0, chunks)
        def _(chunk):
            first_copy, second_copy = copies(first_mat, second_mat, base, chunk)
            first_copy.wait()
            hidden = jnp.maximum(dot(rows[...], in_buf[base + chunk]), 0.0).astype(BF16)
            second_copy.wait()
            total[...] += dot(hidden, down_buf[base + chunk])

    served[...] = total[...].astype(BF16)


def expert_rows(rows, own_in, own_down, other_in, other_down):
    count, width = rows.shape
    units = own_in.shape[1]
    chunks = 2 * units // HIDDEN_CHUNK
    return pl.pallas_call(
        expert_kernel,
        in_specs=[VMEM, ANY, ANY, ANY, ANY],
        out_specs=VMEM,
        out_shape=jax.ShapeDtypeStruct(rows.shape, BF16),
        scratch_shapes=[
            pltpu.VMEM((chunks, width, HIDDEN_CHUNK), BF16),
            pltpu.VMEM((chunks, HIDDEN_CHUNK, width), BF16),
            pltpu.VMEM((count, width), F32),
            pltpu.SemaphoreType.DMA((chunks,)),
            pltpu.SemaphoreType.DMA((chunks,)),
        ],
        compiler_params=pltpu.CompilerParams(vmem_limit_bytes=44 * MIB),
        cost_estimate=pl.CostEstimate(
            flops=8 * count * width * units,
            bytes_accessed=8 * width * units + 4 * count * width,
            transcendentals=0,
        ),
        name="experts",
    )(rows, own_in, own_down, other_in, other_down)


def combine_kernel(after_attn, weights, expert_out, result):
    gates = weights[...]
    coarse = gates.astype(BF16)
    fine = (gates - coarse.astype(F32)).astype(BF16)
    rows = expert_out[...]
    result[...] = (after_attn[...] + (dot(coarse, rows) + dot(fine, rows))).astype(BF16)


def combine(after_attn, weights, expert_out):
    return pl.pallas_call(
        combine_kernel,
        in_specs=[VMEM, VMEM, VMEM],
        out_specs=VMEM,
        out_shape=jax.ShapeDtypeStruct(after_attn.shape, BF16),
        compiler_params=pltpu.CompilerParams(vmem_limit_bytes=16 * MIB),
        cost_estimate=pl.CostEstimate(
            flops=4 * weights.size * after_attn.shape[1],
            bytes_accessed=6 * after_attn.size + 2 * expert_out.size,
            transcendentals=0,
        ),
        name="combine",
    )(after_attn, weights, expert_out)


def local(
    states, cand_len, routes, enc_kv, attn_gain, ffn_gain, w_query, w_out, w_router, w_in, w_down
):
    segment_index = lax.axis_index("segment")
    n_segment = lax.axis_size("segment")
    n_expert = lax.axis_size("expert")
    model_width = states.shape[1]
    experts = w_router.shape[2]
    capacity = 2 * ((5 * CAND_LEN + 4 * experts - 1) // (4 * experts))
    core_pairs = [(i, i ^ 1) for i in range(n_expert)]
    same_core = [list(range(core, n_expert, 2)) for core in range(2)]

    def exchange(rows):
        blocks = rows.reshape(experts, capacity, model_width)
        moved = lax.all_to_all(
            blocks, "expert", split_axis=0, concat_axis=0, axis_index_groups=same_core, tiled=True
        )
        return moved.reshape(rows.shape)

    spread = jnp.repeat(enc_kv[:, 0, :], n_expert, axis=0)
    cached = lax.all_to_all(
        spread, ("segment", "expert"), split_axis=0, concat_axis=0, tiled=True
    )
    own = (w_in[0, 0], w_down[0, 0])
    other = tuple(lax.ppermute(mat, "expert", core_pairs) for mat in own)

    segment = segment_index.astype(jnp.int32).reshape(1)
    route_all = routes[0].reshape(CAND_DEV, CAND_LEN, 2)
    mats = (w_query[0], w_out[0], w_router[0].T)
    outputs = jnp.zeros((CAND_DEV, CAND_LEN, model_width), BF16)
    step_count = CAND_DEV + n_segment - 1
    incoming = None
    for step in range(step_count):
        if step == 0:
            sources = (states,)
        elif step < CAND_DEV:
            sources = (states, incoming)
        else:
            sources = (incoming,)
        after_attn, outgoing, weights = attend(
            step, capacity, segment, cand_len, sources, route_all, cached,
            (attn_gain, ffn_gain), mats,
        )
        served = expert_rows(exchange(outgoing), *own, *other)
        result = combine(after_attn, weights, exchange(served))
        if step + 1 < step_count:
            incoming = lax.ppermute(
                result, "segment", [(i, i + 1) for i in range(n_segment - 1)]
            )
        micro_step = step - segment_index
        active = (micro_step >= 0) & (micro_step < CAND_DEV)
        micro_index = jnp.clip(micro_step, 0, CAND_DEV - 1)
        previous = lax.dynamic_index_in_dim(outputs, micro_index, 0, keepdims=False)
        outputs = lax.dynamic_update_index_in_dim(
            outputs, jnp.where(active, result, previous), micro_index, 0
        )
    return outputs.reshape(1, CAND_DEV * CAND_LEN, model_width)


def solution(mesh):
    return jax.shard_map(
        local,
        mesh=mesh,
        in_specs=(
            P("expert", None),
            P("expert"),
            P("segment", "expert", None),
            P(None, ("segment", "expert"), None),
            P("segment", None),
            P("segment", None),
            P("segment", None, None),
            P("segment", None, None),
            P("segment", None, None),
            P("segment", "expert", None, None),
            P("segment", "expert", None, None),
        ),
        out_specs=P("segment", "expert", None),
        check_vma=False,
    )
```

```python
import functools
import math

import jax
import jax.numpy as jnp
from jax import lax
from jax.experimental import pallas as pl
from jax.experimental.pallas import tpu as pltpu
from jax.sharding import PartitionSpec as P

HEAD_DIM = 128
CAND_LEN = 64
CAND_DEV = 2
HIDDEN_CHUNK = 512
MIB = 1 << 20

EPSILON = 1e-05

VMEM = pl.BlockSpec(memory_space=pltpu.VMEM)
SMEM = pl.BlockSpec(memory_space=pltpu.SMEM)
HBM = pl.BlockSpec(memory_space=pltpu.HBM)
F32 = jnp.float32
BF16 = jnp.bfloat16


def in_hbm(*arrays):
    return [pltpu.with_memory_space_constraint(array, pltpu.HBM) for array in arrays]


def normalize(carried, gain_row):
    average = jnp.mean(carried, axis=-1, keepdims=True)
    centered = carried - average
    variance = jnp.mean(centered * centered, axis=-1, keepdims=True)
    return gain_row * centered * lax.rsqrt(variance + EPSILON)


def dot(left, right, contract=((1,), (0,))):
    return lax.dot_general(left, right, (contract, ((), ())), preferred_element_type=F32)


def attend_kernel(step, capacity, scalars, *refs):
    incoming = states = None
    if step > 0:
        incoming, refs = refs[0], refs[1:]
    if step < CAND_DEV:
        states, refs = refs[0], refs[1:]
    (routes, cached, attn_gain, ffn_gain, w_query, w_out, router_t,
     after_ref, outgoing, weights,
     fresh, gain_buf, router_buf, query_buf, out_buf, context, sems) = refs
    segment = scalars[0]
    fills = [
        (attn_gain, gain_buf.at[0]),
        (ffn_gain, gain_buf.at[1]),
        (w_query, query_buf),
        (w_out, out_buf),
        (router_t, router_buf),
    ]
    if states is not None:
        fills.insert(0, (states.at[pl.ds(step * CAND_LEN, CAND_LEN), :], fresh))
    copies = [pltpu.make_async_copy(*pair, sems.at[i]) for i, pair in enumerate(fills)]
    for copy in copies:
        copy.start()
    if states is not None:
        copies[0].wait()
        copies = copies[1:]

    if step == 0:
        current = fresh[...]
    elif step < CAND_DEV:
        current = jnp.where(segment == 0, fresh[...], incoming[...])
    else:
        current = incoming[...]
    copies[0].wait()
    copies[1].wait()
    carried = current.astype(F32)
    normed = normalize(carried, gain_buf[0]).astype(BF16)
    copies[2].wait()
    queries = dot(normed, query_buf[...]).astype(BF16)
    head_total = queries.shape[1]
    scale = 1.0 / math.sqrt(HEAD_DIM)
    for start in range(0, head_total, HEAD_DIM):
        lanes = slice(start, start + HEAD_DIM)
        scores = dot(queries[:, lanes], cached[:, lanes], ((1,), (1,))) * scale
        exponent = jnp.exp(scores - jnp.max(scores, axis=1, keepdims=True))
        share = (exponent / jnp.sum(exponent, axis=1, keepdims=True)).astype(BF16)
        values = cached[:, head_total + start : head_total + start + HEAD_DIM]
        context[:, lanes] = dot(share, values).astype(BF16)
    copies[3].wait()
    after_attn = carried + dot(context[...], out_buf[...])
    after_ref[...] = after_attn
    ffn_input = normalize(after_attn, gain_buf[1]).astype(BF16)

    rows, experts = after_attn.shape[0], router_t.shape[0]
    copies[4].wait()
    logits = dot(ffn_input, router_buf[...], ((1,), (1,)))
    micro = jnp.clip(step - segment, 0, CAND_DEV - 1)
    live = lax.broadcasted_iota(jnp.int32, (rows, 1), 0) < scalars[1 + micro]
    route = routes[micro]
    labels = lax.broadcasted_iota(jnp.int32, (rows, experts), 1)
    first, second = route[:, 0:1] == labels, route[:, 1:2] == labels
    logit_first = jnp.sum(jnp.where(first, logits, 0.0), axis=1, keepdims=True)
    logit_second = jnp.sum(jnp.where(second, logits, 0.0), axis=1, keepdims=True)
    gate_first = jax.nn.sigmoid(logit_first - logit_second)
    gate_second = 1.0 - gate_first
    named = jnp.where((first | second) & live, 1.0, 0.0).astype(BF16)
    earlier = lax.broadcasted_iota(jnp.int32, (rows, rows), 1) < lax.broadcasted_iota(
        jnp.int32, (rows, rows), 0
    )
    before = dot(jnp.where(earlier, 1.0, 0.0).astype(BF16), named)
    slots = lax.broadcasted_iota(jnp.int32, (rows, experts * capacity), 1)
    chosen = []
    for mask, column in ((first, 0), (second, 1)):
        slot = jnp.sum(jnp.where(mask, before, 0.0), axis=1, keepdims=True).astype(jnp.int32)
        target = route[:, column : column + 1] * capacity + slot
        chosen.append((slots == target) & live)
    select = jnp.where(chosen[0] | chosen[1], 1.0, 0.0).astype(BF16)
    outgoing[...] = dot(select, ffn_input, ((0,), (0,))).astype(BF16)
    weights[...] = jnp.where(chosen[0], gate_first, 0.0) + jnp.where(chosen[1], gate_second, 0.0)


def attend(step, capacity, scalars, states, incoming, routes, cached, gains, mats):
    w_query, w_out, router_t = mats
    width, head_total = w_query.shape
    slot_count = router_t.shape[0] * capacity
    sources, specs = [], []
    if step > 0:
        sources.append(incoming)
        specs.append(VMEM)
    if step < CAND_DEV:
        sources += in_hbm(states)
        specs.append(HBM)
    return pl.pallas_call(
        functools.partial(attend_kernel, step, capacity),
        in_specs=[SMEM] + specs + [VMEM, VMEM, HBM, HBM, HBM, HBM, HBM],
        out_specs=[VMEM, VMEM, VMEM],
        out_shape=[
            jax.ShapeDtypeStruct((CAND_LEN, width), F32),
            jax.ShapeDtypeStruct((slot_count, width), BF16),
            jax.ShapeDtypeStruct((CAND_LEN, slot_count), F32),
        ],
        scratch_shapes=[
            pltpu.VMEM((CAND_LEN, width), BF16),
            pltpu.VMEM((2, 1, width), F32),
            pltpu.VMEM(router_t.shape, BF16),
            pltpu.VMEM(w_query.shape, BF16),
            pltpu.VMEM(w_out.shape, BF16),
            pltpu.VMEM((CAND_LEN, head_total), BF16),
            pltpu.SemaphoreType.DMA((6,)),
        ],
        compiler_params=pltpu.CompilerParams(vmem_limit_bytes=24 * MIB),
        cost_estimate=pl.CostEstimate(
            flops=6 * CAND_LEN * width * head_total,
            bytes_accessed=4 * width * head_total + 8 * CAND_LEN * width,
            transcendentals=0,
        ),
        name="attend",
    )(scalars, *sources, routes, cached, *in_hbm(*gains, w_query, w_out, router_t))


def expert_kernel(rows, own_in, own_down, other_in, other_down, served, in_buf, down_buf, total, in_sems, down_sems):
    chunks = in_buf.shape[0] // 2
    size = in_buf.shape[2]

    def copies(first_mat, second_mat, base, chunk):
        units = pl.ds(pl.multiple_of(chunk * size, size), size)
        slot = base + chunk
        return (
            pltpu.make_async_copy(first_mat.at[:, units], in_buf.at[slot], in_sems.at[slot]),
            pltpu.make_async_copy(second_mat.at[units, :], down_buf.at[slot], down_sems.at[slot]),
        )

    halves = ((own_in, own_down, 0), (other_in, other_down, chunks))
    for first_mat, second_mat, base in halves:
        for chunk in range(chunks):
            for copy in copies(first_mat, second_mat, base, chunk):
                copy.start()
    total[...] = jnp.zeros_like(total)
    for first_mat, second_mat, base in halves:

        @pl.loop(0, chunks)
        def _(chunk):
            first_copy, second_copy = copies(first_mat, second_mat, base, chunk)
            first_copy.wait()
            hidden = jnp.maximum(dot(rows[...], in_buf[base + chunk]), 0.0).astype(BF16)
            second_copy.wait()
            total[...] += dot(hidden, down_buf[base + chunk])

    served[...] = total[...].astype(BF16)


def expert_rows(rows, own_in, own_down, other_in, other_down):
    count, width = rows.shape
    units = own_in.shape[1]
    chunks = 2 * units // HIDDEN_CHUNK
    return pl.pallas_call(
        expert_kernel,
        in_specs=[VMEM, HBM, HBM, HBM, HBM],
        out_specs=VMEM,
        out_shape=jax.ShapeDtypeStruct(rows.shape, BF16),
        scratch_shapes=[
            pltpu.VMEM((chunks, width, HIDDEN_CHUNK), BF16),
            pltpu.VMEM((chunks, HIDDEN_CHUNK, width), BF16),
            pltpu.VMEM((count, width), F32),
            pltpu.SemaphoreType.DMA((chunks,)),
            pltpu.SemaphoreType.DMA((chunks,)),
        ],
        compiler_params=pltpu.CompilerParams(vmem_limit_bytes=44 * MIB),
        cost_estimate=pl.CostEstimate(
            flops=8 * count * width * units,
            bytes_accessed=8 * width * units + 4 * count * width,
            transcendentals=0,
        ),
        name="experts",
    )(rows, *in_hbm(own_in, own_down, other_in, other_down))


def combine_kernel(after_attn, weights, expert_out, result):
    gates = weights[...]
    coarse = gates.astype(BF16)
    fine = (gates - coarse.astype(F32)).astype(BF16)
    rows = expert_out[...]
    result[...] = (after_attn[...] + (dot(coarse, rows) + dot(fine, rows))).astype(BF16)


def combine(after_attn, weights, expert_out):
    return pl.pallas_call(
        combine_kernel,
        in_specs=[VMEM, VMEM, VMEM],
        out_specs=VMEM,
        out_shape=jax.ShapeDtypeStruct(after_attn.shape, BF16),
        compiler_params=pltpu.CompilerParams(vmem_limit_bytes=16 * MIB),
        cost_estimate=pl.CostEstimate(
            flops=4 * weights.size * after_attn.shape[1],
            bytes_accessed=6 * after_attn.size + 2 * expert_out.size,
            transcendentals=0,
        ),
        name="combine",
    )(after_attn, weights, expert_out)


def local(
    states, cand_len, routes, enc_kv, attn_gain, ffn_gain, w_query, w_out, w_router, w_in, w_down
):
    segment_index = lax.axis_index("segment")
    n_segment = lax.axis_size("segment")
    n_expert = lax.axis_size("expert")
    model_width = states.shape[1]
    experts = w_router.shape[2]
    capacity = 2 * ((5 * CAND_LEN + 4 * experts - 1) // (4 * experts))
    core_pairs = [(i, i ^ 1) for i in range(n_expert)]
    same_core = [list(range(core, n_expert, 2)) for core in range(2)]

    def exchange(rows):
        blocks = rows.reshape(experts, capacity, model_width)
        moved = lax.all_to_all(
            blocks, "expert", split_axis=0, concat_axis=0, axis_index_groups=same_core, tiled=True
        )
        return moved.reshape(rows.shape)

    spread = jnp.repeat(enc_kv[:, 0, :], n_expert, axis=0)
    cached = lax.all_to_all(
        spread, ("segment", "expert"), split_axis=0, concat_axis=0, tiled=True
    )
    own = (w_in[0, 0], w_down[0, 0])
    other = tuple(lax.ppermute(mat, "expert", core_pairs) for mat in own)

    scalars = jnp.concatenate([segment_index.astype(jnp.int32).reshape(1), cand_len])
    route_all = routes[0].reshape(CAND_DEV, CAND_LEN, 2)
    mats = (w_query[0], w_out[0], w_router[0].T)
    outputs = jnp.zeros((CAND_DEV, CAND_LEN, model_width), BF16)
    step_count = CAND_DEV + n_segment - 1
    incoming = None
    for step in range(step_count):
        after_attn, outgoing, weights = attend(
            step, capacity, scalars, states, incoming, route_all, cached,
            (attn_gain, ffn_gain), mats,
        )
        served = expert_rows(exchange(outgoing), *own, *other)
        result = combine(after_attn, weights, exchange(served))
        if step + 1 < step_count:
            incoming = lax.ppermute(
                result, "segment", [(i, i + 1) for i in range(n_segment - 1)]
            )
        micro_step = step - segment_index
        active = (micro_step >= 0) & (micro_step < CAND_DEV)
        micro_index = jnp.clip(micro_step, 0, CAND_DEV - 1)
        previous = lax.dynamic_index_in_dim(outputs, micro_index, 0, keepdims=False)
        outputs = lax.dynamic_update_index_in_dim(
            outputs, jnp.where(active, result, previous), micro_index, 0
        )
    return outputs.reshape(1, CAND_DEV * CAND_LEN, model_width)


def solution(mesh):
    return jax.shard_map(
        local,
        mesh=mesh,
        in_specs=(
            P("expert", None),
            P("expert"),
            P("segment", "expert", None),
            P(None, ("segment", "expert"), None),
            P("segment", None),
            P("segment", None),
            P("segment", None, None),
            P("segment", None, None),
            P("segment", None, None),
            P("segment", "expert", None, None),
            P("segment", "expert", None, None),
        ),
        out_specs=P("segment", "expert", None),
        check_vma=False,
    )
```

```python
import functools
import math

import jax
import jax.numpy as jnp
from jax import lax
from jax.experimental import pallas as pl
from jax.experimental.pallas import tpu as pltpu
from jax.sharding import PartitionSpec as P

HEAD_DIM = 128
CAND_LEN = 64
CAND_DEV = 2
HIDDEN_CHUNK = 512
MIB = 1 << 20

EPSILON = 1e-05

VMEM = pl.BlockSpec(memory_space=pltpu.VMEM)
SMEM = pl.BlockSpec(memory_space=pltpu.SMEM)
HBM = pl.BlockSpec(memory_space=pltpu.HBM)
F32 = jnp.float32
BF16 = jnp.bfloat16


def in_hbm(*arrays):
    return [pltpu.with_memory_space_constraint(array, pltpu.HBM) for array in arrays]


def in_vmem(*arrays):
    return [pltpu.with_memory_space_constraint(array, pltpu.VMEM) for array in arrays]


def normalize(carried, gain_row):
    average = jnp.mean(carried, axis=-1, keepdims=True)
    centered = carried - average
    variance = jnp.mean(centered * centered, axis=-1, keepdims=True)
    return gain_row * centered * lax.rsqrt(variance + EPSILON)


def dot(left, right, contract=((1,), (0,))):
    return lax.dot_general(left, right, (contract, ((), ())), preferred_element_type=F32)


def attend_kernel(step, capacity, scalars, *refs):
    incoming = states = None
    if step > 0:
        incoming, refs = refs[0], refs[1:]
    if step < CAND_DEV:
        states, refs = refs[0], refs[1:]
    stream = step == 0
    (routes, cached, attn_gain, ffn_gain, router_t, w_query, w_out,
     after_ref, outgoing, weights), refs = refs[:10], refs[10:]
    if stream:
        sources, (w_query, w_out), refs = (w_query, w_out), refs[:2], refs[2:]
    fresh, gain_buf, router_buf, context, sems = refs
    segment = scalars[0]
    fills = [
        (attn_gain, gain_buf.at[0]),
        (ffn_gain, gain_buf.at[1]),
        (router_t, router_buf),
    ]
    if stream:
        fills += [(sources[0], w_query), (sources[1], w_out)]
    if states is not None:
        fills.insert(0, (states.at[pl.ds(step * CAND_LEN, CAND_LEN), :], fresh))
    copies = [pltpu.make_async_copy(*pair, sems.at[i]) for i, pair in enumerate(fills)]
    for copy in copies:
        copy.start()
    if states is not None:
        copies[0].wait()
        copies = copies[1:]

    if step == 0:
        current = fresh[...]
    elif step < CAND_DEV:
        current = jnp.where(segment == 0, fresh[...], incoming[...])
    else:
        current = incoming[...]
    copies[0].wait()
    copies[1].wait()
    carried = current.astype(F32)
    normed = normalize(carried, gain_buf[0]).astype(BF16)
    if stream:
        copies[3].wait()
    queries = dot(normed, w_query[...]).astype(BF16)
    head_total = queries.shape[1]
    scale = 1.0 / math.sqrt(HEAD_DIM)
    for start in range(0, head_total, HEAD_DIM):
        lanes = slice(start, start + HEAD_DIM)
        scores = dot(queries[:, lanes], cached[:, lanes], ((1,), (1,))) * scale
        exponent = jnp.exp(scores - jnp.max(scores, axis=1, keepdims=True))
        share = (exponent / jnp.sum(exponent, axis=1, keepdims=True)).astype(BF16)
        values = cached[:, head_total + start : head_total + start + HEAD_DIM]
        context[:, lanes] = dot(share, values).astype(BF16)
    if stream:
        copies[4].wait()
    after_attn = carried + dot(context[...], w_out[...])
    after_ref[...] = after_attn
    ffn_input = normalize(after_attn, gain_buf[1]).astype(BF16)

    rows, experts = after_attn.shape[0], router_t.shape[0]
    copies[2].wait()
    logits = dot(ffn_input, router_buf[...], ((1,), (1,)))
    micro = jnp.clip(step - segment, 0, CAND_DEV - 1)
    live = lax.broadcasted_iota(jnp.int32, (rows, 1), 0) < scalars[1 + micro]
    route = routes[micro]
    labels = lax.broadcasted_iota(jnp.int32, (rows, experts), 1)
    first, second = route[:, 0:1] == labels, route[:, 1:2] == labels
    logit_first = jnp.sum(jnp.where(first, logits, 0.0), axis=1, keepdims=True)
    logit_second = jnp.sum(jnp.where(second, logits, 0.0), axis=1, keepdims=True)
    gate_first = jax.nn.sigmoid(logit_first - logit_second)
    gate_second = 1.0 - gate_first
    named = jnp.where((first | second) & live, 1.0, 0.0).astype(BF16)
    earlier = lax.broadcasted_iota(jnp.int32, (rows, rows), 1) < lax.broadcasted_iota(
        jnp.int32, (rows, rows), 0
    )
    before = dot(jnp.where(earlier, 1.0, 0.0).astype(BF16), named)
    slots = lax.broadcasted_iota(jnp.int32, (rows, experts * capacity), 1)
    chosen = []
    for mask, column in ((first, 0), (second, 1)):
        slot = jnp.sum(jnp.where(mask, before, 0.0), axis=1, keepdims=True).astype(jnp.int32)
        target = route[:, column : column + 1] * capacity + slot
        chosen.append((slots == target) & live)
    select = jnp.where(chosen[0] | chosen[1], 1.0, 0.0).astype(BF16)
    outgoing[...] = dot(select, ffn_input, ((0,), (0,))).astype(BF16)
    weights[...] = jnp.where(chosen[0], gate_first, 0.0) + jnp.where(chosen[1], gate_second, 0.0)


def attend(step, capacity, scalars, states, incoming, routes, cached, gains, router_t, mats):
    w_query, w_out = mats
    width, head_total = w_query.shape
    slot_count = router_t.shape[0] * capacity
    stream = step == 0
    sources, specs = [], []
    if step > 0:
        sources.append(incoming)
        specs.append(VMEM)
    if step < CAND_DEV:
        sources += in_hbm(states)
        specs.append(HBM)
    out_shape = [
        jax.ShapeDtypeStruct((CAND_LEN, width), F32),
        jax.ShapeDtypeStruct((slot_count, width), BF16),
        jax.ShapeDtypeStruct((CAND_LEN, slot_count), F32),
    ]
    if stream:
        out_shape += [pltpu.VMEM(mat.shape, BF16) for mat in mats]
    outs = pl.pallas_call(
        functools.partial(attend_kernel, step, capacity),
        in_specs=[SMEM] + specs + [VMEM, VMEM, HBM, HBM, HBM] + [HBM if stream else VMEM] * 2,
        out_specs=[VMEM] * len(out_shape),
        out_shape=out_shape,
        scratch_shapes=[
            pltpu.VMEM((CAND_LEN, width), BF16),
            pltpu.VMEM((2, 1, width), F32),
            pltpu.VMEM(router_t.shape, BF16),
            pltpu.VMEM((CAND_LEN, head_total), BF16),
            pltpu.SemaphoreType.DMA((6,)),
        ],
        compiler_params=pltpu.CompilerParams(vmem_limit_bytes=12 * MIB),
        cost_estimate=pl.CostEstimate(
            flops=6 * CAND_LEN * width * head_total,
            bytes_accessed=4 * width * head_total + 8 * CAND_LEN * width,
            transcendentals=0,
        ),
        name="attend",
    )(
        scalars, *sources, routes, cached, *in_hbm(*gains, router_t),
        *(in_hbm(*mats) if stream else in_vmem(*mats)),
    )
    return outs[:3], (outs[3:] if stream else mats)


def expert_kernel(stream, rows, *refs):
    size = HIDDEN_CHUNK
    if stream:
        sources, served, mats, refs = refs[:4], refs[4], refs[5:9], refs[9:]
        own_hidden, other_hidden, sems = refs
    else:
        mats, (served, own_hidden, other_hidden) = refs[:4], refs[4:]
    own_in, own_down, other_in, other_down = mats

    def chunk_of(i):
        return pl.ds(pl.multiple_of(i * size, size), size)

    def fill(mat, i):
        lanes = chunk_of(i)
        return pltpu.make_async_copy(
            sources[mat].at[:, lanes], mats[mat].at[:, lanes], sems.at[mat, i]
        )

    if stream:
        for pair in ((0, 2), (1, 3)):
            for i in range(own_in.shape[1] // size):
                for mat in pair:
                    fill(mat, i).start()

    @pl.loop(0, own_in.shape[1] // size)
    def _(i):
        units = chunk_of(i)
        if stream:
            fill(0, i).wait()
        own_hidden[:, units] = jnp.maximum(dot(rows[...], own_in[:, units]), 0.0).astype(BF16)
        if stream:
            fill(2, i).wait()
        other_hidden[:, units] = jnp.maximum(dot(rows[...], other_in[:, units]), 0.0).astype(BF16)

    @pl.loop(0, own_down.shape[1] // size)
    def _(i):
        lanes = chunk_of(i)
        if stream:
            fill(1, i).wait()
            fill(3, i).wait()
        served[:, lanes] = (
            dot(own_hidden[...], own_down[:, lanes]) + dot(other_hidden[...], other_down[:, lanes])
        ).astype(BF16)


def expert_rows(rows, mats, stream):
    count, width = rows.shape
    units = mats[0].shape[1]
    scratch = [pltpu.VMEM((count, units), BF16), pltpu.VMEM((count, units), BF16)]
    out_shape = [jax.ShapeDtypeStruct(rows.shape, BF16)]
    if stream:
        scratch.append(pltpu.SemaphoreType.DMA((4, units // HIDDEN_CHUNK)))
        out_shape += [pltpu.VMEM(mat.shape, BF16) for mat in mats]
    outs = pl.pallas_call(
        functools.partial(expert_kernel, stream),
        in_specs=[VMEM] + [HBM if stream else VMEM] * 4,
        out_specs=[VMEM] * len(out_shape),
        out_shape=out_shape,
        scratch_shapes=scratch,
        compiler_params=pltpu.CompilerParams(vmem_limit_bytes=12 * MIB),
        cost_estimate=pl.CostEstimate(
            flops=8 * count * width * units,
            bytes_accessed=8 * width * units + 4 * count * width,
            transcendentals=0,
        ),
        name="experts",
    )(rows, *(in_hbm(*mats) if stream else in_vmem(*mats)))
    return outs[0], (outs[1:] if stream else mats)


def mixed(after_attn, weights, expert_out):
    gates = weights[...]
    coarse = gates.astype(BF16)
    fine = (gates - coarse.astype(F32)).astype(BF16)
    rows = expert_out[...]
    return (after_attn[...] + (dot(coarse, rows) + dot(fine, rows))).astype(BF16)


def combine_kernel(after_attn, weights, expert_out, result):
    result[...] = mixed(after_attn, weights, expert_out)


def place_kernel(after_attn, weights, expert_out, scalars, *refs):
    earlier, (output, result, sems) = refs[:-3], refs[-3:]
    segment = scalars[0]

    def place(source, micro):
        rows = pl.ds(micro * CAND_LEN, CAND_LEN)
        return pltpu.make_async_copy(source, output.at[rows, :], sems.at[micro])

    last = len(earlier)
    for micro in range(CAND_DEV):
        for step in range(micro, last):

            @pl.when(segment + micro == step)
            def _():
                place(earlier[step], micro).start()

    result[...] = mixed(after_attn, weights, expert_out)
    for micro in range(CAND_DEV):

        @pl.when(segment + micro == last)
        def _():
            place(result, micro).start()

    for micro in range(CAND_DEV):
        place(result, micro).wait()


def combine(after_attn, weights, expert_out, scalars=None, earlier=()):
    rows, width = after_attn.shape
    inputs = [after_attn, weights, expert_out]
    specs = [VMEM] * 3
    scratch = []
    out_shape, out_spec = jax.ShapeDtypeStruct((rows, width), BF16), VMEM
    if earlier:
        inputs += [scalars, *in_hbm(*earlier)]
        specs += [SMEM] + [HBM] * len(earlier)
        scratch = [pltpu.VMEM((rows, width), BF16), pltpu.SemaphoreType.DMA((CAND_DEV,))]
        out_shape, out_spec = jax.ShapeDtypeStruct((CAND_DEV * rows, width), BF16), HBM
    return pl.pallas_call(
        place_kernel if earlier else combine_kernel,
        in_specs=specs,
        out_specs=out_spec,
        out_shape=out_shape,
        scratch_shapes=scratch,
        compiler_params=pltpu.CompilerParams(vmem_limit_bytes=8 * MIB),
        cost_estimate=pl.CostEstimate(
            flops=4 * weights.size * width,
            bytes_accessed=6 * after_attn.size + 2 * expert_out.size,
            transcendentals=0,
        ),
        name="combine",
    )(*inputs)


def local(
    states, cand_len, routes, enc_kv, attn_gain, ffn_gain, w_query, w_out, w_router, w_in, w_down
):
    segment_index = lax.axis_index("segment")
    n_segment = lax.axis_size("segment")
    n_expert = lax.axis_size("expert")
    model_width = states.shape[1]
    experts = w_router.shape[2]
    capacity = 2 * ((5 * CAND_LEN + 4 * experts - 1) // (4 * experts))
    core_pairs = [(i, i ^ 1) for i in range(n_expert)]
    same_core = [list(range(core, n_expert, 2)) for core in range(2)]

    def exchange(rows):
        blocks = rows.reshape(experts, capacity, model_width)
        moved = lax.all_to_all(
            blocks, "expert", split_axis=0, concat_axis=0, axis_index_groups=same_core, tiled=True
        )
        return moved.reshape(rows.shape)

    spread = jnp.repeat(enc_kv[:, 0, :], n_expert, axis=0)
    cached = lax.all_to_all(
        spread, ("segment", "expert"), split_axis=0, concat_axis=0, tiled=True
    )
    own = (w_in[0, 0], w_down[0, 0])
    other = tuple(lax.ppermute(mat, "expert", core_pairs) for mat in own)

    scalars = jnp.concatenate([segment_index.astype(jnp.int32).reshape(1), cand_len])
    route_all = routes[0].reshape(CAND_DEV, CAND_LEN, 2)
    router_t = w_router[0].T
    attend_mats = (w_query[0], w_out[0])
    expert_mats = (*own, *other)
    step_count = CAND_DEV + n_segment - 1
    incoming = None
    earlier = []
    for step in range(step_count):
        (after_attn, outgoing, weights), attend_mats = attend(
            step, capacity, scalars, states, incoming, route_all, cached,
            (attn_gain, ffn_gain), router_t, attend_mats,
        )
        served, expert_mats = expert_rows(exchange(outgoing), expert_mats, step == 0)
        expert_out = exchange(served)
        if step + 1 < step_count:
            result = combine(after_attn, weights, expert_out)
            incoming = lax.ppermute(
                result, "segment", [(i, i + 1) for i in range(n_segment - 1)]
            )
            earlier.append(result)
    output = combine(after_attn, weights, expert_out, scalars, earlier)
    return output.reshape(1, CAND_DEV * CAND_LEN, model_width)


def solution(mesh):
    return jax.shard_map(
        local,
        mesh=mesh,
        in_specs=(
            P("expert", None),
            P("expert"),
            P("segment", "expert", None),
            P(None, ("segment", "expert"), None),
            P("segment", None),
            P("segment", None),
            P("segment", None, None),
            P("segment", None, None),
            P("segment", None, None),
            P("segment", "expert", None, None),
            P("segment", "expert", None, None),
        ),
        out_specs=P("segment", "expert", None),
        check_vma=False,
    )
```

```python
import functools
import math

import jax
import jax.numpy as jnp
from jax import lax
from jax.experimental import pallas as pl
from jax.experimental.pallas import tpu as pltpu
from jax.sharding import PartitionSpec as P

HEAD_DIM = 128
CAND_LEN = 64
CAND_DEV = 2
HIDDEN_CHUNK = 512
MIB = 1 << 20

EPSILON = 1e-05

VMEM = pl.BlockSpec(memory_space=pltpu.VMEM)
SMEM = pl.BlockSpec(memory_space=pltpu.SMEM)
HBM = pl.BlockSpec(memory_space=pltpu.HBM)
F32 = jnp.float32
BF16 = jnp.bfloat16


def in_hbm(*arrays):
    return [pltpu.with_memory_space_constraint(array, pltpu.HBM) for array in arrays]


def in_vmem(*arrays):
    return [pltpu.with_memory_space_constraint(array, pltpu.VMEM) for array in arrays]


def normalize(carried, gain_row):
    average = jnp.mean(carried, axis=-1, keepdims=True)
    centered = carried - average
    variance = jnp.mean(centered * centered, axis=-1, keepdims=True)
    return gain_row * centered * lax.rsqrt(variance + EPSILON)


def dot(left, right, contract=((1,), (0,))):
    return lax.dot_general(left, right, (contract, ((), ())), preferred_element_type=F32)


def spread_kernel(copies_of, enc_kv, blocks):
    for layer in range(enc_kv.shape[0]):
        block = enc_kv[layer]
        for i in range(copies_of):
            blocks[layer * copies_of + i] = block


def spread(enc_kv, copies_of):
    layers, _, features = enc_kv.shape
    tiles = enc_kv.reshape(layers, features // HEAD_DIM, HEAD_DIM)
    return pl.pallas_call(
        functools.partial(spread_kernel, copies_of),
        in_specs=[VMEM],
        out_specs=VMEM,
        out_shape=jax.ShapeDtypeStruct((layers * copies_of, *tiles.shape[1:]), BF16),
        compiler_params=pltpu.CompilerParams(vmem_limit_bytes=8 * MIB),
        name="spread",
    )(tiles)


def project_kernel(states, gain, w_query, w_out, queries, query_mat, out_mat, fresh, gain_buf, sems):
    fills = (
        (states.at[pl.ds(0, CAND_LEN), :], fresh),
        (gain, gain_buf),
        (w_query, query_mat),
        (w_out, out_mat),
    )
    copies = [pltpu.make_async_copy(*pair, sems.at[i]) for i, pair in enumerate(fills)]
    for copy in copies:
        copy.start()
    copies[0].wait()
    copies[1].wait()
    normed = normalize(fresh[...].astype(F32), gain_buf[...]).astype(BF16)
    copies[2].wait()
    queries[...] = dot(normed, query_mat[...]).astype(BF16)
    copies[3].wait()


def project(states, gain, mats):
    width, head_total = mats[0].shape
    outs = pl.pallas_call(
        project_kernel,
        in_specs=[HBM] * 4,
        out_specs=[VMEM] * 3,
        out_shape=[
            jax.ShapeDtypeStruct((CAND_LEN, head_total), BF16),
            *(pltpu.VMEM(mat.shape, BF16) for mat in mats),
        ],
        scratch_shapes=[
            pltpu.VMEM((CAND_LEN, width), BF16),
            pltpu.VMEM((1, width), F32),
            pltpu.SemaphoreType.DMA((4,)),
        ],
        compiler_params=pltpu.CompilerParams(vmem_limit_bytes=12 * MIB),
        cost_estimate=pl.CostEstimate(
            flops=2 * CAND_LEN * width * head_total,
            bytes_accessed=4 * width * head_total,
            transcendentals=0,
        ),
        name="project",
    )(*in_hbm(states, gain, *mats))
    return outs[0], outs[1:]


def attend_kernel(step, capacity, scalars, *refs):
    incoming = states = None
    if step > 0:
        incoming, refs = refs[0], refs[1:]
    if step < CAND_DEV:
        states, refs = refs[0], refs[1:]
    if step == 0:
        projected, refs = refs[0], refs[1:]
    (routes, cached, attn_gain, ffn_gain, router_t, w_query, w_out,
     after_ref, outgoing, weights,
     fresh, gain_buf, router_buf, context, sems) = refs
    segment = scalars[0]
    fills = [
        (attn_gain, gain_buf.at[0]),
        (ffn_gain, gain_buf.at[1]),
        (router_t, router_buf),
    ]
    if states is not None:
        fills.insert(0, (states.at[pl.ds(step * CAND_LEN, CAND_LEN), :], fresh))
    copies = [pltpu.make_async_copy(*pair, sems.at[i]) for i, pair in enumerate(fills)]
    for copy in copies:
        copy.start()
    if states is not None:
        copies[0].wait()
        copies = copies[1:]

    if step == 0:
        current = fresh[...]
    elif step < CAND_DEV:
        current = jnp.where(segment == 0, fresh[...], incoming[...])
    else:
        current = incoming[...]
    carried = current.astype(F32)
    copies[0].wait()
    copies[1].wait()
    if step == 0:
        queries = projected[...]
    else:
        normed = normalize(carried, gain_buf[0]).astype(BF16)
        queries = dot(normed, w_query[...]).astype(BF16)
    head_total = queries.shape[1]
    scale = 1.0 / math.sqrt(HEAD_DIM)
    for start in range(0, head_total, HEAD_DIM):
        lanes = slice(start, start + HEAD_DIM)
        scores = dot(queries[:, lanes], cached[:, lanes], ((1,), (1,))) * scale
        exponent = jnp.exp(scores - jnp.max(scores, axis=1, keepdims=True))
        share = (exponent / jnp.sum(exponent, axis=1, keepdims=True)).astype(BF16)
        values = cached[:, head_total + start : head_total + start + HEAD_DIM]
        context[:, lanes] = dot(share, values).astype(BF16)
    after_attn = carried + dot(context[...], w_out[...])
    after_ref[...] = after_attn
    ffn_input = normalize(after_attn, gain_buf[1]).astype(BF16)

    rows, experts = after_attn.shape[0], router_t.shape[0]
    copies[2].wait()
    logits = dot(ffn_input, router_buf[...], ((1,), (1,)))
    micro = jnp.clip(step - segment, 0, CAND_DEV - 1)
    live = lax.broadcasted_iota(jnp.int32, (rows, 1), 0) < scalars[1 + micro]
    route = routes[micro]
    labels = lax.broadcasted_iota(jnp.int32, (rows, experts), 1)
    first, second = route[:, 0:1] == labels, route[:, 1:2] == labels
    logit_first = jnp.sum(jnp.where(first, logits, 0.0), axis=1, keepdims=True)
    logit_second = jnp.sum(jnp.where(second, logits, 0.0), axis=1, keepdims=True)
    gate_first = jax.nn.sigmoid(logit_first - logit_second)
    gate_second = 1.0 - gate_first
    named = jnp.where((first | second) & live, 1.0, 0.0).astype(BF16)
    earlier = lax.broadcasted_iota(jnp.int32, (rows, rows), 1) < lax.broadcasted_iota(
        jnp.int32, (rows, rows), 0
    )
    before = dot(jnp.where(earlier, 1.0, 0.0).astype(BF16), named)
    slots = lax.broadcasted_iota(jnp.int32, (rows, experts * capacity), 1)
    chosen = []
    for mask, column in ((first, 0), (second, 1)):
        slot = jnp.sum(jnp.where(mask, before, 0.0), axis=1, keepdims=True).astype(jnp.int32)
        target = route[:, column : column + 1] * capacity + slot
        chosen.append((slots == target) & live)
    select = jnp.where(chosen[0] | chosen[1], 1.0, 0.0).astype(BF16)
    outgoing[...] = dot(select, ffn_input, ((0,), (0,))).astype(BF16)
    weights[...] = jnp.where(chosen[0], gate_first, 0.0) + jnp.where(chosen[1], gate_second, 0.0)


def attend(step, capacity, scalars, states, incoming, queries, routes, cached, gains, router_t, mats):
    w_query, w_out = mats
    head_total, width = w_out.shape
    slot_count = router_t.shape[0] * capacity
    sources, specs = [], []
    if step > 0:
        sources.append(incoming)
        specs.append(VMEM)
    if step < CAND_DEV:
        sources += in_hbm(states)
        specs.append(HBM)
    if step == 0:
        sources.append(queries)
        specs.append(VMEM)
    return pl.pallas_call(
        functools.partial(attend_kernel, step, capacity),
        in_specs=[SMEM] + specs + [VMEM, VMEM, HBM, HBM, HBM, VMEM, VMEM],
        out_specs=[VMEM] * 3,
        out_shape=[
            jax.ShapeDtypeStruct((CAND_LEN, width), F32),
            jax.ShapeDtypeStruct((slot_count, width), BF16),
            jax.ShapeDtypeStruct((CAND_LEN, slot_count), F32),
        ],
        scratch_shapes=[
            pltpu.VMEM((CAND_LEN, width), BF16),
            pltpu.VMEM((2, 1, width), F32),
            pltpu.VMEM(router_t.shape, BF16),
            pltpu.VMEM((CAND_LEN, head_total), BF16),
            pltpu.SemaphoreType.DMA((4,)),
        ],
        compiler_params=pltpu.CompilerParams(vmem_limit_bytes=12 * MIB),
        cost_estimate=pl.CostEstimate(
            flops=6 * CAND_LEN * width * head_total,
            bytes_accessed=4 * width * head_total + 8 * CAND_LEN * width,
            transcendentals=0,
        ),
        name="attend",
    )(
        scalars, *sources, routes, cached, *in_hbm(*gains, router_t), *in_vmem(w_query, w_out)
    )


def expert_kernel(stream, rows, *refs):
    size = HIDDEN_CHUNK
    if stream:
        sources, served, mats, refs = refs[:4], refs[4], refs[5:9], refs[9:]
        own_hidden, other_hidden, sems = refs
    else:
        mats, (served, own_hidden, other_hidden) = refs[:4], refs[4:]
    own_in, own_down, other_in, other_down = mats

    def chunk_of(i):
        return pl.ds(pl.multiple_of(i * size, size), size)

    def fill(mat, i):
        lanes = chunk_of(i)
        return pltpu.make_async_copy(
            sources[mat].at[:, lanes], mats[mat].at[:, lanes], sems.at[mat, i]
        )

    if stream:
        for pair in ((0, 2), (1, 3)):
            for i in range(own_in.shape[1] // size):
                for mat in pair:
                    fill(mat, i).start()

    @pl.loop(0, own_in.shape[1] // size)
    def _(i):
        units = chunk_of(i)
        if stream:
            fill(0, i).wait()
        own_hidden[:, units] = jnp.maximum(dot(rows[...], own_in[:, units]), 0.0).astype(BF16)
        if stream:
            fill(2, i).wait()
        other_hidden[:, units] = jnp.maximum(dot(rows[...], other_in[:, units]), 0.0).astype(BF16)

    @pl.loop(0, own_down.shape[1] // size)
    def _(i):
        lanes = chunk_of(i)
        if stream:
            fill(1, i).wait()
            fill(3, i).wait()
        served[:, lanes] = (
            dot(own_hidden[...], own_down[:, lanes]) + dot(other_hidden[...], other_down[:, lanes])
        ).astype(BF16)


def expert_rows(rows, mats, stream):
    count, width = rows.shape
    units = mats[0].shape[1]
    scratch = [pltpu.VMEM((count, units), BF16), pltpu.VMEM((count, units), BF16)]
    out_shape = [jax.ShapeDtypeStruct(rows.shape, BF16)]
    if stream:
        scratch.append(pltpu.SemaphoreType.DMA((4, units // HIDDEN_CHUNK)))
        out_shape += [pltpu.VMEM(mat.shape, BF16) for mat in mats]
    outs = pl.pallas_call(
        functools.partial(expert_kernel, stream),
        in_specs=[VMEM] + [HBM if stream else VMEM] * 4,
        out_specs=[VMEM] * len(out_shape),
        out_shape=out_shape,
        scratch_shapes=scratch,
        compiler_params=pltpu.CompilerParams(vmem_limit_bytes=12 * MIB),
        cost_estimate=pl.CostEstimate(
            flops=8 * count * width * units,
            bytes_accessed=8 * width * units + 4 * count * width,
            transcendentals=0,
        ),
        name="experts",
    )(rows, *(in_hbm(*mats) if stream else in_vmem(*mats)))
    return outs[0], (outs[1:] if stream else mats)


def mixed(after_attn, weights, expert_out):
    gates = weights[...]
    coarse = gates.astype(BF16)
    fine = (gates - coarse.astype(F32)).astype(BF16)
    rows = expert_out[...]
    return (after_attn[...] + (dot(coarse, rows) + dot(fine, rows))).astype(BF16)


def combine_kernel(after_attn, weights, expert_out, result):
    result[...] = mixed(after_attn, weights, expert_out)


def place_kernel(after_attn, weights, expert_out, scalars, *refs):
    earlier, (output, result, sems) = refs[:-3], refs[-3:]
    segment = scalars[0]

    def place(source, micro):
        rows = pl.ds(micro * CAND_LEN, CAND_LEN)
        return pltpu.make_async_copy(source, output.at[rows, :], sems.at[micro])

    last = len(earlier)
    for micro in range(CAND_DEV):
        for step in range(micro, last):

            @pl.when(segment + micro == step)
            def _():
                place(earlier[step], micro).start()

    result[...] = mixed(after_attn, weights, expert_out)
    for micro in range(CAND_DEV):

        @pl.when(segment + micro == last)
        def _():
            place(result, micro).start()

    for micro in range(CAND_DEV):
        place(result, micro).wait()


def combine(after_attn, weights, expert_out, scalars=None, earlier=()):
    rows, width = after_attn.shape
    inputs = [after_attn, weights, expert_out]
    specs = [VMEM] * 3
    scratch = []
    out_shape, out_spec = jax.ShapeDtypeStruct((rows, width), BF16), VMEM
    if earlier:
        inputs += [scalars, *in_vmem(*earlier)]
        specs += [SMEM] + [VMEM] * len(earlier)
        scratch = [pltpu.VMEM((rows, width), BF16), pltpu.SemaphoreType.DMA((CAND_DEV,))]
        out_shape, out_spec = jax.ShapeDtypeStruct((CAND_DEV * rows, width), BF16), HBM
    return pl.pallas_call(
        place_kernel if earlier else combine_kernel,
        in_specs=specs,
        out_specs=out_spec,
        out_shape=out_shape,
        scratch_shapes=scratch,
        compiler_params=pltpu.CompilerParams(vmem_limit_bytes=8 * MIB),
        cost_estimate=pl.CostEstimate(
            flops=4 * weights.size * width,
            bytes_accessed=6 * after_attn.size + 2 * expert_out.size,
            transcendentals=0,
        ),
        name="combine",
    )(*inputs)


def local(
    states, cand_len, routes, enc_kv, attn_gain, ffn_gain, w_query, w_out, w_router, w_in, w_down
):
    segment_index = lax.axis_index("segment")
    n_segment = lax.axis_size("segment")
    n_expert = lax.axis_size("expert")
    model_width = states.shape[1]
    experts = w_router.shape[2]
    capacity = 2 * ((5 * CAND_LEN + 4 * experts - 1) // (4 * experts))
    core_pairs = [(i, i ^ 1) for i in range(n_expert)]
    same_core = [list(range(core, n_expert, 2)) for core in range(2)]

    def exchange(rows):
        blocks = rows.reshape(experts, capacity, model_width)
        moved = lax.all_to_all(
            blocks, "expert", split_axis=0, concat_axis=0, axis_index_groups=same_core, tiled=True
        )
        return moved.reshape(rows.shape)

    cached = lax.all_to_all(
        spread(enc_kv, n_expert), ("segment", "expert"), split_axis=0, concat_axis=0, tiled=True
    )
    cached = cached.reshape(cached.shape[0], -1)
    own = (w_in[0, 0], w_down[0, 0])
    other = tuple(lax.ppermute(mat, "expert", core_pairs) for mat in own)

    scalars = jnp.concatenate([segment_index.astype(jnp.int32).reshape(1), cand_len])
    route_all = routes[0].reshape(CAND_DEV, CAND_LEN, 2)
    router_t = w_router[0].T
    queries, attend_mats = project(states, attn_gain, (w_query[0], w_out[0]))
    expert_mats = (*own, *other)
    step_count = CAND_DEV + n_segment - 1
    incoming = None
    earlier = []
    for step in range(step_count):
        after_attn, outgoing, weights = attend(
            step, capacity, scalars, states, incoming, queries, route_all, cached,
            (attn_gain, ffn_gain), router_t, attend_mats,
        )
        served, expert_mats = expert_rows(exchange(outgoing), expert_mats, step == 0)
        expert_out = exchange(served)
        if step + 1 < step_count:
            result = combine(after_attn, weights, expert_out)
            incoming = lax.ppermute(
                result, "segment", [(i, i + 1) for i in range(n_segment - 1)]
            )
            earlier.append(result)
    output = combine(after_attn, weights, expert_out, scalars, earlier)
    return output.reshape(1, CAND_DEV * CAND_LEN, model_width)


def solution(mesh):
    return jax.shard_map(
        local,
        mesh=mesh,
        in_specs=(
            P("expert", None),
            P("expert"),
            P("segment", "expert", None),
            P(None, ("segment", "expert"), None),
            P("segment", None),
            P("segment", None),
            P("segment", None, None),
            P("segment", None, None),
            P("segment", None, None),
            P("segment", "expert", None, None),
            P("segment", "expert", None, None),
        ),
        out_specs=P("segment", "expert", None),
        check_vma=False,
    )
```

```python
import functools
import math

import jax
import jax.numpy as jnp
from jax import lax
from jax.experimental import pallas as pl
from jax.experimental.pallas import tpu as pltpu
from jax.sharding import PartitionSpec as P

HEAD_DIM = 128
CAND_LEN = 64
CAND_DEV = 2
HIDDEN_CHUNK = 512
MIB = 1 << 20

EPSILON = 1e-05

VMEM = pl.BlockSpec(memory_space=pltpu.VMEM)
SMEM = pl.BlockSpec(memory_space=pltpu.SMEM)
HBM = pl.BlockSpec(memory_space=pltpu.HBM)
F32 = jnp.float32
BF16 = jnp.bfloat16


def in_hbm(*arrays):
    return [pltpu.with_memory_space_constraint(array, pltpu.HBM) for array in arrays]


def in_vmem(*arrays):
    return [pltpu.with_memory_space_constraint(array, pltpu.VMEM) for array in arrays]


def normalize(carried, gain_row):
    average = jnp.mean(carried, axis=-1, keepdims=True)
    centered = carried - average
    variance = jnp.mean(centered * centered, axis=-1, keepdims=True)
    return gain_row * centered * lax.rsqrt(variance + EPSILON)


def dot(left, right, contract=((1,), (0,))):
    return lax.dot_general(left, right, (contract, ((), ())), preferred_element_type=F32)


def spread_kernel(copies_of, enc_kv, blocks):
    for layer in range(enc_kv.shape[0]):
        block = enc_kv[layer]
        for i in range(copies_of):
            blocks[layer * copies_of + i] = block


def spread(enc_kv, copies_of):
    layers, _, features = enc_kv.shape
    tiles = enc_kv.reshape(layers, features // HEAD_DIM, HEAD_DIM)
    return pl.pallas_call(
        functools.partial(spread_kernel, copies_of),
        in_specs=[VMEM],
        out_specs=VMEM,
        out_shape=jax.ShapeDtypeStruct((layers * copies_of, *tiles.shape[1:]), BF16),
        compiler_params=pltpu.CompilerParams(vmem_limit_bytes=8 * MIB),
        name="spread",
    )(tiles)


def project_kernel(states, gain, w_query, queries, fresh, gain_buf, query_buf, sems):
    fills = (
        (states.at[pl.ds(0, CAND_LEN), :], fresh),
        (gain, gain_buf),
        (w_query, query_buf),
    )
    copies = [pltpu.make_async_copy(*pair, sems.at[i]) for i, pair in enumerate(fills)]
    for copy in copies:
        copy.start()
    copies[0].wait()
    copies[1].wait()
    normed = normalize(fresh[...].astype(F32), gain_buf[...]).astype(BF16)
    copies[2].wait()
    queries[...] = dot(normed, query_buf[...]).astype(BF16)


def project(states, gain, w_query):
    width, head_total = w_query.shape
    return pl.pallas_call(
        project_kernel,
        in_specs=[HBM] * 3,
        out_specs=VMEM,
        out_shape=jax.ShapeDtypeStruct((CAND_LEN, head_total), BF16),
        scratch_shapes=[
            pltpu.VMEM((CAND_LEN, width), BF16),
            pltpu.VMEM((1, width), F32),
            pltpu.VMEM(w_query.shape, BF16),
            pltpu.SemaphoreType.DMA((3,)),
        ],
        compiler_params=pltpu.CompilerParams(vmem_limit_bytes=12 * MIB),
        cost_estimate=pl.CostEstimate(
            flops=2 * CAND_LEN * width * head_total,
            bytes_accessed=2 * width * head_total,
            transcendentals=0,
        ),
        name="project",
    )(*in_hbm(states, gain, w_query))


def block_diagonal(cached, first_head, blocks):
    sources = cached.shape[0]
    blocks[...] = jnp.zeros_like(blocks)
    for head in range(blocks.shape[1] // HEAD_DIM):
        rows = pl.ds(head * sources, sources)
        blocks[rows, pl.ds(head * HEAD_DIM, HEAD_DIM)] = cached[:, first_head + head, :]


def attend_kernel(step, capacity, *refs):
    segment = lax.axis_index("segment")
    if step == 0:
        (cand_len, queries_in, cached, states, routes_hbm, attn_gain, ffn_gain, router_hbm,
         query_hbm, out_hbm, after_ref, outgoing, weights,
         routes, gains, router, w_query, w_out, keys, values, following,
         fresh, route_buf, sems) = refs
        fills = (
            (states.at[pl.ds(0, CAND_LEN), :], fresh),
            (ffn_gain, gains.at[1]),
            (out_hbm, w_out),
            (router_hbm, router),
            (routes_hbm, route_buf),
            (attn_gain, gains.at[0]),
            (states.at[pl.ds(CAND_LEN, CAND_LEN), :], following),
            (query_hbm, w_query),
        )
        copies = [pltpu.make_async_copy(*pair, sems.at[i]) for i, pair in enumerate(fills)]
        for copy in copies:
            copy.start()
        head_count = w_out.shape[0] // HEAD_DIM
        block_diagonal(cached, 0, keys)
        block_diagonal(cached, head_count, values)
        queries = queries_in[...]
        copies[0].wait()
        carried = fresh[...].astype(F32)
        copies[4].wait()
        copies = copies[:4] + copies[5:]
        position = lax.broadcasted_iota(jnp.int32, (1, CAND_LEN), 1)
        for micro in range(CAND_DEV):
            route = route_buf[:, micro * CAND_LEN : (micro + 1) * CAND_LEN]
            routes[micro] = jnp.where(position < cand_len[micro], route, -1)
    else:
        incoming, refs = refs[0], refs[1:]
        current = incoming[...]
        if step < CAND_DEV:
            current, refs = jnp.where(segment == 0, refs[0][...], current), refs[1:]
        (routes, gains, router, w_query, w_out, keys, values, after_ref, outgoing, weights) = refs
        carried = current.astype(F32)
        normed = normalize(carried, gains[0]).astype(BF16)
        queries = dot(normed, w_query[...]).astype(BF16)

    rows = carried.shape[0]
    sources = keys.shape[0] * HEAD_DIM // keys.shape[1]
    scores = dot(keys[...], queries, ((1,), (1,))) * (1.0 / math.sqrt(HEAD_DIM))
    scores = scores.reshape(-1, sources, rows)
    exponent = jnp.exp(scores - jnp.max(scores, axis=1, keepdims=True))
    share = exponent / jnp.sum(exponent, axis=1, keepdims=True)
    share = share.reshape(-1, rows).astype(BF16)
    context = dot(share, values[...], ((0,), (0,))).astype(BF16)
    if step == 0:
        copies[1].wait()
        copies[2].wait()
    after_attn = carried + dot(context, w_out[...])
    after_ref[...] = after_attn
    ffn_input = normalize(after_attn, gains[1]).astype(BF16)

    if step == 0:
        copies[3].wait()
    experts = router.shape[0]
    logits = dot(router[...], ffn_input, ((1,), (1,)))
    micro = jnp.clip(step - segment, 0, CAND_DEV - 1)
    route = routes[micro]
    labels = lax.broadcasted_iota(jnp.int32, (experts, rows), 0)
    first, second = route[0:1] == labels, route[1:2] == labels
    logit_first = jnp.sum(jnp.where(first, logits, 0.0), axis=0, keepdims=True)
    logit_second = jnp.sum(jnp.where(second, logits, 0.0), axis=0, keepdims=True)
    gate_first = jax.nn.sigmoid(logit_first - logit_second)
    gate_second = 1.0 - gate_first
    named = jnp.where(first | second, 1.0, 0.0).astype(BF16)
    earlier = lax.broadcasted_iota(jnp.int32, (rows, rows), 0) < lax.broadcasted_iota(
        jnp.int32, (rows, rows), 1
    )
    before = dot(named, jnp.where(earlier, 1.0, 0.0).astype(BF16))
    slots = lax.broadcasted_iota(jnp.int32, (experts * capacity, rows), 0)
    chosen = []
    for mask, row in ((first, 0), (second, 1)):
        slot = jnp.sum(jnp.where(mask, before, 0.0), axis=0, keepdims=True).astype(jnp.int32)
        chosen.append(slots == route[row : row + 1] * capacity + slot)
    select = jnp.where(chosen[0] | chosen[1], 1.0, 0.0).astype(BF16)
    outgoing[...] = dot(select, ffn_input).astype(BF16)
    weights[...] = jnp.where(chosen[0], gate_first, 0.0) + jnp.where(chosen[1], gate_second, 0.0)
    if step == 0:
        for copy in copies[4:]:
            copy.wait()


def attend(step, capacity, sources, kept):
    if step == 0:
        cand_len, queries, cached, *params = sources
        _, routes, _, _, router_t, w_query, w_out = params
        head_total, width = w_out.shape
        blocks = (cached.shape[0] * head_total // HEAD_DIM, head_total)
        kept_shapes = [
            pltpu.VMEM((CAND_DEV, 2, CAND_LEN), jnp.int32),
            pltpu.VMEM((2, 1, width), F32),
            *(pltpu.VMEM(array.shape, BF16) for array in (router_t, w_query, w_out)),
            pltpu.VMEM(blocks, BF16),
            pltpu.VMEM(blocks, BF16),
            pltpu.VMEM((CAND_LEN, width), BF16),
        ]
        inputs = [*in_hbm(cand_len), queries, cached, *in_hbm(*params)]
        specs = [SMEM, VMEM, VMEM] + [HBM] * len(params)
        scratch = [
            pltpu.VMEM((CAND_LEN, width), BF16),
            pltpu.VMEM(routes.shape, jnp.int32),
            pltpu.SemaphoreType.DMA((8,)),
        ]
    else:
        _, _, router_t, _, w_out, *_ = kept
        head_total, width = w_out.shape
        kept_shapes, scratch = [], []
        inputs = [*sources, *in_vmem(*kept)]
        specs = [VMEM] * len(inputs)
    slot_count = router_t.shape[0] * capacity
    outs = pl.pallas_call(
        functools.partial(attend_kernel, step, capacity),
        in_specs=specs,
        out_specs=[VMEM] * (3 + len(kept_shapes)),
        out_shape=[
            jax.ShapeDtypeStruct((CAND_LEN, width), F32),
            jax.ShapeDtypeStruct((slot_count, width), BF16),
            jax.ShapeDtypeStruct((slot_count, CAND_LEN), F32),
            *kept_shapes,
        ],
        scratch_shapes=scratch,
        compiler_params=pltpu.CompilerParams(vmem_limit_bytes=12 * MIB),
        cost_estimate=pl.CostEstimate(
            flops=6 * CAND_LEN * width * head_total,
            bytes_accessed=4 * width * head_total + 8 * CAND_LEN * width,
            transcendentals=0,
        ),
        name="attend",
    )(*inputs)
    return outs[:3], outs[3:]


def expert_kernel(stream, rows, *refs):
    size = HIDDEN_CHUNK
    if stream:
        sources, served, mats, refs = refs[:4], refs[4], refs[5:9], refs[9:]
        own_hidden, other_hidden, sems = refs
    else:
        mats, (served, own_hidden, other_hidden) = refs[:4], refs[4:]
    own_in, own_down, other_in, other_down = mats

    def chunk_of(i):
        return pl.ds(pl.multiple_of(i * size, size), size)

    def fill(mat, i):
        lanes = chunk_of(i)
        return pltpu.make_async_copy(
            sources[mat].at[:, lanes], mats[mat].at[:, lanes], sems.at[mat, i]
        )

    if stream:
        for pair in ((0, 2), (1, 3)):
            for i in range(own_in.shape[1] // size):
                for mat in pair:
                    fill(mat, i).start()

    @pl.loop(0, own_in.shape[1] // size, unroll=True)
    def _(i):
        units = chunk_of(i)
        if stream:
            fill(0, i).wait()
        own_hidden[:, units] = jnp.maximum(dot(rows[...], own_in[:, units]), 0.0).astype(BF16)
        if stream:
            fill(2, i).wait()
        other_hidden[:, units] = jnp.maximum(dot(rows[...], other_in[:, units]), 0.0).astype(BF16)

    @pl.loop(0, own_down.shape[1] // size, unroll=True)
    def _(i):
        lanes = chunk_of(i)
        if stream:
            fill(1, i).wait()
            fill(3, i).wait()
        served[:, lanes] = (
            dot(own_hidden[...], own_down[:, lanes]) + dot(other_hidden[...], other_down[:, lanes])
        ).astype(BF16)


def expert_rows(rows, mats, stream):
    count, width = rows.shape
    units = mats[0].shape[1]
    scratch = [pltpu.VMEM((count, units), BF16), pltpu.VMEM((count, units), BF16)]
    out_shape = [jax.ShapeDtypeStruct(rows.shape, BF16)]
    if stream:
        scratch.append(pltpu.SemaphoreType.DMA((4, units // HIDDEN_CHUNK)))
        out_shape += [pltpu.VMEM(mat.shape, BF16) for mat in mats]
    outs = pl.pallas_call(
        functools.partial(expert_kernel, stream),
        in_specs=[VMEM] + [HBM if stream else VMEM] * 4,
        out_specs=[VMEM] * len(out_shape),
        out_shape=out_shape,
        scratch_shapes=scratch,
        compiler_params=pltpu.CompilerParams(vmem_limit_bytes=12 * MIB),
        cost_estimate=pl.CostEstimate(
            flops=8 * count * width * units,
            bytes_accessed=8 * width * units + 4 * count * width,
            transcendentals=0,
        ),
        name="experts",
    )(rows, *(in_hbm(*mats) if stream else in_vmem(*mats)))
    return outs[0], (outs[1:] if stream else mats)


def mixed(after_attn, weights, expert_out):
    gates = weights[...]
    coarse = gates.astype(BF16)
    fine = (gates - coarse.astype(F32)).astype(BF16)
    rows = expert_out[...]
    mixture = dot(coarse, rows, ((0,), (0,))) + dot(fine, rows, ((0,), (0,)))
    return (after_attn[...] + mixture).astype(BF16)


def combine_kernel(after_attn, weights, expert_out, result):
    result[...] = mixed(after_attn, weights, expert_out)


def place_kernel(after_attn, weights, expert_out, *refs):
    earlier, (output, result, sems) = refs[:-3], refs[-3:]
    segment = lax.axis_index("segment")

    def place(source, micro):
        rows = pl.ds(micro * CAND_LEN, CAND_LEN)
        return pltpu.make_async_copy(source, output.at[rows, :], sems.at[micro])

    last = len(earlier)
    for micro in range(CAND_DEV):
        for step in range(micro, last):

            @pl.when(segment + micro == step)
            def _():
                place(earlier[step], micro).start()

    result[...] = mixed(after_attn, weights, expert_out)
    for micro in range(CAND_DEV):

        @pl.when(segment + micro == last)
        def _():
            place(result, micro).start()

    for micro in range(CAND_DEV):
        place(result, micro).wait()


def combine(after_attn, weights, expert_out, earlier=()):
    rows, width = after_attn.shape
    inputs = [after_attn, weights, expert_out]
    specs = [VMEM] * 3
    scratch = []
    out_shape, out_spec = jax.ShapeDtypeStruct((rows, width), BF16), VMEM
    if earlier:
        inputs += in_vmem(*earlier)
        specs += [VMEM] * len(earlier)
        scratch = [pltpu.VMEM((rows, width), BF16), pltpu.SemaphoreType.DMA((CAND_DEV,))]
        out_shape, out_spec = jax.ShapeDtypeStruct((CAND_DEV * rows, width), BF16), HBM
    return pl.pallas_call(
        place_kernel if earlier else combine_kernel,
        in_specs=specs,
        out_specs=out_spec,
        out_shape=out_shape,
        scratch_shapes=scratch,
        compiler_params=pltpu.CompilerParams(vmem_limit_bytes=8 * MIB),
        cost_estimate=pl.CostEstimate(
            flops=4 * weights.size * width,
            bytes_accessed=6 * after_attn.size + 2 * expert_out.size,
            transcendentals=0,
        ),
        name="combine",
    )(*inputs)


def local(
    states, cand_len, routes, enc_kv, attn_gain, ffn_gain, w_query, w_out, w_router, w_in, w_down
):
    n_segment = lax.axis_size("segment")
    n_expert = lax.axis_size("expert")
    model_width = states.shape[1]
    experts = w_router.shape[2]
    capacity = 2 * ((5 * CAND_LEN + 4 * experts - 1) // (4 * experts))
    core_pairs = [(i, i ^ 1) for i in range(n_expert)]
    same_core = [list(range(core, n_expert, 2)) for core in range(2)]

    def exchange(rows):
        blocks = rows.reshape(experts, capacity, model_width)
        moved = lax.all_to_all(
            blocks, "expert", split_axis=0, concat_axis=0, axis_index_groups=same_core, tiled=True
        )
        return moved.reshape(rows.shape)

    cached = lax.all_to_all(
        spread(enc_kv, n_expert), ("segment", "expert"), split_axis=0, concat_axis=0, tiled=True
    )
    own = (w_in[0, 0], w_down[0, 0])
    other = tuple(lax.ppermute(mat, "expert", core_pairs) for mat in own)

    queries = project(states, attn_gain, w_query[0])
    expert_mats = (*own, *other)
    step_count = CAND_DEV + n_segment - 1
    earlier = []
    kept = ()
    for step in range(step_count):
        if step == 0:
            sources = (
                cand_len, queries, cached, states, routes[0].T, attn_gain, ffn_gain,
                w_router[0].T, w_query[0], w_out[0],
            )
        elif step < CAND_DEV:
            sources = (incoming, following)
        else:
            sources = (incoming,)
        (after_attn, outgoing, weights), left = attend(step, capacity, sources, kept)
        if step == 0:
            *kept, following = left
        served, expert_mats = expert_rows(exchange(outgoing), expert_mats, step == 0)
        expert_out = exchange(served)
        if step + 1 < step_count:
            result = combine(after_attn, weights, expert_out)
            incoming = lax.ppermute(
                result, "segment", [(i, i + 1) for i in range(n_segment - 1)]
            )
            earlier.append(result)
    output = combine(after_attn, weights, expert_out, earlier)
    return output.reshape(1, CAND_DEV * CAND_LEN, model_width)


def solution(mesh):
    return jax.shard_map(
        local,
        mesh=mesh,
        in_specs=(
            P("expert", None),
            P("expert"),
            P("segment", "expert", None),
            P(None, ("segment", "expert"), None),
            P("segment", None),
            P("segment", None),
            P("segment", None, None),
            P("segment", None, None),
            P("segment", None, None),
            P("segment", "expert", None, None),
            P("segment", "expert", None, None),
        ),
        out_specs=P("segment", "expert", None),
        check_vma=False,
    )
```

```python
import functools
import math

import jax
import jax.numpy as jnp
from jax import lax
from jax.experimental import pallas as pl
from jax.experimental.pallas import tpu as pltpu
from jax.sharding import PartitionSpec as P

HEAD_DIM = 128
CAND_LEN = 64
CAND_DEV = 2
HIDDEN_CHUNK = 512
MIB = 1 << 20

EPSILON = 1e-05

VMEM = pl.BlockSpec(memory_space=pltpu.VMEM)
SMEM = pl.BlockSpec(memory_space=pltpu.SMEM)
HBM = pl.BlockSpec(memory_space=pltpu.HBM)
F32 = jnp.float32
BF16 = jnp.bfloat16


def in_hbm(*arrays):
    return [pltpu.with_memory_space_constraint(array, pltpu.HBM) for array in arrays]


def in_vmem(*arrays):
    return [pltpu.with_memory_space_constraint(array, pltpu.VMEM) for array in arrays]


def normalize(carried, gain_row):
    average = jnp.mean(carried, axis=-1, keepdims=True)
    centered = carried - average
    variance = jnp.mean(centered * centered, axis=-1, keepdims=True)
    return gain_row * centered * lax.rsqrt(variance + EPSILON)


def dot(left, right, contract=((1,), (0,))):
    return lax.dot_general(left, right, (contract, ((), ())), preferred_element_type=F32)


def spread_kernel(copies_of, enc_kv, blocks):
    for layer in range(enc_kv.shape[0]):
        block = enc_kv[layer]
        for i in range(copies_of):
            blocks[layer * copies_of + i] = block


def spread(enc_kv, copies_of):
    layers, _, features = enc_kv.shape
    tiles = enc_kv.reshape(layers, features // HEAD_DIM, HEAD_DIM)
    return pl.pallas_call(
        functools.partial(spread_kernel, copies_of),
        in_specs=[VMEM],
        out_specs=VMEM,
        out_shape=jax.ShapeDtypeStruct((layers * copies_of, *tiles.shape[1:]), BF16),
        compiler_params=pltpu.CompilerParams(vmem_limit_bytes=8 * MIB),
        name="spread",
    )(tiles)


def block_diagonal(cached, first_head, blocks):
    sources = cached.shape[0]
    blocks[...] = jnp.zeros_like(blocks)
    for head in range(blocks.shape[1] // HEAD_DIM):
        rows = pl.ds(head * sources, sources)
        blocks[rows, pl.ds(head * HEAD_DIM, HEAD_DIM)] = cached[:, first_head + head, :]


def attend_kernel(step, capacity, *refs):
    segment = lax.axis_index("segment")
    if step == 0:
        (cand_len, cached, states, routes_hbm, attn_gain, ffn_gain, router_hbm,
         query_hbm, out_hbm, after_ref, outgoing, weights,
         routes, gains, router, w_query, w_out, keys, values, following,
         fresh, route_buf, sems) = refs
        fills = (
            (states.at[pl.ds(0, CAND_LEN), :], fresh),
            (attn_gain, gains.at[0]),
            (query_hbm, w_query),
            (out_hbm, w_out),
            (ffn_gain, gains.at[1]),
            (router_hbm, router),
            (routes_hbm, route_buf),
            (states.at[pl.ds(CAND_LEN, CAND_LEN), :], following),
        )
        copies = [pltpu.make_async_copy(*pair, sems.at[i]) for i, pair in enumerate(fills)]
        for copy in copies:
            copy.start()
        head_count = w_out.shape[0] // HEAD_DIM
        block_diagonal(cached, 0, keys)
        block_diagonal(cached, head_count, values)
        copies[0].wait()
        copies[1].wait()
        carried = fresh[...].astype(F32)
        normed = normalize(carried, gains[0]).astype(BF16)
        copies[2].wait()
    else:
        incoming, refs = refs[0], refs[1:]
        current = incoming[...]
        if step < CAND_DEV:
            current, refs = jnp.where(segment == 0, refs[0][...], current), refs[1:]
        (routes, gains, router, w_query, w_out, keys, values, after_ref, outgoing, weights) = refs
        carried = current.astype(F32)
        normed = normalize(carried, gains[0]).astype(BF16)
    queries = dot(normed, w_query[...]).astype(BF16)

    rows = carried.shape[0]
    sources = keys.shape[0] * HEAD_DIM // keys.shape[1]
    scores = dot(keys[...], queries, ((1,), (1,))) * (1.0 / math.sqrt(HEAD_DIM))
    scores = scores.reshape(-1, sources, rows)
    exponent = jnp.exp(scores - jnp.max(scores, axis=1, keepdims=True))
    share = exponent / jnp.sum(exponent, axis=1, keepdims=True)
    share = share.reshape(-1, rows).astype(BF16)
    context = dot(share, values[...], ((0,), (0,))).astype(BF16)
    if step == 0:
        copies[3].wait()
        copies[4].wait()
    after_attn = carried + dot(context, w_out[...])
    after_ref[...] = after_attn
    ffn_input = normalize(after_attn, gains[1]).astype(BF16)

    if step == 0:
        for copy in copies[5:]:
            copy.wait()
        position = lax.broadcasted_iota(jnp.int32, (1, CAND_LEN), 1)
        for micro in range(CAND_DEV):
            route = route_buf[:, micro * CAND_LEN : (micro + 1) * CAND_LEN]
            routes[micro] = jnp.where(position < cand_len[micro], route, -1)
    experts = router.shape[0]
    logits = dot(router[...], ffn_input, ((1,), (1,)))
    micro = jnp.clip(step - segment, 0, CAND_DEV - 1)
    route = routes[micro]
    labels = lax.broadcasted_iota(jnp.int32, (experts, rows), 0)
    first, second = route[0:1] == labels, route[1:2] == labels
    logit_first = jnp.sum(jnp.where(first, logits, 0.0), axis=0, keepdims=True)
    logit_second = jnp.sum(jnp.where(second, logits, 0.0), axis=0, keepdims=True)
    gate_first = jax.nn.sigmoid(logit_first - logit_second)
    gate_second = 1.0 - gate_first
    named = jnp.where(first | second, 1.0, 0.0).astype(BF16)
    earlier = lax.broadcasted_iota(jnp.int32, (rows, rows), 0) < lax.broadcasted_iota(
        jnp.int32, (rows, rows), 1
    )
    before = dot(named, jnp.where(earlier, 1.0, 0.0).astype(BF16))
    slots = lax.broadcasted_iota(jnp.int32, (experts * capacity, rows), 0)
    chosen = []
    for mask, row in ((first, 0), (second, 1)):
        slot = jnp.sum(jnp.where(mask, before, 0.0), axis=0, keepdims=True).astype(jnp.int32)
        chosen.append(slots == route[row : row + 1] * capacity + slot)
    select = jnp.where(chosen[0] | chosen[1], 1.0, 0.0).astype(BF16)
    outgoing[...] = dot(select, ffn_input).astype(BF16)
    weights[...] = jnp.where(chosen[0], gate_first, 0.0) + jnp.where(chosen[1], gate_second, 0.0)


def attend(step, capacity, sources, kept):
    if step == 0:
        cand_len, cached, *params = sources
        _, routes, _, _, router_t, w_query, w_out = params
        head_total, width = w_out.shape
        blocks = (cached.shape[0] * head_total // HEAD_DIM, head_total)
        kept_shapes = [
            pltpu.VMEM((CAND_DEV, 2, CAND_LEN), jnp.int32),
            pltpu.VMEM((2, 1, width), F32),
            *(pltpu.VMEM(array.shape, BF16) for array in (router_t, w_query, w_out)),
            pltpu.VMEM(blocks, BF16),
            pltpu.VMEM(blocks, BF16),
            pltpu.VMEM((CAND_LEN, width), BF16),
        ]
        inputs = [*in_hbm(cand_len), cached, *in_hbm(*params)]
        specs = [SMEM, VMEM] + [HBM] * len(params)
        scratch = [
            pltpu.VMEM((CAND_LEN, width), BF16),
            pltpu.VMEM(routes.shape, jnp.int32),
            pltpu.SemaphoreType.DMA((8,)),
        ]
    else:
        _, _, router_t, _, w_out, *_ = kept
        head_total, width = w_out.shape
        kept_shapes, scratch = [], []
        inputs = [*sources, *in_vmem(*kept)]
        specs = [VMEM] * len(inputs)
    slot_count = router_t.shape[0] * capacity
    outs = pl.pallas_call(
        functools.partial(attend_kernel, step, capacity),
        in_specs=specs,
        out_specs=[VMEM] * (3 + len(kept_shapes)),
        out_shape=[
            jax.ShapeDtypeStruct((CAND_LEN, width), F32),
            jax.ShapeDtypeStruct((slot_count, width), BF16),
            jax.ShapeDtypeStruct((slot_count, CAND_LEN), F32),
            *kept_shapes,
        ],
        scratch_shapes=scratch,
        compiler_params=pltpu.CompilerParams(vmem_limit_bytes=12 * MIB),
        cost_estimate=pl.CostEstimate(
            flops=6 * CAND_LEN * width * head_total,
            bytes_accessed=4 * width * head_total + 8 * CAND_LEN * width,
            transcendentals=0,
        ),
        name="attend",
    )(*inputs)
    return outs[:3], outs[3:]


def lane_chunks(mat):
    return [pl.ds(start, HIDDEN_CHUNK) for start in range(0, mat.shape[1], HIDDEN_CHUNK)]


def fill(source, mat, sems):
    copies = [
        pltpu.make_async_copy(source.at[:, lanes], mat.at[:, lanes], sems.at[i])
        for i, lanes in enumerate(lane_chunks(mat))
    ]
    for copy in copies:
        copy.start()
    return copies


def expert_kernel(rows, own_in, own_down, other_in, other_down, served, own_hidden, other_hidden):
    for units in lane_chunks(own_in):
        own_hidden[:, units] = jnp.maximum(dot(rows[...], own_in[:, units]), 0.0).astype(BF16)
        other_hidden[:, units] = jnp.maximum(dot(rows[...], other_in[:, units]), 0.0).astype(BF16)
    for lanes in lane_chunks(own_down):
        served[:, lanes] = (
            dot(own_hidden[...], own_down[:, lanes]) + dot(other_hidden[...], other_down[:, lanes])
        ).astype(BF16)


def own_half_kernel(rows, in_hbm_ref, down_hbm_ref, partial, own_in, own_down, hidden, sems):
    in_copies = fill(in_hbm_ref, own_in, sems.at[0])
    down_copies = fill(down_hbm_ref, own_down, sems.at[1])
    for units, copy in zip(lane_chunks(own_in), in_copies):
        copy.wait()
        hidden[:, units] = jnp.maximum(dot(rows[...], own_in[:, units]), 0.0).astype(BF16)
    for lanes, copy in zip(lane_chunks(own_down), down_copies):
        copy.wait()
        partial[:, lanes] = dot(hidden[...], own_down[:, lanes])


def other_hidden_kernel(rows, in_hbm_ref, hidden, other_in, sems):
    copies = fill(in_hbm_ref, other_in, sems)
    for units, copy in zip(lane_chunks(other_in), copies):
        copy.wait()
        hidden[:, units] = jnp.maximum(dot(rows[...], other_in[:, units]), 0.0).astype(BF16)


def other_out_kernel(hidden, partial, down_hbm_ref, served, other_down, sems):
    copies = fill(down_hbm_ref, other_down, sems)
    for lanes, copy in zip(lane_chunks(other_down), copies):
        copy.wait()
        served[:, lanes] = (partial[:, lanes] + dot(hidden[...], other_down[:, lanes])).astype(BF16)


def expert_call(kernel, name, inputs, streamed, out_shape, scratch):
    count = inputs[0].shape[0]
    mats = [array for array in (*inputs, *streamed) if array.shape[0] != count]
    semaphores = []
    if streamed:
        chunks = streamed[0].shape[1] // HIDDEN_CHUNK
        shape = (chunks,) if len(streamed) == 1 else (len(streamed), chunks)
        semaphores.append(pltpu.SemaphoreType.DMA(shape))
    return pl.pallas_call(
        kernel,
        in_specs=[VMEM] * len(inputs) + [HBM] * len(streamed),
        out_specs=[VMEM] * (1 + len(streamed)),
        out_shape=[out_shape, *(pltpu.VMEM(mat.shape, BF16) for mat in streamed)],
        scratch_shapes=scratch + semaphores,
        compiler_params=pltpu.CompilerParams(vmem_limit_bytes=12 * MIB),
        cost_estimate=pl.CostEstimate(
            flops=2 * count * sum(mat.size for mat in mats),
            bytes_accessed=2 * sum(mat.size for mat in mats),
            transcendentals=0,
        ),
        name=name,
    )(*inputs, *in_hbm(*streamed))


def expert_rows(rows, mats):
    count, units = rows.shape[0], mats[0].shape[1]
    scratch = [pltpu.VMEM((count, units), BF16), pltpu.VMEM((count, units), BF16)]
    shape = jax.ShapeDtypeStruct(rows.shape, BF16)
    return expert_call(expert_kernel, "experts", (rows, *in_vmem(*mats)), (), shape, scratch)[0]


def first_expert_rows(rows, own_in, own_down, other_in, other_down):
    count, units = rows.shape[0], own_in.shape[1]
    hidden_shape = jax.ShapeDtypeStruct((count, units), BF16)
    partial, own_in, own_down = expert_call(
        own_half_kernel, "own_half", (rows,), (own_in, own_down),
        jax.ShapeDtypeStruct(rows.shape, F32), [pltpu.VMEM((count, units), BF16)],
    )
    hidden, other_in = expert_call(
        other_hidden_kernel, "other_hidden", (rows,), (other_in,), hidden_shape, []
    )
    served, other_down = expert_call(
        other_out_kernel, "other_out", (hidden, partial), (other_down,),
        jax.ShapeDtypeStruct(rows.shape, BF16), [],
    )
    return served, (own_in, own_down, other_in, other_down)


def mixed(after_attn, weights, expert_out):
    gates = weights[...]
    coarse = gates.astype(BF16)
    fine = (gates - coarse.astype(F32)).astype(BF16)
    rows = expert_out[...]
    mixture = dot(coarse, rows, ((0,), (0,))) + dot(fine, rows, ((0,), (0,)))
    return (after_attn[...] + mixture).astype(BF16)


def combine_kernel(after_attn, weights, expert_out, result):
    result[...] = mixed(after_attn, weights, expert_out)


def place_kernel(after_attn, weights, expert_out, *refs):
    earlier, (output, result, sems) = refs[:-3], refs[-3:]
    segment = lax.axis_index("segment")

    def place(source, micro):
        rows = pl.ds(micro * CAND_LEN, CAND_LEN)
        return pltpu.make_async_copy(source, output.at[rows, :], sems.at[micro])

    last = len(earlier)
    for micro in range(CAND_DEV):
        for step in range(micro, last):

            @pl.when(segment + micro == step)
            def _():
                place(earlier[step], micro).start()

    result[...] = mixed(after_attn, weights, expert_out)
    for micro in range(CAND_DEV):

        @pl.when(segment + micro == last)
        def _():
            place(result, micro).start()

    for micro in range(CAND_DEV):
        place(result, micro).wait()


def combine(after_attn, weights, expert_out, earlier=()):
    rows, width = after_attn.shape
    inputs = [after_attn, weights, expert_out]
    specs = [VMEM] * 3
    scratch = []
    out_shape, out_spec = jax.ShapeDtypeStruct((rows, width), BF16), VMEM
    if earlier:
        inputs += in_vmem(*earlier)
        specs += [VMEM] * len(earlier)
        scratch = [pltpu.VMEM((rows, width), BF16), pltpu.SemaphoreType.DMA((CAND_DEV,))]
        out_shape, out_spec = jax.ShapeDtypeStruct((CAND_DEV * rows, width), BF16), HBM
    return pl.pallas_call(
        place_kernel if earlier else combine_kernel,
        in_specs=specs,
        out_specs=out_spec,
        out_shape=out_shape,
        scratch_shapes=scratch,
        compiler_params=pltpu.CompilerParams(vmem_limit_bytes=8 * MIB),
        cost_estimate=pl.CostEstimate(
            flops=4 * weights.size * width,
            bytes_accessed=6 * after_attn.size + 2 * expert_out.size,
            transcendentals=0,
        ),
        name="combine",
    )(*inputs)


def local(
    states, cand_len, routes, enc_kv, attn_gain, ffn_gain, w_query, w_out, w_router, w_in, w_down
):
    n_segment = lax.axis_size("segment")
    n_expert = lax.axis_size("expert")
    model_width = states.shape[1]
    experts = w_router.shape[2]
    capacity = 2 * ((5 * CAND_LEN + 4 * experts - 1) // (4 * experts))
    core_pairs = [(i, i ^ 1) for i in range(n_expert)]
    same_core = [list(range(core, n_expert, 2)) for core in range(2)]

    def exchange(rows):
        blocks = rows.reshape(experts, capacity, model_width)
        moved = lax.all_to_all(
            blocks, "expert", split_axis=0, concat_axis=0, axis_index_groups=same_core, tiled=True
        )
        return moved.reshape(rows.shape)

    cached = lax.all_to_all(
        spread(enc_kv, n_expert), ("segment", "expert"), split_axis=0, concat_axis=0, tiled=True
    )
    own = (w_in[0, 0], w_down[0, 0])
    cached, *sent = lax.optimization_barrier((cached, *own))
    other = tuple(lax.ppermute(mat, "expert", core_pairs) for mat in sent)

    step_count = CAND_DEV + n_segment - 1
    earlier = []
    kept = ()
    for step in range(step_count):
        if step == 0:
            sources = (
                cand_len, cached, states, routes[0].T, attn_gain, ffn_gain,
                w_router[0].T, w_query[0], w_out[0],
            )
        elif step < CAND_DEV:
            sources = (incoming, following)
        else:
            sources = (incoming,)
        (after_attn, outgoing, weights), left = attend(step, capacity, sources, kept)
        if step == 0:
            *kept, following = left
        rows = exchange(outgoing)
        if step == 0:
            served, expert_mats = first_expert_rows(rows, *own, *other)
        else:
            served = expert_rows(rows, expert_mats)
        expert_out = exchange(served)
        if step + 1 < step_count:
            result = combine(after_attn, weights, expert_out)
            incoming = lax.ppermute(
                result, "segment", [(i, i + 1) for i in range(n_segment - 1)]
            )
            earlier.append(result)
    output = combine(after_attn, weights, expert_out, earlier)
    return output.reshape(1, CAND_DEV * CAND_LEN, model_width)


def solution(mesh):
    return jax.shard_map(
        local,
        mesh=mesh,
        in_specs=(
            P("expert", None),
            P("expert"),
            P("segment", "expert", None),
            P(None, ("segment", "expert"), None),
            P("segment", None),
            P("segment", None),
            P("segment", None, None),
            P("segment", None, None),
            P("segment", None, None),
            P("segment", "expert", None, None),
            P("segment", "expert", None, None),
        ),
        out_specs=P("segment", "expert", None),
        check_vma=False,
    )
```

```python
import functools
import math

import jax
import jax.numpy as jnp
from jax import lax
from jax.experimental import pallas as pl
from jax.experimental.pallas import tpu as pltpu
from jax.sharding import PartitionSpec as P

HEAD_DIM = 128
CAND_LEN = 64
CAND_DEV = 2
HIDDEN_CHUNK = 512
MIB = 1 << 20

EPSILON = 1e-05

VMEM = pl.BlockSpec(memory_space=pltpu.VMEM)
SMEM = pl.BlockSpec(memory_space=pltpu.SMEM)
HBM = pl.BlockSpec(memory_space=pltpu.HBM)
F32 = jnp.float32
BF16 = jnp.bfloat16


def in_hbm(*arrays):
    return [pltpu.with_memory_space_constraint(array, pltpu.HBM) for array in arrays]


def in_vmem(*arrays):
    return [pltpu.with_memory_space_constraint(array, pltpu.VMEM) for array in arrays]


def split(rows, blocks):
    size = rows.shape[0] // blocks
    return [rows[k * size : (k + 1) * size] for k in range(blocks)]


def joined(blocks):
    if len(blocks) == 1:
        return blocks[0][...]
    return jnp.concatenate([block[...].astype(F32) for block in blocks], axis=0).astype(BF16)


def normalize(carried, gain_row):
    average = jnp.mean(carried, axis=-1, keepdims=True)
    centered = carried - average
    variance = jnp.mean(centered * centered, axis=-1, keepdims=True)
    return gain_row * centered * lax.rsqrt(variance + EPSILON)


def dot(left, right, contract=((1,), (0,))):
    return lax.dot_general(left, right, (contract, ((), ())), preferred_element_type=F32)


def spread_kernel(copies_of, enc_kv, blocks):
    for layer in range(enc_kv.shape[0]):
        block = enc_kv[layer]
        for i in range(copies_of):
            blocks[layer * copies_of + i] = block


def spread(enc_kv, copies_of):
    layers, _, features = enc_kv.shape
    tiles = enc_kv.reshape(layers, features // HEAD_DIM, HEAD_DIM)
    return pl.pallas_call(
        functools.partial(spread_kernel, copies_of),
        in_specs=[VMEM],
        out_specs=VMEM,
        out_shape=jax.ShapeDtypeStruct((layers * copies_of, *tiles.shape[1:]), BF16),
        compiler_params=pltpu.CompilerParams(vmem_limit_bytes=8 * MIB),
        name="spread",
    )(tiles)


def project_kernel(states, gain, w_query, queries, fresh, gain_buf, query_buf, sems):
    fills = (
        (states.at[pl.ds(0, CAND_LEN), :], fresh),
        (gain, gain_buf),
        (w_query, query_buf),
    )
    copies = [pltpu.make_async_copy(*pair, sems.at[i]) for i, pair in enumerate(fills)]
    for copy in copies:
        copy.start()
    copies[0].wait()
    copies[1].wait()
    normed = normalize(fresh[...].astype(F32), gain_buf[...]).astype(BF16)
    copies[2].wait()
    queries[...] = dot(normed, query_buf[...]).astype(BF16)


def project(states, gain, w_query):
    width, head_total = w_query.shape
    return pl.pallas_call(
        project_kernel,
        in_specs=[HBM] * 3,
        out_specs=VMEM,
        out_shape=jax.ShapeDtypeStruct((CAND_LEN, head_total), BF16),
        scratch_shapes=[
            pltpu.VMEM((CAND_LEN, width), BF16),
            pltpu.VMEM((1, width), F32),
            pltpu.VMEM(w_query.shape, BF16),
            pltpu.SemaphoreType.DMA((3,)),
        ],
        compiler_params=pltpu.CompilerParams(vmem_limit_bytes=12 * MIB),
        cost_estimate=pl.CostEstimate(
            flops=2 * CAND_LEN * width * head_total,
            bytes_accessed=2 * width * head_total,
            transcendentals=0,
        ),
        name="project",
    )(*in_hbm(states, gain, w_query))


def block_diagonal(cached, first_head, blocks):
    sources = cached.shape[0]
    blocks[...] = jnp.zeros_like(blocks)
    for head in range(blocks.shape[1] // HEAD_DIM):
        rows = pl.ds(head * sources, sources)
        blocks[rows, pl.ds(head * HEAD_DIM, HEAD_DIM)] = cached[:, first_head + head, :]


def attend_kernel(step, capacity, blocks, *refs):
    segment = lax.axis_index("segment")
    if step == 0:
        (cand_len, queries_in, cached, states, routes_hbm, attn_gain, ffn_gain, router_hbm,
         query_hbm, out_hbm, expert_hbm), refs = refs[:11], refs[11:]
        after_ref, weights, *outgoing = refs[: 2 + blocks]
        (routes, gains, router, w_query, w_out, keys, values, following, expert_mat,
         fresh, route_buf, sems) = refs[2 + blocks :]
        fills = (
            (states.at[pl.ds(0, CAND_LEN), :], fresh),
            (ffn_gain, gains.at[1]),
            (out_hbm, w_out),
            (router_hbm, router),
            (routes_hbm, route_buf),
            (attn_gain, gains.at[0]),
            (states.at[pl.ds(CAND_LEN, CAND_LEN), :], following),
            (query_hbm, w_query),
            (expert_hbm, expert_mat),
        )
        copies = [pltpu.make_async_copy(*pair, sems.at[i]) for i, pair in enumerate(fills)]
        for copy in copies:
            copy.start()
        head_count = w_out.shape[0] // HEAD_DIM
        block_diagonal(cached, 0, keys)
        block_diagonal(cached, head_count, values)
        queries = queries_in[...]
        copies[0].wait()
        carried = fresh[...].astype(F32)
        copies[4].wait()
        copies = copies[:4] + copies[5:]
        position = lax.broadcasted_iota(jnp.int32, (1, CAND_LEN), 1)
        for micro in range(CAND_DEV):
            route = route_buf[:, micro * CAND_LEN : (micro + 1) * CAND_LEN]
            routes[micro] = jnp.where(position < cand_len[micro], route, -1)
    else:
        incoming, refs = refs[0], refs[1:]
        current = incoming[...]
        if step < CAND_DEV:
            current, refs = jnp.where(segment == 0, refs[0][...], current), refs[1:]
        routes, gains, router, w_query, w_out, keys, values, after_ref, weights, *outgoing = refs
        carried = current.astype(F32)
        normed = normalize(carried, gains[0]).astype(BF16)
        queries = dot(normed, w_query[...]).astype(BF16)

    rows = carried.shape[0]
    sources = keys.shape[0] * HEAD_DIM // keys.shape[1]
    scores = dot(keys[...], queries, ((1,), (1,))) * (1.0 / math.sqrt(HEAD_DIM))
    scores = scores.reshape(-1, sources, rows)
    exponent = jnp.exp(scores - jnp.max(scores, axis=1, keepdims=True))
    share = exponent / jnp.sum(exponent, axis=1, keepdims=True)
    share = share.reshape(-1, rows).astype(BF16)
    context = dot(share, values[...], ((0,), (0,))).astype(BF16)
    if step == 0:
        copies[1].wait()
        copies[2].wait()
    after_attn = carried + dot(context, w_out[...])
    after_ref[...] = after_attn
    ffn_input = normalize(after_attn, gains[1]).astype(BF16)

    if step == 0:
        copies[3].wait()
    experts = router.shape[0]
    logits = dot(router[...], ffn_input, ((1,), (1,)))
    micro = jnp.clip(step - segment, 0, CAND_DEV - 1)
    route = routes[micro]
    place = route
    if blocks > 1:
        place = jnp.where(route < 0, route, route ^ (lax.axis_index("expert") // 2))
    labels = lax.broadcasted_iota(jnp.int32, (experts, rows), 0)
    first, second = route[0:1] == labels, route[1:2] == labels
    logit_first = jnp.sum(jnp.where(first, logits, 0.0), axis=0, keepdims=True)
    logit_second = jnp.sum(jnp.where(second, logits, 0.0), axis=0, keepdims=True)
    gate_first = jax.nn.sigmoid(logit_first - logit_second)
    gate_second = 1.0 - gate_first
    named = jnp.where(first | second, 1.0, 0.0).astype(BF16)
    earlier = lax.broadcasted_iota(jnp.int32, (rows, rows), 0) < lax.broadcasted_iota(
        jnp.int32, (rows, rows), 1
    )
    before = dot(named, jnp.where(earlier, 1.0, 0.0).astype(BF16))
    slots = lax.broadcasted_iota(jnp.int32, (experts * capacity, rows), 0)
    chosen = []
    for mask, row in ((first, 0), (second, 1)):
        slot = jnp.sum(jnp.where(mask, before, 0.0), axis=0, keepdims=True).astype(jnp.int32)
        chosen.append(slots == place[row : row + 1] * capacity + slot)
    select = jnp.where(chosen[0] | chosen[1], 1.0, 0.0).astype(BF16)
    buffers = dot(select, ffn_input)
    for buffer, block in zip(split(buffers, blocks), outgoing):
        block[...] = buffer.astype(BF16)
    weights[...] = jnp.where(chosen[0], gate_first, 0.0) + jnp.where(chosen[1], gate_second, 0.0)
    if step == 0:
        for copy in copies[4:]:
            copy.wait()


def attend(step, capacity, blocks, sources, kept):
    if step == 0:
        cand_len, queries, cached, *params = sources
        _, routes, _, _, router_t, w_query, w_out, expert_mat = params
        head_total, width = w_out.shape
        diagonal = (cached.shape[0] * head_total // HEAD_DIM, head_total)
        kept_shapes = [
            pltpu.VMEM((CAND_DEV, 2, CAND_LEN), jnp.int32),
            pltpu.VMEM((2, 1, width), F32),
            *(pltpu.VMEM(array.shape, BF16) for array in (router_t, w_query, w_out)),
            pltpu.VMEM(diagonal, BF16),
            pltpu.VMEM(diagonal, BF16),
            pltpu.VMEM((CAND_LEN, width), BF16),
            pltpu.VMEM(expert_mat.shape, BF16),
        ]
        inputs = [*in_hbm(cand_len), queries, cached, *in_hbm(*params)]
        specs = [SMEM, VMEM, VMEM] + [HBM] * len(params)
        scratch = [
            pltpu.VMEM((CAND_LEN, width), BF16),
            pltpu.VMEM(routes.shape, jnp.int32),
            pltpu.SemaphoreType.DMA((9,)),
        ]
    else:
        _, _, router_t, _, w_out, *_ = kept
        head_total, width = w_out.shape
        kept_shapes, scratch = [], []
        inputs = [*sources, *in_vmem(*kept)]
        specs = [VMEM] * len(inputs)
    slot_count = router_t.shape[0] * capacity
    outs = pl.pallas_call(
        functools.partial(attend_kernel, step, capacity, blocks),
        in_specs=specs,
        out_specs=[VMEM] * (2 + blocks + len(kept_shapes)),
        out_shape=[
            jax.ShapeDtypeStruct((CAND_LEN, width), F32),
            jax.ShapeDtypeStruct((slot_count, CAND_LEN), F32),
            *[jax.ShapeDtypeStruct((slot_count // blocks, width), BF16)] * blocks,
            *kept_shapes,
        ],
        scratch_shapes=scratch,
        compiler_params=pltpu.CompilerParams(vmem_limit_bytes=12 * MIB),
        cost_estimate=pl.CostEstimate(
            flops=6 * CAND_LEN * width * head_total,
            bytes_accessed=4 * width * head_total + 8 * CAND_LEN * width,
            transcendentals=0,
        ),
        name="attend",
    )(*inputs)
    return outs[:2], outs[2 : 2 + blocks], outs[2 + blocks :]


def expert_kernel(blocks, stream, *refs):
    rows_in, refs = refs[:blocks], refs[blocks:]
    own_in, refs = refs[0], refs[1:]
    if stream:
        sources, served, refs = refs[:3], refs[3 : 3 + blocks], refs[3 + blocks :]
        (own_down, other_in, other_down), (rows, own_hidden, other_hidden, sems) = refs[:3], refs[3:]
    else:
        (own_down, other_in, other_down), refs = refs[:3], refs[3:]
        served, (rows, own_hidden, other_hidden) = refs[:blocks], refs[blocks:]
    chunks = [pl.ds(start, HIDDEN_CHUNK) for start in range(0, own_in.shape[1], HIDDEN_CHUNK)]

    def fill(source, mat, i):
        lanes = chunks[i]
        return pltpu.make_async_copy(
            sources[source].at[:, lanes], mat.at[:, lanes], sems.at[source, i]
        )

    if stream:
        for i in range(len(chunks)):
            fill(1, other_in, i).start()
        for i in range(len(chunks)):
            fill(0, own_down, i).start()
            fill(2, other_down, i).start()
    rows[...] = joined(rows_in)
    for units in chunks:
        own_hidden[:, units] = jnp.maximum(dot(rows[...], own_in[:, units]), 0.0).astype(BF16)
    for i, units in enumerate(chunks):
        if stream:
            fill(1, other_in, i).wait()
        other_hidden[:, units] = jnp.maximum(dot(rows[...], other_in[:, units]), 0.0).astype(BF16)
    for i, lanes in enumerate(chunks):
        if stream:
            fill(0, own_down, i).wait()
            fill(2, other_down, i).wait()
        out = dot(own_hidden[...], own_down[:, lanes]) + dot(other_hidden[...], other_down[:, lanes])
        for part, block in zip(split(out, blocks), served):
            block[:, lanes] = part.astype(BF16)


def expert_rows(rows_in, mats, stream):
    blocks = len(rows_in)
    width = rows_in[0].shape[1]
    count = blocks * rows_in[0].shape[0]
    units = mats[0].shape[1]
    scratch = [
        pltpu.VMEM((count, width), BF16),
        pltpu.VMEM((count, units), BF16),
        pltpu.VMEM((count, units), BF16),
    ]
    out_shape = [jax.ShapeDtypeStruct(rows.shape, BF16) for rows in rows_in]
    if stream:
        scratch.append(pltpu.SemaphoreType.DMA((3, units // HIDDEN_CHUNK)))
        out_shape += [pltpu.VMEM(mat.shape, BF16) for mat in mats[1:]]
    outs = pl.pallas_call(
        functools.partial(expert_kernel, blocks, stream),
        in_specs=[VMEM] * (blocks + 1) + [HBM if stream else VMEM] * 3,
        out_specs=[VMEM] * len(out_shape),
        out_shape=out_shape,
        scratch_shapes=scratch,
        compiler_params=pltpu.CompilerParams(vmem_limit_bytes=12 * MIB),
        cost_estimate=pl.CostEstimate(
            flops=8 * count * width * units,
            bytes_accessed=8 * width * units + 4 * count * width,
            transcendentals=0,
        ),
        name="experts",
    )(*rows_in, *in_vmem(mats[0]), *(in_hbm if stream else in_vmem)(*mats[1:]))
    return outs[:blocks], ((mats[0], *outs[blocks:]) if stream else mats)


def mixed(after_attn, weights, blocks):
    gates = weights[...]
    coarse = gates.astype(BF16)
    fine = (gates - coarse.astype(F32)).astype(BF16)
    rows = joined(blocks)
    mixture = dot(coarse, rows, ((0,), (0,))) + dot(fine, rows, ((0,), (0,)))
    return (after_attn[...] + mixture).astype(BF16)


def combine_kernel(blocks, after_attn, weights, *refs):
    result = refs[blocks]
    result[...] = mixed(after_attn, weights, refs[:blocks])


def place_kernel(blocks, after_attn, weights, *refs):
    served, earlier, (output, result, sems) = refs[:blocks], refs[blocks:-3], refs[-3:]
    segment = lax.axis_index("segment")

    def place(source, micro):
        rows = pl.ds(micro * CAND_LEN, CAND_LEN)
        return pltpu.make_async_copy(source, output.at[rows, :], sems.at[micro])

    last = len(earlier)
    for micro in range(CAND_DEV):
        for step in range(micro, last):

            @pl.when(segment + micro == step)
            def _():
                place(earlier[step], micro).start()

    result[...] = mixed(after_attn, weights, served)
    for micro in range(CAND_DEV):

        @pl.when(segment + micro == last)
        def _():
            place(result, micro).start()

    for micro in range(CAND_DEV):
        place(result, micro).wait()


def combine(after_attn, weights, served, earlier=()):
    rows, width = after_attn.shape
    inputs = [after_attn, weights, *served]
    scratch = []
    out_shape, out_spec = jax.ShapeDtypeStruct((rows, width), BF16), VMEM
    if earlier:
        inputs += in_vmem(*earlier)
        scratch = [pltpu.VMEM((rows, width), BF16), pltpu.SemaphoreType.DMA((CAND_DEV,))]
        out_shape, out_spec = jax.ShapeDtypeStruct((CAND_DEV * rows, width), BF16), HBM
    return pl.pallas_call(
        functools.partial(place_kernel if earlier else combine_kernel, len(served)),
        in_specs=[VMEM] * len(inputs),
        out_specs=out_spec,
        out_shape=out_shape,
        scratch_shapes=scratch,
        compiler_params=pltpu.CompilerParams(vmem_limit_bytes=8 * MIB),
        cost_estimate=pl.CostEstimate(
            flops=4 * weights.size * width,
            bytes_accessed=6 * after_attn.size + 2 * weights.shape[0] * width,
            transcendentals=0,
        ),
        name="combine",
    )(*inputs)


def local(
    states, cand_len, routes, enc_kv, attn_gain, ffn_gain, w_query, w_out, w_router, w_in, w_down
):
    n_segment = lax.axis_size("segment")
    n_expert = lax.axis_size("expert")
    model_width = states.shape[1]
    experts = w_router.shape[2]
    capacity = 2 * ((5 * CAND_LEN + 4 * experts - 1) // (4 * experts))
    core_pairs = [(i, i ^ 1) for i in range(n_expert)]
    same_core = [list(range(core, n_expert, 2)) for core in range(2)]
    blocks = experts if experts <= 4 else 1

    def exchange(parts):
        if blocks > 1:
            return [parts[0]] + [
                lax.ppermute(part, "expert", [(i, i ^ (2 * k)) for i in range(n_expert)])
                for k, part in enumerate(parts[1:], 1)
            ]
        rows = parts[0].reshape(experts, capacity, model_width)
        moved = lax.all_to_all(
            rows, "expert", split_axis=0, concat_axis=0, axis_index_groups=same_core, tiled=True
        )
        return [moved.reshape(parts[0].shape)]

    cached = lax.all_to_all(
        spread(enc_kv, n_expert), ("segment", "expert"), split_axis=0, concat_axis=0, tiled=True
    )
    own = (w_in[0, 0], w_down[0, 0])
    other = tuple(lax.ppermute(mat, "expert", core_pairs) for mat in own)

    queries = project(states, attn_gain, w_query[0])
    step_count = CAND_DEV + n_segment - 1
    earlier = []
    kept = ()
    for step in range(step_count):
        if step == 0:
            sources = (
                cand_len, queries, cached, states, routes[0].T, attn_gain, ffn_gain,
                w_router[0].T, w_query[0], w_out[0], own[0],
            )
        elif step < CAND_DEV:
            sources = (incoming, following)
        else:
            sources = (incoming,)
        (after_attn, weights), outgoing, left = attend(step, capacity, blocks, sources, kept)
        if step == 0:
            *kept, following, own_in = left
            expert_mats = (own_in, own[1], *other)
        served, expert_mats = expert_rows(exchange(outgoing), expert_mats, step == 0)
        served = exchange(served)
        if step + 1 < step_count:
            result = combine(after_attn, weights, served)
            incoming = lax.ppermute(
                result, "segment", [(i, i + 1) for i in range(n_segment - 1)]
            )
            earlier.append(result)
    output = combine(after_attn, weights, served, earlier)
    return output.reshape(1, CAND_DEV * CAND_LEN, model_width)


def solution(mesh):
    return jax.shard_map(
        local,
        mesh=mesh,
        in_specs=(
            P("expert", None),
            P("expert"),
            P("segment", "expert", None),
            P(None, ("segment", "expert"), None),
            P("segment", None),
            P("segment", None),
            P("segment", None, None),
            P("segment", None, None),
            P("segment", None, None),
            P("segment", "expert", None, None),
            P("segment", "expert", None, None),
        ),
        out_specs=P("segment", "expert", None),
        check_vma=False,
    )
```

```python
import functools
import math

import jax
import jax.numpy as jnp
from jax import lax
from jax.experimental import pallas as pl
from jax.experimental.pallas import tpu as pltpu
from jax.sharding import PartitionSpec as P

HEAD_DIM = 128
CAND_LEN = 64
CAND_DEV = 2
HIDDEN_CHUNK = 512
MIB = 1 << 20

EPSILON = 1e-05

VMEM = pl.BlockSpec(memory_space=pltpu.VMEM)
SMEM = pl.BlockSpec(memory_space=pltpu.SMEM)
HBM = pl.BlockSpec(memory_space=pltpu.HBM)
F32 = jnp.float32
BF16 = jnp.bfloat16


def in_hbm(*arrays):
    return [pltpu.with_memory_space_constraint(array, pltpu.HBM) for array in arrays]


def in_vmem(*arrays):
    return [pltpu.with_memory_space_constraint(array, pltpu.VMEM) for array in arrays]


def split(rows, blocks):
    size = rows.shape[0] // blocks
    return [rows[k * size : (k + 1) * size] for k in range(blocks)]


def joined(blocks):
    if len(blocks) == 1:
        return blocks[0][...]
    return jnp.concatenate([block[...].astype(F32) for block in blocks], axis=0).astype(BF16)


def normalize(carried, gain_row):
    average = jnp.mean(carried, axis=-1, keepdims=True)
    centered = carried - average
    variance = jnp.mean(centered * centered, axis=-1, keepdims=True)
    return gain_row * centered * lax.rsqrt(variance + EPSILON)


def dot(left, right, contract=((1,), (0,))):
    return lax.dot_general(left, right, (contract, ((), ())), preferred_element_type=F32)


def spread_kernel(copies_of, enc_kv, blocks):
    for layer in range(enc_kv.shape[0]):
        block = enc_kv[layer]
        for i in range(copies_of):
            blocks[layer * copies_of + i] = block


def spread(enc_kv, copies_of):
    layers, _, features = enc_kv.shape
    tiles = enc_kv.reshape(layers, features // HEAD_DIM, HEAD_DIM)
    return pl.pallas_call(
        functools.partial(spread_kernel, copies_of),
        in_specs=[VMEM],
        out_specs=VMEM,
        out_shape=jax.ShapeDtypeStruct((layers * copies_of, *tiles.shape[1:]), BF16),
        compiler_params=pltpu.CompilerParams(vmem_limit_bytes=8 * MIB),
        name="spread",
    )(tiles)


def project_kernel(states, gain, w_query, queries, fresh, gain_buf, query_buf, sems):
    fills = (
        (states.at[pl.ds(0, CAND_LEN), :], fresh),
        (gain, gain_buf),
        (w_query, query_buf),
    )
    copies = [pltpu.make_async_copy(*pair, sems.at[i]) for i, pair in enumerate(fills)]
    for copy in copies:
        copy.start()
    copies[0].wait()
    copies[1].wait()
    normed = normalize(fresh[...].astype(F32), gain_buf[...]).astype(BF16)
    copies[2].wait()
    queries[...] = dot(normed, query_buf[...]).astype(BF16)


def project(states, gain, w_query):
    width, head_total = w_query.shape
    return pl.pallas_call(
        project_kernel,
        in_specs=[HBM] * 3,
        out_specs=VMEM,
        out_shape=jax.ShapeDtypeStruct((CAND_LEN, head_total), BF16),
        scratch_shapes=[
            pltpu.VMEM((CAND_LEN, width), BF16),
            pltpu.VMEM((1, width), F32),
            pltpu.VMEM(w_query.shape, BF16),
            pltpu.SemaphoreType.DMA((3,)),
        ],
        compiler_params=pltpu.CompilerParams(vmem_limit_bytes=12 * MIB),
        cost_estimate=pl.CostEstimate(
            flops=2 * CAND_LEN * width * head_total,
            bytes_accessed=2 * width * head_total,
            transcendentals=0,
        ),
        name="project",
    )(*in_hbm(states, gain, w_query))


def block_diagonal(cached, first_head, blocks):
    sources = cached.shape[0]
    blocks[...] = jnp.zeros_like(blocks)
    for head in range(blocks.shape[1] // HEAD_DIM):
        rows = pl.ds(head * sources, sources)
        blocks[rows, pl.ds(head * HEAD_DIM, HEAD_DIM)] = cached[:, first_head + head, :]


def attend_kernel(step, capacity, blocks, *refs):
    segment = lax.axis_index("segment")
    if step == 0:
        (cand_len, queries_in, cached, states, routes_hbm, attn_gain, ffn_gain, router_hbm,
         query_hbm, out_hbm, expert_hbm), refs = refs[:11], refs[11:]
        after_ref, weights, *outgoing = refs[: 2 + blocks]
        (routes, gains, router, w_query, w_out, keys, values, following, expert_mat,
         fresh, route_buf, sems) = refs[2 + blocks :]
        fills = (
            (states.at[pl.ds(0, CAND_LEN), :], fresh),
            (ffn_gain, gains.at[1]),
            (out_hbm, w_out),
            (router_hbm, router),
            (routes_hbm, route_buf),
            (attn_gain, gains.at[0]),
            (states.at[pl.ds(CAND_LEN, CAND_LEN), :], following),
            (query_hbm, w_query),
            (expert_hbm, expert_mat),
        )
        copies = [pltpu.make_async_copy(*pair, sems.at[i]) for i, pair in enumerate(fills)]
        for copy in copies:
            copy.start()
        head_count = w_out.shape[0] // HEAD_DIM
        block_diagonal(cached, 0, keys)
        block_diagonal(cached, head_count, values)
        queries = queries_in[...]
        copies[0].wait()
        carried = fresh[...].astype(F32)
        copies[4].wait()
        copies = copies[:4] + copies[5:]
        position = lax.broadcasted_iota(jnp.int32, (1, CAND_LEN), 1)
        for micro in range(CAND_DEV):
            route = route_buf[:, micro * CAND_LEN : (micro + 1) * CAND_LEN]
            routes[micro] = jnp.where(position < cand_len[micro], route, -1)
    else:
        incoming, refs = refs[0], refs[1:]
        current = incoming[...]
        if step < CAND_DEV:
            current, refs = jnp.where(segment == 0, refs[0][...], current), refs[1:]
        routes, gains, router, w_query, w_out, keys, values, after_ref, weights, *outgoing = refs
        carried = current.astype(F32)
        normed = normalize(carried, gains[0]).astype(BF16)
        queries = dot(normed, w_query[...]).astype(BF16)

    rows = carried.shape[0]
    sources = keys.shape[0] * HEAD_DIM // keys.shape[1]
    scores = dot(keys[...], queries, ((1,), (1,))) * (1.0 / math.sqrt(HEAD_DIM))
    scores = scores.reshape(-1, sources, rows)
    exponent = jnp.exp(scores - jnp.max(scores, axis=1, keepdims=True))
    share = exponent / jnp.sum(exponent, axis=1, keepdims=True)
    share = share.reshape(-1, rows).astype(BF16)
    context = dot(share, values[...], ((0,), (0,))).astype(BF16)
    if step == 0:
        copies[1].wait()
        copies[2].wait()
    after_attn = carried + dot(context, w_out[...])
    after_ref[...] = after_attn
    ffn_input = normalize(after_attn, gains[1]).astype(BF16)

    if step == 0:
        copies[3].wait()
    experts = router.shape[0]
    logits = dot(router[...], ffn_input, ((1,), (1,)))
    micro = jnp.clip(step - segment, 0, CAND_DEV - 1)
    route = routes[micro]
    place = route
    if blocks > 1:
        place = jnp.where(route < 0, route, route ^ (lax.axis_index("expert") // 2))
    labels = lax.broadcasted_iota(jnp.int32, (experts, rows), 0)
    first, second = route[0:1] == labels, route[1:2] == labels
    logit_first = jnp.sum(jnp.where(first, logits, 0.0), axis=0, keepdims=True)
    logit_second = jnp.sum(jnp.where(second, logits, 0.0), axis=0, keepdims=True)
    gate_first = jax.nn.sigmoid(logit_first - logit_second)
    gate_second = 1.0 - gate_first
    named = jnp.where(first | second, 1.0, 0.0).astype(BF16)
    earlier = lax.broadcasted_iota(jnp.int32, (rows, rows), 0) < lax.broadcasted_iota(
        jnp.int32, (rows, rows), 1
    )
    before = dot(named, jnp.where(earlier, 1.0, 0.0).astype(BF16))
    slots = lax.broadcasted_iota(jnp.int32, (experts * capacity, rows), 0)
    chosen = []
    for mask, row in ((first, 0), (second, 1)):
        slot = jnp.sum(jnp.where(mask, before, 0.0), axis=0, keepdims=True).astype(jnp.int32)
        chosen.append(slots == place[row : row + 1] * capacity + slot)
    select = jnp.where(chosen[0] | chosen[1], 1.0, 0.0).astype(BF16)
    buffers = dot(select, ffn_input)
    for buffer, block in zip(split(buffers, blocks), outgoing):
        block[...] = buffer.astype(BF16)
    weights[...] = jnp.where(chosen[0], gate_first, 0.0) + jnp.where(chosen[1], gate_second, 0.0)
    if step == 0:
        for copy in copies[4:]:
            copy.wait()


def attend(step, capacity, blocks, sources, kept):
    if step == 0:
        cand_len, queries, cached, *params = sources
        _, routes, _, _, router_t, w_query, w_out, expert_mat = params
        head_total, width = w_out.shape
        diagonal = (cached.shape[0] * head_total // HEAD_DIM, head_total)
        kept_shapes = [
            pltpu.VMEM((CAND_DEV, 2, CAND_LEN), jnp.int32),
            pltpu.VMEM((2, 1, width), F32),
            *(pltpu.VMEM(array.shape, BF16) for array in (router_t, w_query, w_out)),
            pltpu.VMEM(diagonal, BF16),
            pltpu.VMEM(diagonal, BF16),
            pltpu.VMEM((CAND_LEN, width), BF16),
            pltpu.VMEM(expert_mat.shape, BF16),
        ]
        inputs = [*in_hbm(cand_len), queries, cached, *in_hbm(*params)]
        specs = [SMEM, VMEM, VMEM] + [HBM] * len(params)
        scratch = [
            pltpu.VMEM((CAND_LEN, width), BF16),
            pltpu.VMEM(routes.shape, jnp.int32),
            pltpu.SemaphoreType.DMA((9,)),
        ]
    else:
        _, _, router_t, _, w_out, *_ = kept
        head_total, width = w_out.shape
        kept_shapes, scratch = [], []
        inputs = [*sources, *in_vmem(*kept)]
        specs = [VMEM] * len(inputs)
    slot_count = router_t.shape[0] * capacity
    outs = pl.pallas_call(
        functools.partial(attend_kernel, step, capacity, blocks),
        in_specs=specs,
        out_specs=[VMEM] * (2 + blocks + len(kept_shapes)),
        out_shape=[
            jax.ShapeDtypeStruct((CAND_LEN, width), F32),
            jax.ShapeDtypeStruct((slot_count, CAND_LEN), F32),
            *[jax.ShapeDtypeStruct((slot_count // blocks, width), BF16)] * blocks,
            *kept_shapes,
        ],
        scratch_shapes=scratch,
        compiler_params=pltpu.CompilerParams(vmem_limit_bytes=12 * MIB),
        cost_estimate=pl.CostEstimate(
            flops=6 * CAND_LEN * width * head_total,
            bytes_accessed=4 * width * head_total + 8 * CAND_LEN * width,
            transcendentals=0,
        ),
        name="attend",
    )(*inputs)
    return outs[:2], outs[2 : 2 + blocks], outs[2 + blocks :]


def expert_kernel(blocks, stream, *refs):
    rows_in, refs = refs[:blocks], refs[blocks:]
    own_in, refs = refs[0], refs[1:]
    if stream:
        sources, served, refs = refs[:3], refs[3 : 3 + blocks], refs[3 + blocks :]
        (own_down, other_in, other_down), (rows, own_hidden, other_hidden, sems) = refs[:3], refs[3:]
    else:
        (own_down, other_in, other_down), refs = refs[:3], refs[3:]
        served, (rows, own_hidden, other_hidden) = refs[:blocks], refs[blocks:]
    chunks = [pl.ds(start, HIDDEN_CHUNK) for start in range(0, own_in.shape[1], HIDDEN_CHUNK)]

    def fill(source, mat, i):
        lanes = chunks[i]
        return pltpu.make_async_copy(
            sources[source].at[:, lanes], mat.at[:, lanes], sems.at[source, i]
        )

    if stream:
        for i in range(len(chunks)):
            fill(1, other_in, i).start()
        for i in range(len(chunks)):
            fill(0, own_down, i).start()
            fill(2, other_down, i).start()
    rows[...] = joined(rows_in)
    for units in chunks:
        own_hidden[:, units] = jnp.maximum(dot(rows[...], own_in[:, units]), 0.0).astype(BF16)
    for i, units in enumerate(chunks):
        if stream:
            fill(1, other_in, i).wait()
        other_hidden[:, units] = jnp.maximum(dot(rows[...], other_in[:, units]), 0.0).astype(BF16)
    for i, lanes in enumerate(chunks):
        if stream:
            fill(0, own_down, i).wait()
            fill(2, other_down, i).wait()
        out = dot(own_hidden[...], own_down[:, lanes]) + dot(other_hidden[...], other_down[:, lanes])
        for part, block in zip(split(out, blocks), served):
            block[:, lanes] = part.astype(BF16)


def expert_rows(rows_in, mats, stream):
    blocks = len(rows_in)
    width = rows_in[0].shape[1]
    count = blocks * rows_in[0].shape[0]
    units = mats[0].shape[1]
    scratch = [
        pltpu.VMEM((count, width), BF16),
        pltpu.VMEM((count, units), BF16),
        pltpu.VMEM((count, units), BF16),
    ]
    out_shape = [jax.ShapeDtypeStruct(rows.shape, BF16) for rows in rows_in]
    if stream:
        scratch.append(pltpu.SemaphoreType.DMA((3, units // HIDDEN_CHUNK)))
        out_shape += [pltpu.VMEM(mat.shape, BF16) for mat in mats[1:]]
    outs = pl.pallas_call(
        functools.partial(expert_kernel, blocks, stream),
        in_specs=[VMEM] * (blocks + 1) + [HBM if stream else VMEM] * 3,
        out_specs=[VMEM] * len(out_shape),
        out_shape=out_shape,
        scratch_shapes=scratch,
        compiler_params=pltpu.CompilerParams(vmem_limit_bytes=12 * MIB),
        cost_estimate=pl.CostEstimate(
            flops=8 * count * width * units,
            bytes_accessed=8 * width * units + 4 * count * width,
            transcendentals=0,
        ),
        name="experts",
    )(*rows_in, *in_vmem(mats[0]), *(in_hbm if stream else in_vmem)(*mats[1:]))
    return outs[:blocks], ((mats[0], *outs[blocks:]) if stream else mats)


def mixed(after_attn, weights, blocks):
    gates = weights[...]
    coarse = gates.astype(BF16)
    fine = (gates - coarse.astype(F32)).astype(BF16)
    rows = joined(blocks)
    mixture = dot(coarse, rows, ((0,), (0,))) + dot(fine, rows, ((0,), (0,)))
    return (after_attn[...] + mixture).astype(BF16)


def combine_kernel(blocks, after_attn, weights, *refs):
    result = refs[blocks]
    result[...] = mixed(after_attn, weights, refs[:blocks])


def place_kernel(blocks, after_attn, weights, *refs):
    served, earlier, (output, result, sems) = refs[:blocks], refs[blocks:-3], refs[-3:]
    segment = lax.axis_index("segment")

    def place(source, micro):
        rows = pl.ds(micro * CAND_LEN, CAND_LEN)
        return pltpu.make_async_copy(source, output.at[rows, :], sems.at[micro])

    last = len(earlier)
    for micro in range(CAND_DEV):
        for step in range(micro, last):

            @pl.when(segment + micro == step)
            def _():
                place(earlier[step], micro).start()

    result[...] = mixed(after_attn, weights, served)
    for micro in range(CAND_DEV):

        @pl.when(segment + micro == last)
        def _():
            place(result, micro).start()

    for micro in range(CAND_DEV):
        place(result, micro).wait()


def combine(after_attn, weights, served, earlier=()):
    rows, width = after_attn.shape
    inputs = [after_attn, weights, *served]
    scratch = []
    out_shape, out_spec = jax.ShapeDtypeStruct((rows, width), BF16), VMEM
    if earlier:
        inputs += in_vmem(*earlier)
        scratch = [pltpu.VMEM((rows, width), BF16), pltpu.SemaphoreType.DMA((CAND_DEV,))]
        out_shape, out_spec = jax.ShapeDtypeStruct((CAND_DEV * rows, width), BF16), HBM
    return pl.pallas_call(
        functools.partial(place_kernel if earlier else combine_kernel, len(served)),
        in_specs=[VMEM] * len(inputs),
        out_specs=out_spec,
        out_shape=out_shape,
        scratch_shapes=scratch,
        compiler_params=pltpu.CompilerParams(vmem_limit_bytes=8 * MIB),
        cost_estimate=pl.CostEstimate(
            flops=4 * weights.size * width,
            bytes_accessed=6 * after_attn.size + 2 * weights.shape[0] * width,
            transcendentals=0,
        ),
        name="combine",
    )(*inputs)


def local(
    states, cand_len, routes, enc_kv, attn_gain, ffn_gain, w_query, w_out, w_router, w_in, w_down
):
    n_segment = lax.axis_size("segment")
    n_expert = lax.axis_size("expert")
    model_width = states.shape[1]
    experts = w_router.shape[2]
    capacity = 2 * ((5 * CAND_LEN + 4 * experts - 1) // (4 * experts))
    core_pairs = [(i, i ^ 1) for i in range(n_expert)]
    same_core = [list(range(core, n_expert, 2)) for core in range(2)]
    blocks = experts if experts <= 4 else 1

    def to_chip(part, k):
        return lax.ppermute(part, "expert", [(i, i ^ (2 * k)) for i in range(n_expert)])

    def exchange(rows):
        parts = rows.reshape(experts, capacity, model_width)
        moved = lax.all_to_all(
            parts, "expert", split_axis=0, concat_axis=0, axis_index_groups=same_core, tiled=True
        )
        return moved.reshape(rows.shape)

    def through_experts(outgoing, mats, stream):
        if blocks == 1:
            served, mats = expert_rows([exchange(outgoing[0])], mats, stream)
            return [exchange(served[0])], mats
        received = {k: to_chip(outgoing[k], k) for k in (1, 3, 2) if k < blocks}
        received[0] = outgoing[0]
        returned = {}
        for group in (range(0, 2), range(2, blocks)):
            if group:
                served, mats = expert_rows([received[k] for k in group], mats, stream)
                stream = False
                for k, rows in reversed(list(zip(group, served))):
                    returned[k] = to_chip(rows, k) if k else rows
        return [returned[k] for k in range(blocks)], mats

    cached = lax.all_to_all(
        spread(enc_kv, n_expert), ("segment", "expert"), split_axis=0, concat_axis=0, tiled=True
    )
    own = (w_in[0, 0], w_down[0, 0])
    other = tuple(lax.ppermute(mat, "expert", core_pairs) for mat in own)

    queries = project(states, attn_gain, w_query[0])
    step_count = CAND_DEV + n_segment - 1
    earlier = []
    kept = ()
    for step in range(step_count):
        if step == 0:
            sources = (
                cand_len, queries, cached, states, routes[0].T, attn_gain, ffn_gain,
                w_router[0].T, w_query[0], w_out[0], own[0],
            )
        elif step < CAND_DEV:
            sources = (incoming, following)
        else:
            sources = (incoming,)
        (after_attn, weights), outgoing, left = attend(step, capacity, blocks, sources, kept)
        if step == 0:
            *kept, following, own_in = left
            expert_mats = (own_in, own[1], *other)
        served, expert_mats = through_experts(outgoing, expert_mats, step == 0)
        if step + 1 < step_count:
            result = combine(after_attn, weights, served)
            incoming = lax.ppermute(
                result, "segment", [(i, i + 1) for i in range(n_segment - 1)]
            )
            earlier.append(result)
    output = combine(after_attn, weights, served, earlier)
    return output.reshape(1, CAND_DEV * CAND_LEN, model_width)


def solution(mesh):
    return jax.shard_map(
        local,
        mesh=mesh,
        in_specs=(
            P("expert", None),
            P("expert"),
            P("segment", "expert", None),
            P(None, ("segment", "expert"), None),
            P("segment", None),
            P("segment", None),
            P("segment", None, None),
            P("segment", None, None),
            P("segment", None, None),
            P("segment", "expert", None, None),
            P("segment", "expert", None, None),
        ),
        out_specs=P("segment", "expert", None),
        check_vma=False,
    )
```

```python
import functools
import math

import jax
import jax.numpy as jnp
from jax import lax
from jax.experimental import pallas as pl
from jax.experimental.pallas import tpu as pltpu
from jax.sharding import PartitionSpec as P

HEAD_DIM = 128
CAND_LEN = 64
CAND_DEV = 2
HIDDEN_CHUNK = 512
MIB = 1 << 20

EPSILON = 1e-05

VMEM = pl.BlockSpec(memory_space=pltpu.VMEM)
SMEM = pl.BlockSpec(memory_space=pltpu.SMEM)
HBM = pl.BlockSpec(memory_space=pltpu.HBM)
F32 = jnp.float32
BF16 = jnp.bfloat16


def in_hbm(*arrays):
    return [pltpu.with_memory_space_constraint(array, pltpu.HBM) for array in arrays]


def in_vmem(*arrays):
    return [pltpu.with_memory_space_constraint(array, pltpu.VMEM) for array in arrays]


def split(rows, blocks):
    size = rows.shape[0] // blocks
    return [rows[k * size : (k + 1) * size] for k in range(blocks)]


def padded(lanes):
    return -(-lanes // 128) * 128


def gate_lanes(width, slot_count):
    starts = (width, width + padded(slot_count))
    return [slice(start, start + slot_count) for start in starts]


def joined(blocks):
    if len(blocks) == 1:
        return blocks[0][...]
    return jnp.concatenate([block[...].astype(F32) for block in blocks], axis=0).astype(BF16)


def mixed(residual, carry, blocks):
    rows = joined(blocks)
    coarse, fine = (carry[:, lanes] for lanes in gate_lanes(rows.shape[1], rows.shape[0]))
    return (residual + (dot(coarse, rows) + dot(fine, rows))).astype(BF16)


def normalize(carried, gain_row):
    average = jnp.mean(carried, axis=-1, keepdims=True)
    centered = carried - average
    variance = jnp.mean(centered * centered, axis=-1, keepdims=True)
    return gain_row * centered * lax.rsqrt(variance + EPSILON)


def dot(left, right, contract=((1,), (0,))):
    return lax.dot_general(left, right, (contract, ((), ())), preferred_element_type=F32)


def spread_kernel(copies_of, enc_kv, blocks):
    for layer in range(enc_kv.shape[0]):
        block = enc_kv[layer]
        for i in range(copies_of):
            blocks[layer * copies_of + i] = block


def spread(enc_kv, copies_of):
    layers, _, features = enc_kv.shape
    tiles = enc_kv.reshape(layers, features // HEAD_DIM, HEAD_DIM)
    return pl.pallas_call(
        functools.partial(spread_kernel, copies_of),
        in_specs=[VMEM],
        out_specs=VMEM,
        out_shape=jax.ShapeDtypeStruct((layers * copies_of, *tiles.shape[1:]), BF16),
        compiler_params=pltpu.CompilerParams(vmem_limit_bytes=8 * MIB),
        name="spread",
    )(tiles)


def project_kernel(states, gain, w_query, queries, fresh, gain_buf, query_buf, sems):
    fills = (
        (states.at[pl.ds(0, CAND_LEN), :], fresh),
        (gain, gain_buf),
        (w_query, query_buf),
    )
    copies = [pltpu.make_async_copy(*pair, sems.at[i]) for i, pair in enumerate(fills)]
    for copy in copies:
        copy.start()
    copies[0].wait()
    copies[1].wait()
    normed = normalize(fresh[...].astype(F32), gain_buf[...]).astype(BF16)
    copies[2].wait()
    queries[...] = dot(normed, query_buf[...]).astype(BF16)


def project(states, gain, w_query):
    width, head_total = w_query.shape
    return pl.pallas_call(
        project_kernel,
        in_specs=[HBM] * 3,
        out_specs=VMEM,
        out_shape=jax.ShapeDtypeStruct((CAND_LEN, head_total), BF16),
        scratch_shapes=[
            pltpu.VMEM((CAND_LEN, width), BF16),
            pltpu.VMEM((1, width), F32),
            pltpu.VMEM(w_query.shape, BF16),
            pltpu.SemaphoreType.DMA((3,)),
        ],
        compiler_params=pltpu.CompilerParams(vmem_limit_bytes=12 * MIB),
        cost_estimate=pl.CostEstimate(
            flops=2 * CAND_LEN * width * head_total,
            bytes_accessed=2 * width * head_total,
            transcendentals=0,
        ),
        name="project",
    )(*in_hbm(states, gain, w_query))


def block_diagonal(cached, first_head, blocks):
    sources = cached.shape[0]
    blocks[...] = jnp.zeros_like(blocks)
    for head in range(blocks.shape[1] // HEAD_DIM):
        rows = pl.ds(head * sources, sources)
        blocks[rows, pl.ds(head * HEAD_DIM, HEAD_DIM)] = cached[:, first_head + head, :]


def attend_kernel(step, capacity, blocks, last, *refs):
    segment = lax.axis_index("segment")
    if step == 0:
        (cand_len, queries_in, cached, states, routes_hbm, attn_gain, ffn_gain, router_hbm,
         query_hbm, out_hbm, expert_hbm), refs = refs[:11], refs[11:]
        carry, *outgoing = refs[: 1 + blocks]
        (routes, gains, router, w_query, w_out, keys, values, following, expert_mat,
         fresh, route_buf, sems) = refs[1 + blocks :]
        fills = (
            (states.at[pl.ds(0, CAND_LEN), :], fresh),
            (ffn_gain, gains.at[1]),
            (out_hbm, w_out),
            (router_hbm, router),
            (routes_hbm, route_buf),
            (attn_gain, gains.at[0]),
            (states.at[pl.ds(CAND_LEN, CAND_LEN), :], following),
            (query_hbm, w_query),
            (expert_hbm, expert_mat),
        )
        copies = [pltpu.make_async_copy(*pair, sems.at[i]) for i, pair in enumerate(fills)]
        for copy in copies:
            copy.start()
        head_count = w_out.shape[0] // HEAD_DIM
        block_diagonal(cached, 0, keys)
        block_diagonal(cached, head_count, values)
        queries = queries_in[...]
        copies[0].wait()
        carried = fresh[...].astype(F32)
        copies[4].wait()
        copies = copies[:4] + copies[5:]
        position = lax.broadcasted_iota(jnp.int32, (1, CAND_LEN), 1)
        for micro in range(CAND_DEV):
            route = route_buf[:, micro * CAND_LEN : (micro + 1) * CAND_LEN]
            routes[micro] = jnp.where(position < cand_len[micro], route, -1)
    else:
        carried_in, served, refs = refs[0], refs[1 : 1 + blocks], refs[1 + blocks :]
        width = served[0].shape[1]
        current = mixed(carried_in[:, :width].astype(F32), carried_in, served)
        if step < CAND_DEV:
            current, refs = jnp.where(segment == 0, refs[0][...], current), refs[1:]
        (routes, gains, router, w_query, w_out, keys, values), refs = refs[:7], refs[7:]
        result, carry, *outgoing = refs[: 2 + blocks]
        result[...] = current
        carried = current.astype(F32)
        normed = normalize(carried, gains[0]).astype(BF16)
        queries = dot(normed, w_query[...]).astype(BF16)

    rows = carried.shape[0]
    sources = keys.shape[0] * HEAD_DIM // keys.shape[1]
    scores = dot(keys[...], queries, ((1,), (1,))) * (1.0 / math.sqrt(HEAD_DIM))
    scores = scores.reshape(-1, sources, rows)
    exponent = jnp.exp(scores - jnp.max(scores, axis=1, keepdims=True))
    share = exponent / jnp.sum(exponent, axis=1, keepdims=True)
    share = share.reshape(-1, rows).astype(BF16)
    context = dot(share, values[...], ((0,), (0,))).astype(BF16)
    if step == 0:
        copies[1].wait()
        copies[2].wait()
    after_attn = carried + dot(context, w_out[...])
    width = after_attn.shape[1]
    carry[:, :width] = after_attn.astype(BF16)
    if last:
        refs[-1][...] = after_attn
    ffn_input = normalize(after_attn, gains[1]).astype(BF16)

    if step == 0:
        copies[3].wait()
    experts = router.shape[0]
    logits = dot(router[...], ffn_input, ((1,), (1,)))
    micro = jnp.clip(step - segment, 0, CAND_DEV - 1)
    route = routes[micro]
    place = route
    if blocks > 1:
        place = jnp.where(route < 0, route, route ^ (lax.axis_index("expert") // 2))
    labels = lax.broadcasted_iota(jnp.int32, (experts, rows), 0)
    first, second = route[0:1] == labels, route[1:2] == labels
    logit_first = jnp.sum(jnp.where(first, logits, 0.0), axis=0, keepdims=True)
    logit_second = jnp.sum(jnp.where(second, logits, 0.0), axis=0, keepdims=True)
    gate_first = jax.nn.sigmoid(logit_first - logit_second)
    gate_second = 1.0 - gate_first
    named = jnp.where(first | second, 1.0, 0.0).astype(BF16)
    earlier = lax.broadcasted_iota(jnp.int32, (rows, rows), 0) < lax.broadcasted_iota(
        jnp.int32, (rows, rows), 1
    )
    before = dot(named, jnp.where(earlier, 1.0, 0.0).astype(BF16))
    slots = lax.broadcasted_iota(jnp.int32, (experts * capacity, rows), 0)
    chosen = []
    for mask, row in ((first, 0), (second, 1)):
        slot = jnp.sum(jnp.where(mask, before, 0.0), axis=0, keepdims=True).astype(jnp.int32)
        chosen.append(slots == place[row : row + 1] * capacity + slot)
    select = jnp.where(chosen[0] | chosen[1], 1.0, 0.0).astype(BF16)
    buffers = dot(select, ffn_input)
    for buffer, block in zip(split(buffers, blocks), outgoing):
        block[...] = buffer.astype(BF16)
    gates = jnp.where(chosen[0], gate_first, 0.0) + jnp.where(chosen[1], gate_second, 0.0)
    gates = gates.T
    coarse = gates.astype(BF16)
    for part, lanes in zip((coarse, gates - coarse.astype(F32)), gate_lanes(width, gates.shape[1])):
        carry[:, lanes] = part.astype(BF16)
    if step == 0:
        for copy in copies[4:]:
            copy.wait()


def attend(step, capacity, blocks, last, sources, kept):
    if step == 0:
        cand_len, queries, cached, *params = sources
        _, routes, _, _, router_t, w_query, w_out, expert_mat = params
        head_total, width = w_out.shape
        diagonal = (cached.shape[0] * head_total // HEAD_DIM, head_total)
        more_shapes = [
            pltpu.VMEM((CAND_DEV, 2, CAND_LEN), jnp.int32),
            pltpu.VMEM((2, 1, width), F32),
            *(pltpu.VMEM(array.shape, BF16) for array in (router_t, w_query, w_out)),
            pltpu.VMEM(diagonal, BF16),
            pltpu.VMEM(diagonal, BF16),
            pltpu.VMEM((CAND_LEN, width), BF16),
            pltpu.VMEM(expert_mat.shape, BF16),
        ]
        inputs = [*in_hbm(cand_len), queries, cached, *in_hbm(*params)]
        specs = [SMEM, VMEM, VMEM] + [HBM] * len(params)
        scratch = [
            pltpu.VMEM((CAND_LEN, width), BF16),
            pltpu.VMEM(routes.shape, jnp.int32),
            pltpu.SemaphoreType.DMA((9,)),
        ]
        first_shapes = []
    else:
        _, _, router_t, _, w_out, *_ = kept
        head_total, width = w_out.shape
        scratch = []
        inputs = [*sources, *in_vmem(*kept)]
        specs = [VMEM] * len(inputs)
        first_shapes = [jax.ShapeDtypeStruct((CAND_LEN, width), BF16)]
        more_shapes = [jax.ShapeDtypeStruct((CAND_LEN, width), F32)] if last else []
    slot_count = router_t.shape[0] * capacity
    carry_width = gate_lanes(width, slot_count)[1].stop - slot_count + padded(slot_count)
    out_shape = [
        *first_shapes,
        jax.ShapeDtypeStruct((CAND_LEN, carry_width), BF16),
        *[jax.ShapeDtypeStruct((slot_count // blocks, width), BF16)] * blocks,
        *more_shapes,
    ]
    outs = pl.pallas_call(
        functools.partial(attend_kernel, step, capacity, blocks, last),
        in_specs=specs,
        out_specs=[VMEM] * len(out_shape),
        out_shape=out_shape,
        scratch_shapes=scratch,
        compiler_params=pltpu.CompilerParams(vmem_limit_bytes=12 * MIB),
        cost_estimate=pl.CostEstimate(
            flops=6 * CAND_LEN * width * head_total,
            bytes_accessed=4 * width * head_total + 8 * CAND_LEN * width,
            transcendentals=0,
        ),
        name="attend",
    )(*inputs)
    result, outs = (outs[0], outs[1:]) if first_shapes else (None, outs)
    return result, outs[0], outs[1 : 1 + blocks], outs[1 + blocks :]


def expert_kernel(blocks, stream, *refs):
    rows_in, refs = refs[:blocks], refs[blocks:]
    own_in, refs = refs[0], refs[1:]
    if stream:
        sources, served, refs = refs[:3], refs[3 : 3 + blocks], refs[3 + blocks :]
        (own_down, other_in, other_down), (rows, own_hidden, other_hidden, sems) = refs[:3], refs[3:]
    else:
        (own_down, other_in, other_down), refs = refs[:3], refs[3:]
        served, (rows, own_hidden, other_hidden) = refs[:blocks], refs[blocks:]
    chunks = [pl.ds(start, HIDDEN_CHUNK) for start in range(0, own_in.shape[1], HIDDEN_CHUNK)]

    def fill(source, mat, i):
        lanes = chunks[i]
        return pltpu.make_async_copy(
            sources[source].at[:, lanes], mat.at[:, lanes], sems.at[source, i]
        )

    if stream:
        for i in range(len(chunks)):
            fill(1, other_in, i).start()
        for i in range(len(chunks)):
            fill(0, own_down, i).start()
            fill(2, other_down, i).start()
    rows[...] = joined(rows_in)
    for units in chunks:
        own_hidden[:, units] = jnp.maximum(dot(rows[...], own_in[:, units]), 0.0).astype(BF16)
    for i, units in enumerate(chunks):
        if stream:
            fill(1, other_in, i).wait()
        other_hidden[:, units] = jnp.maximum(dot(rows[...], other_in[:, units]), 0.0).astype(BF16)
    for i, lanes in enumerate(chunks):
        if stream:
            fill(0, own_down, i).wait()
            fill(2, other_down, i).wait()
        out = dot(own_hidden[...], own_down[:, lanes]) + dot(other_hidden[...], other_down[:, lanes])
        for part, block in zip(split(out, blocks), served):
            block[:, lanes] = part.astype(BF16)


def expert_rows(rows_in, mats, stream):
    blocks = len(rows_in)
    width = rows_in[0].shape[1]
    count = blocks * rows_in[0].shape[0]
    units = mats[0].shape[1]
    scratch = [
        pltpu.VMEM((count, width), BF16),
        pltpu.VMEM((count, units), BF16),
        pltpu.VMEM((count, units), BF16),
    ]
    out_shape = [jax.ShapeDtypeStruct(rows.shape, BF16) for rows in rows_in]
    if stream:
        scratch.append(pltpu.SemaphoreType.DMA((3, units // HIDDEN_CHUNK)))
        out_shape += [pltpu.VMEM(mat.shape, BF16) for mat in mats[1:]]
    outs = pl.pallas_call(
        functools.partial(expert_kernel, blocks, stream),
        in_specs=[VMEM] * (blocks + 1) + [HBM if stream else VMEM] * 3,
        out_specs=[VMEM] * len(out_shape),
        out_shape=out_shape,
        scratch_shapes=scratch,
        compiler_params=pltpu.CompilerParams(vmem_limit_bytes=12 * MIB),
        cost_estimate=pl.CostEstimate(
            flops=8 * count * width * units,
            bytes_accessed=8 * width * units + 4 * count * width,
            transcendentals=0,
        ),
        name="experts",
    )(*rows_in, *in_vmem(mats[0]), *(in_hbm if stream else in_vmem)(*mats[1:]))
    return outs[:blocks], ((mats[0], *outs[blocks:]) if stream else mats)


def combine_kernel(blocks, after_attn, carry, *refs):
    result = refs[blocks]
    result[...] = mixed(after_attn[...], carry, refs[:blocks])


def place_kernel(blocks, after_attn, carry, *refs):
    served, earlier, (output, result, sems) = refs[:blocks], refs[blocks:-3], refs[-3:]
    segment = lax.axis_index("segment")
    end = lax.axis_size("segment") - 1
    back = len(earlier) - (CAND_DEV - 1)

    def place(source, micro):
        rows = pl.ds(micro * CAND_LEN, CAND_LEN)
        return pltpu.make_async_copy(source, output.at[rows, :], sems.at[micro])

    for micro in range(CAND_DEV):
        for step in range(micro, micro + end):

            @pl.when(segment + micro == step)
            def _():
                place(earlier[step], micro).start()

    for micro in range(CAND_DEV - 1):

        @pl.when(segment == end)
        def _():
            place(earlier[back + micro], micro).start()

    result[...] = mixed(after_attn[...], carry, served)

    @pl.when(segment == end)
    def _():
        place(result, CAND_DEV - 1).start()

    for micro in range(CAND_DEV):
        place(result, micro).wait()


def combine(after_attn, carry, served, earlier=()):
    rows, width = after_attn.shape
    inputs = [after_attn, carry, *served]
    scratch = []
    out_shape, out_spec = jax.ShapeDtypeStruct((rows, width), BF16), VMEM
    if earlier:
        inputs += in_vmem(*earlier)
        scratch = [pltpu.VMEM((rows, width), BF16), pltpu.SemaphoreType.DMA((CAND_DEV,))]
        out_shape, out_spec = jax.ShapeDtypeStruct((CAND_DEV * rows, width), BF16), HBM
    return pl.pallas_call(
        functools.partial(place_kernel if earlier else combine_kernel, len(served)),
        in_specs=[VMEM] * len(inputs),
        out_specs=out_spec,
        out_shape=out_shape,
        scratch_shapes=scratch,
        compiler_params=pltpu.CompilerParams(vmem_limit_bytes=8 * MIB),
        cost_estimate=pl.CostEstimate(
            flops=4 * carry.size, bytes_accessed=8 * after_attn.size, transcendentals=0
        ),
        name="combine",
    )(*inputs)


def local(
    states, cand_len, routes, enc_kv, attn_gain, ffn_gain, w_query, w_out, w_router, w_in, w_down
):
    n_segment = lax.axis_size("segment")
    n_expert = lax.axis_size("expert")
    model_width = states.shape[1]
    experts = w_router.shape[2]
    capacity = 2 * ((5 * CAND_LEN + 4 * experts - 1) // (4 * experts))
    core_pairs = [(i, i ^ 1) for i in range(n_expert)]
    same_core = [list(range(core, n_expert, 2)) for core in range(2)]
    blocks = experts if experts <= 4 else 1

    def to_chip(part, k):
        return lax.ppermute(part, "expert", [(i, i ^ (2 * k)) for i in range(n_expert)])

    def onward(part, k=0):
        pairs = [
            (s * n_expert + i, (s + 1) * n_expert + (i ^ (2 * k)))
            for s in range(n_segment - 1)
            for i in range(n_expert)
        ]
        return lax.ppermute(part, ("segment", "expert"), pairs)

    def exchange(parts):
        if blocks > 1:
            return [to_chip(part, k) if k else part for k, part in enumerate(parts)]
        rows = parts[0].reshape(experts, capacity, model_width)
        moved = lax.all_to_all(
            rows, "expert", split_axis=0, concat_axis=0, axis_index_groups=same_core, tiled=True
        )
        return [moved.reshape(parts[0].shape)]

    def exchange_onward(parts):
        if blocks > 1:
            return [onward(part, k) for k, part in enumerate(parts)]
        return [onward(part) for part in exchange(parts)]

    cached = lax.all_to_all(
        spread(enc_kv, n_expert), ("segment", "expert"), split_axis=0, concat_axis=0, tiled=True
    )
    own = (w_in[0, 0], w_down[0, 0])
    other = tuple(lax.ppermute(mat, "expert", core_pairs) for mat in own)

    queries = project(states, attn_gain, w_query[0])
    step_count = CAND_DEV + n_segment - 1
    came_back, own_results = [], []
    kept = ()
    for step in range(step_count):
        if step == 0:
            sources = (
                cand_len, queries, cached, states, routes[0].T, attn_gain, ffn_gain,
                w_router[0].T, w_query[0], w_out[0], own[0],
            )
        elif step < CAND_DEV:
            sources = (carried, *served, following)
        else:
            sources = (carried, *served)
        last = step >= n_segment - 1
        result, carry, outgoing, more = attend(step, capacity, blocks, last, sources, kept)
        if step == 0:
            *kept, following, own_in = more
            expert_mats = (own_in, own[1], *other)
        received = exchange(outgoing)
        if step + 1 < step_count:
            carried = onward(carry)
        if result is not None:
            pairs = [(s + 1, s) for s in range(n_segment - 1)]
            came_back.append(lax.ppermute(result, "segment", pairs))
        out_blocks, expert_mats = expert_rows(received, expert_mats, step == 0)
        if step + 1 < step_count:
            served = exchange_onward(out_blocks)
            if last:
                own_results.append(combine(more[0], carry, exchange(out_blocks)))
    output = combine(more[0], carry, exchange(out_blocks), [*came_back, *own_results])
    return output.reshape(1, CAND_DEV * CAND_LEN, model_width)


def solution(mesh):
    return jax.shard_map(
        local,
        mesh=mesh,
        in_specs=(
            P("expert", None),
            P("expert"),
            P("segment", "expert", None),
            P(None, ("segment", "expert"), None),
            P("segment", None),
            P("segment", None),
            P("segment", None, None),
            P("segment", None, None),
            P("segment", None, None),
            P("segment", "expert", None, None),
            P("segment", "expert", None, None),
        ),
        out_specs=P("segment", "expert", None),
        check_vma=False,
    )
```

```python
import functools
import math

import jax
import jax.numpy as jnp
from jax import lax
from jax.experimental import pallas as pl
from jax.experimental.pallas import tpu as pltpu
from jax.sharding import PartitionSpec as P

HEAD_DIM = 128
CAND_LEN = 64
CAND_DEV = 2
HIDDEN_CHUNK = 512
MIB = 1 << 20

EPSILON = 1e-05

VMEM = pl.BlockSpec(memory_space=pltpu.VMEM)
SMEM = pl.BlockSpec(memory_space=pltpu.SMEM)
HBM = pl.BlockSpec(memory_space=pltpu.HBM)
F32 = jnp.float32
BF16 = jnp.bfloat16


def in_hbm(*arrays):
    return [pltpu.with_memory_space_constraint(array, pltpu.HBM) for array in arrays]


def in_vmem(*arrays):
    return [pltpu.with_memory_space_constraint(array, pltpu.VMEM) for array in arrays]


def split(rows, blocks):
    size = rows.shape[0] // blocks
    return [rows[k * size : (k + 1) * size] for k in range(blocks)]


def joined(blocks):
    if len(blocks) == 1:
        return blocks[0][...]
    return jnp.concatenate([block[...].astype(F32) for block in blocks], axis=0).astype(BF16)


def normalize(carried, gain_row):
    average = jnp.mean(carried, axis=-1, keepdims=True)
    centered = carried - average
    variance = jnp.mean(centered * centered, axis=-1, keepdims=True)
    return gain_row * centered * lax.rsqrt(variance + EPSILON)


def dot(left, right, contract=((1,), (0,))):
    return lax.dot_general(left, right, (contract, ((), ())), preferred_element_type=F32)


def spread_kernel(copies_of, enc_kv, blocks):
    for layer in range(enc_kv.shape[0]):
        block = enc_kv[layer]
        for i in range(copies_of):
            blocks[layer * copies_of + i] = block


def spread(enc_kv, copies_of):
    layers, _, features = enc_kv.shape
    tiles = enc_kv.reshape(layers, features // HEAD_DIM, HEAD_DIM)
    return pl.pallas_call(
        functools.partial(spread_kernel, copies_of),
        in_specs=[VMEM],
        out_specs=VMEM,
        out_shape=jax.ShapeDtypeStruct((layers * copies_of, *tiles.shape[1:]), BF16),
        compiler_params=pltpu.CompilerParams(vmem_limit_bytes=8 * MIB),
        name="spread",
    )(tiles)


def project_kernel(states, gain, w_query, queries, fresh, gain_buf, query_buf, sems):
    fills = (
        (states.at[pl.ds(0, CAND_LEN), :], fresh),
        (gain, gain_buf),
        (w_query, query_buf),
    )
    copies = [pltpu.make_async_copy(*pair, sems.at[i]) for i, pair in enumerate(fills)]
    for copy in copies:
        copy.start()
    copies[0].wait()
    copies[1].wait()
    normed = normalize(fresh[...].astype(F32), gain_buf[...]).astype(BF16)
    copies[2].wait()
    queries[...] = dot(normed, query_buf[...]).astype(BF16)


def project(states, gain, w_query):
    width, head_total = w_query.shape
    return pl.pallas_call(
        project_kernel,
        in_specs=[HBM] * 3,
        out_specs=VMEM,
        out_shape=jax.ShapeDtypeStruct((CAND_LEN, head_total), BF16),
        scratch_shapes=[
            pltpu.VMEM((CAND_LEN, width), BF16),
            pltpu.VMEM((1, width), F32),
            pltpu.VMEM(w_query.shape, BF16),
            pltpu.SemaphoreType.DMA((3,)),
        ],
        compiler_params=pltpu.CompilerParams(vmem_limit_bytes=12 * MIB),
        cost_estimate=pl.CostEstimate(
            flops=2 * CAND_LEN * width * head_total,
            bytes_accessed=2 * width * head_total,
            transcendentals=0,
        ),
        name="project",
    )(*in_hbm(states, gain, w_query))


def block_diagonal(cached, first_head, blocks):
    sources = cached.shape[0]
    blocks[...] = jnp.zeros_like(blocks)
    for head in range(blocks.shape[1] // HEAD_DIM):
        rows = pl.ds(head * sources, sources)
        blocks[rows, pl.ds(head * HEAD_DIM, HEAD_DIM)] = cached[:, first_head + head, :]


def attend_kernel(step, capacity, blocks, *refs):
    segment = lax.axis_index("segment")
    if step == 0:
        (cand_len, queries_in, cached, states, routes_hbm, attn_gain, ffn_gain, router_hbm,
         query_hbm, out_hbm, expert_hbm), refs = refs[:11], refs[11:]
        after_ref, weights, *outgoing = refs[: 2 + blocks]
        (routes, gains, router, w_query, w_out, keys, values, following, expert_mat,
         fresh, route_buf, sems) = refs[2 + blocks :]
        fills = (
            (states.at[pl.ds(0, CAND_LEN), :], fresh),
            (ffn_gain, gains.at[1]),
            (out_hbm, w_out),
            (router_hbm, router),
            (routes_hbm, route_buf),
            (attn_gain, gains.at[0]),
            (states.at[pl.ds(CAND_LEN, CAND_LEN), :], following),
            (query_hbm, w_query),
            (expert_hbm, expert_mat),
        )
        copies = [pltpu.make_async_copy(*pair, sems.at[i]) for i, pair in enumerate(fills)]
        for copy in copies:
            copy.start()
        head_count = w_out.shape[0] // HEAD_DIM
        block_diagonal(cached, 0, keys)
        block_diagonal(cached, head_count, values)
        queries = queries_in[...]
        copies[0].wait()
        carried = fresh[...].astype(F32)
        copies[4].wait()
        copies = copies[:4] + copies[5:]
        position = lax.broadcasted_iota(jnp.int32, (1, CAND_LEN), 1)
        for micro in range(CAND_DEV):
            route = route_buf[:, micro * CAND_LEN : (micro + 1) * CAND_LEN]
            routes[micro] = jnp.where(position < cand_len[micro], route, -1)
    else:
        from_even, from_odd, refs = refs[0], refs[1], refs[2:]
        current = jnp.where(lax.rem(segment, 2) == 1, from_even[...], from_odd[...])
        if step < CAND_DEV:
            current, refs = jnp.where(segment == 0, refs[0][...], current), refs[1:]
        routes, gains, router, w_query, w_out, keys, values, after_ref, weights, *outgoing = refs
        carried = current.astype(F32)
        normed = normalize(carried, gains[0]).astype(BF16)
        queries = dot(normed, w_query[...]).astype(BF16)

    rows = carried.shape[0]
    sources = keys.shape[0] * HEAD_DIM // keys.shape[1]
    scores = dot(keys[...], queries, ((1,), (1,))) * (1.0 / math.sqrt(HEAD_DIM))
    scores = scores.reshape(-1, sources, rows)
    exponent = jnp.exp(scores - jnp.max(scores, axis=1, keepdims=True))
    share = exponent / jnp.sum(exponent, axis=1, keepdims=True)
    share = share.reshape(-1, rows).astype(BF16)
    context = dot(share, values[...], ((0,), (0,))).astype(BF16)
    if step == 0:
        copies[1].wait()
        copies[2].wait()
    after_attn = carried + dot(context, w_out[...])
    after_ref[...] = after_attn
    ffn_input = normalize(after_attn, gains[1]).astype(BF16)

    if step == 0:
        copies[3].wait()
    experts = router.shape[0]
    logits = dot(router[...], ffn_input, ((1,), (1,)))
    micro = jnp.clip(step - segment, 0, CAND_DEV - 1)
    route = routes[micro]
    place = route
    if blocks > 1:
        place = jnp.where(route < 0, route, route ^ (lax.axis_index("expert") // 2))
    labels = lax.broadcasted_iota(jnp.int32, (experts, rows), 0)
    first, second = route[0:1] == labels, route[1:2] == labels
    logit_first = jnp.sum(jnp.where(first, logits, 0.0), axis=0, keepdims=True)
    logit_second = jnp.sum(jnp.where(second, logits, 0.0), axis=0, keepdims=True)
    gate_first = jax.nn.sigmoid(logit_first - logit_second)
    gate_second = 1.0 - gate_first
    named = jnp.where(first | second, 1.0, 0.0).astype(BF16)
    earlier = lax.broadcasted_iota(jnp.int32, (rows, rows), 0) < lax.broadcasted_iota(
        jnp.int32, (rows, rows), 1
    )
    before = dot(named, jnp.where(earlier, 1.0, 0.0).astype(BF16))
    slots = lax.broadcasted_iota(jnp.int32, (experts * capacity, rows), 0)
    chosen = []
    for mask, row in ((first, 0), (second, 1)):
        slot = jnp.sum(jnp.where(mask, before, 0.0), axis=0, keepdims=True).astype(jnp.int32)
        chosen.append(slots == place[row : row + 1] * capacity + slot)
    select = jnp.where(chosen[0] | chosen[1], 1.0, 0.0).astype(BF16)
    buffers = dot(select, ffn_input)
    for buffer, block in zip(split(buffers, blocks), outgoing):
        block[...] = buffer.astype(BF16)
    weights[...] = jnp.where(chosen[0], gate_first, 0.0) + jnp.where(chosen[1], gate_second, 0.0)
    if step == 0:
        for copy in copies[4:]:
            copy.wait()


def attend(step, capacity, blocks, sources, kept):
    if step == 0:
        cand_len, queries, cached, *params = sources
        _, routes, _, _, router_t, w_query, w_out, expert_mat = params
        head_total, width = w_out.shape
        diagonal = (cached.shape[0] * head_total // HEAD_DIM, head_total)
        kept_shapes = [
            pltpu.VMEM((CAND_DEV, 2, CAND_LEN), jnp.int32),
            pltpu.VMEM((2, 1, width), F32),
            *(pltpu.VMEM(array.shape, BF16) for array in (router_t, w_query, w_out)),
            pltpu.VMEM(diagonal, BF16),
            pltpu.VMEM(diagonal, BF16),
            pltpu.VMEM((CAND_LEN, width), BF16),
            pltpu.VMEM(expert_mat.shape, BF16),
        ]
        inputs = [*in_hbm(cand_len), queries, cached, *in_hbm(*params)]
        specs = [SMEM, VMEM, VMEM] + [HBM] * len(params)
        scratch = [
            pltpu.VMEM((CAND_LEN, width), BF16),
            pltpu.VMEM(routes.shape, jnp.int32),
            pltpu.SemaphoreType.DMA((9,)),
        ]
    else:
        _, _, router_t, _, w_out, *_ = kept
        head_total, width = w_out.shape
        kept_shapes, scratch = [], []
        inputs = [*sources, *in_vmem(*kept)]
        specs = [VMEM] * len(inputs)
    slot_count = router_t.shape[0] * capacity
    outs = pl.pallas_call(
        functools.partial(attend_kernel, step, capacity, blocks),
        in_specs=specs,
        out_specs=[VMEM] * (2 + blocks + len(kept_shapes)),
        out_shape=[
            jax.ShapeDtypeStruct((CAND_LEN, width), F32),
            jax.ShapeDtypeStruct((slot_count, CAND_LEN), F32),
            *[jax.ShapeDtypeStruct((slot_count // blocks, width), BF16)] * blocks,
            *kept_shapes,
        ],
        scratch_shapes=scratch,
        compiler_params=pltpu.CompilerParams(vmem_limit_bytes=12 * MIB),
        cost_estimate=pl.CostEstimate(
            flops=6 * CAND_LEN * width * head_total,
            bytes_accessed=4 * width * head_total + 8 * CAND_LEN * width,
            transcendentals=0,
        ),
        name="attend",
    )(*inputs)
    return outs[:2], outs[2 : 2 + blocks], outs[2 + blocks :]


def expert_kernel(blocks, stream, *refs):
    rows_in, refs = refs[:blocks], refs[blocks:]
    own_in, refs = refs[0], refs[1:]
    if stream:
        sources, served, refs = refs[:3], refs[3 : 3 + blocks], refs[3 + blocks :]
        (own_down, other_in, other_down), (rows, own_hidden, other_hidden, sems) = refs[:3], refs[3:]
    else:
        (own_down, other_in, other_down), refs = refs[:3], refs[3:]
        served, (rows, own_hidden, other_hidden) = refs[:blocks], refs[blocks:]
    chunks = [pl.ds(start, HIDDEN_CHUNK) for start in range(0, own_in.shape[1], HIDDEN_CHUNK)]

    def fill(source, mat, i):
        lanes = chunks[i]
        return pltpu.make_async_copy(
            sources[source].at[:, lanes], mat.at[:, lanes], sems.at[source, i]
        )

    if stream:
        for i in range(len(chunks)):
            fill(1, other_in, i).start()
        for i in range(len(chunks)):
            fill(0, own_down, i).start()
            fill(2, other_down, i).start()
    rows[...] = joined(rows_in)
    for units in chunks:
        own_hidden[:, units] = jnp.maximum(dot(rows[...], own_in[:, units]), 0.0).astype(BF16)
    for i, units in enumerate(chunks):
        if stream:
            fill(1, other_in, i).wait()
        other_hidden[:, units] = jnp.maximum(dot(rows[...], other_in[:, units]), 0.0).astype(BF16)
    for i, lanes in enumerate(chunks):
        if stream:
            fill(0, own_down, i).wait()
            fill(2, other_down, i).wait()
        out = dot(own_hidden[...], own_down[:, lanes]) + dot(other_hidden[...], other_down[:, lanes])
        for part, block in zip(split(out, blocks), served):
            block[:, lanes] = part.astype(BF16)


def expert_rows(rows_in, mats, stream):
    blocks = len(rows_in)
    width = rows_in[0].shape[1]
    count = blocks * rows_in[0].shape[0]
    units = mats[0].shape[1]
    scratch = [
        pltpu.VMEM((count, width), BF16),
        pltpu.VMEM((count, units), BF16),
        pltpu.VMEM((count, units), BF16),
    ]
    out_shape = [jax.ShapeDtypeStruct(rows.shape, BF16) for rows in rows_in]
    if stream:
        scratch.append(pltpu.SemaphoreType.DMA((3, units // HIDDEN_CHUNK)))
        out_shape += [pltpu.VMEM(mat.shape, BF16) for mat in mats[1:]]
    outs = pl.pallas_call(
        functools.partial(expert_kernel, blocks, stream),
        in_specs=[VMEM] * (blocks + 1) + [HBM if stream else VMEM] * 3,
        out_specs=[VMEM] * len(out_shape),
        out_shape=out_shape,
        scratch_shapes=scratch,
        compiler_params=pltpu.CompilerParams(vmem_limit_bytes=12 * MIB),
        cost_estimate=pl.CostEstimate(
            flops=8 * count * width * units,
            bytes_accessed=8 * width * units + 4 * count * width,
            transcendentals=0,
        ),
        name="experts",
    )(*rows_in, *in_vmem(mats[0]), *(in_hbm if stream else in_vmem)(*mats[1:]))
    return outs[:blocks], ((mats[0], *outs[blocks:]) if stream else mats)


def mixed(after_attn, weights, blocks):
    gates = weights[...]
    coarse = gates.astype(BF16)
    fine = (gates - coarse.astype(F32)).astype(BF16)
    rows = joined(blocks)
    mixture = dot(coarse, rows, ((0,), (0,))) + dot(fine, rows, ((0,), (0,)))
    return (after_attn[...] + mixture).astype(BF16)


def combine_kernel(blocks, after_attn, weights, *refs):
    result = refs[blocks]
    result[...] = mixed(after_attn, weights, refs[:blocks])


def place_kernel(blocks, after_attn, weights, *refs):
    served, earlier, (output, result, sems) = refs[:blocks], refs[blocks:-3], refs[-3:]
    segment = lax.axis_index("segment")

    def place(source, micro):
        rows = pl.ds(micro * CAND_LEN, CAND_LEN)
        return pltpu.make_async_copy(source, output.at[rows, :], sems.at[micro])

    last = len(earlier)
    for micro in range(CAND_DEV):
        for step in range(micro, last):

            @pl.when(segment + micro == step)
            def _():
                place(earlier[step], micro).start()

    result[...] = mixed(after_attn, weights, served)
    for micro in range(CAND_DEV):

        @pl.when(segment + micro == last)
        def _():
            place(result, micro).start()

    for micro in range(CAND_DEV):
        place(result, micro).wait()


def combine(after_attn, weights, served, earlier=()):
    rows, width = after_attn.shape
    inputs = [after_attn, weights, *served]
    scratch = []
    out_shape, out_spec = jax.ShapeDtypeStruct((rows, width), BF16), VMEM
    if earlier:
        inputs += in_vmem(*earlier)
        scratch = [pltpu.VMEM((rows, width), BF16), pltpu.SemaphoreType.DMA((CAND_DEV,))]
        out_shape, out_spec = jax.ShapeDtypeStruct((CAND_DEV * rows, width), BF16), HBM
    return pl.pallas_call(
        functools.partial(place_kernel if earlier else combine_kernel, len(served)),
        in_specs=[VMEM] * len(inputs),
        out_specs=out_spec,
        out_shape=out_shape,
        scratch_shapes=scratch,
        compiler_params=pltpu.CompilerParams(vmem_limit_bytes=8 * MIB),
        cost_estimate=pl.CostEstimate(
            flops=4 * weights.size * width,
            bytes_accessed=6 * after_attn.size + 2 * weights.shape[0] * width,
            transcendentals=0,
        ),
        name="combine",
    )(*inputs)


def local(
    states, cand_len, routes, enc_kv, attn_gain, ffn_gain, w_query, w_out, w_router, w_in, w_down
):
    n_segment = lax.axis_size("segment")
    n_expert = lax.axis_size("expert")
    model_width = states.shape[1]
    experts = w_router.shape[2]
    capacity = 2 * ((5 * CAND_LEN + 4 * experts - 1) // (4 * experts))
    core_pairs = [(i, i ^ 1) for i in range(n_expert)]
    same_core = [list(range(core, n_expert, 2)) for core in range(2)]
    blocks = experts if experts <= 4 else 1

    def swap_sections(rows, lower):
        pairs = [(s, s + 1) for s in range(lower, n_segment - 1, 2)]
        return lax.ppermute(rows, "segment", pairs + [(t, s) for s, t in pairs])

    def exchange(parts):
        if blocks > 1:
            moved = {0: parts[0]}
            for k in (1, 3, 2):
                if k < blocks:
                    pairs = [(i, i ^ (2 * k)) for i in range(n_expert)]
                    moved[k] = lax.ppermute(parts[k], "expert", pairs)
            return [moved[k] for k in range(blocks)]
        rows = parts[0].reshape(experts, capacity, model_width)
        moved = lax.all_to_all(
            rows, "expert", split_axis=0, concat_axis=0, axis_index_groups=same_core, tiled=True
        )
        return [moved.reshape(parts[0].shape)]

    cached = lax.all_to_all(
        spread(enc_kv, n_expert), ("segment", "expert"), split_axis=0, concat_axis=0, tiled=True
    )
    own = (w_in[0, 0], w_down[0, 0])
    other = tuple(lax.ppermute(mat, "expert", core_pairs) for mat in own)

    queries = project(states, attn_gain, w_query[0])
    step_count = CAND_DEV + n_segment - 1
    earlier = []
    kept = ()
    for step in range(step_count):
        if step == 0:
            sources = (
                cand_len, queries, cached, states, routes[0].T, attn_gain, ffn_gain,
                w_router[0].T, w_query[0], w_out[0], own[0],
            )
        elif step < CAND_DEV:
            sources = (*incoming, following)
        else:
            sources = incoming
        (after_attn, weights), outgoing, left = attend(step, capacity, blocks, sources, kept)
        if step == 0:
            *kept, following, own_in = left
            expert_mats = (own_in, own[1], *other)
        served, expert_mats = expert_rows(exchange(outgoing), expert_mats, step == 0)
        served = exchange(served)
        if step + 1 < step_count:
            result = combine(after_attn, weights, served)
            incoming = [swap_sections(result, lower) for lower in range(2)]
            earlier.append(result)
    output = combine(after_attn, weights, served, earlier)
    return output.reshape(1, CAND_DEV * CAND_LEN, model_width)


def solution(mesh):
    return jax.shard_map(
        local,
        mesh=mesh,
        in_specs=(
            P("expert", None),
            P("expert"),
            P("segment", "expert", None),
            P(None, ("segment", "expert"), None),
            P("segment", None),
            P("segment", None),
            P("segment", None, None),
            P("segment", None, None),
            P("segment", None, None),
            P("segment", "expert", None, None),
            P("segment", "expert", None, None),
        ),
        out_specs=P("segment", "expert", None),
        check_vma=False,
    )
```

```python
import functools
import math

import jax
import jax.numpy as jnp
from jax import lax
from jax.experimental import pallas as pl
from jax.experimental.pallas import tpu as pltpu
from jax.sharding import PartitionSpec as P

HEAD_DIM = 128
CAND_LEN = 64
CAND_DEV = 2
HIDDEN_CHUNK = 512
MIB = 1 << 20

EPSILON = 1e-05

VMEM = pl.BlockSpec(memory_space=pltpu.VMEM)
SMEM = pl.BlockSpec(memory_space=pltpu.SMEM)
HBM = pl.BlockSpec(memory_space=pltpu.HBM)
F32 = jnp.float32
BF16 = jnp.bfloat16


def in_hbm(*arrays):
    return [pltpu.with_memory_space_constraint(array, pltpu.HBM) for array in arrays]


def in_vmem(*arrays):
    return [pltpu.with_memory_space_constraint(array, pltpu.VMEM) for array in arrays]


def split(rows, blocks):
    size = rows.shape[0] // blocks
    return [rows[k * size : (k + 1) * size] for k in range(blocks)]


def joined(blocks):
    if len(blocks) == 1:
        return blocks[0][...]
    return jnp.concatenate([block[...].astype(F32) for block in blocks], axis=0).astype(BF16)


def normalize(carried, gain_row):
    average = jnp.mean(carried, axis=-1, keepdims=True)
    centered = carried - average
    variance = jnp.mean(centered * centered, axis=-1, keepdims=True)
    return gain_row * centered * lax.rsqrt(variance + EPSILON)


def dot(left, right, contract=((1,), (0,))):
    return lax.dot_general(left, right, (contract, ((), ())), preferred_element_type=F32)


def spread_kernel(copies_of, enc_kv, blocks):
    for layer in range(enc_kv.shape[0]):
        block = enc_kv[layer]
        for i in range(copies_of):
            blocks[layer * copies_of + i] = block


def spread(enc_kv, copies_of):
    layers, _, features = enc_kv.shape
    tiles = enc_kv.reshape(layers, features // HEAD_DIM, HEAD_DIM)
    return pl.pallas_call(
        functools.partial(spread_kernel, copies_of),
        in_specs=[VMEM],
        out_specs=VMEM,
        out_shape=jax.ShapeDtypeStruct((layers * copies_of, *tiles.shape[1:]), BF16),
        compiler_params=pltpu.CompilerParams(vmem_limit_bytes=8 * MIB),
        name="spread",
    )(tiles)


def project_kernel(states, gain, w_query, queries, fresh, gain_buf, query_buf, sems):
    fills = (
        (states.at[pl.ds(0, CAND_LEN), :], fresh),
        (gain, gain_buf),
        (w_query, query_buf),
    )
    copies = [pltpu.make_async_copy(*pair, sems.at[i]) for i, pair in enumerate(fills)]
    for copy in copies:
        copy.start()
    copies[0].wait()
    copies[1].wait()
    normed = normalize(fresh[...].astype(F32), gain_buf[...]).astype(BF16)
    copies[2].wait()
    queries[...] = dot(normed, query_buf[...]).astype(BF16)


def project(states, gain, w_query):
    width, head_total = w_query.shape
    return pl.pallas_call(
        project_kernel,
        in_specs=[HBM] * 3,
        out_specs=VMEM,
        out_shape=jax.ShapeDtypeStruct((CAND_LEN, head_total), BF16),
        scratch_shapes=[
            pltpu.VMEM((CAND_LEN, width), BF16),
            pltpu.VMEM((1, width), F32),
            pltpu.VMEM(w_query.shape, BF16),
            pltpu.SemaphoreType.DMA((3,)),
        ],
        compiler_params=pltpu.CompilerParams(vmem_limit_bytes=12 * MIB),
        cost_estimate=pl.CostEstimate(
            flops=2 * CAND_LEN * width * head_total,
            bytes_accessed=2 * width * head_total,
            transcendentals=0,
        ),
        name="project",
    )(*in_hbm(states, gain, w_query))


def block_diagonal(cached, first_head, blocks):
    sources = cached.shape[0]
    blocks[...] = jnp.zeros_like(blocks)
    for head in range(blocks.shape[1] // HEAD_DIM):
        rows = pl.ds(head * sources, sources)
        blocks[rows, pl.ds(head * HEAD_DIM, HEAD_DIM)] = cached[:, first_head + head, :]


def has_candidate(step):
    micro = step - lax.axis_index("segment")
    return (micro >= 0) & (micro < CAND_DEV)


def later_attend_kernel(step, capacity, blocks, *refs):
    @pl.when(has_candidate(step))
    def _():
        attend_kernel(step, capacity, blocks, *refs)


def attend_kernel(step, capacity, blocks, *refs):
    segment = lax.axis_index("segment")
    if step == 0:
        (cand_len, queries_in, cached, states, routes_hbm, attn_gain, ffn_gain, router_hbm,
         query_hbm, out_hbm, expert_hbm), refs = refs[:11], refs[11:]
        after_ref, weights, *outgoing = refs[: 2 + blocks]
        (routes, gains, router, w_query, w_out, keys, values, following, expert_mat,
         fresh, route_buf, sems) = refs[2 + blocks :]
        fills = (
            (states.at[pl.ds(0, CAND_LEN), :], fresh),
            (ffn_gain, gains.at[1]),
            (out_hbm, w_out),
            (router_hbm, router),
            (routes_hbm, route_buf),
            (attn_gain, gains.at[0]),
            (states.at[pl.ds(CAND_LEN, CAND_LEN), :], following),
            (query_hbm, w_query),
            (expert_hbm, expert_mat),
        )
        copies = [pltpu.make_async_copy(*pair, sems.at[i]) for i, pair in enumerate(fills)]
        for copy in copies:
            copy.start()
        head_count = w_out.shape[0] // HEAD_DIM
        block_diagonal(cached, 0, keys)
        block_diagonal(cached, head_count, values)
        queries = queries_in[...]
        copies[0].wait()
        carried = fresh[...].astype(F32)
        copies[4].wait()
        copies = copies[:4] + copies[5:]
        position = lax.broadcasted_iota(jnp.int32, (1, CAND_LEN), 1)
        for micro in range(CAND_DEV):
            route = route_buf[:, micro * CAND_LEN : (micro + 1) * CAND_LEN]
            routes[micro] = jnp.where(position < cand_len[micro], route, -1)
    else:
        incoming, refs = refs[0], refs[1:]
        current = incoming[...]
        if step < CAND_DEV:
            current, refs = jnp.where(segment == 0, refs[0][...], current), refs[1:]
        routes, gains, router, w_query, w_out, keys, values, after_ref, weights, *outgoing = refs
        carried = current.astype(F32)
        normed = normalize(carried, gains[0]).astype(BF16)
        queries = dot(normed, w_query[...]).astype(BF16)

    rows = carried.shape[0]
    sources = keys.shape[0] * HEAD_DIM // keys.shape[1]
    scores = dot(keys[...], queries, ((1,), (1,))) * (1.0 / math.sqrt(HEAD_DIM))
    scores = scores.reshape(-1, sources, rows)
    exponent = jnp.exp(scores - jnp.max(scores, axis=1, keepdims=True))
    share = exponent / jnp.sum(exponent, axis=1, keepdims=True)
    share = share.reshape(-1, rows).astype(BF16)
    context = dot(share, values[...], ((0,), (0,))).astype(BF16)
    if step == 0:
        copies[1].wait()
        copies[2].wait()
    after_attn = carried + dot(context, w_out[...])
    after_ref[...] = after_attn
    ffn_input = normalize(after_attn, gains[1]).astype(BF16)

    if step == 0:
        copies[3].wait()
    experts = router.shape[0]
    logits = dot(router[...], ffn_input, ((1,), (1,)))
    micro = jnp.clip(step - segment, 0, CAND_DEV - 1)
    route = routes[micro]
    place = route
    if blocks > 1:
        place = jnp.where(route < 0, route, route ^ (lax.axis_index("expert") // 2))
    labels = lax.broadcasted_iota(jnp.int32, (experts, rows), 0)
    first, second = route[0:1] == labels, route[1:2] == labels
    logit_first = jnp.sum(jnp.where(first, logits, 0.0), axis=0, keepdims=True)
    logit_second = jnp.sum(jnp.where(second, logits, 0.0), axis=0, keepdims=True)
    gate_first = jax.nn.sigmoid(logit_first - logit_second)
    gate_second = 1.0 - gate_first
    named = jnp.where(first | second, 1.0, 0.0).astype(BF16)
    earlier = lax.broadcasted_iota(jnp.int32, (rows, rows), 0) < lax.broadcasted_iota(
        jnp.int32, (rows, rows), 1
    )
    before = dot(named, jnp.where(earlier, 1.0, 0.0).astype(BF16))
    slots = lax.broadcasted_iota(jnp.int32, (experts * capacity, rows), 0)
    chosen = []
    for mask, row in ((first, 0), (second, 1)):
        slot = jnp.sum(jnp.where(mask, before, 0.0), axis=0, keepdims=True).astype(jnp.int32)
        chosen.append(slots == place[row : row + 1] * capacity + slot)
    select = jnp.where(chosen[0] | chosen[1], 1.0, 0.0).astype(BF16)
    buffers = dot(select, ffn_input)
    for buffer, block in zip(split(buffers, blocks), outgoing):
        block[...] = buffer.astype(BF16)
    weights[...] = jnp.where(chosen[0], gate_first, 0.0) + jnp.where(chosen[1], gate_second, 0.0)
    if step == 0:
        for copy in copies[4:]:
            copy.wait()


def attend(step, capacity, blocks, sources, kept):
    if step == 0:
        cand_len, queries, cached, *params = sources
        _, routes, _, _, router_t, w_query, w_out, expert_mat = params
        head_total, width = w_out.shape
        diagonal = (cached.shape[0] * head_total // HEAD_DIM, head_total)
        kept_shapes = [
            pltpu.VMEM((CAND_DEV, 2, CAND_LEN), jnp.int32),
            pltpu.VMEM((2, 1, width), F32),
            *(pltpu.VMEM(array.shape, BF16) for array in (router_t, w_query, w_out)),
            pltpu.VMEM(diagonal, BF16),
            pltpu.VMEM(diagonal, BF16),
            pltpu.VMEM((CAND_LEN, width), BF16),
            pltpu.VMEM(expert_mat.shape, BF16),
        ]
        inputs = [*in_hbm(cand_len), queries, cached, *in_hbm(*params)]
        specs = [SMEM, VMEM, VMEM] + [HBM] * len(params)
        scratch = [
            pltpu.VMEM((CAND_LEN, width), BF16),
            pltpu.VMEM(routes.shape, jnp.int32),
            pltpu.SemaphoreType.DMA((9,)),
        ]
    else:
        _, _, router_t, _, w_out, *_ = kept
        head_total, width = w_out.shape
        kept_shapes, scratch = [], []
        inputs = [*sources, *in_vmem(*kept)]
        specs = [VMEM] * len(inputs)
    slot_count = router_t.shape[0] * capacity
    outs = pl.pallas_call(
        functools.partial(
            later_attend_kernel if step else attend_kernel, step, capacity, blocks
        ),
        in_specs=specs,
        out_specs=[VMEM] * (2 + blocks + len(kept_shapes)),
        out_shape=[
            jax.ShapeDtypeStruct((CAND_LEN, width), F32),
            jax.ShapeDtypeStruct((slot_count, CAND_LEN), F32),
            *[jax.ShapeDtypeStruct((slot_count // blocks, width), BF16)] * blocks,
            *kept_shapes,
        ],
        scratch_shapes=scratch,
        compiler_params=pltpu.CompilerParams(vmem_limit_bytes=12 * MIB),
        cost_estimate=pl.CostEstimate(
            flops=6 * CAND_LEN * width * head_total,
            bytes_accessed=4 * width * head_total + 8 * CAND_LEN * width,
            transcendentals=0,
        ),
        name="attend",
    )(*inputs)
    return outs[:2], outs[2 : 2 + blocks], outs[2 + blocks :]


def expert_kernel(blocks, stream, *refs):
    rows_in, refs = refs[:blocks], refs[blocks:]
    own_in, refs = refs[0], refs[1:]
    if stream:
        sources, served, refs = refs[:3], refs[3 : 3 + blocks], refs[3 + blocks :]
        (own_down, other_in, other_down), (rows, own_hidden, other_hidden, sems) = refs[:3], refs[3:]
    else:
        (own_down, other_in, other_down), refs = refs[:3], refs[3:]
        served, (rows, own_hidden, other_hidden) = refs[:blocks], refs[blocks:]
    chunks = [pl.ds(start, HIDDEN_CHUNK) for start in range(0, own_in.shape[1], HIDDEN_CHUNK)]

    def fill(source, mat, i):
        lanes = chunks[i]
        return pltpu.make_async_copy(
            sources[source].at[:, lanes], mat.at[:, lanes], sems.at[source, i]
        )

    if stream:
        for i in range(len(chunks)):
            fill(1, other_in, i).start()
        for i in range(len(chunks)):
            fill(0, own_down, i).start()
            fill(2, other_down, i).start()
    rows[...] = joined(rows_in)
    for units in chunks:
        own_hidden[:, units] = jnp.maximum(dot(rows[...], own_in[:, units]), 0.0).astype(BF16)
    for i, units in enumerate(chunks):
        if stream:
            fill(1, other_in, i).wait()
        other_hidden[:, units] = jnp.maximum(dot(rows[...], other_in[:, units]), 0.0).astype(BF16)
    for i, lanes in enumerate(chunks):
        if stream:
            fill(0, own_down, i).wait()
            fill(2, other_down, i).wait()
        out = dot(own_hidden[...], own_down[:, lanes]) + dot(other_hidden[...], other_down[:, lanes])
        for part, block in zip(split(out, blocks), served):
            block[:, lanes] = part.astype(BF16)


def later_expert_kernel(step, blocks, *refs):
    @pl.when(has_candidate(step))
    def _():
        expert_kernel(blocks, False, *refs)


def expert_rows(rows_in, mats, step):
    blocks, stream = len(rows_in), step == 0
    width = rows_in[0].shape[1]
    count = blocks * rows_in[0].shape[0]
    units = mats[0].shape[1]
    scratch = [
        pltpu.VMEM((count, width), BF16),
        pltpu.VMEM((count, units), BF16),
        pltpu.VMEM((count, units), BF16),
    ]
    out_shape = [jax.ShapeDtypeStruct(rows.shape, BF16) for rows in rows_in]
    if stream:
        scratch.append(pltpu.SemaphoreType.DMA((3, units // HIDDEN_CHUNK)))
        out_shape += [pltpu.VMEM(mat.shape, BF16) for mat in mats[1:]]
    outs = pl.pallas_call(
        functools.partial(expert_kernel, blocks, True)
        if stream
        else functools.partial(later_expert_kernel, step, blocks),
        in_specs=[VMEM] * (blocks + 1) + [HBM if stream else VMEM] * 3,
        out_specs=[VMEM] * len(out_shape),
        out_shape=out_shape,
        scratch_shapes=scratch,
        compiler_params=pltpu.CompilerParams(vmem_limit_bytes=12 * MIB),
        cost_estimate=pl.CostEstimate(
            flops=8 * count * width * units,
            bytes_accessed=8 * width * units + 4 * count * width,
            transcendentals=0,
        ),
        name="experts",
    )(*rows_in, *in_vmem(mats[0]), *(in_hbm if stream else in_vmem)(*mats[1:]))
    return outs[:blocks], ((mats[0], *outs[blocks:]) if stream else mats)


def mixed(after_attn, weights, blocks):
    gates = weights[...]
    coarse = gates.astype(BF16)
    fine = (gates - coarse.astype(F32)).astype(BF16)
    rows = joined(blocks)
    mixture = dot(coarse, rows, ((0,), (0,))) + dot(fine, rows, ((0,), (0,)))
    return (after_attn[...] + mixture).astype(BF16)


def combine_kernel(blocks, after_attn, weights, *refs):
    result = refs[blocks]
    result[...] = mixed(after_attn, weights, refs[:blocks])


def place_kernel(blocks, after_attn, weights, *refs):
    served, earlier, (output, result, sems) = refs[:blocks], refs[blocks:-3], refs[-3:]
    segment = lax.axis_index("segment")

    def place(source, micro):
        rows = pl.ds(micro * CAND_LEN, CAND_LEN)
        return pltpu.make_async_copy(source, output.at[rows, :], sems.at[micro])

    last = len(earlier)
    for micro in range(CAND_DEV):
        for step in range(micro, last):

            @pl.when(segment + micro == step)
            def _():
                place(earlier[step], micro).start()

    result[...] = mixed(after_attn, weights, served)
    for micro in range(CAND_DEV):

        @pl.when(segment + micro == last)
        def _():
            place(result, micro).start()

    for micro in range(CAND_DEV):
        place(result, micro).wait()


def combine(after_attn, weights, served, earlier=()):
    rows, width = after_attn.shape
    inputs = [after_attn, weights, *served]
    scratch = []
    out_shape, out_spec = jax.ShapeDtypeStruct((rows, width), BF16), VMEM
    if earlier:
        inputs += in_vmem(*earlier)
        scratch = [pltpu.VMEM((rows, width), BF16), pltpu.SemaphoreType.DMA((CAND_DEV,))]
        out_shape, out_spec = jax.ShapeDtypeStruct((CAND_DEV * rows, width), BF16), HBM
    return pl.pallas_call(
        functools.partial(place_kernel if earlier else combine_kernel, len(served)),
        in_specs=[VMEM] * len(inputs),
        out_specs=out_spec,
        out_shape=out_shape,
        scratch_shapes=scratch,
        compiler_params=pltpu.CompilerParams(vmem_limit_bytes=8 * MIB),
        cost_estimate=pl.CostEstimate(
            flops=4 * weights.size * width,
            bytes_accessed=6 * after_attn.size + 2 * weights.shape[0] * width,
            transcendentals=0,
        ),
        name="combine",
    )(*inputs)


def local(
    states, cand_len, routes, enc_kv, attn_gain, ffn_gain, w_query, w_out, w_router, w_in, w_down
):
    n_segment = lax.axis_size("segment")
    n_expert = lax.axis_size("expert")
    model_width = states.shape[1]
    experts = w_router.shape[2]
    capacity = 2 * ((5 * CAND_LEN + 4 * experts - 1) // (4 * experts))
    core_pairs = [(i, i ^ 1) for i in range(n_expert)]
    same_core = [list(range(core, n_expert, 2)) for core in range(2)]
    blocks = experts if experts <= 4 else 1

    def exchange(parts):
        if blocks > 1:
            return [parts[0]] + [
                lax.ppermute(part, "expert", [(i, i ^ (2 * k)) for i in range(n_expert)])
                for k, part in enumerate(parts[1:], 1)
            ]
        rows = parts[0].reshape(experts, capacity, model_width)
        moved = lax.all_to_all(
            rows, "expert", split_axis=0, concat_axis=0, axis_index_groups=same_core, tiled=True
        )
        return [moved.reshape(parts[0].shape)]

    cached = lax.all_to_all(
        spread(enc_kv, n_expert), ("segment", "expert"), split_axis=0, concat_axis=0, tiled=True
    )
    own = (w_in[0, 0], w_down[0, 0])
    other = tuple(lax.ppermute(mat, "expert", core_pairs) for mat in own)

    queries = project(states, attn_gain, w_query[0])
    step_count = CAND_DEV + n_segment - 1
    earlier = []
    kept = ()
    for step in range(step_count):
        if step == 0:
            sources = (
                cand_len, queries, cached, states, routes[0].T, attn_gain, ffn_gain,
                w_router[0].T, w_query[0], w_out[0], own[0],
            )
        elif step < CAND_DEV:
            sources = (incoming, following)
        else:
            sources = (incoming,)
        (after_attn, weights), outgoing, left = attend(step, capacity, blocks, sources, kept)
        if step == 0:
            *kept, following, own_in = left
            expert_mats = (own_in, own[1], *other)
        served, expert_mats = expert_rows(exchange(outgoing), expert_mats, step)
        served = exchange(served)
        if step + 1 < step_count:
            result = combine(after_attn, weights, served)
            incoming = lax.ppermute(
                result, "segment", [(i, i + 1) for i in range(n_segment - 1)]
            )
            earlier.append(result)
    output = combine(after_attn, weights, served, earlier)
    return output.reshape(1, CAND_DEV * CAND_LEN, model_width)


def solution(mesh):
    return jax.shard_map(
        local,
        mesh=mesh,
        in_specs=(
            P("expert", None),
            P("expert"),
            P("segment", "expert", None),
            P(None, ("segment", "expert"), None),
            P("segment", None),
            P("segment", None),
            P("segment", None, None),
            P("segment", None, None),
            P("segment", None, None),
            P("segment", "expert", None, None),
            P("segment", "expert", None, None),
        ),
        out_specs=P("segment", "expert", None),
        check_vma=False,
    )
```

```python
import functools
import math

import jax
import jax.numpy as jnp
from jax import lax
from jax.experimental import pallas as pl
from jax.experimental.pallas import tpu as pltpu
from jax.sharding import PartitionSpec as P

HEAD_DIM = 128
CAND_LEN = 64
CAND_DEV = 2
HIDDEN_CHUNK = 512
MIB = 1 << 20

EPSILON = 1e-05

VMEM = pl.BlockSpec(memory_space=pltpu.VMEM)
SMEM = pl.BlockSpec(memory_space=pltpu.SMEM)
HBM = pl.BlockSpec(memory_space=pltpu.HBM)
F32 = jnp.float32
BF16 = jnp.bfloat16


def in_hbm(*arrays):
    return [pltpu.with_memory_space_constraint(array, pltpu.HBM) for array in arrays]


def in_vmem(*arrays):
    return [pltpu.with_memory_space_constraint(array, pltpu.VMEM) for array in arrays]


def split(rows, blocks):
    size = rows.shape[0] // blocks
    return [rows[k * size : (k + 1) * size] for k in range(blocks)]


def joined(blocks):
    if len(blocks) == 1:
        return blocks[0][...]
    return jnp.concatenate([block[...].astype(F32) for block in blocks], axis=0).astype(BF16)


def normalize(carried, gain_row):
    average = jnp.mean(carried, axis=-1, keepdims=True)
    centered = carried - average
    variance = jnp.mean(centered * centered, axis=-1, keepdims=True)
    return gain_row * centered * lax.rsqrt(variance + EPSILON)


def dot(left, right, contract=((1,), (0,))):
    return lax.dot_general(left, right, (contract, ((), ())), preferred_element_type=F32)


def in_parallel(pairs, sems):
    copies = [pltpu.make_async_copy(*pair, sems.at[i]) for i, pair in enumerate(pairs)]
    for copy in copies:
        copy.start()
    return copies


def spread_kernel(enc_kv, *blocks):
    segment = lax.axis_index("segment")
    for distance, block in enumerate(blocks):
        block[...] = enc_kv[lax.rem(segment + distance, len(blocks))]


def spread(enc_kv):
    layers, _, features = enc_kv.shape
    tiles = enc_kv.reshape(layers, features // HEAD_DIM, HEAD_DIM)
    return pl.pallas_call(
        spread_kernel,
        in_specs=[VMEM],
        out_specs=[VMEM] * layers,
        out_shape=[jax.ShapeDtypeStruct(tiles.shape[1:], BF16)] * layers,
        compiler_params=pltpu.CompilerParams(vmem_limit_bytes=8 * MIB),
        name="spread",
    )(tiles)


def stack_kernel(*refs):
    *blocks, stacked = refs
    for i, block in enumerate(blocks):
        stacked[i] = block[...]


def stack(blocks):
    return pl.pallas_call(
        stack_kernel,
        in_specs=[VMEM] * len(blocks),
        out_specs=VMEM,
        out_shape=jax.ShapeDtypeStruct((len(blocks), *blocks[0].shape), BF16),
        compiler_params=pltpu.CompilerParams(vmem_limit_bytes=8 * MIB),
        name="stack",
    )(*blocks)


def project_kernel(states, attn_gain, ffn_gain, query_hbm, queries, w_query, gains, fresh, following, sems):
    copies = in_parallel(
        (
            (states.at[pl.ds(0, CAND_LEN), :], fresh),
            (attn_gain, gains.at[0]),
            (query_hbm, w_query),
            (ffn_gain, gains.at[1]),
            (states.at[pl.ds(CAND_LEN, CAND_LEN), :], following),
        ),
        sems,
    )
    copies[0].wait()
    copies[1].wait()
    normed = normalize(fresh[...].astype(F32), gains[0]).astype(BF16)
    copies[2].wait()
    queries[...] = dot(normed, w_query[...]).astype(BF16)
    copies[3].wait()
    copies[4].wait()


def project(states, attn_gain, ffn_gain, w_query):
    width, head_total = w_query.shape
    return pl.pallas_call(
        project_kernel,
        in_specs=[HBM] * 4,
        out_specs=[VMEM] * 5,
        out_shape=[
            jax.ShapeDtypeStruct((CAND_LEN, head_total), BF16),
            pltpu.VMEM(w_query.shape, BF16),
            pltpu.VMEM((2, 1, width), F32),
            pltpu.VMEM((CAND_LEN, width), BF16),
            pltpu.VMEM((CAND_LEN, width), BF16),
        ],
        scratch_shapes=[pltpu.SemaphoreType.DMA((5,))],
        compiler_params=pltpu.CompilerParams(vmem_limit_bytes=12 * MIB),
        cost_estimate=pl.CostEstimate(
            flops=2 * CAND_LEN * width * head_total,
            bytes_accessed=2 * width * head_total,
            transcendentals=0,
        ),
        name="project",
    )(*in_hbm(states, attn_gain, ffn_gain, w_query))


def load_kernel(count, _, *refs):
    for copy in in_parallel(list(zip(refs[:count], refs[count : 2 * count])), refs[-1]):
        copy.wait()


def load(after, mats):
    return pl.pallas_call(
        functools.partial(load_kernel, len(mats)),
        in_specs=[VMEM] + [HBM] * len(mats),
        out_specs=[VMEM] * len(mats),
        out_shape=[pltpu.VMEM(mat.shape, BF16) for mat in mats],
        scratch_shapes=[pltpu.SemaphoreType.DMA((len(mats),))],
        compiler_params=pltpu.CompilerParams(vmem_limit_bytes=8 * MIB),
        cost_estimate=pl.CostEstimate(
            flops=0, bytes_accessed=4 * sum(mat.size for mat in mats), transcendentals=0
        ),
        name="load",
    )(after, *in_hbm(*mats))


def block_diagonal(pieces, first_head, blocks):
    positions = pieces.shape[0]
    blocks[...] = jnp.zeros_like(blocks)
    for head in range(blocks.shape[1] // HEAD_DIM):
        rows = pl.ds(head * positions, positions)
        blocks[rows, pl.ds(head * HEAD_DIM, HEAD_DIM)] = pieces[:, first_head + head, :]


def attend_kernel(step, capacity, blocks, piece_count, *refs):
    segment = lax.axis_index("segment")
    if step == 0:
        (cand_len, queries_in, fresh, gains, w_query, w_out, _, routes_hbm, router_hbm, down_hbm,
         *pieces), refs = refs[: 10 + piece_count], refs[10 + piece_count :]
        after_ref, weights, *outgoing = refs[: 2 + blocks]
        routes, router, keys, values, own_down, cached, route_buf, sems = refs[2 + blocks :]
        copies = in_parallel(
            ((routes_hbm, route_buf), (router_hbm, router), (down_hbm, own_down)), sems
        )
        head_count = w_out.shape[0] // HEAD_DIM
        size = cached.shape[0] // piece_count
        for i, piece in enumerate(pieces):
            cached[pl.ds(i * size, size)] = piece[...]
        block_diagonal(cached, 0, keys)
        block_diagonal(cached, head_count, values)
        queries = queries_in[...]
        carried = fresh[...].astype(F32)
        copies[0].wait()
        position = lax.broadcasted_iota(jnp.int32, (1, CAND_LEN), 1)
        for micro in range(CAND_DEV):
            route = route_buf[:, micro * CAND_LEN : (micro + 1) * CAND_LEN]
            routes[micro] = jnp.where(position < cand_len[micro], route, -1)
    else:
        incoming, refs = refs[0], refs[1:]
        current = incoming[...]
        if step < CAND_DEV:
            current, refs = jnp.where(segment == 0, refs[0][...], current), refs[1:]
        routes, gains, router, w_query, w_out, keys, values, after_ref, weights, *outgoing = refs
        carried = current.astype(F32)
        normed = normalize(carried, gains[0]).astype(BF16)
        queries = dot(normed, w_query[...]).astype(BF16)

    rows = carried.shape[0]
    sources = keys.shape[0] * HEAD_DIM // keys.shape[1]
    scores = dot(keys[...], queries, ((1,), (1,))) * (1.0 / math.sqrt(HEAD_DIM))
    scores = scores.reshape(-1, sources, rows)
    exponent = jnp.exp(scores - jnp.max(scores, axis=1, keepdims=True))
    share = exponent / jnp.sum(exponent, axis=1, keepdims=True)
    share = share.reshape(-1, rows).astype(BF16)
    context = dot(share, values[...], ((0,), (0,))).astype(BF16)
    after_attn = carried + dot(context, w_out[...])
    after_ref[...] = after_attn
    ffn_input = normalize(after_attn, gains[1]).astype(BF16)

    if step == 0:
        copies[1].wait()
    experts = router.shape[0]
    logits = dot(router[...], ffn_input, ((1,), (1,)))
    micro = jnp.clip(step - segment, 0, CAND_DEV - 1)
    route = routes[micro]
    place = route
    if blocks > 1:
        place = jnp.where(route < 0, route, route ^ (lax.axis_index("expert") // 2))
    labels = lax.broadcasted_iota(jnp.int32, (experts, rows), 0)
    first, second = route[0:1] == labels, route[1:2] == labels
    logit_first = jnp.sum(jnp.where(first, logits, 0.0), axis=0, keepdims=True)
    logit_second = jnp.sum(jnp.where(second, logits, 0.0), axis=0, keepdims=True)
    gate_first = jax.nn.sigmoid(logit_first - logit_second)
    gate_second = 1.0 - gate_first
    named = jnp.where(first | second, 1.0, 0.0).astype(BF16)
    earlier = lax.broadcasted_iota(jnp.int32, (rows, rows), 0) < lax.broadcasted_iota(
        jnp.int32, (rows, rows), 1
    )
    before = dot(named, jnp.where(earlier, 1.0, 0.0).astype(BF16))
    slots = lax.broadcasted_iota(jnp.int32, (experts * capacity, rows), 0)
    chosen = []
    for mask, row in ((first, 0), (second, 1)):
        slot = jnp.sum(jnp.where(mask, before, 0.0), axis=0, keepdims=True).astype(jnp.int32)
        chosen.append(slots == place[row : row + 1] * capacity + slot)
    select = jnp.where(chosen[0] | chosen[1], 1.0, 0.0).astype(BF16)
    buffers = dot(select, ffn_input)
    for buffer, block in zip(split(buffers, blocks), outgoing):
        block[...] = buffer.astype(BF16)
    weights[...] = jnp.where(chosen[0], gate_first, 0.0) + jnp.where(chosen[1], gate_second, 0.0)
    if step == 0:
        copies[2].wait()


def attend(step, capacity, blocks, sources, kept):
    piece_count = 0
    if step == 0:
        cand_len, queries, fresh, routes, router_t, down_mat, *pieces = sources
        piece_count = len(pieces)
        gains, w_query, w_out, own_in = kept
        head_total, width = w_out.shape
        positions = sum(piece.shape[0] for piece in pieces)
        diagonal = (positions * head_total // HEAD_DIM, head_total)
        kept_shapes = [
            pltpu.VMEM((CAND_DEV, 2, CAND_LEN), jnp.int32),
            pltpu.VMEM(router_t.shape, BF16),
            pltpu.VMEM(diagonal, BF16),
            pltpu.VMEM(diagonal, BF16),
            pltpu.VMEM(down_mat.shape, BF16),
        ]
        inputs = [
            *in_hbm(cand_len), queries, *in_vmem(fresh, gains, w_query, w_out, own_in),
            *in_hbm(routes, router_t, down_mat), *pieces,
        ]
        specs = [SMEM] + [VMEM] * 6 + [HBM] * 3 + [VMEM] * piece_count
        scratch = [
            pltpu.VMEM((positions, *pieces[0].shape[1:]), BF16),
            pltpu.VMEM(routes.shape, jnp.int32),
            pltpu.SemaphoreType.DMA((3,)),
        ]
    else:
        _, _, router_t, _, w_out, *_ = kept
        head_total, width = w_out.shape
        kept_shapes, scratch = [], []
        inputs = [*sources, *in_vmem(*kept)]
        specs = [VMEM] * len(inputs)
    slot_count = router_t.shape[0] * capacity
    outs = pl.pallas_call(
        functools.partial(attend_kernel, step, capacity, blocks, piece_count),
        in_specs=specs,
        out_specs=[VMEM] * (2 + blocks + len(kept_shapes)),
        out_shape=[
            jax.ShapeDtypeStruct((CAND_LEN, width), F32),
            jax.ShapeDtypeStruct((slot_count, CAND_LEN), F32),
            *[jax.ShapeDtypeStruct((slot_count // blocks, width), BF16)] * blocks,
            *kept_shapes,
        ],
        scratch_shapes=scratch,
        compiler_params=pltpu.CompilerParams(vmem_limit_bytes=12 * MIB),
        cost_estimate=pl.CostEstimate(
            flops=6 * CAND_LEN * width * head_total,
            bytes_accessed=4 * width * head_total + 8 * CAND_LEN * width,
            transcendentals=0,
        ),
        name="attend",
    )(*inputs)
    return outs[:2], outs[2 : 2 + blocks], outs[2 + blocks :]


def expert_kernel(blocks, stream, *refs):
    rows_in, refs = refs[:blocks], refs[blocks:]
    (own_in, own_down), refs = refs[:2], refs[2:]
    if stream:
        sources, served, refs = refs[:2], refs[2 : 2 + blocks], refs[2 + blocks :]
        (other_in, other_down), (rows, own_hidden, other_hidden, sems) = refs[:2], refs[2:]
    else:
        (other_in, other_down), refs = refs[:2], refs[2:]
        served, (rows, own_hidden, other_hidden) = refs[:blocks], refs[blocks:]
    chunks = [pl.ds(start, HIDDEN_CHUNK) for start in range(0, own_in.shape[1], HIDDEN_CHUNK)]

    def fill(source, mat, i):
        lanes = chunks[i]
        return pltpu.make_async_copy(
            sources[source].at[:, lanes], mat.at[:, lanes], sems.at[source, i]
        )

    if stream:
        for i in range(len(chunks)):
            fill(0, other_in, i).start()
        for i in range(len(chunks)):
            fill(1, other_down, i).start()
    rows[...] = joined(rows_in)
    for units in chunks:
        own_hidden[:, units] = jnp.maximum(dot(rows[...], own_in[:, units]), 0.0).astype(BF16)
    for i, units in enumerate(chunks):
        if stream:
            fill(0, other_in, i).wait()
        other_hidden[:, units] = jnp.maximum(dot(rows[...], other_in[:, units]), 0.0).astype(BF16)
    for i, lanes in enumerate(chunks):
        if stream:
            fill(1, other_down, i).wait()
        out = dot(own_hidden[...], own_down[:, lanes]) + dot(other_hidden[...], other_down[:, lanes])
        for part, block in zip(split(out, blocks), served):
            block[:, lanes] = part.astype(BF16)


def expert_rows(rows_in, mats, stream):
    blocks = len(rows_in)
    width = rows_in[0].shape[1]
    count = blocks * rows_in[0].shape[0]
    units = mats[0].shape[1]
    scratch = [
        pltpu.VMEM((count, width), BF16),
        pltpu.VMEM((count, units), BF16),
        pltpu.VMEM((count, units), BF16),
    ]
    out_shape = [jax.ShapeDtypeStruct(rows.shape, BF16) for rows in rows_in]
    if stream:
        scratch.append(pltpu.SemaphoreType.DMA((2, units // HIDDEN_CHUNK)))
        out_shape += [pltpu.VMEM(mat.shape, BF16) for mat in mats[2:]]
    outs = pl.pallas_call(
        functools.partial(expert_kernel, blocks, stream),
        in_specs=[VMEM] * (blocks + 2) + [HBM if stream else VMEM] * 2,
        out_specs=[VMEM] * len(out_shape),
        out_shape=out_shape,
        scratch_shapes=scratch,
        compiler_params=pltpu.CompilerParams(vmem_limit_bytes=12 * MIB),
        cost_estimate=pl.CostEstimate(
            flops=8 * count * width * units,
            bytes_accessed=8 * width * units + 4 * count * width,
            transcendentals=0,
        ),
        name="experts",
    )(*rows_in, *in_vmem(*mats[:2]), *(in_hbm if stream else in_vmem)(*mats[2:]))
    return outs[:blocks], ((*mats[:2], *outs[blocks:]) if stream else mats)


def mixed(after_attn, weights, blocks):
    gates = weights[...]
    coarse = gates.astype(BF16)
    fine = (gates - coarse.astype(F32)).astype(BF16)
    rows = joined(blocks)
    mixture = dot(coarse, rows, ((0,), (0,))) + dot(fine, rows, ((0,), (0,)))
    return (after_attn[...] + mixture).astype(BF16)


def combine_kernel(blocks, after_attn, weights, *refs):
    result = refs[blocks]
    result[...] = mixed(after_attn, weights, refs[:blocks])


def place_kernel(blocks, after_attn, weights, *refs):
    served, earlier, (output, result, sems) = refs[:blocks], refs[blocks:-3], refs[-3:]
    segment = lax.axis_index("segment")

    def place(source, micro):
        rows = pl.ds(micro * CAND_LEN, CAND_LEN)
        return pltpu.make_async_copy(source, output.at[rows, :], sems.at[micro])

    last = len(earlier)
    for micro in range(CAND_DEV):
        for step in range(micro, last):

            @pl.when(segment + micro == step)
            def _():
                place(earlier[step], micro).start()

    result[...] = mixed(after_attn, weights, served)
    for micro in range(CAND_DEV):

        @pl.when(segment + micro == last)
        def _():
            place(result, micro).start()

    for micro in range(CAND_DEV):
        place(result, micro).wait()


def combine(after_attn, weights, served, earlier=()):
    rows, width = after_attn.shape
    inputs = [after_attn, weights, *served]
    scratch = []
    out_shape, out_spec = jax.ShapeDtypeStruct((rows, width), BF16), VMEM
    if earlier:
        inputs += in_vmem(*earlier)
        scratch = [pltpu.VMEM((rows, width), BF16), pltpu.SemaphoreType.DMA((CAND_DEV,))]
        out_shape, out_spec = jax.ShapeDtypeStruct((CAND_DEV * rows, width), BF16), HBM
    return pl.pallas_call(
        functools.partial(place_kernel if earlier else combine_kernel, len(served)),
        in_specs=[VMEM] * len(inputs),
        out_specs=out_spec,
        out_shape=out_shape,
        scratch_shapes=scratch,
        compiler_params=pltpu.CompilerParams(vmem_limit_bytes=8 * MIB),
        cost_estimate=pl.CostEstimate(
            flops=4 * weights.size * width,
            bytes_accessed=6 * after_attn.size + 2 * weights.shape[0] * width,
            transcendentals=0,
        ),
        name="combine",
    )(*inputs)


def local(
    states, cand_len, routes, enc_kv, attn_gain, ffn_gain, w_query, w_out, w_router, w_in, w_down
):
    n_segment = lax.axis_size("segment")
    n_expert = lax.axis_size("expert")
    model_width = states.shape[1]
    experts = w_router.shape[2]
    capacity = 2 * ((5 * CAND_LEN + 4 * experts - 1) // (4 * experts))
    core_pairs = [(i, i ^ 1) for i in range(n_expert)]
    same_core = [list(range(core, n_expert, 2)) for core in range(2)]
    blocks = experts if experts <= 4 else 1

    def exchange(parts):
        if blocks > 1:
            return [parts[0]] + [
                lax.ppermute(part, "expert", [(i, i ^ (2 * k)) for i in range(n_expert)])
                for k, part in enumerate(parts[1:], 1)
            ]
        rows = parts[0].reshape(experts, capacity, model_width)
        moved = lax.all_to_all(
            rows, "expert", split_axis=0, concat_axis=0, axis_index_groups=same_core, tiled=True
        )
        return [moved.reshape(parts[0].shape)]

    blocks_out = spread(enc_kv)
    layer_kv = [blocks_out[0]] + [
        lax.ppermute(block, "segment", [(s, (s + d) % n_segment) for s in range(n_segment)])
        for d, block in enumerate(blocks_out[1:], 1)
    ]
    layer_kv = stack(layer_kv)
    if n_expert <= 8:
        pieces = [layer_kv] + [
            lax.ppermute(layer_kv, "expert", [(i, i ^ j) for i in range(n_expert)])
            for j in range(1, n_expert)
        ]
    else:
        pieces = [lax.all_gather(layer_kv, "expert", axis=0, tiled=True)]
    own = (w_in[0, 0], w_down[0, 0])
    other = tuple(lax.ppermute(mat, "expert", core_pairs) for mat in own)

    queries, query_mat, gains, fresh, following = project(
        states, attn_gain, ffn_gain, w_query[0]
    )
    out_mat, own_in = load(layer_kv, (w_out[0], own[0]))
    kept = (gains, query_mat, out_mat, own_in)
    step_count = CAND_DEV + n_segment - 1
    earlier = []
    for step in range(step_count):
        if step == 0:
            sources = (
                cand_len, queries, fresh, routes[0].T, w_router[0].T, own[1], *pieces
            )
        elif step < CAND_DEV:
            sources = (incoming, following)
        else:
            sources = (incoming,)
        (after_attn, weights), outgoing, left = attend(step, capacity, blocks, sources, kept)
        if step == 0:
            route_rows, router_t, keys, values, own_down = left
            kept = (route_rows, gains, router_t, query_mat, out_mat, keys, values)
            expert_mats = (own_in, own_down, *other)
        served, expert_mats = expert_rows(exchange(outgoing), expert_mats, step == 0)
        served = exchange(served)
        if step + 1 < step_count:
            result = combine(after_attn, weights, served)
            incoming = lax.ppermute(
                result, "segment", [(i, i + 1) for i in range(n_segment - 1)]
            )
            earlier.append(result)
    output = combine(after_attn, weights, served, earlier)
    return output.reshape(1, CAND_DEV * CAND_LEN, model_width)


def solution(mesh):
    return jax.shard_map(
        local,
        mesh=mesh,
        in_specs=(
            P("expert", None),
            P("expert"),
            P("segment", "expert", None),
            P(None, ("segment", "expert"), None),
            P("segment", None),
            P("segment", None),
            P("segment", None, None),
            P("segment", None, None),
            P("segment", None, None),
            P("segment", "expert", None, None),
            P("segment", "expert", None, None),
        ),
        out_specs=P("segment", "expert", None),
        check_vma=False,
    )
```

```python
import functools
import math

import jax
import jax.numpy as jnp
from jax import lax
from jax.experimental import pallas as pl
from jax.experimental.pallas import tpu as pltpu
from jax.sharding import PartitionSpec as P

HEAD_DIM = 128
CAND_LEN = 64
CAND_DEV = 2
HIDDEN_CHUNK = 512
MIB = 1 << 20

EPSILON = 1e-05

VMEM = pl.BlockSpec(memory_space=pltpu.VMEM)
SMEM = pl.BlockSpec(memory_space=pltpu.SMEM)
HBM = pl.BlockSpec(memory_space=pltpu.HBM)
F32 = jnp.float32
BF16 = jnp.bfloat16


def in_hbm(*arrays):
    return [pltpu.with_memory_space_constraint(array, pltpu.HBM) for array in arrays]


def in_vmem(*arrays):
    return [pltpu.with_memory_space_constraint(array, pltpu.VMEM) for array in arrays]


def split(rows, blocks):
    size = rows.shape[0] // blocks
    return [rows[k * size : (k + 1) * size] for k in range(blocks)]


def joined(blocks):
    if len(blocks) == 1:
        return blocks[0][...]
    return jnp.concatenate([block[...].astype(F32) for block in blocks], axis=0).astype(BF16)


def normalize(carried, gain_row):
    average = jnp.mean(carried, axis=-1, keepdims=True)
    centered = carried - average
    variance = jnp.mean(centered * centered, axis=-1, keepdims=True)
    return gain_row * centered * lax.rsqrt(variance + EPSILON)


def dot(left, right, contract=((1,), (0,))):
    return lax.dot_general(left, right, (contract, ((), ())), preferred_element_type=F32)


def spread_kernel(copies_of, enc_kv, blocks):
    for layer in range(enc_kv.shape[0]):
        block = enc_kv[layer]
        for i in range(copies_of):
            blocks[layer * copies_of + i] = block


def spread(enc_kv, copies_of):
    layers, _, features = enc_kv.shape
    tiles = enc_kv.reshape(layers, features // HEAD_DIM, HEAD_DIM)
    return pl.pallas_call(
        functools.partial(spread_kernel, copies_of),
        in_specs=[VMEM],
        out_specs=VMEM,
        out_shape=jax.ShapeDtypeStruct((layers * copies_of, *tiles.shape[1:]), BF16),
        compiler_params=pltpu.CompilerParams(vmem_limit_bytes=8 * MIB),
        name="spread",
    )(tiles)


def project_kernel(states, gain, w_query, queries, fresh, gain_buf, query_buf, sems):
    fills = (
        (states.at[pl.ds(0, CAND_LEN), :], fresh),
        (gain, gain_buf),
        (w_query, query_buf),
    )
    copies = [pltpu.make_async_copy(*pair, sems.at[i]) for i, pair in enumerate(fills)]
    for copy in copies:
        copy.start()
    copies[0].wait()
    copies[1].wait()
    normed = normalize(fresh[...].astype(F32), gain_buf[...]).astype(BF16)
    copies[2].wait()
    queries[...] = dot(normed, query_buf[...]).astype(BF16)


def project(states, gain, w_query):
    width, head_total = w_query.shape
    return pl.pallas_call(
        project_kernel,
        in_specs=[HBM] * 3,
        out_specs=VMEM,
        out_shape=jax.ShapeDtypeStruct((CAND_LEN, head_total), BF16),
        scratch_shapes=[
            pltpu.VMEM((CAND_LEN, width), BF16),
            pltpu.VMEM((1, width), F32),
            pltpu.VMEM(w_query.shape, BF16),
            pltpu.SemaphoreType.DMA((3,)),
        ],
        compiler_params=pltpu.CompilerParams(vmem_limit_bytes=12 * MIB),
        cost_estimate=pl.CostEstimate(
            flops=2 * CAND_LEN * width * head_total,
            bytes_accessed=2 * width * head_total,
            transcendentals=0,
        ),
        name="project",
    )(*in_hbm(states, gain, w_query))


def block_diagonal(cached, first_head, blocks):
    sources = cached.shape[0]
    blocks[...] = jnp.zeros_like(blocks)
    for head in range(blocks.shape[1] // HEAD_DIM):
        rows = pl.ds(head * sources, sources)
        blocks[rows, pl.ds(head * HEAD_DIM, HEAD_DIM)] = cached[:, first_head + head, :]


def attend_kernel(step, capacity, blocks, marked, *refs):
    segment = lax.axis_index("segment")
    if step == 0:
        (cand_len, queries_in, cached, states, routes_hbm, attn_gain, ffn_gain, router_hbm,
         query_hbm, out_hbm, expert_hbm), refs = refs[:11], refs[11:]
        after_ref, weights, *outgoing = refs[: 2 + blocks]
        (routes, gains, router, w_query, w_out, keys, values, following, expert_mat,
         fresh, route_buf, sems) = refs[2 + blocks :]
        fills = (
            (states.at[pl.ds(0, CAND_LEN), :], fresh),
            (ffn_gain, gains.at[1]),
            (out_hbm, w_out),
            (router_hbm, router),
            (routes_hbm, route_buf),
            (attn_gain, gains.at[0]),
            (states.at[pl.ds(CAND_LEN, CAND_LEN), :], following),
            (query_hbm, w_query),
            (expert_hbm, expert_mat),
        )
        copies = [pltpu.make_async_copy(*pair, sems.at[i]) for i, pair in enumerate(fills)]
        for copy in copies:
            copy.start()
        head_count = w_out.shape[0] // HEAD_DIM
        block_diagonal(cached, 0, keys)
        block_diagonal(cached, head_count, values)
        queries = queries_in[...]
        copies[0].wait()
        carried = fresh[...].astype(F32)
        copies[4].wait()
        copies = copies[:4] + copies[5:]
        position = lax.broadcasted_iota(jnp.int32, (1, CAND_LEN), 1)
        for micro in range(CAND_DEV):
            route = route_buf[:, micro * CAND_LEN : (micro + 1) * CAND_LEN]
            routes[micro] = jnp.where(position < cand_len[micro], route, -1)
    else:
        incoming, refs = refs[0], refs[1:]
        if marked:
            refs = refs[1:]
        current = incoming[...]
        if step < CAND_DEV:
            current, refs = jnp.where(segment == 0, refs[0][...], current), refs[1:]
        routes, gains, router, w_query, w_out, keys, values, after_ref, weights, *outgoing = refs
        carried = current.astype(F32)
        normed = normalize(carried, gains[0]).astype(BF16)
        queries = dot(normed, w_query[...]).astype(BF16)

    rows = carried.shape[0]
    sources = keys.shape[0] * HEAD_DIM // keys.shape[1]
    scores = dot(keys[...], queries, ((1,), (1,))) * (1.0 / math.sqrt(HEAD_DIM))
    scores = scores.reshape(-1, sources, rows)
    exponent = jnp.exp(scores - jnp.max(scores, axis=1, keepdims=True))
    share = exponent / jnp.sum(exponent, axis=1, keepdims=True)
    share = share.reshape(-1, rows).astype(BF16)
    context = dot(share, values[...], ((0,), (0,))).astype(BF16)
    if step == 0:
        copies[1].wait()
        copies[2].wait()
    after_attn = carried + dot(context, w_out[...])
    after_ref[...] = after_attn
    ffn_input = normalize(after_attn, gains[1]).astype(BF16)

    if step == 0:
        copies[3].wait()
    experts = router.shape[0]
    logits = dot(router[...], ffn_input, ((1,), (1,)))
    micro = jnp.clip(step - segment, 0, CAND_DEV - 1)
    route = routes[micro]
    place = route
    if blocks > 1:
        place = jnp.where(route < 0, route, route ^ (lax.axis_index("expert") // 2))
    labels = lax.broadcasted_iota(jnp.int32, (experts, rows), 0)
    first, second = route[0:1] == labels, route[1:2] == labels
    logit_first = jnp.sum(jnp.where(first, logits, 0.0), axis=0, keepdims=True)
    logit_second = jnp.sum(jnp.where(second, logits, 0.0), axis=0, keepdims=True)
    gate_first = jax.nn.sigmoid(logit_first - logit_second)
    gate_second = 1.0 - gate_first
    named = jnp.where(first | second, 1.0, 0.0).astype(BF16)
    earlier = lax.broadcasted_iota(jnp.int32, (rows, rows), 0) < lax.broadcasted_iota(
        jnp.int32, (rows, rows), 1
    )
    before = dot(named, jnp.where(earlier, 1.0, 0.0).astype(BF16))
    slots = lax.broadcasted_iota(jnp.int32, (experts * capacity, rows), 0)
    chosen = []
    for mask, row in ((first, 0), (second, 1)):
        slot = jnp.sum(jnp.where(mask, before, 0.0), axis=0, keepdims=True).astype(jnp.int32)
        chosen.append(slots == place[row : row + 1] * capacity + slot)
    select = jnp.where(chosen[0] | chosen[1], 1.0, 0.0).astype(BF16)
    buffers = dot(select, ffn_input)
    for buffer, block in zip(split(buffers, blocks), outgoing):
        block[...] = buffer.astype(BF16)
    weights[...] = jnp.where(chosen[0], gate_first, 0.0) + jnp.where(chosen[1], gate_second, 0.0)
    if step == 0:
        for copy in copies[4:]:
            copy.wait()


def attend(step, capacity, blocks, marked, sources, kept):
    if step == 0:
        cand_len, queries, cached, *params = sources
        _, routes, _, _, router_t, w_query, w_out, expert_mat = params
        head_total, width = w_out.shape
        diagonal = (cached.shape[0] * head_total // HEAD_DIM, head_total)
        kept_shapes = [
            pltpu.VMEM((CAND_DEV, 2, CAND_LEN), jnp.int32),
            pltpu.VMEM((2, 1, width), F32),
            *(pltpu.VMEM(array.shape, BF16) for array in (router_t, w_query, w_out)),
            pltpu.VMEM(diagonal, BF16),
            pltpu.VMEM(diagonal, BF16),
            pltpu.VMEM((CAND_LEN, width), BF16),
            pltpu.VMEM(expert_mat.shape, BF16),
        ]
        inputs = [*in_hbm(cand_len), queries, cached, *in_hbm(*params)]
        specs = [SMEM, VMEM, VMEM] + [HBM] * len(params)
        scratch = [
            pltpu.VMEM((CAND_LEN, width), BF16),
            pltpu.VMEM(routes.shape, jnp.int32),
            pltpu.SemaphoreType.DMA((9,)),
        ]
    else:
        _, _, router_t, _, w_out, *_ = kept
        head_total, width = w_out.shape
        kept_shapes, scratch = [], []
        inputs = [*sources, *in_vmem(*kept)]
        specs = [VMEM] * len(inputs)
    slot_count = router_t.shape[0] * capacity
    outs = pl.pallas_call(
        functools.partial(attend_kernel, step, capacity, blocks, marked),
        in_specs=specs,
        out_specs=[VMEM] * (2 + blocks + len(kept_shapes)),
        out_shape=[
            jax.ShapeDtypeStruct((CAND_LEN, width), F32),
            jax.ShapeDtypeStruct((slot_count, CAND_LEN), F32),
            *[jax.ShapeDtypeStruct((slot_count // blocks, width), BF16)] * blocks,
            *kept_shapes,
        ],
        scratch_shapes=scratch,
        compiler_params=pltpu.CompilerParams(vmem_limit_bytes=12 * MIB),
        cost_estimate=pl.CostEstimate(
            flops=6 * CAND_LEN * width * head_total,
            bytes_accessed=4 * width * head_total + 8 * CAND_LEN * width,
            transcendentals=0,
        ),
        name="attend",
    )(*inputs)
    return outs[:2], outs[2 : 2 + blocks], outs[2 + blocks :]


def expert_kernel(blocks, stream, *refs):
    rows_in, refs = refs[:blocks], refs[blocks:]
    own_in, refs = refs[0], refs[1:]
    if stream:
        sources, served, refs = refs[:3], refs[3 : 3 + blocks], refs[3 + blocks :]
        (own_down, other_in, other_down), (rows, own_hidden, other_hidden, sems) = refs[:3], refs[3:]
    else:
        (own_down, other_in, other_down), refs = refs[:3], refs[3:]
        served, (rows, own_hidden, other_hidden) = refs[:blocks], refs[blocks:]
    size = HIDDEN_CHUNK if stream else 2 * HIDDEN_CHUNK
    chunks = [pl.ds(start, size) for start in range(0, own_in.shape[1], size)]

    def fill(source, mat, i):
        lanes = chunks[i]
        return pltpu.make_async_copy(
            sources[source].at[:, lanes], mat.at[:, lanes], sems.at[source, i]
        )

    if stream:
        for i in range(len(chunks)):
            fill(1, other_in, i).start()
        for i in range(len(chunks)):
            fill(0, own_down, i).start()
            fill(2, other_down, i).start()
    rows[...] = joined(rows_in)
    for units in chunks:
        own_hidden[:, units] = jnp.maximum(dot(rows[...], own_in[:, units]), 0.0).astype(BF16)
    for i, units in enumerate(chunks):
        if stream:
            fill(1, other_in, i).wait()
        other_hidden[:, units] = jnp.maximum(dot(rows[...], other_in[:, units]), 0.0).astype(BF16)
    for i, lanes in enumerate(chunks):
        if stream:
            fill(0, own_down, i).wait()
            fill(2, other_down, i).wait()
        out = dot(own_hidden[...], own_down[:, lanes]) + dot(other_hidden[...], other_down[:, lanes])
        for part, block in zip(split(out, blocks), served):
            block[:, lanes] = part.astype(BF16)


def expert_rows(rows_in, mats, stream):
    blocks = len(rows_in)
    width = rows_in[0].shape[1]
    count = blocks * rows_in[0].shape[0]
    units = mats[0].shape[1]
    scratch = [
        pltpu.VMEM((count, width), BF16),
        pltpu.VMEM((count, units), BF16),
        pltpu.VMEM((count, units), BF16),
    ]
    out_shape = [jax.ShapeDtypeStruct(rows.shape, BF16) for rows in rows_in]
    if stream:
        scratch.append(pltpu.SemaphoreType.DMA((3, units // HIDDEN_CHUNK)))
        out_shape += [pltpu.VMEM(mat.shape, BF16) for mat in mats[1:]]
    outs = pl.pallas_call(
        functools.partial(expert_kernel, blocks, stream),
        in_specs=[VMEM] * (blocks + 1) + [HBM if stream else VMEM] * 3,
        out_specs=[VMEM] * len(out_shape),
        out_shape=out_shape,
        scratch_shapes=scratch,
        compiler_params=pltpu.CompilerParams(vmem_limit_bytes=12 * MIB),
        cost_estimate=pl.CostEstimate(
            flops=8 * count * width * units,
            bytes_accessed=8 * width * units + 4 * count * width,
            transcendentals=0,
        ),
        name="experts",
    )(*rows_in, *in_vmem(mats[0]), *(in_hbm if stream else in_vmem)(*mats[1:]))
    return outs[:blocks], ((mats[0], *outs[blocks:]) if stream else mats)


def mixed(after_attn, weights, blocks):
    gates = weights[...]
    coarse = gates.astype(BF16)
    fine = (gates - coarse.astype(F32)).astype(BF16)
    rows = joined(blocks)
    mixture = dot(coarse, rows, ((0,), (0,))) + dot(fine, rows, ((0,), (0,)))
    return (after_attn[...] + mixture).astype(BF16)


def combine_kernel(blocks, after_attn, weights, *refs):
    result, marks = refs[blocks], refs[blocks + 1 :]
    mixture = mixed(after_attn, weights, refs[:blocks])
    result[...] = mixture
    for mark in marks:
        mark[...] = mixture[: mark.shape[0], : mark.shape[1]]


def place_kernel(blocks, after_attn, weights, *refs):
    served, earlier, (output, result, sems) = refs[:blocks], refs[blocks:-3], refs[-3:]
    segment = lax.axis_index("segment")

    def place(source, micro):
        rows = pl.ds(micro * CAND_LEN, CAND_LEN)
        return pltpu.make_async_copy(source, output.at[rows, :], sems.at[micro])

    last = len(earlier)
    for micro in range(CAND_DEV):
        for step in range(micro, last):

            @pl.when(segment + micro == step)
            def _():
                place(earlier[step], micro).start()

    result[...] = mixed(after_attn, weights, served)
    for micro in range(CAND_DEV):

        @pl.when(segment + micro == last)
        def _():
            place(result, micro).start()

    for micro in range(CAND_DEV):
        place(result, micro).wait()


def combine(after_attn, weights, served, earlier=(), marked=False):
    rows, width = after_attn.shape
    inputs = [after_attn, weights, *served]
    scratch = []
    out_shape, out_spec = jax.ShapeDtypeStruct((rows, width), BF16), VMEM
    if earlier:
        inputs += in_vmem(*earlier)
        scratch = [pltpu.VMEM((rows, width), BF16), pltpu.SemaphoreType.DMA((CAND_DEV,))]
        out_shape, out_spec = jax.ShapeDtypeStruct((CAND_DEV * rows, width), BF16), HBM
    if marked:
        out_shape, out_spec = (out_shape, jax.ShapeDtypeStruct((16, 128), BF16)), (VMEM, VMEM)
    return pl.pallas_call(
        functools.partial(place_kernel if earlier else combine_kernel, len(served)),
        in_specs=[VMEM] * len(inputs),
        out_specs=out_spec,
        out_shape=out_shape,
        scratch_shapes=scratch,
        compiler_params=pltpu.CompilerParams(vmem_limit_bytes=8 * MIB),
        cost_estimate=pl.CostEstimate(
            flops=4 * weights.size * width,
            bytes_accessed=6 * after_attn.size + 2 * weights.shape[0] * width,
            transcendentals=0,
        ),
        name="combine",
    )(*inputs)


def local(
    states, cand_len, routes, enc_kv, attn_gain, ffn_gain, w_query, w_out, w_router, w_in, w_down
):
    n_segment = lax.axis_size("segment")
    n_expert = lax.axis_size("expert")
    model_width = states.shape[1]
    experts = w_router.shape[2]
    capacity = 2 * ((5 * CAND_LEN + 4 * experts - 1) // (4 * experts))
    core_pairs = [(i, i ^ 1) for i in range(n_expert)]
    same_core = [list(range(core, n_expert, 2)) for core in range(2)]
    blocks = experts if experts <= 4 else 1

    def exchange(parts):
        if blocks > 1:
            return [parts[0]] + [
                lax.ppermute(part, "expert", [(i, i ^ (2 * k)) for i in range(n_expert)])
                for k, part in enumerate(parts[1:], 1)
            ]
        rows = parts[0].reshape(experts, capacity, model_width)
        moved = lax.all_to_all(
            rows, "expert", split_axis=0, concat_axis=0, axis_index_groups=same_core, tiled=True
        )
        return [moved.reshape(parts[0].shape)]

    cached = lax.all_to_all(
        spread(enc_kv, n_expert), ("segment", "expert"), split_axis=0, concat_axis=0, tiled=True
    )
    own = (w_in[0, 0], w_down[0, 0])
    other = tuple(lax.ppermute(mat, "expert", core_pairs) for mat in own)

    queries = project(states, attn_gain, w_query[0])
    step_count = CAND_DEV + n_segment - 1
    earlier, marks = [], []
    kept = ()
    for step in range(step_count):
        if step == 0:
            sources = (
                cand_len, queries, cached, states, routes[0].T, attn_gain, ffn_gain,
                w_router[0].T, w_query[0], w_out[0], own[0],
            )
        elif step < CAND_DEV:
            sources = (incoming, following)
        else:
            sources = (incoming, *marks)
        (after_attn, weights), outgoing, left = attend(
            step, capacity, blocks, bool(marks), sources, kept
        )
        if step == 0:
            *kept, following, own_in = left
            expert_mats = (own_in, own[1], *other)
        served, expert_mats = expert_rows(exchange(outgoing), expert_mats, step == 0)
        served = exchange(served)
        if step + 1 < step_count:
            marked = step >= CAND_DEV
            result = combine(after_attn, weights, served, marked=marked)
            if marked:
                result, mark = result
                pairs = [(i, i + 1) for i in range(0, n_expert, 2)]
                marks = [lax.ppermute(mark, "expert", pairs)]
            incoming = lax.ppermute(
                result, "segment", [(i, i + 1) for i in range(n_segment - 1)]
            )
            earlier.append(result)
    output = combine(after_attn, weights, served, earlier)
    return output.reshape(1, CAND_DEV * CAND_LEN, model_width)


def solution(mesh):
    return jax.shard_map(
        local,
        mesh=mesh,
        in_specs=(
            P("expert", None),
            P("expert"),
            P("segment", "expert", None),
            P(None, ("segment", "expert"), None),
            P("segment", None),
            P("segment", None),
            P("segment", None, None),
            P("segment", None, None),
            P("segment", None, None),
            P("segment", "expert", None, None),
            P("segment", "expert", None, None),
        ),
        out_specs=P("segment", "expert", None),
        check_vma=False,
    )
```

```python
import functools
import math

import jax
import jax.numpy as jnp
from jax import lax
from jax.experimental import pallas as pl
from jax.experimental.pallas import tpu as pltpu
from jax.sharding import PartitionSpec as P

HEAD_DIM = 128
CAND_LEN = 64
CAND_DEV = 2
HIDDEN_CHUNK = 512
MIB = 1 << 20

EPSILON = 1e-05

VMEM = pl.BlockSpec(memory_space=pltpu.VMEM)
SMEM = pl.BlockSpec(memory_space=pltpu.SMEM)
HBM = pl.BlockSpec(memory_space=pltpu.HBM)
F32 = jnp.float32
BF16 = jnp.bfloat16


def in_hbm(*arrays):
    return [pltpu.with_memory_space_constraint(array, pltpu.HBM) for array in arrays]


def in_vmem(*arrays):
    return [pltpu.with_memory_space_constraint(array, pltpu.VMEM) for array in arrays]


def split(rows, blocks):
    size = rows.shape[0] // blocks
    return [rows[k * size : (k + 1) * size] for k in range(blocks)]


def joined(blocks):
    if len(blocks) == 1:
        return blocks[0][...]
    return jnp.concatenate([block[...].astype(F32) for block in blocks], axis=0).astype(BF16)


def normalize(carried, gain_row):
    average = jnp.mean(carried, axis=-1, keepdims=True)
    centered = carried - average
    variance = jnp.mean(centered * centered, axis=-1, keepdims=True)
    return gain_row * centered * lax.rsqrt(variance + EPSILON)


def dot(left, right, contract=((1,), (0,))):
    return lax.dot_general(left, right, (contract, ((), ())), preferred_element_type=F32)


def spread_kernel(copies_of, enc_kv, blocks):
    for layer in range(enc_kv.shape[0]):
        block = enc_kv[layer]
        for i in range(copies_of):
            blocks[layer * copies_of + i] = block


def spread(enc_kv, copies_of):
    layers, _, features = enc_kv.shape
    tiles = enc_kv.reshape(layers, features // HEAD_DIM, HEAD_DIM)
    return pl.pallas_call(
        functools.partial(spread_kernel, copies_of),
        in_specs=[VMEM],
        out_specs=VMEM,
        out_shape=jax.ShapeDtypeStruct((layers * copies_of, *tiles.shape[1:]), BF16),
        compiler_params=pltpu.CompilerParams(vmem_limit_bytes=8 * MIB),
        name="spread",
    )(tiles)


def project_kernel(states, gain, w_query, queries, fresh, gain_buf, query_buf, sems):
    fills = (
        (states.at[pl.ds(0, CAND_LEN), :], fresh),
        (gain, gain_buf),
        (w_query, query_buf),
    )
    copies = [pltpu.make_async_copy(*pair, sems.at[i]) for i, pair in enumerate(fills)]
    for copy in copies:
        copy.start()
    copies[0].wait()
    copies[1].wait()
    normed = normalize(fresh[...].astype(F32), gain_buf[...]).astype(BF16)
    copies[2].wait()
    queries[...] = dot(normed, query_buf[...]).astype(BF16)


def project(states, gain, w_query):
    width, head_total = w_query.shape
    return pl.pallas_call(
        project_kernel,
        in_specs=[HBM] * 3,
        out_specs=VMEM,
        out_shape=jax.ShapeDtypeStruct((CAND_LEN, head_total), BF16),
        scratch_shapes=[
            pltpu.VMEM((CAND_LEN, width), BF16),
            pltpu.VMEM((1, width), F32),
            pltpu.VMEM(w_query.shape, BF16),
            pltpu.SemaphoreType.DMA((3,)),
        ],
        compiler_params=pltpu.CompilerParams(vmem_limit_bytes=12 * MIB),
        cost_estimate=pl.CostEstimate(
            flops=2 * CAND_LEN * width * head_total,
            bytes_accessed=2 * width * head_total,
            transcendentals=0,
        ),
        name="project",
    )(*in_hbm(states, gain, w_query))


def block_diagonal(cached, first_head, blocks):
    sources = cached.shape[0]
    blocks[...] = jnp.zeros_like(blocks)
    for head in range(blocks.shape[1] // HEAD_DIM):
        rows = pl.ds(head * sources, sources)
        blocks[rows, pl.ds(head * HEAD_DIM, HEAD_DIM)] = cached[:, first_head + head, :]


def has_candidate(step):
    micro = step - lax.axis_index("segment")
    return (micro >= 0) & (micro < CAND_DEV)


def later_attend_kernel(step, capacity, blocks, *refs):
    @pl.when(has_candidate(step))
    def _():
        attend_kernel(step, capacity, blocks, *refs)


def attend_kernel(step, capacity, blocks, *refs):
    segment = lax.axis_index("segment")
    if step == 0:
        (cand_len, queries_in, cached, states, routes_hbm, attn_gain, ffn_gain, router_hbm,
         query_hbm, out_hbm, expert_hbm), refs = refs[:11], refs[11:]
        after_ref, weights, *outgoing = refs[: 2 + blocks]
        (routes, gains, router, w_query, w_out, keys, values, following, expert_mat,
         fresh, route_buf, sems) = refs[2 + blocks :]
        fills = (
            (states.at[pl.ds(0, CAND_LEN), :], fresh),
            (ffn_gain, gains.at[1]),
            (out_hbm, w_out),
            (router_hbm, router),
            (routes_hbm, route_buf),
            (attn_gain, gains.at[0]),
            (states.at[pl.ds(CAND_LEN, CAND_LEN), :], following),
            (query_hbm, w_query),
            (expert_hbm, expert_mat),
        )
        copies = [pltpu.make_async_copy(*pair, sems.at[i]) for i, pair in enumerate(fills)]
        for copy in copies:
            copy.start()
        head_count = w_out.shape[0] // HEAD_DIM
        block_diagonal(cached, 0, keys)
        block_diagonal(cached, head_count, values)
        queries = queries_in[...]
        copies[0].wait()
        carried = fresh[...].astype(F32)
        copies[4].wait()
        copies = copies[:4] + copies[5:]
        position = lax.broadcasted_iota(jnp.int32, (1, CAND_LEN), 1)
        for micro in range(CAND_DEV):
            route = route_buf[:, micro * CAND_LEN : (micro + 1) * CAND_LEN]
            routes[micro] = jnp.where(position < cand_len[micro], route, -1)
    else:
        incoming, refs = refs[0], refs[1:]
        current = incoming[...]
        if step < CAND_DEV:
            current, refs = jnp.where(segment == 0, refs[0][...], current), refs[1:]
        (routes, gains, router, w_query, w_out, keys, values, after_ref, weights), refs = (
            refs[:9], refs[9:]
        )
        outgoing, marks = refs[:blocks], refs[blocks:]
        for mark in marks:
            mark[...] = current[: mark.shape[0], : mark.shape[1]]
        carried = current.astype(F32)
        normed = normalize(carried, gains[0]).astype(BF16)
        queries = dot(normed, w_query[...]).astype(BF16)

    rows = carried.shape[0]
    sources = keys.shape[0] * HEAD_DIM // keys.shape[1]
    scores = dot(keys[...], queries, ((1,), (1,))) * (1.0 / math.sqrt(HEAD_DIM))
    scores = scores.reshape(-1, sources, rows)
    exponent = jnp.exp(scores - jnp.max(scores, axis=1, keepdims=True))
    share = exponent / jnp.sum(exponent, axis=1, keepdims=True)
    share = share.reshape(-1, rows).astype(BF16)
    context = dot(share, values[...], ((0,), (0,))).astype(BF16)
    if step == 0:
        copies[1].wait()
        copies[2].wait()
    after_attn = carried + dot(context, w_out[...])
    after_ref[...] = after_attn
    ffn_input = normalize(after_attn, gains[1]).astype(BF16)

    if step == 0:
        copies[3].wait()
    experts = router.shape[0]
    logits = dot(router[...], ffn_input, ((1,), (1,)))
    micro = jnp.clip(step - segment, 0, CAND_DEV - 1)
    route = routes[micro]
    place = route
    if blocks > 1:
        place = jnp.where(route < 0, route, route ^ (lax.axis_index("expert") // 2))
    labels = lax.broadcasted_iota(jnp.int32, (experts, rows), 0)
    first, second = route[0:1] == labels, route[1:2] == labels
    logit_first = jnp.sum(jnp.where(first, logits, 0.0), axis=0, keepdims=True)
    logit_second = jnp.sum(jnp.where(second, logits, 0.0), axis=0, keepdims=True)
    gate_first = jax.nn.sigmoid(logit_first - logit_second)
    gate_second = 1.0 - gate_first
    named = jnp.where(first | second, 1.0, 0.0).astype(BF16)
    earlier = lax.broadcasted_iota(jnp.int32, (rows, rows), 0) < lax.broadcasted_iota(
        jnp.int32, (rows, rows), 1
    )
    before = dot(named, jnp.where(earlier, 1.0, 0.0).astype(BF16))
    slots = lax.broadcasted_iota(jnp.int32, (experts * capacity, rows), 0)
    chosen = []
    for mask, row in ((first, 0), (second, 1)):
        slot = jnp.sum(jnp.where(mask, before, 0.0), axis=0, keepdims=True).astype(jnp.int32)
        chosen.append(slots == place[row : row + 1] * capacity + slot)
    select = jnp.where(chosen[0] | chosen[1], 1.0, 0.0).astype(BF16)
    buffers = dot(select, ffn_input)
    for buffer, block in zip(split(buffers, blocks), outgoing):
        block[...] = buffer.astype(BF16)
    weights[...] = jnp.where(chosen[0], gate_first, 0.0) + jnp.where(chosen[1], gate_second, 0.0)
    if step == 0:
        for copy in copies[4:]:
            copy.wait()


def attend(step, capacity, blocks, marked, sources, kept):
    if step == 0:
        cand_len, queries, cached, *params = sources
        _, routes, _, _, router_t, w_query, w_out, expert_mat = params
        head_total, width = w_out.shape
        diagonal = (cached.shape[0] * head_total // HEAD_DIM, head_total)
        kept_shapes = [
            pltpu.VMEM((CAND_DEV, 2, CAND_LEN), jnp.int32),
            pltpu.VMEM((2, 1, width), F32),
            *(pltpu.VMEM(array.shape, BF16) for array in (router_t, w_query, w_out)),
            pltpu.VMEM(diagonal, BF16),
            pltpu.VMEM(diagonal, BF16),
            pltpu.VMEM((CAND_LEN, width), BF16),
            pltpu.VMEM(expert_mat.shape, BF16),
        ]
        inputs = [*in_hbm(cand_len), queries, cached, *in_hbm(*params)]
        specs = [SMEM, VMEM, VMEM] + [HBM] * len(params)
        scratch = [
            pltpu.VMEM((CAND_LEN, width), BF16),
            pltpu.VMEM(routes.shape, jnp.int32),
            pltpu.SemaphoreType.DMA((9,)),
        ]
    else:
        _, _, router_t, _, w_out, *_ = kept
        head_total, width = w_out.shape
        kept_shapes = [jax.ShapeDtypeStruct((16, 128), BF16)] if marked else []
        scratch = []
        inputs = [*sources, *in_vmem(*kept)]
        specs = [VMEM] * len(inputs)
    slot_count = router_t.shape[0] * capacity
    outs = pl.pallas_call(
        functools.partial(
            later_attend_kernel if step else attend_kernel, step, capacity, blocks
        ),
        in_specs=specs,
        out_specs=[VMEM] * (2 + blocks + len(kept_shapes)),
        out_shape=[
            jax.ShapeDtypeStruct((CAND_LEN, width), F32),
            jax.ShapeDtypeStruct((slot_count, CAND_LEN), F32),
            *[jax.ShapeDtypeStruct((slot_count // blocks, width), BF16)] * blocks,
            *kept_shapes,
        ],
        scratch_shapes=scratch,
        compiler_params=pltpu.CompilerParams(vmem_limit_bytes=12 * MIB),
        cost_estimate=pl.CostEstimate(
            flops=6 * CAND_LEN * width * head_total,
            bytes_accessed=4 * width * head_total + 8 * CAND_LEN * width,
            transcendentals=0,
        ),
        name="attend",
    )(*inputs)
    return outs[:2], outs[2 : 2 + blocks], outs[2 + blocks :]


def expert_kernel(blocks, stream, *refs):
    rows_in, refs = refs[:blocks], refs[blocks:]
    own_in, refs = refs[0], refs[1:]
    if stream:
        sources, served, refs = refs[:3], refs[3 : 3 + blocks], refs[3 + blocks :]
        (own_down, other_in, other_down), (rows, own_hidden, other_hidden, sems) = refs[:3], refs[3:]
    else:
        (own_down, other_in, other_down), refs = refs[:3], refs[3:]
        served, (rows, own_hidden, other_hidden) = refs[:blocks], refs[blocks:]
    chunks = [pl.ds(start, HIDDEN_CHUNK) for start in range(0, own_in.shape[1], HIDDEN_CHUNK)]

    def fill(source, mat, i):
        lanes = chunks[i]
        return pltpu.make_async_copy(
            sources[source].at[:, lanes], mat.at[:, lanes], sems.at[source, i]
        )

    if stream:
        for i in range(len(chunks)):
            fill(1, other_in, i).start()
        for i in range(len(chunks)):
            fill(0, own_down, i).start()
            fill(2, other_down, i).start()
    rows[...] = joined(rows_in)
    for units in chunks:
        own_hidden[:, units] = jnp.maximum(dot(rows[...], own_in[:, units]), 0.0).astype(BF16)
    for i, units in enumerate(chunks):
        if stream:
            fill(1, other_in, i).wait()
        other_hidden[:, units] = jnp.maximum(dot(rows[...], other_in[:, units]), 0.0).astype(BF16)
    for i, lanes in enumerate(chunks):
        if stream:
            fill(0, own_down, i).wait()
            fill(2, other_down, i).wait()
        out = dot(own_hidden[...], own_down[:, lanes]) + dot(other_hidden[...], other_down[:, lanes])
        for part, block in zip(split(out, blocks), served):
            block[:, lanes] = part.astype(BF16)


def later_expert_kernel(step, blocks, mark_count, *refs):
    refs = refs[mark_count:]

    @pl.when(has_candidate(step))
    def _():
        expert_kernel(blocks, False, *refs)


def expert_rows(rows_in, mats, step, marks=()):
    blocks, stream = len(rows_in), step == 0
    width = rows_in[0].shape[1]
    count = blocks * rows_in[0].shape[0]
    units = mats[0].shape[1]
    scratch = [
        pltpu.VMEM((count, width), BF16),
        pltpu.VMEM((count, units), BF16),
        pltpu.VMEM((count, units), BF16),
    ]
    out_shape = [jax.ShapeDtypeStruct(rows.shape, BF16) for rows in rows_in]
    if stream:
        scratch.append(pltpu.SemaphoreType.DMA((3, units // HIDDEN_CHUNK)))
        out_shape += [pltpu.VMEM(mat.shape, BF16) for mat in mats[1:]]
    outs = pl.pallas_call(
        functools.partial(expert_kernel, blocks, True)
        if stream
        else functools.partial(later_expert_kernel, step, blocks, len(marks)),
        in_specs=[VMEM] * (len(marks) + blocks + 1) + [HBM if stream else VMEM] * 3,
        out_specs=[VMEM] * len(out_shape),
        out_shape=out_shape,
        scratch_shapes=scratch,
        compiler_params=pltpu.CompilerParams(vmem_limit_bytes=12 * MIB),
        cost_estimate=pl.CostEstimate(
            flops=8 * count * width * units,
            bytes_accessed=8 * width * units + 4 * count * width,
            transcendentals=0,
        ),
        name="experts",
    )(*marks, *rows_in, *in_vmem(mats[0]), *(in_hbm if stream else in_vmem)(*mats[1:]))
    return outs[:blocks], ((mats[0], *outs[blocks:]) if stream else mats)


def mixed(after_attn, weights, blocks):
    gates = weights[...]
    coarse = gates.astype(BF16)
    fine = (gates - coarse.astype(F32)).astype(BF16)
    rows = joined(blocks)
    mixture = dot(coarse, rows, ((0,), (0,))) + dot(fine, rows, ((0,), (0,)))
    return (after_attn[...] + mixture).astype(BF16)


def combine_kernel(blocks, after_attn, weights, *refs):
    result = refs[blocks]
    result[...] = mixed(after_attn, weights, refs[:blocks])


def place_kernel(blocks, after_attn, weights, *refs):
    served, earlier, (output, result, sems) = refs[:blocks], refs[blocks:-3], refs[-3:]
    segment = lax.axis_index("segment")

    def place(source, micro):
        rows = pl.ds(micro * CAND_LEN, CAND_LEN)
        return pltpu.make_async_copy(source, output.at[rows, :], sems.at[micro])

    last = len(earlier)
    for micro in range(CAND_DEV):
        for step in range(micro, last):

            @pl.when(segment + micro == step)
            def _():
                place(earlier[step], micro).start()

    result[...] = mixed(after_attn, weights, served)
    for micro in range(CAND_DEV):

        @pl.when(segment + micro == last)
        def _():
            place(result, micro).start()

    for micro in range(CAND_DEV):
        place(result, micro).wait()


def combine(after_attn, weights, served, earlier=()):
    rows, width = after_attn.shape
    inputs = [after_attn, weights, *served]
    scratch = []
    out_shape, out_spec = jax.ShapeDtypeStruct((rows, width), BF16), VMEM
    if earlier:
        inputs += in_vmem(*earlier)
        scratch = [pltpu.VMEM((rows, width), BF16), pltpu.SemaphoreType.DMA((CAND_DEV,))]
        out_shape, out_spec = jax.ShapeDtypeStruct((CAND_DEV * rows, width), BF16), HBM
    return pl.pallas_call(
        functools.partial(place_kernel if earlier else combine_kernel, len(served)),
        in_specs=[VMEM] * len(inputs),
        out_specs=out_spec,
        out_shape=out_shape,
        scratch_shapes=scratch,
        compiler_params=pltpu.CompilerParams(vmem_limit_bytes=8 * MIB),
        cost_estimate=pl.CostEstimate(
            flops=4 * weights.size * width,
            bytes_accessed=6 * after_attn.size + 2 * weights.shape[0] * width,
            transcendentals=0,
        ),
        name="combine",
    )(*inputs)


def local(
    states, cand_len, routes, enc_kv, attn_gain, ffn_gain, w_query, w_out, w_router, w_in, w_down
):
    n_segment = lax.axis_size("segment")
    n_expert = lax.axis_size("expert")
    model_width = states.shape[1]
    experts = w_router.shape[2]
    capacity = 2 * ((5 * CAND_LEN + 4 * experts - 1) // (4 * experts))
    core_pairs = [(i, i ^ 1) for i in range(n_expert)]
    same_core = [list(range(core, n_expert, 2)) for core in range(2)]
    blocks = experts if experts <= 4 else 1

    def exchange(parts):
        if blocks > 1:
            return [parts[0]] + [
                lax.ppermute(part, "expert", [(i, i ^ (2 * k)) for i in range(n_expert)])
                for k, part in enumerate(parts[1:], 1)
            ]
        rows = parts[0].reshape(experts, capacity, model_width)
        moved = lax.all_to_all(
            rows, "expert", split_axis=0, concat_axis=0, axis_index_groups=same_core, tiled=True
        )
        return [moved.reshape(parts[0].shape)]

    cached = lax.all_to_all(
        spread(enc_kv, n_expert), ("segment", "expert"), split_axis=0, concat_axis=0, tiled=True
    )
    own = (w_in[0, 0], w_down[0, 0])
    other = tuple(lax.ppermute(mat, "expert", core_pairs) for mat in own)

    queries = project(states, attn_gain, w_query[0])
    step_count = CAND_DEV + n_segment - 1
    earlier = []
    kept = ()
    for step in range(step_count):
        if step == 0:
            sources = (
                cand_len, queries, cached, states, routes[0].T, attn_gain, ffn_gain,
                w_router[0].T, w_query[0], w_out[0], own[0],
            )
        elif step < CAND_DEV:
            sources = (incoming, following)
        else:
            sources = (incoming,)
        marked = step > CAND_DEV
        (after_attn, weights), outgoing, left = attend(
            step, capacity, blocks, marked, sources, kept
        )
        if step == 0:
            *kept, following, own_in = left
            expert_mats = (own_in, own[1], *other)
        received = exchange(outgoing)
        marks = ()
        if marked:
            pairs = [(i, i + 1) for i in range(0, n_expert, 2)]
            marks = (lax.ppermute(left[0], "expert", pairs),)
        served, expert_mats = expert_rows(received, expert_mats, step, marks)
        served = exchange(served)
        if step + 1 < step_count:
            result = combine(after_attn, weights, served)
            incoming = lax.ppermute(
                result, "segment", [(i, i + 1) for i in range(n_segment - 1)]
            )
            earlier.append(result)
    output = combine(after_attn, weights, served, earlier)
    return output.reshape(1, CAND_DEV * CAND_LEN, model_width)


def solution(mesh):
    return jax.shard_map(
        local,
        mesh=mesh,
        in_specs=(
            P("expert", None),
            P("expert"),
            P("segment", "expert", None),
            P(None, ("segment", "expert"), None),
            P("segment", None),
            P("segment", None),
            P("segment", None, None),
            P("segment", None, None),
            P("segment", None, None),
            P("segment", "expert", None, None),
            P("segment", "expert", None, None),
        ),
        out_specs=P("segment", "expert", None),
        check_vma=False,
    )
```

```python
import functools
import math

import jax
import jax.numpy as jnp
from jax import lax
from jax.experimental import pallas as pl
from jax.experimental.pallas import tpu as pltpu
from jax.sharding import PartitionSpec as P

HEAD_DIM = 128
CAND_LEN = 64
CAND_DEV = 2
HIDDEN_CHUNK = 512
MIB = 1 << 20

EPSILON = 1e-05

VMEM = pl.BlockSpec(memory_space=pltpu.VMEM)
SMEM = pl.BlockSpec(memory_space=pltpu.SMEM)
HBM = pl.BlockSpec(memory_space=pltpu.HBM)
F32 = jnp.float32
BF16 = jnp.bfloat16


def in_hbm(*arrays):
    return [pltpu.with_memory_space_constraint(array, pltpu.HBM) for array in arrays]


def in_vmem(*arrays):
    return [pltpu.with_memory_space_constraint(array, pltpu.VMEM) for array in arrays]


def split(rows, blocks):
    size = rows.shape[0] // blocks
    return [rows[k * size : (k + 1) * size] for k in range(blocks)]


def joined(blocks):
    if len(blocks) == 1:
        return blocks[0][...]
    return jnp.concatenate([block[...].astype(F32) for block in blocks], axis=0).astype(BF16)


def normalize(carried, gain_row):
    average = jnp.mean(carried, axis=-1, keepdims=True)
    centered = carried - average
    variance = jnp.mean(centered * centered, axis=-1, keepdims=True)
    return gain_row * centered * lax.rsqrt(variance + EPSILON)


def dot(left, right, contract=((1,), (0,))):
    return lax.dot_general(left, right, (contract, ((), ())), preferred_element_type=F32)


def spread_kernel(copies_of, enc_kv, blocks):
    for layer in range(enc_kv.shape[0]):
        block = enc_kv[layer]
        for i in range(copies_of):
            blocks[layer * copies_of + i] = block


def spread(enc_kv, copies_of):
    layers, _, features = enc_kv.shape
    tiles = enc_kv.reshape(layers, features // HEAD_DIM, HEAD_DIM)
    return pl.pallas_call(
        functools.partial(spread_kernel, copies_of),
        in_specs=[VMEM],
        out_specs=VMEM,
        out_shape=jax.ShapeDtypeStruct((layers * copies_of, *tiles.shape[1:]), BF16),
        compiler_params=pltpu.CompilerParams(vmem_limit_bytes=8 * MIB),
        name="spread",
    )(tiles)


def project_kernel(states, gain, w_query, queries, fresh, gain_buf, query_buf, sems):
    fills = (
        (states.at[pl.ds(0, CAND_LEN), :], fresh),
        (gain, gain_buf),
        (w_query, query_buf),
    )
    copies = [pltpu.make_async_copy(*pair, sems.at[i]) for i, pair in enumerate(fills)]
    for copy in copies:
        copy.start()
    copies[0].wait()
    copies[1].wait()
    normed = normalize(fresh[...].astype(F32), gain_buf[...]).astype(BF16)
    copies[2].wait()
    queries[...] = dot(normed, query_buf[...]).astype(BF16)


def project(states, gain, w_query):
    width, head_total = w_query.shape
    return pl.pallas_call(
        project_kernel,
        in_specs=[HBM] * 3,
        out_specs=VMEM,
        out_shape=jax.ShapeDtypeStruct((CAND_LEN, head_total), BF16),
        scratch_shapes=[
            pltpu.VMEM((CAND_LEN, width), BF16),
            pltpu.VMEM((1, width), F32),
            pltpu.VMEM(w_query.shape, BF16),
            pltpu.SemaphoreType.DMA((3,)),
        ],
        compiler_params=pltpu.CompilerParams(vmem_limit_bytes=12 * MIB),
        cost_estimate=pl.CostEstimate(
            flops=2 * CAND_LEN * width * head_total,
            bytes_accessed=2 * width * head_total,
            transcendentals=0,
        ),
        name="project",
    )(*in_hbm(states, gain, w_query))


def block_diagonal(cached, first_head, blocks):
    sources = cached.shape[0]
    blocks[...] = jnp.zeros_like(blocks)
    for head in range(blocks.shape[1] // HEAD_DIM):
        rows = pl.ds(head * sources, sources)
        blocks[rows, pl.ds(head * HEAD_DIM, HEAD_DIM)] = cached[:, first_head + head, :]


def has_candidate(step):
    micro = step - lax.axis_index("segment")
    return (micro >= 0) & (micro < CAND_DEV)


def later_attend_kernel(step, capacity, blocks, *refs):
    @pl.when(has_candidate(step))
    def _():
        attend_kernel(step, capacity, blocks, *refs)


def attend_kernel(step, capacity, blocks, *refs):
    segment = lax.axis_index("segment")
    if step == 0:
        (cand_len, queries_in, cached, states, routes_hbm, attn_gain, ffn_gain, router_hbm,
         query_hbm, out_hbm, expert_hbm), refs = refs[:11], refs[11:]
        after_ref, weights, *outgoing = refs[: 2 + blocks]
        (routes, gains, router, w_query, w_out, keys, values, following, expert_mat,
         fresh, route_buf, sems) = refs[2 + blocks :]
        fills = (
            (states.at[pl.ds(0, CAND_LEN), :], fresh),
            (ffn_gain, gains.at[1]),
            (out_hbm, w_out),
            (router_hbm, router),
            (routes_hbm, route_buf),
            (attn_gain, gains.at[0]),
            (states.at[pl.ds(CAND_LEN, CAND_LEN), :], following),
            (query_hbm, w_query),
            (expert_hbm, expert_mat),
        )
        copies = [pltpu.make_async_copy(*pair, sems.at[i]) for i, pair in enumerate(fills)]
        for copy in copies:
            copy.start()
        head_count = w_out.shape[0] // HEAD_DIM
        block_diagonal(cached, 0, keys)
        block_diagonal(cached, head_count, values)
        queries = queries_in[...]
        copies[0].wait()
        carried = fresh[...].astype(F32)
        copies[4].wait()
        copies = copies[:4] + copies[5:]
        position = lax.broadcasted_iota(jnp.int32, (1, CAND_LEN), 1)
        for micro in range(CAND_DEV):
            route = route_buf[:, micro * CAND_LEN : (micro + 1) * CAND_LEN]
            routes[micro] = jnp.where(position < cand_len[micro], route, -1)
    else:
        incoming, refs = refs[0], refs[1:]
        current = incoming[...]
        if step < CAND_DEV:
            current, refs = jnp.where(segment == 0, refs[0][...], current), refs[1:]
        (routes, gains, router, w_query, w_out, keys, values, after_ref, weights), refs = (
            refs[:9], refs[9:]
        )
        outgoing, marks = refs[:blocks], refs[blocks:]
        for mark in marks:
            mark[...] = current[: mark.shape[0], : mark.shape[1]]
        carried = current.astype(F32)
        normed = normalize(carried, gains[0]).astype(BF16)
        queries = dot(normed, w_query[...]).astype(BF16)

    rows = carried.shape[0]
    sources = keys.shape[0] * HEAD_DIM // keys.shape[1]
    scores = dot(keys[...], queries, ((1,), (1,))) * (1.0 / math.sqrt(HEAD_DIM))
    scores = scores.reshape(-1, sources, rows)
    exponent = jnp.exp(scores - jnp.max(scores, axis=1, keepdims=True))
    share = exponent / jnp.sum(exponent, axis=1, keepdims=True)
    share = share.reshape(-1, rows).astype(BF16)
    context = dot(share, values[...], ((0,), (0,))).astype(BF16)
    if step == 0:
        copies[1].wait()
        copies[2].wait()
    after_attn = carried + dot(context, w_out[...])
    after_ref[...] = after_attn
    ffn_input = normalize(after_attn, gains[1]).astype(BF16)

    if step == 0:
        copies[3].wait()
    experts = router.shape[0]
    logits = dot(router[...], ffn_input, ((1,), (1,)))
    micro = jnp.clip(step - segment, 0, CAND_DEV - 1)
    route = routes[micro]
    place = route
    if blocks > 1:
        place = jnp.where(route < 0, route, route ^ (lax.axis_index("expert") // 2))
    labels = lax.broadcasted_iota(jnp.int32, (experts, rows), 0)
    first, second = route[0:1] == labels, route[1:2] == labels
    logit_first = jnp.sum(jnp.where(first, logits, 0.0), axis=0, keepdims=True)
    logit_second = jnp.sum(jnp.where(second, logits, 0.0), axis=0, keepdims=True)
    gate_first = jax.nn.sigmoid(logit_first - logit_second)
    gate_second = 1.0 - gate_first
    named = jnp.where(first | second, 1.0, 0.0).astype(BF16)
    earlier = lax.broadcasted_iota(jnp.int32, (rows, rows), 0) < lax.broadcasted_iota(
        jnp.int32, (rows, rows), 1
    )
    before = dot(named, jnp.where(earlier, 1.0, 0.0).astype(BF16))
    slots = lax.broadcasted_iota(jnp.int32, (experts * capacity, rows), 0)
    chosen = []
    for mask, row in ((first, 0), (second, 1)):
        slot = jnp.sum(jnp.where(mask, before, 0.0), axis=0, keepdims=True).astype(jnp.int32)
        chosen.append(slots == place[row : row + 1] * capacity + slot)
    select = jnp.where(chosen[0] | chosen[1], 1.0, 0.0).astype(BF16)
    buffers = dot(select, ffn_input)
    for buffer, block in zip(split(buffers, blocks), outgoing):
        block[...] = buffer.astype(BF16)
    weights[...] = jnp.where(chosen[0], gate_first, 0.0) + jnp.where(chosen[1], gate_second, 0.0)
    if step == 0:
        for copy in copies[4:]:
            copy.wait()


def attend(step, capacity, blocks, marked, sources, kept):
    if step == 0:
        cand_len, queries, cached, *params = sources
        _, routes, _, _, router_t, w_query, w_out, expert_mat = params
        head_total, width = w_out.shape
        diagonal = (cached.shape[0] * head_total // HEAD_DIM, head_total)
        kept_shapes = [
            pltpu.VMEM((CAND_DEV, 2, CAND_LEN), jnp.int32),
            pltpu.VMEM((2, 1, width), F32),
            *(pltpu.VMEM(array.shape, BF16) for array in (router_t, w_query, w_out)),
            pltpu.VMEM(diagonal, BF16),
            pltpu.VMEM(diagonal, BF16),
            pltpu.VMEM((CAND_LEN, width), BF16),
            pltpu.VMEM(expert_mat.shape, BF16),
        ]
        inputs = [*in_hbm(cand_len), queries, cached, *in_hbm(*params)]
        specs = [SMEM, VMEM, VMEM] + [HBM] * len(params)
        scratch = [
            pltpu.VMEM((CAND_LEN, width), BF16),
            pltpu.VMEM(routes.shape, jnp.int32),
            pltpu.SemaphoreType.DMA((9,)),
        ]
    else:
        _, _, router_t, _, w_out, *_ = kept
        head_total, width = w_out.shape
        kept_shapes = [jax.ShapeDtypeStruct((16, 128), BF16)] if marked else []
        scratch = []
        inputs = [*sources, *in_vmem(*kept)]
        specs = [VMEM] * len(inputs)
    slot_count = router_t.shape[0] * capacity
    outs = pl.pallas_call(
        functools.partial(
            later_attend_kernel if step else attend_kernel, step, capacity, blocks
        ),
        in_specs=specs,
        out_specs=[VMEM] * (2 + blocks + len(kept_shapes)),
        out_shape=[
            jax.ShapeDtypeStruct((CAND_LEN, width), F32),
            jax.ShapeDtypeStruct((slot_count, CAND_LEN), F32),
            *[jax.ShapeDtypeStruct((slot_count // blocks, width), BF16)] * blocks,
            *kept_shapes,
        ],
        scratch_shapes=scratch,
        compiler_params=pltpu.CompilerParams(vmem_limit_bytes=12 * MIB),
        cost_estimate=pl.CostEstimate(
            flops=6 * CAND_LEN * width * head_total,
            bytes_accessed=4 * width * head_total + 8 * CAND_LEN * width,
            transcendentals=0,
        ),
        name="attend",
    )(*inputs)
    return outs[:2], outs[2 : 2 + blocks], outs[2 + blocks :]


def expert_kernel(blocks, stream, mark_count, *refs):
    refs = refs[mark_count:]
    rows_in, (own_in, own_down), refs = refs[:blocks], refs[blocks : blocks + 2], refs[blocks + 2 :]
    if stream:
        sources, served, refs = refs[:2], refs[2 : 2 + blocks], refs[2 + blocks :]
        (other_in, other_down), (rows, own_hidden, other_hidden, sems) = refs[:2], refs[2:]
    else:
        (other_in, other_down), refs = refs[:2], refs[2:]
        served, (rows, own_hidden, other_hidden) = refs[:blocks], refs[blocks:]
    chunks = [pl.ds(start, HIDDEN_CHUNK) for start in range(0, own_in.shape[1], HIDDEN_CHUNK)]

    def fill(source, mat, i):
        lanes = chunks[i]
        return pltpu.make_async_copy(
            sources[source].at[:, lanes], mat.at[:, lanes], sems.at[source, i]
        )

    if stream:
        for i in range(len(chunks)):
            fill(0, other_in, i).start()
        for i in range(len(chunks)):
            fill(1, other_down, i).start()
    rows[...] = joined(rows_in)
    for units in chunks:
        own_hidden[:, units] = jnp.maximum(dot(rows[...], own_in[:, units]), 0.0).astype(BF16)
    for i, units in enumerate(chunks):
        if stream:
            fill(0, other_in, i).wait()
        other_hidden[:, units] = jnp.maximum(dot(rows[...], other_in[:, units]), 0.0).astype(BF16)
    for i, lanes in enumerate(chunks):
        if stream:
            fill(1, other_down, i).wait()
        out = dot(own_hidden[...], own_down[:, lanes]) + dot(other_hidden[...], other_down[:, lanes])
        for part, block in zip(split(out, blocks), served):
            block[:, lanes] = part.astype(BF16)


def expert_rows(rows_in, mats, step, marks=()):
    blocks, stream = len(rows_in), step == 0
    width = rows_in[0].shape[1]
    count = blocks * rows_in[0].shape[0]
    units = mats[0].shape[1]
    scratch = [
        pltpu.VMEM((count, width), BF16),
        pltpu.VMEM((count, units), BF16),
        pltpu.VMEM((count, units), BF16),
    ]
    out_shape = [jax.ShapeDtypeStruct(rows.shape, BF16) for rows in rows_in]
    if stream:
        scratch.append(pltpu.SemaphoreType.DMA((2, units // HIDDEN_CHUNK)))
        out_shape += [pltpu.VMEM(mat.shape, BF16) for mat in mats[2:]]
    outs = pl.pallas_call(
        functools.partial(expert_kernel, blocks, stream, len(marks)),
        in_specs=[VMEM] * (len(marks) + blocks + 2) + [HBM if stream else VMEM] * 2,
        out_specs=[VMEM] * len(out_shape),
        out_shape=out_shape,
        scratch_shapes=scratch,
        compiler_params=pltpu.CompilerParams(vmem_limit_bytes=12 * MIB),
        cost_estimate=pl.CostEstimate(
            flops=8 * count * width * units,
            bytes_accessed=8 * width * units + 4 * count * width,
            transcendentals=0,
        ),
        name="experts",
    )(*marks, *rows_in, *in_vmem(*mats[:2]), *(in_hbm if stream else in_vmem)(*mats[2:]))
    return outs[:blocks], ((*mats[:2], *outs[blocks:]) if stream else mats)


def mixed(after_attn, weights, blocks):
    gates = weights[...]
    coarse = gates.astype(BF16)
    fine = (gates - coarse.astype(F32)).astype(BF16)
    rows = joined(blocks)
    mixture = dot(coarse, rows, ((0,), (0,))) + dot(fine, rows, ((0,), (0,)))
    return (after_attn[...] + mixture).astype(BF16)


def combine_kernel(blocks, after_attn, weights, *refs):
    result = refs[blocks]
    result[...] = mixed(after_attn, weights, refs[:blocks])


def place_kernel(blocks, after_attn, weights, *refs):
    served, earlier, (output, result, sems) = refs[:blocks], refs[blocks:-3], refs[-3:]
    segment = lax.axis_index("segment")

    def place(source, micro):
        rows = pl.ds(micro * CAND_LEN, CAND_LEN)
        return pltpu.make_async_copy(source, output.at[rows, :], sems.at[micro])

    last = len(earlier)
    for micro in range(CAND_DEV):
        for step in range(micro, last):

            @pl.when(segment + micro == step)
            def _():
                place(earlier[step], micro).start()

    result[...] = mixed(after_attn, weights, served)
    for micro in range(CAND_DEV):

        @pl.when(segment + micro == last)
        def _():
            place(result, micro).start()

    for micro in range(CAND_DEV):
        place(result, micro).wait()


def combine(after_attn, weights, served, earlier=()):
    rows, width = after_attn.shape
    inputs = [after_attn, weights, *served]
    scratch = []
    out_shape, out_spec = jax.ShapeDtypeStruct((rows, width), BF16), VMEM
    if earlier:
        inputs += in_vmem(*earlier)
        scratch = [pltpu.VMEM((rows, width), BF16), pltpu.SemaphoreType.DMA((CAND_DEV,))]
        out_shape, out_spec = jax.ShapeDtypeStruct((CAND_DEV * rows, width), BF16), HBM
    return pl.pallas_call(
        functools.partial(place_kernel if earlier else combine_kernel, len(served)),
        in_specs=[VMEM] * len(inputs),
        out_specs=out_spec,
        out_shape=out_shape,
        scratch_shapes=scratch,
        compiler_params=pltpu.CompilerParams(vmem_limit_bytes=8 * MIB),
        cost_estimate=pl.CostEstimate(
            flops=4 * weights.size * width,
            bytes_accessed=6 * after_attn.size + 2 * weights.shape[0] * width,
            transcendentals=0,
        ),
        name="combine",
    )(*inputs)


def local(
    states, cand_len, routes, enc_kv, attn_gain, ffn_gain, w_query, w_out, w_router, w_in, w_down
):
    n_segment = lax.axis_size("segment")
    n_expert = lax.axis_size("expert")
    model_width = states.shape[1]
    experts = w_router.shape[2]
    capacity = 2 * ((5 * CAND_LEN + 4 * experts - 1) // (4 * experts))
    core_pairs = [(i, i ^ 1) for i in range(n_expert)]
    same_core = [list(range(core, n_expert, 2)) for core in range(2)]
    blocks = experts if experts <= 4 else 1

    def exchange(parts):
        if blocks > 1:
            return [parts[0]] + [
                lax.ppermute(part, "expert", [(i, i ^ (2 * k)) for i in range(n_expert)])
                for k, part in enumerate(parts[1:], 1)
            ]
        rows = parts[0].reshape(experts, capacity, model_width)
        moved = lax.all_to_all(
            rows, "expert", split_axis=0, concat_axis=0, axis_index_groups=same_core, tiled=True
        )
        return [moved.reshape(parts[0].shape)]

    cached = lax.all_to_all(
        spread(enc_kv, n_expert), ("segment", "expert"), split_axis=0, concat_axis=0, tiled=True
    )
    own = (w_in[0, 0], w_down[0, 0])
    other = tuple(lax.ppermute(mat, "expert", core_pairs) for mat in own)

    queries = project(states, attn_gain, w_query[0])
    step_count = CAND_DEV + n_segment - 1
    earlier = []
    kept = ()
    for step in range(step_count):
        if step == 0:
            sources = (
                cand_len, queries, cached, states, routes[0].T, attn_gain, ffn_gain,
                w_router[0].T, w_query[0], w_out[0], own[0],
            )
        elif step < CAND_DEV:
            sources = (incoming, following)
        else:
            sources = (incoming,)
        marked = step > CAND_DEV
        (after_attn, weights), outgoing, left = attend(
            step, capacity, blocks, marked, sources, kept
        )
        if step == 0:
            *kept, following, own_in = left
            expert_mats = (own_in, own[1], *other)
        received = exchange(outgoing)
        marks = ()
        if marked:
            pairs = [(i, i + 1) for i in range(0, n_expert, 2)]
            marks = (lax.ppermute(left[0], "expert", pairs),)
        served, expert_mats = expert_rows(received, expert_mats, step, marks)
        served = exchange(served)
        if step + 1 < step_count:
            result = combine(after_attn, weights, served)
            incoming = lax.ppermute(
                result, "segment", [(i, i + 1) for i in range(n_segment - 1)]
            )
            earlier.append(result)
    output = combine(after_attn, weights, served, earlier)
    return output.reshape(1, CAND_DEV * CAND_LEN, model_width)


def solution(mesh):
    return jax.shard_map(
        local,
        mesh=mesh,
        in_specs=(
            P("expert", None),
            P("expert"),
            P("segment", "expert", None),
            P(None, ("segment", "expert"), None),
            P("segment", None),
            P("segment", None),
            P("segment", None, None),
            P("segment", None, None),
            P("segment", None, None),
            P("segment", "expert", None, None),
            P("segment", "expert", None, None),
        ),
        out_specs=P("segment", "expert", None),
        check_vma=False,
    )
```

```python
import functools
import math

import jax
import jax.numpy as jnp
from jax import lax
from jax.experimental import pallas as pl
from jax.experimental.pallas import tpu as pltpu
from jax.sharding import PartitionSpec as P

HEAD_DIM = 128
CAND_LEN = 64
CAND_DEV = 2
HIDDEN_CHUNK = 512
MIB = 1 << 20

EPSILON = 1e-05

VMEM = pl.BlockSpec(memory_space=pltpu.VMEM)
SMEM = pl.BlockSpec(memory_space=pltpu.SMEM)
HBM = pl.BlockSpec(memory_space=pltpu.HBM)
F32 = jnp.float32
BF16 = jnp.bfloat16


def in_hbm(*arrays):
    return [pltpu.with_memory_space_constraint(array, pltpu.HBM) for array in arrays]


def in_vmem(*arrays):
    return [pltpu.with_memory_space_constraint(array, pltpu.VMEM) for array in arrays]


def split(rows, blocks):
    size = rows.shape[0] // blocks
    return [rows[k * size : (k + 1) * size] for k in range(blocks)]


def joined(blocks):
    if len(blocks) == 1:
        return blocks[0][...]
    return jnp.concatenate([block[...].astype(F32) for block in blocks], axis=0).astype(BF16)


def normalize(carried, gain_row):
    average = jnp.mean(carried, axis=-1, keepdims=True)
    centered = carried - average
    variance = jnp.mean(centered * centered, axis=-1, keepdims=True)
    return gain_row * centered * lax.rsqrt(variance + EPSILON)


def dot(left, right, contract=((1,), (0,))):
    return lax.dot_general(left, right, (contract, ((), ())), preferred_element_type=F32)


def spread_kernel(copies_of, enc_kv, blocks):
    for layer in range(enc_kv.shape[0]):
        block = enc_kv[layer : layer + 1, :].reshape(blocks.shape[1:])
        for i in range(copies_of):
            blocks[layer * copies_of + i] = block


def spread(enc_kv, copies_of):
    layers, _, features = enc_kv.shape
    return pl.pallas_call(
        functools.partial(spread_kernel, copies_of),
        in_specs=[VMEM],
        out_specs=VMEM,
        out_shape=jax.ShapeDtypeStruct(
            (layers * copies_of, features // HEAD_DIM, HEAD_DIM), BF16
        ),
        compiler_params=pltpu.CompilerParams(vmem_limit_bytes=8 * MIB),
        name="spread",
    )(*in_hbm(enc_kv.reshape(layers, features)))


def project_kernel(states, gain, w_query, queries, fresh, gain_buf, query_buf, sems):
    fills = (
        (states.at[pl.ds(0, CAND_LEN), :], fresh),
        (gain, gain_buf),
        (w_query, query_buf),
    )
    copies = [pltpu.make_async_copy(*pair, sems.at[i]) for i, pair in enumerate(fills)]
    for copy in copies:
        copy.start()
    copies[0].wait()
    copies[1].wait()
    normed = normalize(fresh[...].astype(F32), gain_buf[...]).astype(BF16)
    copies[2].wait()
    queries[...] = dot(normed, query_buf[...]).astype(BF16)


def project(states, gain, w_query):
    width, head_total = w_query.shape
    return pl.pallas_call(
        project_kernel,
        in_specs=[HBM] * 3,
        out_specs=VMEM,
        out_shape=jax.ShapeDtypeStruct((CAND_LEN, head_total), BF16),
        scratch_shapes=[
            pltpu.VMEM((CAND_LEN, width), BF16),
            pltpu.VMEM((1, width), F32),
            pltpu.VMEM(w_query.shape, BF16),
            pltpu.SemaphoreType.DMA((3,)),
        ],
        compiler_params=pltpu.CompilerParams(vmem_limit_bytes=12 * MIB),
        cost_estimate=pl.CostEstimate(
            flops=2 * CAND_LEN * width * head_total,
            bytes_accessed=2 * width * head_total,
            transcendentals=0,
        ),
        name="project",
    )(*in_hbm(states, gain, w_query))


def block_diagonal(cached, first_head, blocks):
    sources = cached.shape[0]
    blocks[...] = jnp.zeros_like(blocks)
    for head in range(blocks.shape[1] // HEAD_DIM):
        rows = pl.ds(head * sources, sources)
        blocks[rows, pl.ds(head * HEAD_DIM, HEAD_DIM)] = cached[:, first_head + head, :]


def chosen_slots(step, capacity, blocks, routes, experts):
    micro = jnp.clip(step - lax.axis_index("segment"), 0, CAND_DEV - 1)
    route = routes[micro]
    rows = route.shape[1]
    labels = lax.broadcasted_iota(jnp.int32, (experts, rows), 0)
    first, second = route[0:1] == labels, route[1:2] == labels
    place = route
    if blocks > 1:
        place = jnp.where(route < 0, route, route ^ (lax.axis_index("expert") // 2))
    named = jnp.where(first | second, 1.0, 0.0).astype(BF16)
    earlier = lax.broadcasted_iota(jnp.int32, (rows, rows), 0) < lax.broadcasted_iota(
        jnp.int32, (rows, rows), 1
    )
    before = dot(named, jnp.where(earlier, 1.0, 0.0).astype(BF16))
    slots = lax.broadcasted_iota(jnp.int32, (experts * capacity, rows), 0)
    chosen = []
    for mask, row in ((first, 0), (second, 1)):
        slot = jnp.sum(jnp.where(mask, before, 0.0), axis=0, keepdims=True).astype(jnp.int32)
        chosen.append(slots == place[row : row + 1] * capacity + slot)
    return chosen


def gate_kernel(step, capacity, blocks, ffn_input, routes, router, weights):
    experts = router.shape[0]
    micro = jnp.clip(step - lax.axis_index("segment"), 0, CAND_DEV - 1)
    route = routes[micro]
    labels = lax.broadcasted_iota(jnp.int32, (experts, route.shape[1]), 0)
    logits = dot(router[...], ffn_input[...], ((1,), (1,)))
    picked = [
        jnp.sum(jnp.where(route[row : row + 1] == labels, logits, 0.0), axis=0, keepdims=True)
        for row in range(2)
    ]
    gate_first = jax.nn.sigmoid(picked[0] - picked[1])
    gate_second = 1.0 - gate_first
    chosen = chosen_slots(step, capacity, blocks, routes, experts)
    weights[...] = jnp.where(chosen[0], gate_first, 0.0) + jnp.where(chosen[1], gate_second, 0.0)


def gate(step, capacity, blocks, ffn_input, routes, router):
    experts, width = router.shape
    return pl.pallas_call(
        functools.partial(gate_kernel, step, capacity, blocks),
        in_specs=[VMEM] * 3,
        out_specs=VMEM,
        out_shape=jax.ShapeDtypeStruct((experts * capacity, CAND_LEN), F32),
        compiler_params=pltpu.CompilerParams(vmem_limit_bytes=8 * MIB),
        cost_estimate=pl.CostEstimate(
            flops=2 * CAND_LEN * width * 128, bytes_accessed=2 * ffn_input.size, transcendentals=0
        ),
        name="gate",
    )(ffn_input, *in_vmem(routes, router))


def has_candidate(step):
    micro = step - lax.axis_index("segment")
    return (micro >= 0) & (micro < CAND_DEV)


def later_attend_kernel(step, capacity, blocks, *refs):
    @pl.when(has_candidate(step))
    def _():
        attend_kernel(step, capacity, blocks, *refs)


def attend_kernel(step, capacity, blocks, *refs):
    segment = lax.axis_index("segment")
    if step == 0:
        (cand_len, queries_in, cached, states, routes_hbm, attn_gain, ffn_gain, router_hbm,
         query_hbm, out_hbm, expert_hbm), refs = refs[:11], refs[11:]
        after_ref, ffn_ref, *outgoing = refs[: 2 + blocks]
        (routes, gains, router, w_query, w_out, keys, values, following, expert_mat,
         fresh, route_buf, sems) = refs[2 + blocks :]
        fills = (
            (states.at[pl.ds(0, CAND_LEN), :], fresh),
            (ffn_gain, gains.at[1]),
            (out_hbm, w_out),
            (router_hbm, router),
            (routes_hbm, route_buf),
            (attn_gain, gains.at[0]),
            (states.at[pl.ds(CAND_LEN, CAND_LEN), :], following),
            (query_hbm, w_query),
            (expert_hbm, expert_mat),
        )
        copies = [pltpu.make_async_copy(*pair, sems.at[i]) for i, pair in enumerate(fills)]
        for copy in copies:
            copy.start()
        head_count = w_out.shape[0] // HEAD_DIM
        block_diagonal(cached, 0, keys)
        block_diagonal(cached, head_count, values)
        queries = queries_in[...]
        copies[0].wait()
        carried = fresh[...].astype(F32)
        copies[4].wait()
        copies = copies[:4] + copies[5:]
        position = lax.broadcasted_iota(jnp.int32, (1, CAND_LEN), 1)
        for micro in range(CAND_DEV):
            route = route_buf[:, micro * CAND_LEN : (micro + 1) * CAND_LEN]
            routes[micro] = jnp.where(position < cand_len[micro], route, -1)
    else:
        incoming, refs = refs[0], refs[1:]
        current = incoming[...]
        if step < CAND_DEV:
            current, refs = jnp.where(segment == 0, refs[0][...], current), refs[1:]
        (routes, gains, router, w_query, w_out, keys, values, after_ref, ffn_ref), refs = (
            refs[:9], refs[9:]
        )
        outgoing, marks = refs[:blocks], refs[blocks:]
        for mark in marks:
            mark[...] = current[: mark.shape[0], : mark.shape[1]]
        carried = current.astype(F32)
        normed = normalize(carried, gains[0]).astype(BF16)
        queries = dot(normed, w_query[...]).astype(BF16)

    rows = carried.shape[0]
    sources = keys.shape[0] * HEAD_DIM // keys.shape[1]
    scores = dot(keys[...], queries, ((1,), (1,))) * (1.0 / math.sqrt(HEAD_DIM))
    scores = scores.reshape(-1, sources, rows)
    exponent = jnp.exp(scores - jnp.max(scores, axis=1, keepdims=True))
    share = exponent / jnp.sum(exponent, axis=1, keepdims=True)
    share = share.reshape(-1, rows).astype(BF16)
    context = dot(share, values[...], ((0,), (0,))).astype(BF16)
    if step == 0:
        copies[1].wait()
        copies[2].wait()
    after_attn = carried + dot(context, w_out[...])
    after_ref[...] = after_attn
    ffn_input = normalize(after_attn, gains[1]).astype(BF16)

    rows_in_slots = chosen_slots(step, capacity, blocks, routes, router.shape[0])
    select = jnp.where(rows_in_slots[0] | rows_in_slots[1], 1.0, 0.0).astype(BF16)
    buffers = dot(select, ffn_input)
    for buffer, block in zip(split(buffers, blocks), outgoing):
        block[...] = buffer.astype(BF16)
    ffn_ref[...] = ffn_input
    if step == 0:
        for copy in copies[3:]:
            copy.wait()


def attend(step, capacity, blocks, marked, sources, kept):
    if step == 0:
        cand_len, queries, cached, *params = sources
        _, routes, _, _, router_t, w_query, w_out, expert_mat = params
        head_total, width = w_out.shape
        diagonal = (cached.shape[0] * head_total // HEAD_DIM, head_total)
        kept_shapes = [
            pltpu.VMEM((CAND_DEV, 2, CAND_LEN), jnp.int32),
            pltpu.VMEM((2, 1, width), F32),
            *(pltpu.VMEM(array.shape, BF16) for array in (router_t, w_query, w_out)),
            pltpu.VMEM(diagonal, BF16),
            pltpu.VMEM(diagonal, BF16),
            pltpu.VMEM((CAND_LEN, width), BF16),
            pltpu.VMEM(expert_mat.shape, BF16),
        ]
        inputs = [*in_hbm(cand_len), queries, cached, *in_hbm(*params)]
        specs = [SMEM, VMEM, VMEM] + [HBM] * len(params)
        scratch = [
            pltpu.VMEM((CAND_LEN, width), BF16),
            pltpu.VMEM(routes.shape, jnp.int32),
            pltpu.SemaphoreType.DMA((9,)),
        ]
    else:
        _, _, router_t, _, w_out, *_ = kept
        head_total, width = w_out.shape
        kept_shapes = [jax.ShapeDtypeStruct((16, 128), BF16)] if marked else []
        scratch = []
        inputs = [*sources, *in_vmem(*kept)]
        specs = [VMEM] * len(inputs)
    slot_count = router_t.shape[0] * capacity
    outs = pl.pallas_call(
        functools.partial(
            later_attend_kernel if step else attend_kernel, step, capacity, blocks
        ),
        in_specs=specs,
        out_specs=[VMEM] * (2 + blocks + len(kept_shapes)),
        out_shape=[
            jax.ShapeDtypeStruct((CAND_LEN, width), F32),
            jax.ShapeDtypeStruct((CAND_LEN, width), BF16),
            *[jax.ShapeDtypeStruct((slot_count // blocks, width), BF16)] * blocks,
            *kept_shapes,
        ],
        scratch_shapes=scratch,
        compiler_params=pltpu.CompilerParams(vmem_limit_bytes=12 * MIB),
        cost_estimate=pl.CostEstimate(
            flops=6 * CAND_LEN * width * head_total,
            bytes_accessed=4 * width * head_total + 8 * CAND_LEN * width,
            transcendentals=0,
        ),
        name="attend",
    )(*inputs)
    return outs[:2], outs[2 : 2 + blocks], outs[2 + blocks :]


def expert_kernel(blocks, stream, mark_count, *refs):
    refs = refs[mark_count:]
    rows_in, refs = refs[:blocks], refs[blocks:]
    own_in, refs = refs[0], refs[1:]
    if stream:
        sources, served, refs = refs[:3], refs[3 : 3 + blocks], refs[3 + blocks :]
        (own_down, other_in, other_down), (rows, own_hidden, other_hidden, sems) = refs[:3], refs[3:]
    else:
        (own_down, other_in, other_down), refs = refs[:3], refs[3:]
        served, (rows, own_hidden, other_hidden) = refs[:blocks], refs[blocks:]
    chunks = [pl.ds(start, HIDDEN_CHUNK) for start in range(0, own_in.shape[1], HIDDEN_CHUNK)]

    def fill(source, mat, i):
        lanes = chunks[i]
        return pltpu.make_async_copy(
            sources[source].at[:, lanes], mat.at[:, lanes], sems.at[source, i]
        )

    if stream:
        for i in range(len(chunks)):
            fill(1, other_in, i).start()
        for i in range(len(chunks)):
            fill(0, own_down, i).start()
            fill(2, other_down, i).start()
    rows[...] = joined(rows_in)
    for units in chunks:
        own_hidden[:, units] = jnp.maximum(dot(rows[...], own_in[:, units]), 0.0).astype(BF16)
    for i, units in enumerate(chunks):
        if stream:
            fill(1, other_in, i).wait()
        other_hidden[:, units] = jnp.maximum(dot(rows[...], other_in[:, units]), 0.0).astype(BF16)
    for i, lanes in enumerate(chunks):
        if stream:
            fill(0, own_down, i).wait()
            fill(2, other_down, i).wait()
        out = dot(own_hidden[...], own_down[:, lanes]) + dot(other_hidden[...], other_down[:, lanes])
        for part, block in zip(split(out, blocks), served):
            block[:, lanes] = part.astype(BF16)


def expert_rows(rows_in, mats, step, marks=()):
    blocks, stream = len(rows_in), step == 0
    width = rows_in[0].shape[1]
    count = blocks * rows_in[0].shape[0]
    units = mats[0].shape[1]
    scratch = [
        pltpu.VMEM((count, width), BF16),
        pltpu.VMEM((count, units), BF16),
        pltpu.VMEM((count, units), BF16),
    ]
    out_shape = [jax.ShapeDtypeStruct(rows.shape, BF16) for rows in rows_in]
    if stream:
        scratch.append(pltpu.SemaphoreType.DMA((3, units // HIDDEN_CHUNK)))
        out_shape += [pltpu.VMEM(mat.shape, BF16) for mat in mats[1:]]
    outs = pl.pallas_call(
        functools.partial(expert_kernel, blocks, stream, len(marks)),
        in_specs=[VMEM] * (len(marks) + blocks + 1) + [HBM if stream else VMEM] * 3,
        out_specs=[VMEM] * len(out_shape),
        out_shape=out_shape,
        scratch_shapes=scratch,
        compiler_params=pltpu.CompilerParams(vmem_limit_bytes=12 * MIB),
        cost_estimate=pl.CostEstimate(
            flops=8 * count * width * units,
            bytes_accessed=8 * width * units + 4 * count * width,
            transcendentals=0,
        ),
        name="experts",
    )(*marks, *rows_in, *in_vmem(mats[0]), *(in_hbm if stream else in_vmem)(*mats[1:]))
    return outs[:blocks], ((mats[0], *outs[blocks:]) if stream else mats)


def mixed(after_attn, weights, blocks):
    gates = weights[...]
    coarse = gates.astype(BF16)
    fine = (gates - coarse.astype(F32)).astype(BF16)
    rows = joined(blocks)
    mixture = dot(coarse, rows, ((0,), (0,))) + dot(fine, rows, ((0,), (0,)))
    return (after_attn[...] + mixture).astype(BF16)


def combine_kernel(blocks, after_attn, weights, *refs):
    result = refs[blocks]
    result[...] = mixed(after_attn, weights, refs[:blocks])


def place_kernel(blocks, after_attn, weights, *refs):
    served, earlier, (output, result, sems) = refs[:blocks], refs[blocks:-3], refs[-3:]
    segment = lax.axis_index("segment")

    def place(source, micro):
        rows = pl.ds(micro * CAND_LEN, CAND_LEN)
        return pltpu.make_async_copy(source, output.at[rows, :], sems.at[micro])

    last = len(earlier)
    for micro in range(CAND_DEV):
        for step in range(micro, last):

            @pl.when(segment + micro == step)
            def _():
                place(earlier[step], micro).start()

    result[...] = mixed(after_attn, weights, served)
    for micro in range(CAND_DEV):

        @pl.when(segment + micro == last)
        def _():
            place(result, micro).start()

    for micro in range(CAND_DEV):
        place(result, micro).wait()


def combine(after_attn, weights, served, earlier=()):
    rows, width = after_attn.shape
    inputs = [after_attn, weights, *served]
    scratch = []
    out_shape, out_spec = jax.ShapeDtypeStruct((rows, width), BF16), VMEM
    if earlier:
        inputs += in_vmem(*earlier)
        scratch = [pltpu.VMEM((rows, width), BF16), pltpu.SemaphoreType.DMA((CAND_DEV,))]
        out_shape, out_spec = jax.ShapeDtypeStruct((CAND_DEV * rows, width), BF16), HBM
    return pl.pallas_call(
        functools.partial(place_kernel if earlier else combine_kernel, len(served)),
        in_specs=[VMEM] * len(inputs),
        out_specs=out_spec,
        out_shape=out_shape,
        scratch_shapes=scratch,
        compiler_params=pltpu.CompilerParams(vmem_limit_bytes=8 * MIB),
        cost_estimate=pl.CostEstimate(
            flops=4 * weights.size * width,
            bytes_accessed=6 * after_attn.size + 2 * weights.shape[0] * width,
            transcendentals=0,
        ),
        name="combine",
    )(*inputs)


def local(
    states, cand_len, routes, enc_kv, attn_gain, ffn_gain, w_query, w_out, w_router, w_in, w_down
):
    n_segment = lax.axis_size("segment")
    n_expert = lax.axis_size("expert")
    model_width = states.shape[1]
    experts = w_router.shape[2]
    capacity = 2 * ((5 * CAND_LEN + 4 * experts - 1) // (4 * experts))
    core_pairs = [(i, i ^ 1) for i in range(n_expert)]
    same_core = [list(range(core, n_expert, 2)) for core in range(2)]
    blocks = experts if experts <= 4 else 1

    def exchange(parts):
        if blocks > 1:
            return [parts[0]] + [
                lax.ppermute(part, "expert", [(i, i ^ (2 * k)) for i in range(n_expert)])
                for k, part in enumerate(parts[1:], 1)
            ]
        rows = parts[0].reshape(experts, capacity, model_width)
        moved = lax.all_to_all(
            rows, "expert", split_axis=0, concat_axis=0, axis_index_groups=same_core, tiled=True
        )
        return [moved.reshape(parts[0].shape)]

    cached = lax.all_to_all(
        spread(enc_kv, n_expert), ("segment", "expert"), split_axis=0, concat_axis=0, tiled=True
    )
    own = (w_in[0, 0], w_down[0, 0])
    other = tuple(lax.ppermute(mat, "expert", core_pairs) for mat in own)

    queries = project(states, attn_gain, w_query[0])
    step_count = CAND_DEV + n_segment - 1
    earlier = []
    kept = ()
    for step in range(step_count):
        if step == 0:
            sources = (
                cand_len, queries, cached, states, routes[0].T, attn_gain, ffn_gain,
                w_router[0].T, w_query[0], w_out[0], own[0],
            )
        elif step < CAND_DEV:
            sources = (incoming, following)
        else:
            sources = (incoming,)
        marked = step > CAND_DEV
        (after_attn, ffn_input), outgoing, left = attend(
            step, capacity, blocks, marked, sources, kept
        )
        if step == 0:
            *kept, following, own_in = left
            expert_mats = (own_in, own[1], *other)
        weights = gate(step, capacity, blocks, ffn_input, kept[0], kept[2])
        received = exchange(outgoing)
        marks = ()
        if marked:
            pairs = [(i, i + 1) for i in range(0, n_expert, 2)]
            marks = (lax.ppermute(left[0], "expert", pairs),)
        served, expert_mats = expert_rows(received, expert_mats, step, marks)
        served = exchange(served)
        if step + 1 < step_count:
            result = combine(after_attn, weights, served)
            incoming = lax.ppermute(
                result, "segment", [(i, i + 1) for i in range(n_segment - 1)]
            )
            earlier.append(result)
    output = combine(after_attn, weights, served, earlier)
    return output.reshape(1, CAND_DEV * CAND_LEN, model_width)


def solution(mesh):
    return jax.shard_map(
        local,
        mesh=mesh,
        in_specs=(
            P("expert", None),
            P("expert"),
            P("segment", "expert", None),
            P(None, ("segment", "expert"), None),
            P("segment", None),
            P("segment", None),
            P("segment", None, None),
            P("segment", None, None),
            P("segment", None, None),
            P("segment", "expert", None, None),
            P("segment", "expert", None, None),
        ),
        out_specs=P("segment", "expert", None),
        check_vma=False,
    )
```

```python
import functools
import math

import jax
import jax.numpy as jnp
from jax import lax
from jax.experimental import pallas as pl
from jax.experimental.pallas import tpu as pltpu
from jax.sharding import PartitionSpec as P

HEAD_DIM = 128
CAND_LEN = 64
CAND_DEV = 2
HIDDEN_CHUNK = 256
MIB = 1 << 20

EPSILON = 1e-05

VMEM = pl.BlockSpec(memory_space=pltpu.VMEM)
SMEM = pl.BlockSpec(memory_space=pltpu.SMEM)
HBM = pl.BlockSpec(memory_space=pltpu.HBM)
F32 = jnp.float32
BF16 = jnp.bfloat16


def in_hbm(*arrays):
    return [pltpu.with_memory_space_constraint(array, pltpu.HBM) for array in arrays]


def in_vmem(*arrays):
    return [pltpu.with_memory_space_constraint(array, pltpu.VMEM) for array in arrays]


def split(rows, blocks):
    size = rows.shape[0] // blocks
    return [rows[k * size : (k + 1) * size] for k in range(blocks)]


def joined(blocks):
    if len(blocks) == 1:
        return blocks[0][...]
    return jnp.concatenate([block[...].astype(F32) for block in blocks], axis=0).astype(BF16)


def normalize(carried, gain_row):
    average = jnp.mean(carried, axis=-1, keepdims=True)
    centered = carried - average
    variance = jnp.mean(centered * centered, axis=-1, keepdims=True)
    return gain_row * centered * lax.rsqrt(variance + EPSILON)


def dot(left, right, contract=((1,), (0,))):
    return lax.dot_general(left, right, (contract, ((), ())), preferred_element_type=F32)


def spread_kernel(copies_of, enc_kv, blocks):
    for layer in range(enc_kv.shape[0]):
        block = enc_kv[layer : layer + 1, :].reshape(blocks.shape[1:])
        for i in range(copies_of):
            blocks[layer * copies_of + i] = block


def spread(enc_kv, copies_of):
    layers, _, features = enc_kv.shape
    return pl.pallas_call(
        functools.partial(spread_kernel, copies_of),
        in_specs=[VMEM],
        out_specs=VMEM,
        out_shape=jax.ShapeDtypeStruct(
            (layers * copies_of, features // HEAD_DIM, HEAD_DIM), BF16
        ),
        compiler_params=pltpu.CompilerParams(vmem_limit_bytes=8 * MIB),
        name="spread",
    )(*in_hbm(enc_kv.reshape(layers, features)))


def project_kernel(states, gain, w_query, queries, fresh, gain_buf, query_buf, sems):
    fills = (
        (states.at[pl.ds(0, CAND_LEN), :], fresh),
        (gain, gain_buf),
        (w_query, query_buf),
    )
    copies = [pltpu.make_async_copy(*pair, sems.at[i]) for i, pair in enumerate(fills)]
    for copy in copies:
        copy.start()
    copies[0].wait()
    copies[1].wait()
    normed = normalize(fresh[...].astype(F32), gain_buf[...]).astype(BF16)
    copies[2].wait()
    queries[...] = dot(normed, query_buf[...]).astype(BF16)


def project(states, gain, w_query):
    width, head_total = w_query.shape
    return pl.pallas_call(
        project_kernel,
        in_specs=[HBM] * 3,
        out_specs=VMEM,
        out_shape=jax.ShapeDtypeStruct((CAND_LEN, head_total), BF16),
        scratch_shapes=[
            pltpu.VMEM((CAND_LEN, width), BF16),
            pltpu.VMEM((1, width), F32),
            pltpu.VMEM(w_query.shape, BF16),
            pltpu.SemaphoreType.DMA((3,)),
        ],
        compiler_params=pltpu.CompilerParams(vmem_limit_bytes=12 * MIB),
        cost_estimate=pl.CostEstimate(
            flops=2 * CAND_LEN * width * head_total,
            bytes_accessed=2 * width * head_total,
            transcendentals=0,
        ),
        name="project",
    )(*in_hbm(states, gain, w_query))


def block_diagonal(cached, first_head, blocks):
    sources = cached.shape[0]
    blocks[...] = jnp.zeros_like(blocks)
    for head in range(blocks.shape[1] // HEAD_DIM):
        rows = pl.ds(head * sources, sources)
        blocks[rows, pl.ds(head * HEAD_DIM, HEAD_DIM)] = cached[:, first_head + head, :]


def chosen_slots(step, capacity, blocks, routes, experts):
    micro = jnp.clip(step - lax.axis_index("segment"), 0, CAND_DEV - 1)
    route = routes[micro]
    rows = route.shape[1]
    labels = lax.broadcasted_iota(jnp.int32, (experts, rows), 0)
    first, second = route[0:1] == labels, route[1:2] == labels
    place = route
    if blocks > 1:
        place = jnp.where(route < 0, route, route ^ (lax.axis_index("expert") // 2))
    named = jnp.where(first | second, 1.0, 0.0).astype(BF16)
    earlier = lax.broadcasted_iota(jnp.int32, (rows, rows), 0) < lax.broadcasted_iota(
        jnp.int32, (rows, rows), 1
    )
    before = dot(named, jnp.where(earlier, 1.0, 0.0).astype(BF16))
    slots = lax.broadcasted_iota(jnp.int32, (experts * capacity, rows), 0)
    chosen = []
    for mask, row in ((first, 0), (second, 1)):
        slot = jnp.sum(jnp.where(mask, before, 0.0), axis=0, keepdims=True).astype(jnp.int32)
        chosen.append(slots == place[row : row + 1] * capacity + slot)
    return chosen


def gate_kernel(step, capacity, blocks, ffn_input, routes, router, weights):
    experts = router.shape[0]
    micro = jnp.clip(step - lax.axis_index("segment"), 0, CAND_DEV - 1)
    route = routes[micro]
    labels = lax.broadcasted_iota(jnp.int32, (experts, route.shape[1]), 0)
    logits = dot(router[...], ffn_input[...], ((1,), (1,)))
    picked = [
        jnp.sum(jnp.where(route[row : row + 1] == labels, logits, 0.0), axis=0, keepdims=True)
        for row in range(2)
    ]
    gate_first = jax.nn.sigmoid(picked[0] - picked[1])
    gate_second = 1.0 - gate_first
    chosen = chosen_slots(step, capacity, blocks, routes, experts)
    weights[...] = jnp.where(chosen[0], gate_first, 0.0) + jnp.where(chosen[1], gate_second, 0.0)


def gate(step, capacity, blocks, ffn_input, routes, router):
    experts, width = router.shape
    return pl.pallas_call(
        functools.partial(gate_kernel, step, capacity, blocks),
        in_specs=[VMEM] * 3,
        out_specs=VMEM,
        out_shape=jax.ShapeDtypeStruct((experts * capacity, CAND_LEN), F32),
        compiler_params=pltpu.CompilerParams(vmem_limit_bytes=8 * MIB),
        cost_estimate=pl.CostEstimate(
            flops=2 * CAND_LEN * width * 128, bytes_accessed=2 * ffn_input.size, transcendentals=0
        ),
        name="gate",
    )(ffn_input, *in_vmem(routes, router))


def has_candidate(step):
    micro = step - lax.axis_index("segment")
    return (micro >= 0) & (micro < CAND_DEV)


def later_attend_kernel(step, capacity, blocks, *refs):
    @pl.when(has_candidate(step))
    def _():
        attend_kernel(step, capacity, blocks, *refs)


def attend_kernel(step, capacity, blocks, *refs):
    segment = lax.axis_index("segment")
    if step == 0:
        (cand_len, queries_in, cached, states, routes_hbm, attn_gain, ffn_gain, router_hbm,
         query_hbm, out_hbm, expert_hbm), refs = refs[:11], refs[11:]
        after_ref, ffn_ref, *outgoing = refs[: 2 + blocks]
        (routes, gains, router, w_query, w_out, keys, values, following, expert_mat,
         fresh, route_buf, sems) = refs[2 + blocks :]
        fills = (
            (states.at[pl.ds(0, CAND_LEN), :], fresh),
            (ffn_gain, gains.at[1]),
            (out_hbm, w_out),
            (router_hbm, router),
            (routes_hbm, route_buf),
            (attn_gain, gains.at[0]),
            (states.at[pl.ds(CAND_LEN, CAND_LEN), :], following),
            (query_hbm, w_query),
            (expert_hbm, expert_mat),
        )
        copies = [pltpu.make_async_copy(*pair, sems.at[i]) for i, pair in enumerate(fills)]
        for copy in copies:
            copy.start()
        head_count = w_out.shape[0] // HEAD_DIM
        block_diagonal(cached, 0, keys)
        block_diagonal(cached, head_count, values)
        queries = queries_in[...]
        copies[0].wait()
        carried = fresh[...].astype(F32)
        copies[4].wait()
        copies = copies[:4] + copies[5:]
        position = lax.broadcasted_iota(jnp.int32, (1, CAND_LEN), 1)
        for micro in range(CAND_DEV):
            route = route_buf[:, micro * CAND_LEN : (micro + 1) * CAND_LEN]
            routes[micro] = jnp.where(position < cand_len[micro], route, -1)
    else:
        incoming, refs = refs[0], refs[1:]
        current = incoming[...]
        if step < CAND_DEV:
            current, refs = jnp.where(segment == 0, refs[0][...], current), refs[1:]
        (routes, gains, router, w_query, w_out, keys, values, after_ref, ffn_ref), refs = (
            refs[:9], refs[9:]
        )
        outgoing, marks = refs[:blocks], refs[blocks:]
        for mark in marks:
            mark[...] = current[: mark.shape[0], : mark.shape[1]]
        carried = current.astype(F32)
        normed = normalize(carried, gains[0]).astype(BF16)
        queries = dot(normed, w_query[...]).astype(BF16)

    rows = carried.shape[0]
    sources = keys.shape[0] * HEAD_DIM // keys.shape[1]
    scores = dot(keys[...], queries, ((1,), (1,))) * (1.0 / math.sqrt(HEAD_DIM))
    scores = scores.reshape(-1, sources, rows)
    exponent = jnp.exp(scores - jnp.max(scores, axis=1, keepdims=True))
    share = exponent / jnp.sum(exponent, axis=1, keepdims=True)
    share = share.reshape(-1, rows).astype(BF16)
    context = dot(share, values[...], ((0,), (0,))).astype(BF16)
    if step == 0:
        copies[1].wait()
        copies[2].wait()
    after_attn = carried + dot(context, w_out[...])
    after_ref[...] = after_attn
    ffn_input = normalize(after_attn, gains[1]).astype(BF16)

    rows_in_slots = chosen_slots(step, capacity, blocks, routes, router.shape[0])
    select = jnp.where(rows_in_slots[0] | rows_in_slots[1], 1.0, 0.0).astype(BF16)
    buffers = dot(select, ffn_input)
    for buffer, block in zip(split(buffers, blocks), outgoing):
        block[...] = buffer.astype(BF16)
    ffn_ref[...] = ffn_input
    if step == 0:
        for copy in copies[3:]:
            copy.wait()


def attend(step, capacity, blocks, marked, sources, kept):
    if step == 0:
        cand_len, queries, cached, *params = sources
        _, routes, _, _, router_t, w_query, w_out, expert_mat = params
        head_total, width = w_out.shape
        diagonal = (cached.shape[0] * head_total // HEAD_DIM, head_total)
        kept_shapes = [
            pltpu.VMEM((CAND_DEV, 2, CAND_LEN), jnp.int32),
            pltpu.VMEM((2, 1, width), F32),
            *(pltpu.VMEM(array.shape, BF16) for array in (router_t, w_query, w_out)),
            pltpu.VMEM(diagonal, BF16),
            pltpu.VMEM(diagonal, BF16),
            pltpu.VMEM((CAND_LEN, width), BF16),
            pltpu.VMEM(expert_mat.shape, BF16),
        ]
        inputs = [*in_hbm(cand_len), queries, cached, *in_hbm(*params)]
        specs = [SMEM, VMEM, VMEM] + [HBM] * len(params)
        scratch = [
            pltpu.VMEM((CAND_LEN, width), BF16),
            pltpu.VMEM(routes.shape, jnp.int32),
            pltpu.SemaphoreType.DMA((9,)),
        ]
    else:
        _, _, router_t, _, w_out, *_ = kept
        head_total, width = w_out.shape
        kept_shapes = [jax.ShapeDtypeStruct((16, 128), BF16)] if marked else []
        scratch = []
        inputs = [*sources, *in_vmem(*kept)]
        specs = [VMEM] * len(inputs)
    slot_count = router_t.shape[0] * capacity
    outs = pl.pallas_call(
        functools.partial(
            later_attend_kernel if step else attend_kernel, step, capacity, blocks
        ),
        in_specs=specs,
        out_specs=[VMEM] * (2 + blocks + len(kept_shapes)),
        out_shape=[
            jax.ShapeDtypeStruct((CAND_LEN, width), F32),
            jax.ShapeDtypeStruct((CAND_LEN, width), BF16),
            *[jax.ShapeDtypeStruct((slot_count // blocks, width), BF16)] * blocks,
            *kept_shapes,
        ],
        scratch_shapes=scratch,
        compiler_params=pltpu.CompilerParams(vmem_limit_bytes=12 * MIB),
        cost_estimate=pl.CostEstimate(
            flops=6 * CAND_LEN * width * head_total,
            bytes_accessed=4 * width * head_total + 8 * CAND_LEN * width,
            transcendentals=0,
        ),
        name="attend",
    )(*inputs)
    return outs[:2], outs[2 : 2 + blocks], outs[2 + blocks :]


def expert_kernel(blocks, stream, mark_count, *refs):
    refs = refs[mark_count:]
    rows_in, refs = refs[:blocks], refs[blocks:]
    own_in, refs = refs[0], refs[1:]
    if stream:
        sources, served, refs = refs[:3], refs[3 : 3 + blocks], refs[3 + blocks :]
        (own_down, other_in, other_down), (rows, own_hidden, other_hidden, sems) = refs[:3], refs[3:]
    else:
        (own_down, other_in, other_down), refs = refs[:3], refs[3:]
        served, (rows, own_hidden, other_hidden) = refs[:blocks], refs[blocks:]
    chunks = [pl.ds(start, HIDDEN_CHUNK) for start in range(0, own_in.shape[1], HIDDEN_CHUNK)]

    def fill(source, mat, i):
        lanes = chunks[i]
        return pltpu.make_async_copy(
            sources[source].at[:, lanes], mat.at[:, lanes], sems.at[source, i]
        )

    if stream:
        for i in range(len(chunks)):
            fill(1, other_in, i).start()
        for i in range(len(chunks)):
            fill(0, own_down, i).start()
            fill(2, other_down, i).start()
    rows[...] = joined(rows_in)
    for units in chunks:
        own_hidden[:, units] = jnp.maximum(dot(rows[...], own_in[:, units]), 0.0).astype(BF16)
    for i, units in enumerate(chunks):
        if stream:
            fill(1, other_in, i).wait()
        other_hidden[:, units] = jnp.maximum(dot(rows[...], other_in[:, units]), 0.0).astype(BF16)
    for i, lanes in enumerate(chunks):
        if stream:
            fill(0, own_down, i).wait()
        out = dot(own_hidden[...], own_down[:, lanes])
        if stream:
            fill(2, other_down, i).wait()
        out = out + dot(other_hidden[...], other_down[:, lanes])
        for part, block in zip(split(out, blocks), served):
            block[:, lanes] = part.astype(BF16)


def expert_rows(rows_in, mats, step, marks=()):
    blocks, stream = len(rows_in), step == 0
    width = rows_in[0].shape[1]
    count = blocks * rows_in[0].shape[0]
    units = mats[0].shape[1]
    scratch = [
        pltpu.VMEM((count, width), BF16),
        pltpu.VMEM((count, units), BF16),
        pltpu.VMEM((count, units), BF16),
    ]
    out_shape = [jax.ShapeDtypeStruct(rows.shape, BF16) for rows in rows_in]
    if stream:
        scratch.append(pltpu.SemaphoreType.DMA((3, units // HIDDEN_CHUNK)))
        out_shape += [pltpu.VMEM(mat.shape, BF16) for mat in mats[1:]]
    outs = pl.pallas_call(
        functools.partial(expert_kernel, blocks, stream, len(marks)),
        in_specs=[VMEM] * (len(marks) + blocks + 1) + [HBM if stream else VMEM] * 3,
        out_specs=[VMEM] * len(out_shape),
        out_shape=out_shape,
        scratch_shapes=scratch,
        compiler_params=pltpu.CompilerParams(vmem_limit_bytes=12 * MIB),
        cost_estimate=pl.CostEstimate(
            flops=8 * count * width * units,
            bytes_accessed=8 * width * units + 4 * count * width,
            transcendentals=0,
        ),
        name="experts",
    )(*marks, *rows_in, *in_vmem(mats[0]), *(in_hbm if stream else in_vmem)(*mats[1:]))
    return outs[:blocks], ((mats[0], *outs[blocks:]) if stream else mats)


def mixed(after_attn, weights, blocks):
    gates = weights[...]
    coarse = gates.astype(BF16)
    fine = (gates - coarse.astype(F32)).astype(BF16)
    rows = joined(blocks)
    mixture = dot(coarse, rows, ((0,), (0,))) + dot(fine, rows, ((0,), (0,)))
    return (after_attn[...] + mixture).astype(BF16)


def combine_kernel(blocks, after_attn, weights, *refs):
    result = refs[blocks]
    result[...] = mixed(after_attn, weights, refs[:blocks])


def place_kernel(blocks, after_attn, weights, *refs):
    served, earlier, (output, result, sems) = refs[:blocks], refs[blocks:-3], refs[-3:]
    segment = lax.axis_index("segment")

    def place(source, micro):
        rows = pl.ds(micro * CAND_LEN, CAND_LEN)
        return pltpu.make_async_copy(source, output.at[rows, :], sems.at[micro])

    last = len(earlier)
    for micro in range(CAND_DEV):
        for step in range(micro, last):

            @pl.when(segment + micro == step)
            def _():
                place(earlier[step], micro).start()

    result[...] = mixed(after_attn, weights, served)
    for micro in range(CAND_DEV):

        @pl.when(segment + micro == last)
        def _():
            place(result, micro).start()

    for micro in range(CAND_DEV):
        place(result, micro).wait()


def combine(after_attn, weights, served, earlier=()):
    rows, width = after_attn.shape
    inputs = [after_attn, weights, *served]
    scratch = []
    out_shape, out_spec = jax.ShapeDtypeStruct((rows, width), BF16), VMEM
    if earlier:
        inputs += in_vmem(*earlier)
        scratch = [pltpu.VMEM((rows, width), BF16), pltpu.SemaphoreType.DMA((CAND_DEV,))]
        out_shape, out_spec = jax.ShapeDtypeStruct((CAND_DEV * rows, width), BF16), HBM
    return pl.pallas_call(
        functools.partial(place_kernel if earlier else combine_kernel, len(served)),
        in_specs=[VMEM] * len(inputs),
        out_specs=out_spec,
        out_shape=out_shape,
        scratch_shapes=scratch,
        compiler_params=pltpu.CompilerParams(vmem_limit_bytes=8 * MIB),
        cost_estimate=pl.CostEstimate(
            flops=4 * weights.size * width,
            bytes_accessed=6 * after_attn.size + 2 * weights.shape[0] * width,
            transcendentals=0,
        ),
        name="combine",
    )(*inputs)


def local(
    states, cand_len, routes, enc_kv, attn_gain, ffn_gain, w_query, w_out, w_router, w_in, w_down
):
    n_segment = lax.axis_size("segment")
    n_expert = lax.axis_size("expert")
    model_width = states.shape[1]
    experts = w_router.shape[2]
    capacity = 2 * ((5 * CAND_LEN + 4 * experts - 1) // (4 * experts))
    core_pairs = [(i, i ^ 1) for i in range(n_expert)]
    same_core = [list(range(core, n_expert, 2)) for core in range(2)]
    blocks = experts if experts <= 4 else 1

    def exchange(parts):
        if blocks > 1:
            return [parts[0]] + [
                lax.ppermute(part, "expert", [(i, i ^ (2 * k)) for i in range(n_expert)])
                for k, part in enumerate(parts[1:], 1)
            ]
        rows = parts[0].reshape(experts, capacity, model_width)
        moved = lax.all_to_all(
            rows, "expert", split_axis=0, concat_axis=0, axis_index_groups=same_core, tiled=True
        )
        return [moved.reshape(parts[0].shape)]

    cached = lax.all_to_all(
        spread(enc_kv, n_expert), ("segment", "expert"), split_axis=0, concat_axis=0, tiled=True
    )
    own = (w_in[0, 0], w_down[0, 0])
    other = tuple(lax.ppermute(mat, "expert", core_pairs) for mat in own)

    queries = project(states, attn_gain, w_query[0])
    step_count = CAND_DEV + n_segment - 1
    earlier = []
    kept = ()
    for step in range(step_count):
        if step == 0:
            sources = (
                cand_len, queries, cached, states, routes[0].T, attn_gain, ffn_gain,
                w_router[0].T, w_query[0], w_out[0], own[0],
            )
        elif step < CAND_DEV:
            sources = (incoming, following)
        else:
            sources = (incoming,)
        marked = step > CAND_DEV
        (after_attn, ffn_input), outgoing, left = attend(
            step, capacity, blocks, marked, sources, kept
        )
        if step == 0:
            *kept, following, own_in = left
            expert_mats = (own_in, own[1], *other)
        weights = gate(step, capacity, blocks, ffn_input, kept[0], kept[2])
        received = exchange(outgoing)
        marks = ()
        if marked:
            pairs = [(i, i + 1) for i in range(0, n_expert, 2)]
            marks = (lax.ppermute(left[0], "expert", pairs),)
        served, expert_mats = expert_rows(received, expert_mats, step, marks)
        served = exchange(served)
        if step + 1 < step_count:
            result = combine(after_attn, weights, served)
            incoming = lax.ppermute(
                result, "segment", [(i, i + 1) for i in range(n_segment - 1)]
            )
            earlier.append(result)
    output = combine(after_attn, weights, served, earlier)
    return output.reshape(1, CAND_DEV * CAND_LEN, model_width)


def solution(mesh):
    return jax.shard_map(
        local,
        mesh=mesh,
        in_specs=(
            P("expert", None),
            P("expert"),
            P("segment", "expert", None),
            P(None, ("segment", "expert"), None),
            P("segment", None),
            P("segment", None),
            P("segment", None, None),
            P("segment", None, None),
            P("segment", None, None),
            P("segment", "expert", None, None),
            P("segment", "expert", None, None),
        ),
        out_specs=P("segment", "expert", None),
        check_vma=False,
    )
```

```python
import functools
import math

import jax
import jax.numpy as jnp
from jax import lax
from jax.experimental import pallas as pl
from jax.experimental.pallas import tpu as pltpu
from jax.sharding import PartitionSpec as P

HEAD_DIM = 128
CAND_LEN = 64
CAND_DEV = 2
HIDDEN_CHUNK = 512
STREAM_CHUNK = 1024
MIB = 1 << 20

EPSILON = 1e-05

VMEM = pl.BlockSpec(memory_space=pltpu.VMEM)
SMEM = pl.BlockSpec(memory_space=pltpu.SMEM)
HBM = pl.BlockSpec(memory_space=pltpu.HBM)
F32 = jnp.float32
BF16 = jnp.bfloat16


def in_hbm(*arrays):
    return [pltpu.with_memory_space_constraint(array, pltpu.HBM) for array in arrays]


def in_vmem(*arrays):
    return [pltpu.with_memory_space_constraint(array, pltpu.VMEM) for array in arrays]


def split(rows, blocks):
    size = rows.shape[0] // blocks
    return [rows[k * size : (k + 1) * size] for k in range(blocks)]


def joined(blocks):
    if len(blocks) == 1:
        return blocks[0][...]
    return jnp.concatenate([block[...].astype(F32) for block in blocks], axis=0).astype(BF16)


def normalize(carried, gain_row):
    average = jnp.mean(carried, axis=-1, keepdims=True)
    centered = carried - average
    variance = jnp.mean(centered * centered, axis=-1, keepdims=True)
    return gain_row * centered * lax.rsqrt(variance + EPSILON)


def dot(left, right, contract=((1,), (0,))):
    return lax.dot_general(left, right, (contract, ((), ())), preferred_element_type=F32)


def spread_kernel(copies_of, enc_kv, blocks):
    for layer in range(enc_kv.shape[0]):
        block = enc_kv[layer : layer + 1, :].reshape(blocks.shape[1:])
        for i in range(copies_of):
            blocks[layer * copies_of + i] = block


def spread(enc_kv, copies_of):
    layers, _, features = enc_kv.shape
    return pl.pallas_call(
        functools.partial(spread_kernel, copies_of),
        in_specs=[VMEM],
        out_specs=VMEM,
        out_shape=jax.ShapeDtypeStruct(
            (layers * copies_of, features // HEAD_DIM, HEAD_DIM), BF16
        ),
        compiler_params=pltpu.CompilerParams(vmem_limit_bytes=8 * MIB),
        name="spread",
    )(*in_hbm(enc_kv.reshape(layers, features)))


def project_kernel(states, gain, w_query, queries, fresh, gain_buf, query_buf, sems):
    fills = (
        (states.at[pl.ds(0, CAND_LEN), :], fresh),
        (gain, gain_buf),
        (w_query, query_buf),
    )
    copies = [pltpu.make_async_copy(*pair, sems.at[i]) for i, pair in enumerate(fills)]
    for copy in copies:
        copy.start()
    copies[0].wait()
    copies[1].wait()
    normed = normalize(fresh[...].astype(F32), gain_buf[...]).astype(BF16)
    copies[2].wait()
    queries[...] = dot(normed, query_buf[...]).astype(BF16)


def project(states, gain, w_query):
    width, head_total = w_query.shape
    return pl.pallas_call(
        project_kernel,
        in_specs=[HBM] * 3,
        out_specs=VMEM,
        out_shape=jax.ShapeDtypeStruct((CAND_LEN, head_total), BF16),
        scratch_shapes=[
            pltpu.VMEM((CAND_LEN, width), BF16),
            pltpu.VMEM((1, width), F32),
            pltpu.VMEM(w_query.shape, BF16),
            pltpu.SemaphoreType.DMA((3,)),
        ],
        compiler_params=pltpu.CompilerParams(vmem_limit_bytes=12 * MIB),
        cost_estimate=pl.CostEstimate(
            flops=2 * CAND_LEN * width * head_total,
            bytes_accessed=2 * width * head_total,
            transcendentals=0,
        ),
        name="project",
    )(*in_hbm(states, gain, w_query))


def block_diagonal(cached, first_head, blocks):
    sources = cached.shape[0]
    blocks[...] = jnp.zeros_like(blocks)
    for head in range(blocks.shape[1] // HEAD_DIM):
        rows = pl.ds(head * sources, sources)
        blocks[rows, pl.ds(head * HEAD_DIM, HEAD_DIM)] = cached[:, first_head + head, :]


def chosen_slots(step, capacity, blocks, routes, experts):
    micro = jnp.clip(step - lax.axis_index("segment"), 0, CAND_DEV - 1)
    route = routes[micro]
    rows = route.shape[1]
    labels = lax.broadcasted_iota(jnp.int32, (experts, rows), 0)
    first, second = route[0:1] == labels, route[1:2] == labels
    place = route
    if blocks > 1:
        place = jnp.where(route < 0, route, route ^ (lax.axis_index("expert") // 2))
    named = jnp.where(first | second, 1.0, 0.0).astype(BF16)
    earlier = lax.broadcasted_iota(jnp.int32, (rows, rows), 0) < lax.broadcasted_iota(
        jnp.int32, (rows, rows), 1
    )
    before = dot(named, jnp.where(earlier, 1.0, 0.0).astype(BF16))
    slots = lax.broadcasted_iota(jnp.int32, (experts * capacity, rows), 0)
    chosen = []
    for mask, row in ((first, 0), (second, 1)):
        slot = jnp.sum(jnp.where(mask, before, 0.0), axis=0, keepdims=True).astype(jnp.int32)
        chosen.append(slots == place[row : row + 1] * capacity + slot)
    return chosen


def gate_kernel(step, capacity, blocks, ffn_input, routes, router, weights):
    experts = router.shape[0]
    micro = jnp.clip(step - lax.axis_index("segment"), 0, CAND_DEV - 1)
    route = routes[micro]
    labels = lax.broadcasted_iota(jnp.int32, (experts, route.shape[1]), 0)
    logits = dot(router[...], ffn_input[...], ((1,), (1,)))
    picked = [
        jnp.sum(jnp.where(route[row : row + 1] == labels, logits, 0.0), axis=0, keepdims=True)
        for row in range(2)
    ]
    gate_first = jax.nn.sigmoid(picked[0] - picked[1])
    gate_second = 1.0 - gate_first
    chosen = chosen_slots(step, capacity, blocks, routes, experts)
    weights[...] = jnp.where(chosen[0], gate_first, 0.0) + jnp.where(chosen[1], gate_second, 0.0)


def gate(step, capacity, blocks, ffn_input, routes, router):
    experts, width = router.shape
    return pl.pallas_call(
        functools.partial(gate_kernel, step, capacity, blocks),
        in_specs=[VMEM] * 3,
        out_specs=VMEM,
        out_shape=jax.ShapeDtypeStruct((experts * capacity, CAND_LEN), F32),
        compiler_params=pltpu.CompilerParams(vmem_limit_bytes=8 * MIB),
        cost_estimate=pl.CostEstimate(
            flops=2 * CAND_LEN * width * 128, bytes_accessed=2 * ffn_input.size, transcendentals=0
        ),
        name="gate",
    )(ffn_input, *in_vmem(routes, router))


def has_candidate(step):
    micro = step - lax.axis_index("segment")
    return (micro >= 0) & (micro < CAND_DEV)


def later_attend_kernel(step, capacity, blocks, *refs):
    @pl.when(has_candidate(step))
    def _():
        attend_kernel(step, capacity, blocks, *refs)


def attend_kernel(step, capacity, blocks, *refs):
    segment = lax.axis_index("segment")
    if step == 0:
        (cand_len, queries_in, cached, states, routes_hbm, attn_gain, ffn_gain, router_hbm,
         query_hbm, out_hbm, expert_hbm), refs = refs[:11], refs[11:]
        after_ref, ffn_ref, *outgoing = refs[: 2 + blocks]
        (routes, gains, router, w_query, w_out, keys, values, following, expert_mat,
         fresh, route_buf, sems) = refs[2 + blocks :]
        fills = (
            (states.at[pl.ds(0, CAND_LEN), :], fresh),
            (ffn_gain, gains.at[1]),
            (out_hbm, w_out),
            (router_hbm, router),
            (routes_hbm, route_buf),
            (attn_gain, gains.at[0]),
            (states.at[pl.ds(CAND_LEN, CAND_LEN), :], following),
            (query_hbm, w_query),
            (expert_hbm, expert_mat),
        )
        copies = [pltpu.make_async_copy(*pair, sems.at[i]) for i, pair in enumerate(fills)]
        for copy in copies:
            copy.start()
        head_count = w_out.shape[0] // HEAD_DIM
        block_diagonal(cached, 0, keys)
        block_diagonal(cached, head_count, values)
        queries = queries_in[...]
        copies[0].wait()
        carried = fresh[...].astype(F32)
        copies[4].wait()
        copies = copies[:4] + copies[5:]
        position = lax.broadcasted_iota(jnp.int32, (1, CAND_LEN), 1)
        for micro in range(CAND_DEV):
            route = route_buf[:, micro * CAND_LEN : (micro + 1) * CAND_LEN]
            routes[micro] = jnp.where(position < cand_len[micro], route, -1)
    else:
        incoming, refs = refs[0], refs[1:]
        current = incoming[...]
        if step < CAND_DEV:
            current, refs = jnp.where(segment == 0, refs[0][...], current), refs[1:]
        (routes, gains, router, w_query, w_out, keys, values, after_ref, ffn_ref), refs = (
            refs[:9], refs[9:]
        )
        outgoing, marks = refs[:blocks], refs[blocks:]
        for mark in marks:
            mark[...] = current[: mark.shape[0], : mark.shape[1]]
        carried = current.astype(F32)
        normed = normalize(carried, gains[0]).astype(BF16)
        queries = dot(normed, w_query[...]).astype(BF16)

    rows = carried.shape[0]
    sources = keys.shape[0] * HEAD_DIM // keys.shape[1]
    scores = dot(keys[...], queries, ((1,), (1,))) * (1.0 / math.sqrt(HEAD_DIM))
    scores = scores.reshape(-1, sources, rows)
    exponent = jnp.exp(scores - jnp.max(scores, axis=1, keepdims=True))
    share = exponent / jnp.sum(exponent, axis=1, keepdims=True)
    share = share.reshape(-1, rows).astype(BF16)
    context = dot(share, values[...], ((0,), (0,))).astype(BF16)
    if step == 0:
        copies[1].wait()
        copies[2].wait()
    after_attn = carried + dot(context, w_out[...])
    after_ref[...] = after_attn
    ffn_input = normalize(after_attn, gains[1]).astype(BF16)

    rows_in_slots = chosen_slots(step, capacity, blocks, routes, router.shape[0])
    select = jnp.where(rows_in_slots[0] | rows_in_slots[1], 1.0, 0.0).astype(BF16)
    buffers = dot(select, ffn_input)
    for buffer, block in zip(split(buffers, blocks), outgoing):
        block[...] = buffer.astype(BF16)
    ffn_ref[...] = ffn_input
    if step == 0:
        for copy in copies[3:]:
            copy.wait()


def attend(step, capacity, blocks, marked, sources, kept):
    if step == 0:
        cand_len, queries, cached, *params = sources
        _, routes, _, _, router_t, w_query, w_out, expert_mat = params
        head_total, width = w_out.shape
        diagonal = (cached.shape[0] * head_total // HEAD_DIM, head_total)
        kept_shapes = [
            pltpu.VMEM((CAND_DEV, 2, CAND_LEN), jnp.int32),
            pltpu.VMEM((2, 1, width), F32),
            *(pltpu.VMEM(array.shape, BF16) for array in (router_t, w_query, w_out)),
            pltpu.VMEM(diagonal, BF16),
            pltpu.VMEM(diagonal, BF16),
            pltpu.VMEM((CAND_LEN, width), BF16),
            pltpu.VMEM(expert_mat.shape, BF16),
        ]
        inputs = [*in_hbm(cand_len), queries, cached, *in_hbm(*params)]
        specs = [SMEM, VMEM, VMEM] + [HBM] * len(params)
        scratch = [
            pltpu.VMEM((CAND_LEN, width), BF16),
            pltpu.VMEM(routes.shape, jnp.int32),
            pltpu.SemaphoreType.DMA((9,)),
        ]
    else:
        _, _, router_t, _, w_out, *_ = kept
        head_total, width = w_out.shape
        kept_shapes = [jax.ShapeDtypeStruct((16, 128), BF16)] if marked else []
        scratch = []
        inputs = [*sources, *in_vmem(*kept)]
        specs = [VMEM] * len(inputs)
    slot_count = router_t.shape[0] * capacity
    outs = pl.pallas_call(
        functools.partial(
            later_attend_kernel if step else attend_kernel, step, capacity, blocks
        ),
        in_specs=specs,
        out_specs=[VMEM] * (2 + blocks + len(kept_shapes)),
        out_shape=[
            jax.ShapeDtypeStruct((CAND_LEN, width), F32),
            jax.ShapeDtypeStruct((CAND_LEN, width), BF16),
            *[jax.ShapeDtypeStruct((slot_count // blocks, width), BF16)] * blocks,
            *kept_shapes,
        ],
        scratch_shapes=scratch,
        compiler_params=pltpu.CompilerParams(vmem_limit_bytes=12 * MIB),
        cost_estimate=pl.CostEstimate(
            flops=6 * CAND_LEN * width * head_total,
            bytes_accessed=4 * width * head_total + 8 * CAND_LEN * width,
            transcendentals=0,
        ),
        name="attend",
    )(*inputs)
    return outs[:2], outs[2 : 2 + blocks], outs[2 + blocks :]


def expert_kernel(blocks, stream, mark_count, *refs):
    refs = refs[mark_count:]
    rows_in, refs = refs[:blocks], refs[blocks:]
    own_in, refs = refs[0], refs[1:]
    if stream:
        sources, served, refs = refs[:3], refs[3 : 3 + blocks], refs[3 + blocks :]
        (own_down, other_in, other_down), refs = refs[:3], refs[3:]
        rows, own_hidden, other_hidden, partial, sems = refs
    else:
        (own_down, other_in, other_down), refs = refs[:3], refs[3:]
        served, (rows, own_hidden, other_hidden) = refs[:blocks], refs[blocks:]
    size = STREAM_CHUNK if stream else HIDDEN_CHUNK
    chunks = [pl.ds(start, size) for start in range(0, own_in.shape[1], size)]

    def fill(source, mat):
        copies = [
            pltpu.make_async_copy(
                sources[source].at[:, lanes], mat.at[:, lanes], sems.at[source, i]
            )
            for i, lanes in enumerate(chunks)
        ]
        for copy in copies:
            copy.start()
        return copies

    def hidden_of(mat, units):
        return jnp.maximum(dot(rows[...], mat[:, units]), 0.0).astype(BF16)

    def serve(out, lanes):
        for part, block in zip(split(out, blocks), served):
            block[:, lanes] = part.astype(BF16)

    if not stream:
        rows[...] = joined(rows_in)
        for units in chunks:
            own_hidden[:, units] = hidden_of(own_in, units)
            other_hidden[:, units] = hidden_of(other_in, units)
        for lanes in chunks:
            out = dot(own_hidden[...], own_down[:, lanes])
            serve(out + dot(other_hidden[...], other_down[:, lanes]), lanes)
        return

    own_down_copies = fill(0, own_down)
    other_in_copies = fill(1, other_in)
    other_down_copies = fill(2, other_down)
    rows[...] = joined(rows_in)
    for units in chunks:
        own_hidden[:, units] = hidden_of(own_in, units)
    for lanes, copy in zip(chunks, own_down_copies):
        copy.wait()
        partial[:, lanes] = dot(own_hidden[...], own_down[:, lanes])
    for units, copy in zip(chunks, other_in_copies):
        copy.wait()
        other_hidden[:, units] = hidden_of(other_in, units)
    for lanes, copy in zip(chunks, other_down_copies):
        copy.wait()
        serve(partial[:, lanes] + dot(other_hidden[...], other_down[:, lanes]), lanes)


def expert_rows(rows_in, mats, step, marks=()):
    blocks, stream = len(rows_in), step == 0
    width = rows_in[0].shape[1]
    count = blocks * rows_in[0].shape[0]
    units = mats[0].shape[1]
    scratch = [
        pltpu.VMEM((count, width), BF16),
        pltpu.VMEM((count, units), BF16),
        pltpu.VMEM((count, units), BF16),
    ]
    out_shape = [jax.ShapeDtypeStruct(rows.shape, BF16) for rows in rows_in]
    if stream:
        scratch += [
            pltpu.VMEM((count, width), F32),
            pltpu.SemaphoreType.DMA((3, units // STREAM_CHUNK)),
        ]
        out_shape += [pltpu.VMEM(mat.shape, BF16) for mat in mats[1:]]
    outs = pl.pallas_call(
        functools.partial(expert_kernel, blocks, stream, len(marks)),
        in_specs=[VMEM] * (len(marks) + blocks + 1) + [HBM if stream else VMEM] * 3,
        out_specs=[VMEM] * len(out_shape),
        out_shape=out_shape,
        scratch_shapes=scratch,
        compiler_params=pltpu.CompilerParams(vmem_limit_bytes=12 * MIB),
        cost_estimate=pl.CostEstimate(
            flops=8 * count * width * units,
            bytes_accessed=8 * width * units + 4 * count * width,
            transcendentals=0,
        ),
        name="experts",
    )(*marks, *rows_in, *in_vmem(mats[0]), *(in_hbm if stream else in_vmem)(*mats[1:]))
    return outs[:blocks], ((mats[0], *outs[blocks:]) if stream else mats)


def mixed(after_attn, weights, blocks):
    gates = weights[...]
    coarse = gates.astype(BF16)
    fine = (gates - coarse.astype(F32)).astype(BF16)
    rows = joined(blocks)
    mixture = dot(coarse, rows, ((0,), (0,))) + dot(fine, rows, ((0,), (0,)))
    return (after_attn[...] + mixture).astype(BF16)


def combine_kernel(blocks, after_attn, weights, *refs):
    result = refs[blocks]
    result[...] = mixed(after_attn, weights, refs[:blocks])


def place_kernel(blocks, after_attn, weights, *refs):
    served, earlier, (output, result, sems) = refs[:blocks], refs[blocks:-3], refs[-3:]
    segment = lax.axis_index("segment")

    def place(source, micro):
        rows = pl.ds(micro * CAND_LEN, CAND_LEN)
        return pltpu.make_async_copy(source, output.at[rows, :], sems.at[micro])

    last = len(earlier)
    for micro in range(CAND_DEV):
        for step in range(micro, last):

            @pl.when(segment + micro == step)
            def _():
                place(earlier[step], micro).start()

    result[...] = mixed(after_attn, weights, served)
    for micro in range(CAND_DEV):

        @pl.when(segment + micro == last)
        def _():
            place(result, micro).start()

    for micro in range(CAND_DEV):
        place(result, micro).wait()


def combine(after_attn, weights, served, earlier=()):
    rows, width = after_attn.shape
    inputs = [after_attn, weights, *served]
    scratch = []
    out_shape, out_spec = jax.ShapeDtypeStruct((rows, width), BF16), VMEM
    if earlier:
        inputs += in_vmem(*earlier)
        scratch = [pltpu.VMEM((rows, width), BF16), pltpu.SemaphoreType.DMA((CAND_DEV,))]
        out_shape, out_spec = jax.ShapeDtypeStruct((CAND_DEV * rows, width), BF16), HBM
    return pl.pallas_call(
        functools.partial(place_kernel if earlier else combine_kernel, len(served)),
        in_specs=[VMEM] * len(inputs),
        out_specs=out_spec,
        out_shape=out_shape,
        scratch_shapes=scratch,
        compiler_params=pltpu.CompilerParams(vmem_limit_bytes=8 * MIB),
        cost_estimate=pl.CostEstimate(
            flops=4 * weights.size * width,
            bytes_accessed=6 * after_attn.size + 2 * weights.shape[0] * width,
            transcendentals=0,
        ),
        name="combine",
    )(*inputs)


def local(
    states, cand_len, routes, enc_kv, attn_gain, ffn_gain, w_query, w_out, w_router, w_in, w_down
):
    n_segment = lax.axis_size("segment")
    n_expert = lax.axis_size("expert")
    model_width = states.shape[1]
    experts = w_router.shape[2]
    capacity = 2 * ((5 * CAND_LEN + 4 * experts - 1) // (4 * experts))
    core_pairs = [(i, i ^ 1) for i in range(n_expert)]
    same_core = [list(range(core, n_expert, 2)) for core in range(2)]
    blocks = experts if experts <= 4 else 1

    def exchange(parts):
        if blocks > 1:
            return [parts[0]] + [
                lax.ppermute(part, "expert", [(i, i ^ (2 * k)) for i in range(n_expert)])
                for k, part in enumerate(parts[1:], 1)
            ]
        rows = parts[0].reshape(experts, capacity, model_width)
        moved = lax.all_to_all(
            rows, "expert", split_axis=0, concat_axis=0, axis_index_groups=same_core, tiled=True
        )
        return [moved.reshape(parts[0].shape)]

    cached = lax.all_to_all(
        spread(enc_kv, n_expert), ("segment", "expert"), split_axis=0, concat_axis=0, tiled=True
    )
    own = (w_in[0, 0], w_down[0, 0])
    other = tuple(lax.ppermute(mat, "expert", core_pairs) for mat in own)

    queries = project(states, attn_gain, w_query[0])
    step_count = CAND_DEV + n_segment - 1
    earlier = []
    kept = ()
    for step in range(step_count):
        if step == 0:
            sources = (
                cand_len, queries, cached, states, routes[0].T, attn_gain, ffn_gain,
                w_router[0].T, w_query[0], w_out[0], own[0],
            )
        elif step < CAND_DEV:
            sources = (incoming, following)
        else:
            sources = (incoming,)
        marked = step > CAND_DEV
        (after_attn, ffn_input), outgoing, left = attend(
            step, capacity, blocks, marked, sources, kept
        )
        if step == 0:
            *kept, following, own_in = left
            expert_mats = (own_in, own[1], *other)
        weights = gate(step, capacity, blocks, ffn_input, kept[0], kept[2])
        received = exchange(outgoing)
        marks = ()
        if marked:
            pairs = [(i, i + 1) for i in range(0, n_expert, 2)]
            marks = (lax.ppermute(left[0], "expert", pairs),)
        served, expert_mats = expert_rows(received, expert_mats, step, marks)
        served = exchange(served)
        if step + 1 < step_count:
            result = combine(after_attn, weights, served)
            incoming = lax.ppermute(
                result, "segment", [(i, i + 1) for i in range(n_segment - 1)]
            )
            earlier.append(result)
    output = combine(after_attn, weights, served, earlier)
    return output.reshape(1, CAND_DEV * CAND_LEN, model_width)


def solution(mesh):
    return jax.shard_map(
        local,
        mesh=mesh,
        in_specs=(
            P("expert", None),
            P("expert"),
            P("segment", "expert", None),
            P(None, ("segment", "expert"), None),
            P("segment", None),
            P("segment", None),
            P("segment", None, None),
            P("segment", None, None),
            P("segment", None, None),
            P("segment", "expert", None, None),
            P("segment", "expert", None, None),
        ),
        out_specs=P("segment", "expert", None),
        check_vma=False,
    )
```

```python
import functools
import math

import jax
import jax.numpy as jnp
from jax import lax
from jax.experimental import pallas as pl
from jax.experimental.pallas import tpu as pltpu
from jax.sharding import PartitionSpec as P

HEAD_DIM = 128
CAND_LEN = 64
CAND_DEV = 2
HIDDEN_CHUNK = 512
STREAM_CHUNK = 1024
MIB = 1 << 20

EPSILON = 1e-05

VMEM = pl.BlockSpec(memory_space=pltpu.VMEM)
SMEM = pl.BlockSpec(memory_space=pltpu.SMEM)
HBM = pl.BlockSpec(memory_space=pltpu.HBM)
F32 = jnp.float32
BF16 = jnp.bfloat16


def in_hbm(*arrays):
    return [pltpu.with_memory_space_constraint(array, pltpu.HBM) for array in arrays]


def in_vmem(*arrays):
    return [pltpu.with_memory_space_constraint(array, pltpu.VMEM) for array in arrays]


def split(rows, blocks):
    size = rows.shape[0] // blocks
    return [rows[k * size : (k + 1) * size] for k in range(blocks)]


def joined(blocks):
    if len(blocks) == 1:
        return blocks[0][...]
    return jnp.concatenate([block[...].astype(F32) for block in blocks], axis=0).astype(BF16)


def normalize(carried, gain_row):
    average = jnp.mean(carried, axis=-1, keepdims=True)
    centered = carried - average
    variance = jnp.mean(centered * centered, axis=-1, keepdims=True)
    return gain_row * centered * lax.rsqrt(variance + EPSILON)


def dot(left, right, contract=((1,), (0,))):
    return lax.dot_general(left, right, (contract, ((), ())), preferred_element_type=F32)


def spread_kernel(copies_of, enc_kv, blocks):
    for layer in range(enc_kv.shape[0]):
        block = enc_kv[layer : layer + 1, :].reshape(blocks.shape[1:])
        for i in range(copies_of):
            blocks[layer * copies_of + i] = block


def spread(enc_kv, copies_of):
    layers, _, features = enc_kv.shape
    return pl.pallas_call(
        functools.partial(spread_kernel, copies_of),
        in_specs=[VMEM],
        out_specs=VMEM,
        out_shape=jax.ShapeDtypeStruct(
            (layers * copies_of, features // HEAD_DIM, HEAD_DIM), BF16
        ),
        compiler_params=pltpu.CompilerParams(vmem_limit_bytes=8 * MIB),
        name="spread",
    )(*in_hbm(enc_kv.reshape(layers, features)))


def project_kernel(states, gain, w_query, queries, fresh, gain_buf, query_buf, sems):
    fills = (
        (states.at[pl.ds(0, CAND_LEN), :], fresh),
        (gain, gain_buf),
        (w_query, query_buf),
    )
    copies = [pltpu.make_async_copy(*pair, sems.at[i]) for i, pair in enumerate(fills)]
    for copy in copies:
        copy.start()
    copies[0].wait()
    copies[1].wait()
    normed = normalize(fresh[...].astype(F32), gain_buf[...]).astype(BF16)
    copies[2].wait()
    queries[...] = dot(normed, query_buf[...]).astype(BF16)


def project(states, gain, w_query):
    width, head_total = w_query.shape
    return pl.pallas_call(
        project_kernel,
        in_specs=[HBM] * 3,
        out_specs=VMEM,
        out_shape=jax.ShapeDtypeStruct((CAND_LEN, head_total), BF16),
        scratch_shapes=[
            pltpu.VMEM((CAND_LEN, width), BF16),
            pltpu.VMEM((1, width), F32),
            pltpu.VMEM(w_query.shape, BF16),
            pltpu.SemaphoreType.DMA((3,)),
        ],
        compiler_params=pltpu.CompilerParams(vmem_limit_bytes=12 * MIB),
        cost_estimate=pl.CostEstimate(
            flops=2 * CAND_LEN * width * head_total,
            bytes_accessed=2 * width * head_total,
            transcendentals=0,
        ),
        name="project",
    )(*in_hbm(states, gain, w_query))


def block_diagonal(cached, first_head, blocks):
    sources = cached.shape[0]
    blocks[...] = jnp.zeros_like(blocks)
    for head in range(blocks.shape[1] // HEAD_DIM):
        rows = pl.ds(head * sources, sources)
        blocks[rows, pl.ds(head * HEAD_DIM, HEAD_DIM)] = cached[:, first_head + head, :]


def chosen_slots(step, capacity, blocks, routes, experts):
    micro = jnp.clip(step - lax.axis_index("segment"), 0, CAND_DEV - 1)
    route = routes[micro]
    rows = route.shape[1]
    labels = lax.broadcasted_iota(jnp.int32, (experts, rows), 0)
    first, second = route[0:1] == labels, route[1:2] == labels
    place = route
    if blocks > 1:
        place = jnp.where(route < 0, route, route ^ (lax.axis_index("expert") // 2))
    named = jnp.where(first | second, 1.0, 0.0).astype(BF16)
    earlier = lax.broadcasted_iota(jnp.int32, (rows, rows), 0) < lax.broadcasted_iota(
        jnp.int32, (rows, rows), 1
    )
    before = dot(named, jnp.where(earlier, 1.0, 0.0).astype(BF16))
    slots = lax.broadcasted_iota(jnp.int32, (experts * capacity, rows), 0)
    chosen = []
    for mask, row in ((first, 0), (second, 1)):
        slot = jnp.sum(jnp.where(mask, before, 0.0), axis=0, keepdims=True).astype(jnp.int32)
        chosen.append(slots == place[row : row + 1] * capacity + slot)
    return chosen


def gate_kernel(step, capacity, blocks, ffn_input, routes, router, weights):
    experts = router.shape[0]
    micro = jnp.clip(step - lax.axis_index("segment"), 0, CAND_DEV - 1)
    route = routes[micro]
    labels = lax.broadcasted_iota(jnp.int32, (experts, route.shape[1]), 0)
    logits = dot(router[...], ffn_input[...], ((1,), (1,)))
    picked = [
        jnp.sum(jnp.where(route[row : row + 1] == labels, logits, 0.0), axis=0, keepdims=True)
        for row in range(2)
    ]
    gate_first = jax.nn.sigmoid(picked[0] - picked[1])
    gate_second = 1.0 - gate_first
    chosen = chosen_slots(step, capacity, blocks, routes, experts)
    weights[...] = jnp.where(chosen[0], gate_first, 0.0) + jnp.where(chosen[1], gate_second, 0.0)


def gate(step, capacity, blocks, ffn_input, routes, router):
    experts, width = router.shape
    return pl.pallas_call(
        functools.partial(gate_kernel, step, capacity, blocks),
        in_specs=[VMEM] * 3,
        out_specs=VMEM,
        out_shape=jax.ShapeDtypeStruct((experts * capacity, CAND_LEN), F32),
        compiler_params=pltpu.CompilerParams(vmem_limit_bytes=8 * MIB),
        cost_estimate=pl.CostEstimate(
            flops=2 * CAND_LEN * width * 128, bytes_accessed=2 * ffn_input.size, transcendentals=0
        ),
        name="gate",
    )(ffn_input, *in_vmem(routes, router))


def has_candidate(step):
    micro = step - lax.axis_index("segment")
    return (micro >= 0) & (micro < CAND_DEV)


def later_attend_kernel(step, capacity, blocks, *refs):
    @pl.when(has_candidate(step))
    def _():
        attend_kernel(step, capacity, blocks, *refs)


def attend_kernel(step, capacity, blocks, *refs):
    segment = lax.axis_index("segment")
    if step == 0:
        (cand_len, queries_in, cached, states, routes_hbm, attn_gain, ffn_gain, router_hbm,
         query_hbm, out_hbm), refs = refs[:10], refs[10:]
        after_ref, ffn_ref, *outgoing = refs[: 2 + blocks]
        (routes, gains, router, w_query, w_out, keys, values, following,
         fresh, route_buf, sems) = refs[2 + blocks :]
        fills = (
            (states.at[pl.ds(0, CAND_LEN), :], fresh),
            (ffn_gain, gains.at[1]),
            (out_hbm, w_out),
            (router_hbm, router),
            (routes_hbm, route_buf),
            (attn_gain, gains.at[0]),
            (states.at[pl.ds(CAND_LEN, CAND_LEN), :], following),
            (query_hbm, w_query),
        )
        copies = [pltpu.make_async_copy(*pair, sems.at[i]) for i, pair in enumerate(fills)]
        for copy in copies:
            copy.start()
        head_count = w_out.shape[0] // HEAD_DIM
        block_diagonal(cached, 0, keys)
        block_diagonal(cached, head_count, values)
        queries = queries_in[...]
        copies[0].wait()
        carried = fresh[...].astype(F32)
        copies[4].wait()
        copies = copies[:4] + copies[5:]
        position = lax.broadcasted_iota(jnp.int32, (1, CAND_LEN), 1)
        for micro in range(CAND_DEV):
            route = route_buf[:, micro * CAND_LEN : (micro + 1) * CAND_LEN]
            routes[micro] = jnp.where(position < cand_len[micro], route, -1)
    else:
        incoming, refs = refs[0], refs[1:]
        current = incoming[...]
        if step < CAND_DEV:
            current, refs = jnp.where(segment == 0, refs[0][...], current), refs[1:]
        (routes, gains, router, w_query, w_out, keys, values, after_ref, ffn_ref), refs = (
            refs[:9], refs[9:]
        )
        outgoing, marks = refs[:blocks], refs[blocks:]
        for mark in marks:
            mark[...] = current[: mark.shape[0], : mark.shape[1]]
        carried = current.astype(F32)
        normed = normalize(carried, gains[0]).astype(BF16)
        queries = dot(normed, w_query[...]).astype(BF16)

    rows = carried.shape[0]
    sources = keys.shape[0] * HEAD_DIM // keys.shape[1]
    scores = dot(keys[...], queries, ((1,), (1,))) * (1.0 / math.sqrt(HEAD_DIM))
    scores = scores.reshape(-1, sources, rows)
    exponent = jnp.exp(scores - jnp.max(scores, axis=1, keepdims=True))
    share = exponent / jnp.sum(exponent, axis=1, keepdims=True)
    share = share.reshape(-1, rows).astype(BF16)
    context = dot(share, values[...], ((0,), (0,))).astype(BF16)
    if step == 0:
        copies[1].wait()
        copies[2].wait()
    after_attn = carried + dot(context, w_out[...])
    after_ref[...] = after_attn
    ffn_input = normalize(after_attn, gains[1]).astype(BF16)

    rows_in_slots = chosen_slots(step, capacity, blocks, routes, router.shape[0])
    select = jnp.where(rows_in_slots[0] | rows_in_slots[1], 1.0, 0.0).astype(BF16)
    buffers = dot(select, ffn_input)
    for buffer, block in zip(split(buffers, blocks), outgoing):
        block[...] = buffer.astype(BF16)
    ffn_ref[...] = ffn_input
    if step == 0:
        for copy in copies[3:]:
            copy.wait()


def attend(step, capacity, blocks, marked, sources, kept):
    if step == 0:
        cand_len, queries, cached, *params = sources
        _, routes, _, _, router_t, w_query, w_out = params
        head_total, width = w_out.shape
        diagonal = (cached.shape[0] * head_total // HEAD_DIM, head_total)
        kept_shapes = [
            pltpu.VMEM((CAND_DEV, 2, CAND_LEN), jnp.int32),
            pltpu.VMEM((2, 1, width), F32),
            *(pltpu.VMEM(array.shape, BF16) for array in (router_t, w_query, w_out)),
            pltpu.VMEM(diagonal, BF16),
            pltpu.VMEM(diagonal, BF16),
            pltpu.VMEM((CAND_LEN, width), BF16),
        ]
        inputs = [*in_hbm(cand_len), queries, cached, *in_hbm(*params)]
        specs = [SMEM, VMEM, VMEM] + [HBM] * len(params)
        scratch = [
            pltpu.VMEM((CAND_LEN, width), BF16),
            pltpu.VMEM(routes.shape, jnp.int32),
            pltpu.SemaphoreType.DMA((8,)),
        ]
    else:
        _, _, router_t, _, w_out, *_ = kept
        head_total, width = w_out.shape
        kept_shapes = [jax.ShapeDtypeStruct((16, 128), BF16)] if marked else []
        scratch = []
        inputs = [*sources, *in_vmem(*kept)]
        specs = [VMEM] * len(inputs)
    slot_count = router_t.shape[0] * capacity
    outs = pl.pallas_call(
        functools.partial(
            later_attend_kernel if step else attend_kernel, step, capacity, blocks
        ),
        in_specs=specs,
        out_specs=[VMEM] * (2 + blocks + len(kept_shapes)),
        out_shape=[
            jax.ShapeDtypeStruct((CAND_LEN, width), F32),
            jax.ShapeDtypeStruct((CAND_LEN, width), BF16),
            *[jax.ShapeDtypeStruct((slot_count // blocks, width), BF16)] * blocks,
            *kept_shapes,
        ],
        scratch_shapes=scratch,
        compiler_params=pltpu.CompilerParams(vmem_limit_bytes=12 * MIB),
        cost_estimate=pl.CostEstimate(
            flops=6 * CAND_LEN * width * head_total,
            bytes_accessed=4 * width * head_total + 8 * CAND_LEN * width,
            transcendentals=0,
        ),
        name="attend",
    )(*inputs)
    return outs[:2], outs[2 : 2 + blocks], outs[2 + blocks :]


def load_kernel(count, _, *refs):
    sources, mats, sems = refs[:count], refs[count : 2 * count], refs[-1]
    copies = [
        pltpu.make_async_copy(source, mat, sems.at[i])
        for i, (source, mat) in enumerate(zip(sources, mats))
    ]
    for copy in copies:
        copy.start()
    for copy in copies:
        copy.wait()


def load(after, mats):
    return pl.pallas_call(
        functools.partial(load_kernel, len(mats)),
        in_specs=[VMEM] + [HBM] * len(mats),
        out_specs=[VMEM] * len(mats),
        out_shape=[pltpu.VMEM(mat.shape, BF16) for mat in mats],
        scratch_shapes=[pltpu.SemaphoreType.DMA((len(mats),))],
        compiler_params=pltpu.CompilerParams(vmem_limit_bytes=8 * MIB),
        cost_estimate=pl.CostEstimate(
            flops=0, bytes_accessed=2 * sum(mat.size for mat in mats), transcendentals=0
        ),
        name="load",
    )(after, *in_hbm(*mats))


def expert_kernel(blocks, stream, mark_count, *refs):
    refs = refs[mark_count:]
    rows_in, refs = refs[:blocks], refs[blocks:]
    (own_in, own_down), refs = refs[:2], refs[2:]
    if stream:
        sources, served, refs = refs[:2], refs[2 : 2 + blocks], refs[2 + blocks :]
        other_in, other_down, rows, own_hidden, other_hidden, partial, sems = refs
    else:
        (other_in, other_down), refs = refs[:2], refs[2:]
        served, (rows, own_hidden, other_hidden) = refs[:blocks], refs[blocks:]
    size = STREAM_CHUNK if stream else HIDDEN_CHUNK
    chunks = [pl.ds(start, size) for start in range(0, own_in.shape[1], size)]

    def fill(source, mat):
        copies = [
            pltpu.make_async_copy(
                sources[source].at[:, lanes], mat.at[:, lanes], sems.at[source, i]
            )
            for i, lanes in enumerate(chunks)
        ]
        for copy in copies:
            copy.start()
        return copies

    def hidden_of(mat, units):
        return jnp.maximum(dot(rows[...], mat[:, units]), 0.0).astype(BF16)

    def serve(out, lanes):
        for part, block in zip(split(out, blocks), served):
            block[:, lanes] = part.astype(BF16)

    if not stream:
        rows[...] = joined(rows_in)
        for units in chunks:
            own_hidden[:, units] = hidden_of(own_in, units)
            other_hidden[:, units] = hidden_of(other_in, units)
        for lanes in chunks:
            out = dot(own_hidden[...], own_down[:, lanes])
            serve(out + dot(other_hidden[...], other_down[:, lanes]), lanes)
        return

    other_in_copies = fill(0, other_in)
    other_down_copies = fill(1, other_down)
    rows[...] = joined(rows_in)
    for units in chunks:
        own_hidden[:, units] = hidden_of(own_in, units)
    for lanes in chunks:
        partial[:, lanes] = dot(own_hidden[...], own_down[:, lanes])
    for units, copy in zip(chunks, other_in_copies):
        copy.wait()
        other_hidden[:, units] = hidden_of(other_in, units)
    for lanes, copy in zip(chunks, other_down_copies):
        copy.wait()
        serve(partial[:, lanes] + dot(other_hidden[...], other_down[:, lanes]), lanes)


def expert_rows(rows_in, mats, step, marks=()):
    blocks, stream = len(rows_in), step == 0
    width = rows_in[0].shape[1]
    count = blocks * rows_in[0].shape[0]
    units = mats[0].shape[1]
    scratch = [
        pltpu.VMEM((count, width), BF16),
        pltpu.VMEM((count, units), BF16),
        pltpu.VMEM((count, units), BF16),
    ]
    out_shape = [jax.ShapeDtypeStruct(rows.shape, BF16) for rows in rows_in]
    if stream:
        scratch += [
            pltpu.VMEM((count, width), F32),
            pltpu.SemaphoreType.DMA((2, units // STREAM_CHUNK)),
        ]
        out_shape += [pltpu.VMEM(mat.shape, BF16) for mat in mats[2:]]
    outs = pl.pallas_call(
        functools.partial(expert_kernel, blocks, stream, len(marks)),
        in_specs=[VMEM] * (len(marks) + blocks + 2) + [HBM if stream else VMEM] * 2,
        out_specs=[VMEM] * len(out_shape),
        out_shape=out_shape,
        scratch_shapes=scratch,
        compiler_params=pltpu.CompilerParams(vmem_limit_bytes=12 * MIB),
        cost_estimate=pl.CostEstimate(
            flops=8 * count * width * units,
            bytes_accessed=8 * width * units + 4 * count * width,
            transcendentals=0,
        ),
        name="experts",
    )(*marks, *rows_in, *in_vmem(*mats[:2]), *(in_hbm if stream else in_vmem)(*mats[2:]))
    return outs[:blocks], ((*mats[:2], *outs[blocks:]) if stream else mats)


def mixed(after_attn, weights, blocks):
    gates = weights[...]
    coarse = gates.astype(BF16)
    fine = (gates - coarse.astype(F32)).astype(BF16)
    rows = joined(blocks)
    mixture = dot(coarse, rows, ((0,), (0,))) + dot(fine, rows, ((0,), (0,)))
    return (after_attn[...] + mixture).astype(BF16)


def combine_kernel(blocks, after_attn, weights, *refs):
    result = refs[blocks]
    result[...] = mixed(after_attn, weights, refs[:blocks])


def place_kernel(blocks, after_attn, weights, *refs):
    served, earlier, (output, result, sems) = refs[:blocks], refs[blocks:-3], refs[-3:]
    segment = lax.axis_index("segment")

    def place(source, micro):
        rows = pl.ds(micro * CAND_LEN, CAND_LEN)
        return pltpu.make_async_copy(source, output.at[rows, :], sems.at[micro])

    last = len(earlier)
    for micro in range(CAND_DEV):
        for step in range(micro, last):

            @pl.when(segment + micro == step)
            def _():
                place(earlier[step], micro).start()

    result[...] = mixed(after_attn, weights, served)
    for micro in range(CAND_DEV):

        @pl.when(segment + micro == last)
        def _():
            place(result, micro).start()

    for micro in range(CAND_DEV):
        place(result, micro).wait()


def combine(after_attn, weights, served, earlier=()):
    rows, width = after_attn.shape
    inputs = [after_attn, weights, *served]
    scratch = []
    out_shape, out_spec = jax.ShapeDtypeStruct((rows, width), BF16), VMEM
    if earlier:
        inputs += in_vmem(*earlier)
        scratch = [pltpu.VMEM((rows, width), BF16), pltpu.SemaphoreType.DMA((CAND_DEV,))]
        out_shape, out_spec = jax.ShapeDtypeStruct((CAND_DEV * rows, width), BF16), HBM
    return pl.pallas_call(
        functools.partial(place_kernel if earlier else combine_kernel, len(served)),
        in_specs=[VMEM] * len(inputs),
        out_specs=out_spec,
        out_shape=out_shape,
        scratch_shapes=scratch,
        compiler_params=pltpu.CompilerParams(vmem_limit_bytes=8 * MIB),
        cost_estimate=pl.CostEstimate(
            flops=4 * weights.size * width,
            bytes_accessed=6 * after_attn.size + 2 * weights.shape[0] * width,
            transcendentals=0,
        ),
        name="combine",
    )(*inputs)


def local(
    states, cand_len, routes, enc_kv, attn_gain, ffn_gain, w_query, w_out, w_router, w_in, w_down
):
    n_segment = lax.axis_size("segment")
    n_expert = lax.axis_size("expert")
    model_width = states.shape[1]
    experts = w_router.shape[2]
    capacity = 2 * ((5 * CAND_LEN + 4 * experts - 1) // (4 * experts))
    core_pairs = [(i, i ^ 1) for i in range(n_expert)]
    same_core = [list(range(core, n_expert, 2)) for core in range(2)]
    blocks = experts if experts <= 4 else 1

    def exchange(parts):
        if blocks > 1:
            return [parts[0]] + [
                lax.ppermute(part, "expert", [(i, i ^ (2 * k)) for i in range(n_expert)])
                for k, part in enumerate(parts[1:], 1)
            ]
        rows = parts[0].reshape(experts, capacity, model_width)
        moved = lax.all_to_all(
            rows, "expert", split_axis=0, concat_axis=0, axis_index_groups=same_core, tiled=True
        )
        return [moved.reshape(parts[0].shape)]

    cached = lax.all_to_all(
        spread(enc_kv, n_expert), ("segment", "expert"), split_axis=0, concat_axis=0, tiled=True
    )
    own = (w_in[0, 0], w_down[0, 0])
    other = tuple(lax.ppermute(mat, "expert", core_pairs) for mat in own)

    queries = project(states, attn_gain, w_query[0])
    step_count = CAND_DEV + n_segment - 1
    earlier = []
    kept = ()
    for step in range(step_count):
        if step == 0:
            sources = (
                cand_len, queries, cached, states, routes[0].T, attn_gain, ffn_gain,
                w_router[0].T, w_query[0], w_out[0],
            )
        elif step < CAND_DEV:
            sources = (incoming, following)
        else:
            sources = (incoming,)
        marked = step > CAND_DEV
        (after_attn, ffn_input), outgoing, left = attend(
            step, capacity, blocks, marked, sources, kept
        )
        if step == 0:
            *kept, following = left
            expert_mats = (*load(ffn_input, own), *other)
        weights = gate(step, capacity, blocks, ffn_input, kept[0], kept[2])
        received = exchange(outgoing)
        marks = ()
        if marked:
            pairs = [(i, i + 1) for i in range(0, n_expert, 2)]
            marks = (lax.ppermute(left[0], "expert", pairs),)
        served, expert_mats = expert_rows(received, expert_mats, step, marks)
        served = exchange(served)
        if step + 1 < step_count:
            result = combine(after_attn, weights, served)
            incoming = lax.ppermute(
                result, "segment", [(i, i + 1) for i in range(n_segment - 1)]
            )
            earlier.append(result)
    output = combine(after_attn, weights, served, earlier)
    return output.reshape(1, CAND_DEV * CAND_LEN, model_width)


def solution(mesh):
    return jax.shard_map(
        local,
        mesh=mesh,
        in_specs=(
            P("expert", None),
            P("expert"),
            P("segment", "expert", None),
            P(None, ("segment", "expert"), None),
            P("segment", None),
            P("segment", None),
            P("segment", None, None),
            P("segment", None, None),
            P("segment", None, None),
            P("segment", "expert", None, None),
            P("segment", "expert", None, None),
        ),
        out_specs=P("segment", "expert", None),
        check_vma=False,
    )
```

```python
import functools
import math

import jax
import jax.numpy as jnp
from jax import lax
from jax.experimental import pallas as pl
from jax.experimental.pallas import tpu as pltpu
from jax.sharding import PartitionSpec as P

HEAD_DIM = 128
CAND_LEN = 64
CAND_DEV = 2
HIDDEN_CHUNK = 512
STREAM_CHUNK = 1024
MIB = 1 << 20

EPSILON = 1e-05

VMEM = pl.BlockSpec(memory_space=pltpu.VMEM)
SMEM = pl.BlockSpec(memory_space=pltpu.SMEM)
HBM = pl.BlockSpec(memory_space=pltpu.HBM)
F32 = jnp.float32
BF16 = jnp.bfloat16


def in_hbm(*arrays):
    return [pltpu.with_memory_space_constraint(array, pltpu.HBM) for array in arrays]


def in_vmem(*arrays):
    return [pltpu.with_memory_space_constraint(array, pltpu.VMEM) for array in arrays]


def split(rows, blocks):
    size = rows.shape[0] // blocks
    return [rows[k * size : (k + 1) * size] for k in range(blocks)]


def joined(blocks):
    if len(blocks) == 1:
        return blocks[0][...]
    return jnp.concatenate([block[...].astype(F32) for block in blocks], axis=0).astype(BF16)


def normalize(carried, gain_row):
    average = jnp.mean(carried, axis=-1, keepdims=True)
    centered = carried - average
    variance = jnp.mean(centered * centered, axis=-1, keepdims=True)
    return gain_row * centered * lax.rsqrt(variance + EPSILON)


def dot(left, right, contract=((1,), (0,))):
    return lax.dot_general(left, right, (contract, ((), ())), preferred_element_type=F32)


def spread_kernel(copies_of, enc_kv, blocks):
    for layer in range(enc_kv.shape[0]):
        block = enc_kv[layer : layer + 1, :].reshape(blocks.shape[1:])
        for i in range(copies_of):
            blocks[layer * copies_of + i] = block


def spread(enc_kv, copies_of):
    layers, _, features = enc_kv.shape
    return pl.pallas_call(
        functools.partial(spread_kernel, copies_of),
        in_specs=[VMEM],
        out_specs=VMEM,
        out_shape=jax.ShapeDtypeStruct(
            (layers * copies_of, features // HEAD_DIM, HEAD_DIM), BF16
        ),
        compiler_params=pltpu.CompilerParams(vmem_limit_bytes=8 * MIB),
        name="spread",
    )(*in_hbm(enc_kv.reshape(layers, features)))


def project_kernel(states, gain, w_query, queries, fresh, gain_buf, query_buf, sems):
    fills = (
        (states.at[pl.ds(0, CAND_LEN), :], fresh),
        (gain, gain_buf),
        (w_query, query_buf),
    )
    copies = [pltpu.make_async_copy(*pair, sems.at[i]) for i, pair in enumerate(fills)]
    for copy in copies:
        copy.start()
    copies[0].wait()
    copies[1].wait()
    normed = normalize(fresh[...].astype(F32), gain_buf[...]).astype(BF16)
    copies[2].wait()
    queries[...] = dot(normed, query_buf[...]).astype(BF16)


def project(states, gain, w_query):
    width, head_total = w_query.shape
    return pl.pallas_call(
        project_kernel,
        in_specs=[HBM] * 3,
        out_specs=VMEM,
        out_shape=jax.ShapeDtypeStruct((CAND_LEN, head_total), BF16),
        scratch_shapes=[
            pltpu.VMEM((CAND_LEN, width), BF16),
            pltpu.VMEM((1, width), F32),
            pltpu.VMEM(w_query.shape, BF16),
            pltpu.SemaphoreType.DMA((3,)),
        ],
        compiler_params=pltpu.CompilerParams(vmem_limit_bytes=8 * MIB),
        cost_estimate=pl.CostEstimate(
            flops=2 * CAND_LEN * width * head_total,
            bytes_accessed=2 * width * head_total,
            transcendentals=0,
        ),
        name="project",
    )(*in_hbm(states, gain, w_query))


def block_diagonal(cached, first_head, blocks):
    sources = cached.shape[0]
    blocks[...] = jnp.zeros_like(blocks)
    for head in range(blocks.shape[1] // HEAD_DIM):
        rows = pl.ds(head * sources, sources)
        blocks[rows, pl.ds(head * HEAD_DIM, HEAD_DIM)] = cached[:, first_head + head, :]


def chosen_slots(step, capacity, blocks, routes, experts):
    micro = jnp.clip(step - lax.axis_index("segment"), 0, CAND_DEV - 1)
    route = routes[micro]
    rows = route.shape[1]
    labels = lax.broadcasted_iota(jnp.int32, (experts, rows), 0)
    first, second = route[0:1] == labels, route[1:2] == labels
    place = route
    if blocks > 1:
        place = jnp.where(route < 0, route, route ^ (lax.axis_index("expert") // 2))
    named = jnp.where(first | second, 1.0, 0.0).astype(BF16)
    earlier = lax.broadcasted_iota(jnp.int32, (rows, rows), 0) < lax.broadcasted_iota(
        jnp.int32, (rows, rows), 1
    )
    before = dot(named, jnp.where(earlier, 1.0, 0.0).astype(BF16))
    slots = lax.broadcasted_iota(jnp.int32, (experts * capacity, rows), 0)
    chosen = []
    for mask, row in ((first, 0), (second, 1)):
        slot = jnp.sum(jnp.where(mask, before, 0.0), axis=0, keepdims=True).astype(jnp.int32)
        chosen.append(slots == place[row : row + 1] * capacity + slot)
    return chosen


def gate_kernel(step, capacity, blocks, ffn_input, routes, router, weights):
    experts = router.shape[0]
    micro = jnp.clip(step - lax.axis_index("segment"), 0, CAND_DEV - 1)
    route = routes[micro]
    labels = lax.broadcasted_iota(jnp.int32, (experts, route.shape[1]), 0)
    logits = dot(router[...], ffn_input[...], ((1,), (1,)))
    picked = [
        jnp.sum(jnp.where(route[row : row + 1] == labels, logits, 0.0), axis=0, keepdims=True)
        for row in range(2)
    ]
    gate_first = jax.nn.sigmoid(picked[0] - picked[1])
    gate_second = 1.0 - gate_first
    chosen = chosen_slots(step, capacity, blocks, routes, experts)
    weights[...] = jnp.where(chosen[0], gate_first, 0.0) + jnp.where(chosen[1], gate_second, 0.0)


def gate(step, capacity, blocks, ffn_input, routes, router):
    experts, width = router.shape
    return pl.pallas_call(
        functools.partial(gate_kernel, step, capacity, blocks),
        in_specs=[VMEM] * 3,
        out_specs=VMEM,
        out_shape=jax.ShapeDtypeStruct((experts * capacity, CAND_LEN), F32),
        compiler_params=pltpu.CompilerParams(vmem_limit_bytes=8 * MIB),
        cost_estimate=pl.CostEstimate(
            flops=2 * CAND_LEN * width * 128, bytes_accessed=2 * ffn_input.size, transcendentals=0
        ),
        name="gate",
    )(ffn_input, *in_vmem(routes, router))


def has_candidate(step):
    micro = step - lax.axis_index("segment")
    return (micro >= 0) & (micro < CAND_DEV)


def later_attend_kernel(step, capacity, blocks, *refs):
    @pl.when(has_candidate(step))
    def _():
        attend_kernel(step, capacity, blocks, *refs)


def attend_kernel(step, capacity, blocks, *refs):
    segment = lax.axis_index("segment")
    if step == 0:
        (cand_len, queries_in, cached, states, routes_hbm, attn_gain, ffn_gain, router_hbm,
         query_hbm, out_hbm), refs = refs[:10], refs[10:]
        after_ref, ffn_ref, *outgoing = refs[: 2 + blocks]
        (routes, gains, router, w_query, w_out, keys, values, following,
         fresh, route_buf, sems) = refs[2 + blocks :]
        fills = (
            (states.at[pl.ds(0, CAND_LEN), :], fresh),
            (ffn_gain, gains.at[1]),
            (out_hbm, w_out),
            (router_hbm, router),
            (routes_hbm, route_buf),
            (attn_gain, gains.at[0]),
            (states.at[pl.ds(CAND_LEN, CAND_LEN), :], following),
            (query_hbm, w_query),
        )
        copies = [pltpu.make_async_copy(*pair, sems.at[i]) for i, pair in enumerate(fills)]
        for copy in copies:
            copy.start()
        head_count = w_out.shape[0] // HEAD_DIM
        block_diagonal(cached, 0, keys)
        block_diagonal(cached, head_count, values)
        queries = queries_in[...]
        copies[0].wait()
        carried = fresh[...].astype(F32)
        copies[4].wait()
        copies = copies[:4] + copies[5:]
        position = lax.broadcasted_iota(jnp.int32, (1, CAND_LEN), 1)
        for micro in range(CAND_DEV):
            route = route_buf[:, micro * CAND_LEN : (micro + 1) * CAND_LEN]
            routes[micro] = jnp.where(position < cand_len[micro], route, -1)
    else:
        incoming, refs = refs[0], refs[1:]
        current = incoming[...]
        if step < CAND_DEV:
            current, refs = jnp.where(segment == 0, refs[0][...], current), refs[1:]
        (routes, gains, router, w_query, w_out, keys, values, after_ref, ffn_ref), refs = (
            refs[:9], refs[9:]
        )
        outgoing, marks = refs[:blocks], refs[blocks:]
        for mark in marks:
            mark[...] = current[: mark.shape[0], : mark.shape[1]]
        carried = current.astype(F32)
        normed = normalize(carried, gains[0]).astype(BF16)
        queries = dot(normed, w_query[...]).astype(BF16)

    rows = carried.shape[0]
    sources = keys.shape[0] * HEAD_DIM // keys.shape[1]
    scores = dot(keys[...], queries, ((1,), (1,))) * (1.0 / math.sqrt(HEAD_DIM))
    scores = scores.reshape(-1, sources, rows)
    exponent = jnp.exp(scores - jnp.max(scores, axis=1, keepdims=True))
    share = exponent / jnp.sum(exponent, axis=1, keepdims=True)
    share = share.reshape(-1, rows).astype(BF16)
    context = dot(share, values[...], ((0,), (0,))).astype(BF16)
    if step == 0:
        copies[1].wait()
        copies[2].wait()
    after_attn = carried + dot(context, w_out[...])
    after_ref[...] = after_attn
    ffn_input = normalize(after_attn, gains[1]).astype(BF16)

    rows_in_slots = chosen_slots(step, capacity, blocks, routes, router.shape[0])
    select = jnp.where(rows_in_slots[0] | rows_in_slots[1], 1.0, 0.0).astype(BF16)
    buffers = dot(select, ffn_input)
    for buffer, block in zip(split(buffers, blocks), outgoing):
        block[...] = buffer.astype(BF16)
    ffn_ref[...] = ffn_input
    if step == 0:
        for copy in copies[3:]:
            copy.wait()


def attend(step, capacity, blocks, marked, sources, kept):
    if step == 0:
        cand_len, queries, cached, *params = sources
        _, routes, _, _, router_t, w_query, w_out = params
        head_total, width = w_out.shape
        diagonal = (cached.shape[0] * head_total // HEAD_DIM, head_total)
        kept_shapes = [
            pltpu.VMEM((CAND_DEV, 2, CAND_LEN), jnp.int32),
            pltpu.VMEM((2, 1, width), F32),
            *(pltpu.VMEM(array.shape, BF16) for array in (router_t, w_query, w_out)),
            pltpu.VMEM(diagonal, BF16),
            pltpu.VMEM(diagonal, BF16),
            pltpu.VMEM((CAND_LEN, width), BF16),
        ]
        inputs = [*in_hbm(cand_len), queries, cached, *in_hbm(*params)]
        specs = [SMEM, VMEM, VMEM] + [HBM] * len(params)
        scratch = [
            pltpu.VMEM((CAND_LEN, width), BF16),
            pltpu.VMEM(routes.shape, jnp.int32),
            pltpu.SemaphoreType.DMA((8,)),
        ]
    else:
        _, _, router_t, _, w_out, *_ = kept
        head_total, width = w_out.shape
        kept_shapes = [jax.ShapeDtypeStruct((16, 128), BF16)] if marked else []
        scratch = []
        inputs = [*sources, *in_vmem(*kept)]
        specs = [VMEM] * len(inputs)
    slot_count = router_t.shape[0] * capacity
    outs = pl.pallas_call(
        functools.partial(
            later_attend_kernel if step else attend_kernel, step, capacity, blocks
        ),
        in_specs=specs,
        out_specs=[VMEM] * (2 + blocks + len(kept_shapes)),
        out_shape=[
            jax.ShapeDtypeStruct((CAND_LEN, width), F32),
            jax.ShapeDtypeStruct((CAND_LEN, width), BF16),
            *[jax.ShapeDtypeStruct((slot_count // blocks, width), BF16)] * blocks,
            *kept_shapes,
        ],
        scratch_shapes=scratch,
        compiler_params=pltpu.CompilerParams(vmem_limit_bytes=8 * MIB),
        cost_estimate=pl.CostEstimate(
            flops=6 * CAND_LEN * width * head_total,
            bytes_accessed=4 * width * head_total + 8 * CAND_LEN * width,
            transcendentals=0,
        ),
        name="attend",
    )(*inputs)
    return outs[:2], outs[2 : 2 + blocks], outs[2 + blocks :]


def load_kernel(count, _, *refs):
    sources, mats, sems = refs[:count], refs[count : 2 * count], refs[-1]
    copies = [
        pltpu.make_async_copy(source, mat, sems.at[i])
        for i, (source, mat) in enumerate(zip(sources, mats))
    ]
    for copy in copies:
        copy.start()
    for copy in copies:
        copy.wait()


def load(after, mats):
    return pl.pallas_call(
        functools.partial(load_kernel, len(mats)),
        in_specs=[VMEM] + [HBM] * len(mats),
        out_specs=[VMEM] * len(mats),
        out_shape=[pltpu.VMEM(mat.shape, BF16) for mat in mats],
        scratch_shapes=[pltpu.SemaphoreType.DMA((len(mats),))],
        compiler_params=pltpu.CompilerParams(vmem_limit_bytes=8 * MIB),
        cost_estimate=pl.CostEstimate(
            flops=0, bytes_accessed=2 * sum(mat.size for mat in mats), transcendentals=0
        ),
        name="load",
    )(after, *in_hbm(*mats))


def expert_kernel(blocks, stream, mark_count, *refs):
    refs = refs[mark_count:]
    rows_in, refs = refs[:blocks], refs[blocks:]
    (own_in, own_down), refs = refs[:2], refs[2:]
    if stream:
        sources, served, refs = refs[:2], refs[2 : 2 + blocks], refs[2 + blocks :]
        other_in, other_down, rows, own_hidden, other_hidden, partial, sems = refs
    else:
        (other_in, other_down), refs = refs[:2], refs[2:]
        served, (rows, own_hidden, other_hidden) = refs[:blocks], refs[blocks:]
    size = STREAM_CHUNK if stream else HIDDEN_CHUNK
    chunks = [pl.ds(start, size) for start in range(0, own_in.shape[1], size)]

    def fill(source, mat):
        copies = [
            pltpu.make_async_copy(
                sources[source].at[:, lanes], mat.at[:, lanes], sems.at[source, i]
            )
            for i, lanes in enumerate(chunks)
        ]
        for copy in copies:
            copy.start()
        return copies

    def hidden_of(mat, units):
        return jnp.maximum(dot(rows[...], mat[:, units]), 0.0).astype(BF16)

    def serve(out, lanes):
        for part, block in zip(split(out, blocks), served):
            block[:, lanes] = part.astype(BF16)

    if not stream:
        rows[...] = joined(rows_in)
        for units in chunks:
            own_hidden[:, units] = hidden_of(own_in, units)
            other_hidden[:, units] = hidden_of(other_in, units)
        for lanes in chunks:
            out = dot(own_hidden[...], own_down[:, lanes])
            serve(out + dot(other_hidden[...], other_down[:, lanes]), lanes)
        return

    other_in_copies = fill(0, other_in)
    other_down_copies = fill(1, other_down)
    rows[...] = joined(rows_in)
    for units in chunks:
        own_hidden[:, units] = hidden_of(own_in, units)
    for lanes in chunks:
        partial[:, lanes] = dot(own_hidden[...], own_down[:, lanes])
    for units, copy in zip(chunks, other_in_copies):
        copy.wait()
        other_hidden[:, units] = hidden_of(other_in, units)
    for lanes, copy in zip(chunks, other_down_copies):
        copy.wait()
        serve(partial[:, lanes] + dot(other_hidden[...], other_down[:, lanes]), lanes)


def expert_rows(rows_in, mats, step, marks=()):
    blocks, stream = len(rows_in), step == 0
    width = rows_in[0].shape[1]
    count = blocks * rows_in[0].shape[0]
    units = mats[0].shape[1]
    scratch = [
        pltpu.VMEM((count, width), BF16),
        pltpu.VMEM((count, units), BF16),
        pltpu.VMEM((count, units), BF16),
    ]
    out_shape = [jax.ShapeDtypeStruct(rows.shape, BF16) for rows in rows_in]
    if stream:
        scratch += [
            pltpu.VMEM((count, width), F32),
            pltpu.SemaphoreType.DMA((2, units // STREAM_CHUNK)),
        ]
        out_shape += [pltpu.VMEM(mat.shape, BF16) for mat in mats[2:]]
    outs = pl.pallas_call(
        functools.partial(expert_kernel, blocks, stream, len(marks)),
        in_specs=[VMEM] * (len(marks) + blocks + 2) + [HBM if stream else VMEM] * 2,
        out_specs=[VMEM] * len(out_shape),
        out_shape=out_shape,
        scratch_shapes=scratch,
        compiler_params=pltpu.CompilerParams(vmem_limit_bytes=8 * MIB),
        cost_estimate=pl.CostEstimate(
            flops=8 * count * width * units,
            bytes_accessed=8 * width * units + 4 * count * width,
            transcendentals=0,
        ),
        name="experts",
    )(*marks, *rows_in, *in_vmem(*mats[:2]), *(in_hbm if stream else in_vmem)(*mats[2:]))
    return outs[:blocks], ((*mats[:2], *outs[blocks:]) if stream else mats)


def mixed(after_attn, weights, blocks):
    gates = weights[...]
    coarse = gates.astype(BF16)
    fine = (gates - coarse.astype(F32)).astype(BF16)
    rows = joined(blocks)
    mixture = dot(coarse, rows, ((0,), (0,))) + dot(fine, rows, ((0,), (0,)))
    return (after_attn[...] + mixture).astype(BF16)


def combine_kernel(blocks, after_attn, weights, *refs):
    result = refs[blocks]
    result[...] = mixed(after_attn, weights, refs[:blocks])


def place_kernel(blocks, after_attn, weights, *refs):
    served, earlier, (output, result, sems) = refs[:blocks], refs[blocks:-3], refs[-3:]
    segment = lax.axis_index("segment")

    def place(source, micro):
        rows = pl.ds(micro * CAND_LEN, CAND_LEN)
        return pltpu.make_async_copy(source, output.at[rows, :], sems.at[micro])

    last = len(earlier)
    for micro in range(CAND_DEV):
        for step in range(micro, last):

            @pl.when(segment + micro == step)
            def _():
                place(earlier[step], micro).start()

    result[...] = mixed(after_attn, weights, served)
    for micro in range(CAND_DEV):

        @pl.when(segment + micro == last)
        def _():
            place(result, micro).start()

    for micro in range(CAND_DEV):
        place(result, micro).wait()


def combine(after_attn, weights, served, earlier=()):
    rows, width = after_attn.shape
    inputs = [after_attn, weights, *served]
    scratch = []
    out_shape, out_spec = jax.ShapeDtypeStruct((rows, width), BF16), VMEM
    if earlier:
        inputs += in_vmem(*earlier)
        scratch = [pltpu.VMEM((rows, width), BF16), pltpu.SemaphoreType.DMA((CAND_DEV,))]
        out_shape, out_spec = jax.ShapeDtypeStruct((CAND_DEV * rows, width), BF16), HBM
    return pl.pallas_call(
        functools.partial(place_kernel if earlier else combine_kernel, len(served)),
        in_specs=[VMEM] * len(inputs),
        out_specs=out_spec,
        out_shape=out_shape,
        scratch_shapes=scratch,
        compiler_params=pltpu.CompilerParams(vmem_limit_bytes=8 * MIB),
        cost_estimate=pl.CostEstimate(
            flops=4 * weights.size * width,
            bytes_accessed=6 * after_attn.size + 2 * weights.shape[0] * width,
            transcendentals=0,
        ),
        name="combine",
    )(*inputs)


def local(
    states, cand_len, routes, enc_kv, attn_gain, ffn_gain, w_query, w_out, w_router, w_in, w_down
):
    n_segment = lax.axis_size("segment")
    n_expert = lax.axis_size("expert")
    model_width = states.shape[1]
    experts = w_router.shape[2]
    capacity = 2 * ((5 * CAND_LEN + 4 * experts - 1) // (4 * experts))
    core_pairs = [(i, i ^ 1) for i in range(n_expert)]
    same_core = [list(range(core, n_expert, 2)) for core in range(2)]
    blocks = experts if experts <= 4 else 1

    def exchange(parts):
        if blocks > 1:
            return [parts[0]] + [
                lax.ppermute(part, "expert", [(i, i ^ (2 * k)) for i in range(n_expert)])
                for k, part in enumerate(parts[1:], 1)
            ]
        rows = parts[0].reshape(experts, capacity, model_width)
        moved = lax.all_to_all(
            rows, "expert", split_axis=0, concat_axis=0, axis_index_groups=same_core, tiled=True
        )
        return [moved.reshape(parts[0].shape)]

    cached = lax.all_to_all(
        spread(enc_kv, n_expert), ("segment", "expert"), split_axis=0, concat_axis=0, tiled=True
    )
    own = (w_in[0, 0], w_down[0, 0])
    other = tuple(lax.ppermute(mat, "expert", core_pairs) for mat in own)

    queries = project(states, attn_gain, w_query[0])
    step_count = CAND_DEV + n_segment - 1
    earlier = []
    kept = ()
    for step in range(step_count):
        if step == 0:
            sources = (
                cand_len, queries, cached, states, routes[0].T, attn_gain, ffn_gain,
                w_router[0].T, w_query[0], w_out[0],
            )
        elif step < CAND_DEV:
            sources = (incoming, following)
        else:
            sources = (incoming,)
        marked = step > CAND_DEV
        (after_attn, ffn_input), outgoing, left = attend(
            step, capacity, blocks, marked, sources, kept
        )
        if step == 0:
            *kept, following = left
            expert_mats = (*load(ffn_input, own), *other)
        weights = gate(step, capacity, blocks, ffn_input, kept[0], kept[2])
        received = exchange(outgoing)
        marks = ()
        if marked:
            pairs = [(i, i + 1) for i in range(0, n_expert, 2)]
            marks = (lax.ppermute(left[0], "expert", pairs),)
        served, expert_mats = expert_rows(received, expert_mats, step, marks)
        served = exchange(served)
        if step + 1 < step_count:
            result = combine(after_attn, weights, served)
            incoming = lax.ppermute(
                result, "segment", [(i, i + 1) for i in range(n_segment - 1)]
            )
            earlier.append(result)
    output = combine(after_attn, weights, served, earlier)
    return output.reshape(1, CAND_DEV * CAND_LEN, model_width)


def solution(mesh):
    return jax.shard_map(
        local,
        mesh=mesh,
        in_specs=(
            P("expert", None),
            P("expert"),
            P("segment", "expert", None),
            P(None, ("segment", "expert"), None),
            P("segment", None),
            P("segment", None),
            P("segment", None, None),
            P("segment", None, None),
            P("segment", None, None),
            P("segment", "expert", None, None),
            P("segment", "expert", None, None),
        ),
        out_specs=P("segment", "expert", None),
        check_vma=False,
    )
```

```python
import functools
import math

import jax
import jax.numpy as jnp
from jax import lax
from jax.experimental import pallas as pl
from jax.experimental.pallas import tpu as pltpu
from jax.sharding import PartitionSpec as P

HEAD_DIM = 128
CAND_LEN = 64
CAND_DEV = 2
HIDDEN_CHUNK = 512
STREAM_CHUNK = 1024
MIB = 1 << 20

EPSILON = 1e-05

VMEM = pl.BlockSpec(memory_space=pltpu.VMEM)
SMEM = pl.BlockSpec(memory_space=pltpu.SMEM)
HBM = pl.BlockSpec(memory_space=pltpu.HBM)
F32 = jnp.float32
BF16 = jnp.bfloat16


def in_hbm(*arrays):
    return [pltpu.with_memory_space_constraint(array, pltpu.HBM) for array in arrays]


def in_vmem(*arrays):
    return [pltpu.with_memory_space_constraint(array, pltpu.VMEM) for array in arrays]


def split(rows, blocks):
    size = rows.shape[0] // blocks
    return [rows[k * size : (k + 1) * size] for k in range(blocks)]


def joined(blocks):
    if len(blocks) == 1:
        return blocks[0][...]
    return jnp.concatenate([block[...].astype(F32) for block in blocks], axis=0).astype(BF16)


def normalize(carried, gain_row):
    average = jnp.mean(carried, axis=-1, keepdims=True)
    centered = carried - average
    variance = jnp.mean(centered * centered, axis=-1, keepdims=True)
    return gain_row * centered * lax.rsqrt(variance + EPSILON)


def dot(left, right, contract=((1,), (0,))):
    return lax.dot_general(left, right, (contract, ((), ())), preferred_element_type=F32)


def spread_kernel(copies_of, enc_kv, blocks):
    for layer in range(enc_kv.shape[0]):
        block = enc_kv[layer : layer + 1, :].reshape(blocks.shape[1:])
        for i in range(copies_of):
            blocks[layer * copies_of + i] = block


def spread(enc_kv, copies_of):
    layers, _, features = enc_kv.shape
    return pl.pallas_call(
        functools.partial(spread_kernel, copies_of),
        in_specs=[VMEM],
        out_specs=VMEM,
        out_shape=jax.ShapeDtypeStruct(
            (layers * copies_of, features // HEAD_DIM, HEAD_DIM), BF16
        ),
        compiler_params=pltpu.CompilerParams(vmem_limit_bytes=8 * MIB),
        name="spread",
    )(*in_hbm(enc_kv.reshape(layers, features)))


def project_kernel(states, gain, w_query, queries, fresh, gain_buf, query_buf, sems):
    fills = (
        (states.at[pl.ds(0, CAND_LEN), :], fresh),
        (gain, gain_buf),
        (w_query, query_buf),
    )
    copies = [pltpu.make_async_copy(*pair, sems.at[i]) for i, pair in enumerate(fills)]
    for copy in copies:
        copy.start()
    copies[0].wait()
    copies[1].wait()
    normed = normalize(fresh[...].astype(F32), gain_buf[...]).astype(BF16)
    copies[2].wait()
    queries[...] = dot(normed, query_buf[...]).astype(BF16)


def project(states, gain, w_query):
    width, head_total = w_query.shape
    return pl.pallas_call(
        project_kernel,
        in_specs=[HBM] * 3,
        out_specs=VMEM,
        out_shape=jax.ShapeDtypeStruct((CAND_LEN, head_total), BF16),
        scratch_shapes=[
            pltpu.VMEM((CAND_LEN, width), BF16),
            pltpu.VMEM((1, width), F32),
            pltpu.VMEM(w_query.shape, BF16),
            pltpu.SemaphoreType.DMA((3,)),
        ],
        compiler_params=pltpu.CompilerParams(vmem_limit_bytes=8 * MIB),
        cost_estimate=pl.CostEstimate(
            flops=2 * CAND_LEN * width * head_total,
            bytes_accessed=2 * width * head_total,
            transcendentals=0,
        ),
        name="project",
    )(*in_hbm(states, gain, w_query))


def block_diagonal(cached, first_head, blocks):
    sources = cached.shape[0]
    blocks[...] = jnp.zeros_like(blocks)
    for head in range(blocks.shape[1] // HEAD_DIM):
        rows = pl.ds(head * sources, sources)
        blocks[rows, pl.ds(head * HEAD_DIM, HEAD_DIM)] = cached[:, first_head + head, :]


def chosen_slots(step, capacity, blocks, routes, experts):
    micro = jnp.clip(step - lax.axis_index("segment"), 0, CAND_DEV - 1)
    route = routes[micro]
    rows = route.shape[1]
    labels = lax.broadcasted_iota(jnp.int32, (experts, rows), 0)
    first, second = route[0:1] == labels, route[1:2] == labels
    place = route
    if blocks > 1:
        place = jnp.where(route < 0, route, route ^ (lax.axis_index("expert") // 2))
    named = jnp.where(first | second, 1.0, 0.0).astype(BF16)
    earlier = lax.broadcasted_iota(jnp.int32, (rows, rows), 0) < lax.broadcasted_iota(
        jnp.int32, (rows, rows), 1
    )
    before = dot(named, jnp.where(earlier, 1.0, 0.0).astype(BF16))
    slots = lax.broadcasted_iota(jnp.int32, (experts * capacity, rows), 0)
    chosen = []
    for mask, row in ((first, 0), (second, 1)):
        slot = jnp.sum(jnp.where(mask, before, 0.0), axis=0, keepdims=True).astype(jnp.int32)
        chosen.append(slots == place[row : row + 1] * capacity + slot)
    return chosen


def gate_kernel(step, capacity, blocks, ffn_input, routes, router, weights):
    experts = router.shape[0]
    micro = jnp.clip(step - lax.axis_index("segment"), 0, CAND_DEV - 1)
    route = routes[micro]
    labels = lax.broadcasted_iota(jnp.int32, (experts, route.shape[1]), 0)
    logits = dot(router[...], ffn_input[...], ((1,), (1,)))
    picked = [
        jnp.sum(jnp.where(route[row : row + 1] == labels, logits, 0.0), axis=0, keepdims=True)
        for row in range(2)
    ]
    gate_first = jax.nn.sigmoid(picked[0] - picked[1])
    gate_second = 1.0 - gate_first
    chosen = chosen_slots(step, capacity, blocks, routes, experts)
    weights[...] = jnp.where(chosen[0], gate_first, 0.0) + jnp.where(chosen[1], gate_second, 0.0)


def gate(step, capacity, blocks, ffn_input, routes, router):
    experts, width = router.shape
    return pl.pallas_call(
        functools.partial(gate_kernel, step, capacity, blocks),
        in_specs=[VMEM] * 3,
        out_specs=VMEM,
        out_shape=jax.ShapeDtypeStruct((experts * capacity, CAND_LEN), F32),
        compiler_params=pltpu.CompilerParams(vmem_limit_bytes=8 * MIB),
        cost_estimate=pl.CostEstimate(
            flops=2 * CAND_LEN * width * 128, bytes_accessed=2 * ffn_input.size, transcendentals=0
        ),
        name="gate",
    )(ffn_input, *in_vmem(routes, router))


def has_candidate(step):
    micro = step - lax.axis_index("segment")
    return (micro >= 0) & (micro < CAND_DEV)


def later_attend_kernel(step, capacity, blocks, *refs):
    @pl.when(has_candidate(step))
    def _():
        attend_kernel(step, capacity, blocks, *refs)


def attend_kernel(step, capacity, blocks, *refs):
    segment = lax.axis_index("segment")
    if step == 0:
        (cand_len, queries_in, cached, states, routes_hbm, attn_gain, ffn_gain, router_hbm,
         query_hbm, out_hbm, expert_hbm), refs = refs[:11], refs[11:]
        after_ref, ffn_ref, *outgoing = refs[: 2 + blocks]
        (routes, gains, router, w_query, w_out, keys, values, following, expert_mat,
         fresh, route_buf, sems) = refs[2 + blocks :]
        fills = (
            (states.at[pl.ds(0, CAND_LEN), :], fresh),
            (ffn_gain, gains.at[1]),
            (out_hbm, w_out),
            (router_hbm, router),
            (routes_hbm, route_buf),
            (attn_gain, gains.at[0]),
            (states.at[pl.ds(CAND_LEN, CAND_LEN), :], following),
            (query_hbm, w_query),
            (expert_hbm, expert_mat),
        )
        copies = [pltpu.make_async_copy(*pair, sems.at[i]) for i, pair in enumerate(fills)]
        for copy in copies:
            copy.start()
        head_count = w_out.shape[0] // HEAD_DIM
        block_diagonal(cached, 0, keys)
        block_diagonal(cached, head_count, values)
        queries = queries_in[...]
        copies[0].wait()
        carried = fresh[...].astype(F32)
        copies[4].wait()
        copies = copies[:4] + copies[5:]
        position = lax.broadcasted_iota(jnp.int32, (1, CAND_LEN), 1)
        for micro in range(CAND_DEV):
            route = route_buf[:, micro * CAND_LEN : (micro + 1) * CAND_LEN]
            routes[micro] = jnp.where(position < cand_len[micro], route, -1)
    else:
        incoming, refs = refs[0], refs[1:]
        current = incoming[...]
        if step < CAND_DEV:
            current, refs = jnp.where(segment == 0, refs[0][...], current), refs[1:]
        (routes, gains, router, w_query, w_out, keys, values, after_ref, ffn_ref), refs = (
            refs[:9], refs[9:]
        )
        outgoing, marks = refs[:blocks], refs[blocks:]
        for mark in marks:
            mark[...] = current[: mark.shape[0], : mark.shape[1]]
        carried = current.astype(F32)
        normed = normalize(carried, gains[0]).astype(BF16)
        queries = dot(normed, w_query[...]).astype(BF16)

    rows = carried.shape[0]
    sources = keys.shape[0] * HEAD_DIM // keys.shape[1]
    scores = dot(keys[...], queries, ((1,), (1,))) * (1.0 / math.sqrt(HEAD_DIM))
    scores = scores.reshape(-1, sources, rows)
    exponent = jnp.exp(scores - jnp.max(scores, axis=1, keepdims=True))
    share = exponent / jnp.sum(exponent, axis=1, keepdims=True)
    share = share.reshape(-1, rows).astype(BF16)
    context = dot(share, values[...], ((0,), (0,))).astype(BF16)
    if step == 0:
        copies[1].wait()
        copies[2].wait()
    after_attn = carried + dot(context, w_out[...])
    after_ref[...] = after_attn
    ffn_input = normalize(after_attn, gains[1]).astype(BF16)

    rows_in_slots = chosen_slots(step, capacity, blocks, routes, router.shape[0])
    select = jnp.where(rows_in_slots[0] | rows_in_slots[1], 1.0, 0.0).astype(BF16)
    buffers = dot(select, ffn_input)
    for buffer, block in zip(split(buffers, blocks), outgoing):
        block[...] = buffer.astype(BF16)
    ffn_ref[...] = ffn_input
    if step == 0:
        for copy in copies[3:]:
            copy.wait()


def attend(step, capacity, blocks, marked, sources, kept):
    if step == 0:
        cand_len, queries, cached, *params = sources
        _, routes, _, _, router_t, w_query, w_out, expert_mat = params
        head_total, width = w_out.shape
        diagonal = (cached.shape[0] * head_total // HEAD_DIM, head_total)
        kept_shapes = [
            pltpu.VMEM((CAND_DEV, 2, CAND_LEN), jnp.int32),
            pltpu.VMEM((2, 1, width), F32),
            *(pltpu.VMEM(array.shape, BF16) for array in (router_t, w_query, w_out)),
            pltpu.VMEM(diagonal, BF16),
            pltpu.VMEM(diagonal, BF16),
            pltpu.VMEM((CAND_LEN, width), BF16),
            pltpu.VMEM(expert_mat.shape, BF16),
        ]
        inputs = [*in_hbm(cand_len), queries, cached, *in_hbm(*params)]
        specs = [SMEM, VMEM, VMEM] + [HBM] * len(params)
        scratch = [
            pltpu.VMEM((CAND_LEN, width), BF16),
            pltpu.VMEM(routes.shape, jnp.int32),
            pltpu.SemaphoreType.DMA((9,)),
        ]
    else:
        _, _, router_t, _, w_out, *_ = kept
        head_total, width = w_out.shape
        kept_shapes = [jax.ShapeDtypeStruct((16, 128), BF16)] if marked else []
        scratch = []
        inputs = [*sources, *in_vmem(*kept)]
        specs = [VMEM] * len(inputs)
    slot_count = router_t.shape[0] * capacity
    outs = pl.pallas_call(
        functools.partial(
            later_attend_kernel if step else attend_kernel, step, capacity, blocks
        ),
        in_specs=specs,
        out_specs=[VMEM] * (2 + blocks + len(kept_shapes)),
        out_shape=[
            jax.ShapeDtypeStruct((CAND_LEN, width), F32),
            jax.ShapeDtypeStruct((CAND_LEN, width), BF16),
            *[jax.ShapeDtypeStruct((slot_count // blocks, width), BF16)] * blocks,
            *kept_shapes,
        ],
        scratch_shapes=scratch,
        compiler_params=pltpu.CompilerParams(vmem_limit_bytes=8 * MIB),
        cost_estimate=pl.CostEstimate(
            flops=6 * CAND_LEN * width * head_total,
            bytes_accessed=4 * width * head_total + 8 * CAND_LEN * width,
            transcendentals=0,
        ),
        name="attend",
    )(*inputs)
    return outs[:2], outs[2 : 2 + blocks], outs[2 + blocks :]


def load_kernel(count, _, *refs):
    sources, mats, sems = refs[:count], refs[count : 2 * count], refs[-1]
    copies = [
        pltpu.make_async_copy(source, mat, sems.at[i])
        for i, (source, mat) in enumerate(zip(sources, mats))
    ]
    for copy in copies:
        copy.start()
    for copy in copies:
        copy.wait()


def load(after, mats):
    return pl.pallas_call(
        functools.partial(load_kernel, len(mats)),
        in_specs=[VMEM] + [HBM] * len(mats),
        out_specs=[VMEM] * len(mats),
        out_shape=[pltpu.VMEM(mat.shape, BF16) for mat in mats],
        scratch_shapes=[pltpu.SemaphoreType.DMA((len(mats),))],
        compiler_params=pltpu.CompilerParams(vmem_limit_bytes=8 * MIB),
        cost_estimate=pl.CostEstimate(
            flops=0, bytes_accessed=2 * sum(mat.size for mat in mats), transcendentals=0
        ),
        name="load",
    )(after, *in_hbm(*mats))


def expert_kernel(blocks, stream, mark_count, *refs):
    refs = refs[mark_count:]
    rows_in, refs = refs[:blocks], refs[blocks:]
    (own_in, own_down), refs = refs[:2], refs[2:]
    if stream:
        sources, served, refs = refs[:2], refs[2 : 2 + blocks], refs[2 + blocks :]
        other_in, other_down, rows, own_hidden, other_hidden, partial, sems = refs
    else:
        (other_in, other_down), refs = refs[:2], refs[2:]
        served, (rows, own_hidden, other_hidden) = refs[:blocks], refs[blocks:]
    size = STREAM_CHUNK if stream else HIDDEN_CHUNK
    chunks = [pl.ds(start, size) for start in range(0, own_in.shape[1], size)]

    def fill(source, mat):
        copies = [
            pltpu.make_async_copy(
                sources[source].at[:, lanes], mat.at[:, lanes], sems.at[source, i]
            )
            for i, lanes in enumerate(chunks)
        ]
        for copy in copies:
            copy.start()
        return copies

    def hidden_of(mat, units):
        return jnp.maximum(dot(rows[...], mat[:, units]), 0.0).astype(BF16)

    def serve(out, lanes):
        for part, block in zip(split(out, blocks), served):
            block[:, lanes] = part.astype(BF16)

    if not stream:
        rows[...] = joined(rows_in)
        for units in chunks:
            own_hidden[:, units] = hidden_of(own_in, units)
            other_hidden[:, units] = hidden_of(other_in, units)
        for lanes in chunks:
            out = dot(own_hidden[...], own_down[:, lanes])
            serve(out + dot(other_hidden[...], other_down[:, lanes]), lanes)
        return

    other_in_copies = fill(0, other_in)
    other_down_copies = fill(1, other_down)
    rows[...] = joined(rows_in)
    for units in chunks:
        own_hidden[:, units] = hidden_of(own_in, units)
    for lanes in chunks:
        partial[:, lanes] = dot(own_hidden[...], own_down[:, lanes])
    for units, copy in zip(chunks, other_in_copies):
        copy.wait()
        other_hidden[:, units] = hidden_of(other_in, units)
    for lanes, copy in zip(chunks, other_down_copies):
        copy.wait()
        serve(partial[:, lanes] + dot(other_hidden[...], other_down[:, lanes]), lanes)


def expert_rows(rows_in, mats, step, marks=()):
    blocks, stream = len(rows_in), step == 0
    width = rows_in[0].shape[1]
    count = blocks * rows_in[0].shape[0]
    units = mats[0].shape[1]
    scratch = [
        pltpu.VMEM((count, width), BF16),
        pltpu.VMEM((count, units), BF16),
        pltpu.VMEM((count, units), BF16),
    ]
    out_shape = [jax.ShapeDtypeStruct(rows.shape, BF16) for rows in rows_in]
    if stream:
        scratch += [
            pltpu.VMEM((count, width), F32),
            pltpu.SemaphoreType.DMA((2, units // STREAM_CHUNK)),
        ]
        out_shape += [pltpu.VMEM(mat.shape, BF16) for mat in mats[2:]]
    outs = pl.pallas_call(
        functools.partial(expert_kernel, blocks, stream, len(marks)),
        in_specs=[VMEM] * (len(marks) + blocks + 2) + [HBM if stream else VMEM] * 2,
        out_specs=[VMEM] * len(out_shape),
        out_shape=out_shape,
        scratch_shapes=scratch,
        compiler_params=pltpu.CompilerParams(vmem_limit_bytes=8 * MIB),
        cost_estimate=pl.CostEstimate(
            flops=8 * count * width * units,
            bytes_accessed=8 * width * units + 4 * count * width,
            transcendentals=0,
        ),
        name="experts",
    )(*marks, *rows_in, *in_vmem(*mats[:2]), *(in_hbm if stream else in_vmem)(*mats[2:]))
    return outs[:blocks], ((*mats[:2], *outs[blocks:]) if stream else mats)


def mixed(after_attn, weights, blocks):
    gates = weights[...]
    coarse = gates.astype(BF16)
    fine = (gates - coarse.astype(F32)).astype(BF16)
    rows = joined(blocks)
    mixture = dot(coarse, rows, ((0,), (0,))) + dot(fine, rows, ((0,), (0,)))
    return (after_attn[...] + mixture).astype(BF16)


def combine_kernel(blocks, after_attn, weights, *refs):
    result = refs[blocks]
    result[...] = mixed(after_attn, weights, refs[:blocks])


def place_kernel(blocks, after_attn, weights, *refs):
    served, earlier, (output, result, sems) = refs[:blocks], refs[blocks:-3], refs[-3:]
    segment = lax.axis_index("segment")

    def place(source, micro):
        rows = pl.ds(micro * CAND_LEN, CAND_LEN)
        return pltpu.make_async_copy(source, output.at[rows, :], sems.at[micro])

    last = len(earlier)
    for micro in range(CAND_DEV):
        for step in range(micro, last):

            @pl.when(segment + micro == step)
            def _():
                place(earlier[step], micro).start()

    result[...] = mixed(after_attn, weights, served)
    for micro in range(CAND_DEV):

        @pl.when(segment + micro == last)
        def _():
            place(result, micro).start()

    for micro in range(CAND_DEV):
        place(result, micro).wait()


def combine(after_attn, weights, served, earlier=()):
    rows, width = after_attn.shape
    inputs = [after_attn, weights, *served]
    scratch = []
    out_shape, out_spec = jax.ShapeDtypeStruct((rows, width), BF16), VMEM
    if earlier:
        inputs += in_vmem(*earlier)
        scratch = [pltpu.VMEM((rows, width), BF16), pltpu.SemaphoreType.DMA((CAND_DEV,))]
        out_shape, out_spec = jax.ShapeDtypeStruct((CAND_DEV * rows, width), BF16), HBM
    return pl.pallas_call(
        functools.partial(place_kernel if earlier else combine_kernel, len(served)),
        in_specs=[VMEM] * len(inputs),
        out_specs=out_spec,
        out_shape=out_shape,
        scratch_shapes=scratch,
        compiler_params=pltpu.CompilerParams(vmem_limit_bytes=8 * MIB),
        cost_estimate=pl.CostEstimate(
            flops=4 * weights.size * width,
            bytes_accessed=6 * after_attn.size + 2 * weights.shape[0] * width,
            transcendentals=0,
        ),
        name="combine",
    )(*inputs)


def local(
    states, cand_len, routes, enc_kv, attn_gain, ffn_gain, w_query, w_out, w_router, w_in, w_down
):
    n_segment = lax.axis_size("segment")
    n_expert = lax.axis_size("expert")
    model_width = states.shape[1]
    experts = w_router.shape[2]
    capacity = 2 * ((5 * CAND_LEN + 4 * experts - 1) // (4 * experts))
    core_pairs = [(i, i ^ 1) for i in range(n_expert)]
    same_core = [list(range(core, n_expert, 2)) for core in range(2)]
    blocks = experts if experts <= 4 else 1

    def exchange(parts):
        if blocks > 1:
            return [parts[0]] + [
                lax.ppermute(part, "expert", [(i, i ^ (2 * k)) for i in range(n_expert)])
                for k, part in enumerate(parts[1:], 1)
            ]
        rows = parts[0].reshape(experts, capacity, model_width)
        moved = lax.all_to_all(
            rows, "expert", split_axis=0, concat_axis=0, axis_index_groups=same_core, tiled=True
        )
        return [moved.reshape(parts[0].shape)]

    cached = lax.all_to_all(
        spread(enc_kv, n_expert), ("segment", "expert"), split_axis=0, concat_axis=0, tiled=True
    )
    own = (w_in[0, 0], w_down[0, 0])
    other = tuple(lax.ppermute(mat, "expert", core_pairs) for mat in own)

    queries = project(states, attn_gain, w_query[0])
    step_count = CAND_DEV + n_segment - 1
    earlier = []
    kept = ()
    for step in range(step_count):
        if step == 0:
            sources = (
                cand_len, queries, cached, states, routes[0].T, attn_gain, ffn_gain,
                w_router[0].T, w_query[0], w_out[0], own[0],
            )
        elif step < CAND_DEV:
            sources = (incoming, following)
        else:
            sources = (incoming,)
        marked = step > CAND_DEV
        (after_attn, ffn_input), outgoing, left = attend(
            step, capacity, blocks, marked, sources, kept
        )
        if step == 0:
            *kept, following, own_in = left
            expert_mats = (own_in, *load(ffn_input, own[1:]), *other)
        weights = gate(step, capacity, blocks, ffn_input, kept[0], kept[2])
        received = exchange(outgoing)
        marks = ()
        if marked:
            pairs = [(i, i + 1) for i in range(0, n_expert, 2)]
            marks = (lax.ppermute(left[0], "expert", pairs),)
        served, expert_mats = expert_rows(received, expert_mats, step, marks)
        served = exchange(served)
        if step + 1 < step_count:
            result = combine(after_attn, weights, served)
            incoming = lax.ppermute(
                result, "segment", [(i, i + 1) for i in range(n_segment - 1)]
            )
            earlier.append(result)
    output = combine(after_attn, weights, served, earlier)
    return output.reshape(1, CAND_DEV * CAND_LEN, model_width)


def solution(mesh):
    return jax.shard_map(
        local,
        mesh=mesh,
        in_specs=(
            P("expert", None),
            P("expert"),
            P("segment", "expert", None),
            P(None, ("segment", "expert"), None),
            P("segment", None),
            P("segment", None),
            P("segment", None, None),
            P("segment", None, None),
            P("segment", None, None),
            P("segment", "expert", None, None),
            P("segment", "expert", None, None),
        ),
        out_specs=P("segment", "expert", None),
        check_vma=False,
    )
```
